32 devices in a mesh: dp: 8 (over z, x), fsdp: 4 (over y, core).
Axes of the slice: x: 2, y: 2, z: 4, core: 2. Of those that a mesh axis runs over, the one named last changes fastest.
Arguments:
- hidden_in: bfloat16 [8, 2048, 1024], P('dp', 'fsdp'), may hold values from -6 to 6
- params: bfloat16 [12591104], P(('dp', 'fsdp'))
- cotangent: bfloat16 [8, 2048, 1024], P('dp', 'fsdp'), may hold values from -6 to 6
- source_ids: int32 [8], P('dp'), may hold values from 0 to 15
- corpus_weight: float32 [16], replicated, may hold values from 0.3 to 3
- positions: int32 [8, 2048], P('dp', 'fsdp'), may hold values from 0 to 2047, as said below
Outputs:
- output: bfloat16 [8, 2048, 1024], P('dp', 'fsdp')
- input_grad: bfloat16 [8, 2048, 1024], P('dp', 'fsdp')
- param_grads: float32 [12591104], P(('dp', 'fsdp'))
- statistics: float32 [2], replicated
The draws below stay inside these ranges and needn't reach their ends.
Inputs may be any that keep to these rules, and one draw needn't show every extreme that they name: Each row is a pack of documents: a row begins at position 0, positions rise by one along the row and fall back to 0 where a new document starts; some row is a single document.
All inputs are finite; a program needn't handle non-finite values.
Results may differ from the reference program's by a relative error of at most 0.015.
Values may be sent and summed in bfloat16 or wider, within the bound.
A program may use at most 256 MiB of HBM per device.

```python
import math
import jax
import jax.numpy as jnp
from jax import lax

D = 1024
HEADS = 16
HEAD_DIM = 64
FF = 4096
LENGTH = 2048
SOURCES = 16
ROWS = 8
PARAMS = 12591104


def draw_params(key, part):
    key = jax.random.fold_in(key, 5)
    matrix_count = 4 * D * D + 2 * D * FF
    entries = jax.random.normal(key, (matrix_count,), jnp.float32)
    factors = jnp.concatenate([jnp.full((3 * D * D,), 1.0 / math.sqrt(D), jnp.float32), jnp.full((D * D,), 8.0 / math.sqrt(D), jnp.float32), jnp.full((D * FF,), 1.0 / math.sqrt(D), jnp.float32), jnp.full((FF * D,), 1.0 / math.sqrt(FF), jnp.float32)])
    gain_rows = jax.random.uniform(jax.random.fold_in(key, 1), (4, D), jnp.float32, 0.5, 1.5)
    shifts = jax.random.uniform(jax.random.fold_in(key, 2), (4, D), jnp.float32, -0.5, 0.5)
    norm_rows = jnp.stack([gain_rows, shifts], axis=1).reshape(8 * D)
    return jnp.concatenate([entries * factors, norm_rows]).astype(jnp.bfloat16)


def draw_positions(key, part):
    key = jax.random.fold_in(key, 11)
    spacing = max(4, LENGTH // 8)
    picks = jax.random.randint(key, (ROWS, LENGTH), 0, spacing, dtype=jnp.int32)
    index_row = jnp.arange(LENGTH, dtype=jnp.int32)[None, :]
    starts = (picks == 0) | (index_row == 0)
    row_index = jnp.arange(ROWS, dtype=jnp.int32)[:, None]
    starts = jnp.where(row_index == 0, index_row == 0, starts)
    marked = jnp.where(starts, index_row, jnp.zeros_like(picks))
    last_start = lax.cummax(marked, axis=1)
    return (index_row - last_start).astype(jnp.int32)


def plant(drawn, rng, smallest, top_value):
    shape = drawn.shape
    index_at = [jax.random.randint(jax.random.fold_in(rng, axis), (), 0, shape[axis]) for axis in range(len(shape))]
    drawn = drawn.at[tuple(index_at)].set(smallest)
    longest = shape.index(max(shape))
    index_at[longest] = (index_at[longest] + 1) % shape[longest]
    return drawn.at[tuple(index_at)].set(top_value)


def level_of(rng, shape, shards, low, largest):
    def one(axis_at, blocks):
        heights = jax.random.uniform(jax.random.fold_in(jax.random.fold_in(rng, 6), axis_at), (blocks,), jnp.float32, low / len(shards), largest / len(shards))
        return jnp.repeat(jnp.exp(heights), shape[axis_at] // blocks).reshape((-1,) + (1,) * (len(shape) - axis_at - 1))

    factor_of = one(*shards[0])
    for cut in shards[1:]:
        factor_of = factor_of * one(*cut)
    return factor_of


def scatter_about(rng, extent, scale, limit, split=(), kind=jnp.bfloat16):
    array = scale * jax.random.normal(rng, extent, jnp.float32)
    if split:
        array = array * level_of(rng, extent, split, -0.22, 0.18)
    return jnp.clip(array, -limit, limit).astype(kind)


def setup_inputs(seed: int = 0) -> dict:
    arg_keys = jax.random.split(jax.random.key(seed), 7)
    hidden_in = scatter_about(arg_keys[0], (ROWS, LENGTH, D), 1.0, 6.0, ((0, 8), (1, 4)))
    params = draw_params(jax.random.fold_in(arg_keys[6], 71), 0)
    cotangent = scatter_about(arg_keys[2], (ROWS, LENGTH, D), 1.0, 6.0, ((0, 8), (1, 4)))
    source_ids = plant(jax.random.randint(arg_keys[3], (ROWS,), 0, SOURCES), jax.random.fold_in(arg_keys[3], 1), 0, SOURCES - 1).astype(jnp.int32)
    corpus_weight = jnp.clip(jnp.exp(jax.random.uniform(arg_keys[4], (SOURCES,), jnp.float32, math.log(0.3), math.log(3.0))), 0.3, 3.0)
    positions = draw_positions(jax.random.fold_in(arg_keys[6], 71), 0)
    return {"hidden_in": hidden_in, "params": params, "cotangent": cotangent, "source_ids": source_ids, "corpus_weight": corpus_weight, "positions": positions}


EPSILON = 1e-05
MASKED = -1e+30
HIGHEST = lax.Precision.HIGHEST

@jax.custom_vjp
def low(v):
    return lax.optimization_barrier(v.astype(jnp.bfloat16)).astype(jnp.float32)

@jax.custom_vjp
def low_back(v):
    return v

def low_keep(v):
    return (low(v), None)

def low_pass(kept, grad):
    return (grad,)

def back_keep(v):
    return (v, None)

def back_low(kept, grad):
    return (low(grad),)
low.defvjp(low_keep, low_pass)
low_back.defvjp(back_keep, back_low)

def unpack(flat_params):
    end_qkv = 3 * D * D
    end_out = end_qkv + D * D
    end_up = end_out + D * FF
    end_down = end_up + FF * D
    return (flat_params[:end_qkv].reshape(D, 3 * D), flat_params[end_qkv:end_out].reshape(D, D), flat_params[end_out:end_up].reshape(D, FF), flat_params[end_up:end_down].reshape(FF, D), flat_params[end_down:].reshape(8, D))

def layer_norm(values, gain_row, shift_row):
    center = values - lax.optimization_barrier(jnp.mean(values, axis=-1, keepdims=True))
    spread = lax.optimization_barrier(jnp.mean(center * center, axis=-1, keepdims=True))
    return center * lax.rsqrt(spread + EPSILON) * gain_row + shift_row

def rotate(values, cosine, sine_table):
    half_dim = HEAD_DIM // 2
    front_half = values[..., :half_dim]
    back_half = values[..., half_dim:]
    return jnp.concatenate([front_half * cosine - back_half * sine_table, back_half * cosine + front_half * sine_table], axis=-1)

def attend(queries, key_rows, value_rows):
    block_rows = min(512, LENGTH)
    score_scale = 1.0 / math.sqrt(HEAD_DIM)
    key_index = jnp.arange(LENGTH)

    def one_block(inputs):
        query_block, first_row = inputs
        scores = jnp.einsum('qhd,khd->hqk', query_block, key_rows, precision=HIGHEST) * score_scale
        scores = low_back(scores)
        query_index = first_row + jnp.arange(block_rows)
        allowed = key_index[None, :] <= query_index[:, None]
        scores = jnp.where(allowed[None], scores, MASKED)
        weights = low(jax.nn.softmax(scores, axis=-1))
        return jnp.einsum('hqk,khd->qhd', weights, value_rows, precision=HIGHEST)
    blocks = queries.reshape(LENGTH // block_rows, block_rows, HEADS, HEAD_DIM)
    firsts = jnp.arange(LENGTH // block_rows) * block_rows
    result = lax.map(jax.checkpoint(one_block), (blocks, firsts))
    return result.reshape(LENGTH, D)

def block_row(flat_params, hidden_row, cosine, sine_table):
    w_qkv, w_out, w_up, w_down, norm_rows = unpack(flat_params)
    normed = low(layer_norm(hidden_row, norm_rows[0], norm_rows[1]))
    mixed_rows = low_back(jnp.dot(normed, w_qkv, precision=HIGHEST))
    shape_heads = (LENGTH, HEADS, HEAD_DIM)
    queries = low(rotate(mixed_rows[:, :D].reshape(shape_heads), cosine, sine_table))
    key_rows = low(rotate(mixed_rows[:, D:2 * D].reshape(shape_heads), cosine, sine_table))
    value_rows = low(mixed_rows[:, 2 * D:].reshape(shape_heads))
    attended = low(low_back(attend(queries, key_rows, value_rows)))
    branch = low_back(jnp.dot(attended, w_out, precision=HIGHEST))
    residual = hidden_row + layer_norm(branch, norm_rows[2], norm_rows[3])
    entered = low(layer_norm(residual, norm_rows[4], norm_rows[5]))
    lifted = low_back(jnp.dot(entered, w_up, precision=HIGHEST))
    activated = low(jax.nn.gelu(lifted))
    lowered = low_back(jnp.dot(activated, w_down, precision=HIGHEST))
    output = residual + layer_norm(lowered, norm_rows[6], norm_rows[7])
    squares = jnp.stack([jnp.sum(lax.optimization_barrier(jnp.mean(branch * branch, axis=-1))), jnp.sum(lax.optimization_barrier(jnp.mean(lowered * lowered, axis=-1)))])
    return (output, squares)

def reference(hidden_in, params, cotangent, source_ids, corpus_weight, positions):
    flat_params = params.astype(jnp.float32)
    half_dim = HEAD_DIM // 2
    frequency = jnp.exp(jnp.arange(half_dim, dtype=jnp.float32) * (-2.0 * math.log(10000.0) / HEAD_DIM))
    source_table = jnp.arange(SOURCES)
    row_scale = lax.optimization_barrier(jnp.sum(jnp.where(source_ids[:, None] == source_table[None, :], corpus_weight[None, :], 0.0), axis=1))

    def step(total, row_inputs):
        hidden_row, cot_row, position_row, scale_row = row_inputs
        angles = position_row.astype(jnp.float32)[:, None] * frequency[None, :]
        cosine = jnp.cos(angles)[:, None, :]
        sine_table = jnp.sin(angles)[:, None, :]

        def forward(flat_values, hidden_values):
            return block_row(flat_values, hidden_values, cosine, sine_table)
        output, pullback, squares = jax.vjp(forward, flat_params, hidden_row.astype(jnp.float32), has_aux=True)
        grad_params, grad_input = pullback(cot_row.astype(jnp.float32) * scale_row)
        return (total + grad_params, (output.astype(jnp.bfloat16), grad_input.astype(jnp.bfloat16), squares))
    param_grads, (output, input_grad, squares) = lax.scan(step, jnp.zeros((PARAMS,), jnp.float32), (hidden_in, cotangent, positions, row_scale))
    statistics = lax.optimization_barrier(jnp.sum(squares, axis=0)) / (ROWS * LENGTH)
    return (output, input_grad, param_grads, statistics)
```

```python
import functools
import math

import jax
import jax.numpy as jnp
from jax import lax
from jax.experimental import pallas as pl
from jax.experimental.pallas import tpu as pltpu
from jax.sharding import PartitionSpec as P

D = 1024
HEADS = 16
HEAD_DIM = 64
FF = 4096
EPSILON = 1e-05
MASKED = -1e30
SCALE = 1.0 / math.sqrt(HEAD_DIM)
LOG2E = 1.4426950408889634

MESH = pl.DeviceIdType.MESH
bf = jnp.bfloat16
f32 = jnp.float32
SHARD = 384
NATURAL = 3074
MIB = 2**20

VM = pl.BlockSpec(memory_space=pltpu.VMEM)
ANY = pl.BlockSpec(memory_space=pl.ANY)
DMA = pltpu.SemaphoreType.DMA


def params_for(collective=None, mib=48):
    if collective is None:
        return pltpu.CompilerParams(vmem_limit_bytes=mib * MIB)
    return pltpu.CompilerParams(
        collective_id=collective, has_side_effects=True, vmem_limit_bytes=mib * MIB
    )


def coords():
    dp, fs = lax.axis_index("dp"), lax.axis_index("fsdp")
    return dp // 2, lax.rem(dp, 2), fs // 2, lax.rem(fs, 2)


def dev(z, x, y, c):
    return (z * 2 + x, y * 2 + c)


def linear(i):
    return (i // 4, lax.rem(i, 4))


def remote(src, dst, send, recv, to):
    return pltpu.make_async_remote_copy(
        src_ref=src, dst_ref=dst, send_sem=send, recv_sem=recv, device_id=to, device_id_type=MESH
    )


def greet(bar, device):
    pl.semaphore_signal(bar, inc=1, device_id=device, device_id_type=MESH)


def meet_neighbours(z, x, y, c, plane, more=0):
    bar = pltpu.get_barrier_semaphore()
    for device in plane:
        greet(bar, device)

    @pl.when(z < 3)
    def _():
        greet(bar, dev(z + 1, x, y, c))

    @pl.when(z > 0)
    def _():
        greet(bar, dev(z - 1, x, y, c))

    line = jnp.where(z < 3, 1, 0) + jnp.where(z > 0, 1, 0)
    pl.semaphore_wait(bar, len(plane) + line + more)


def add_rows(dst, *srcs):
    total = srcs[0][...].astype(f32)
    for part in srcs[1:]:
        total = total + part[...].astype(f32)
    dst[...] = total.astype(dst.dtype)


def add_tiles(dst, rows, *srcs):
    for at in range(0, rows, 16):
        add_rows(dst.at[at : at + 16], *[part.at[at : at + 16] for part in srcs])


def first_kernel(
    p_ref, h_ref, pos_ref,
    hid_ref, wq_ref, can_ref, nrm_ref, posall_ref,
    ext, tail, units, us, ur, hs, hr, ns, nr, ps, pr, ls,
):
    z, x, y, c = coords()
    xn, yn, cn = 1 - x, 1 - y, 1 - c
    s = (z * 2 + x) * 4 + y * 2 + c
    f = y * 2 + c
    nxt, prv = lax.rem(s + 1, 32), lax.rem(s + 31, 32)
    core = dev(z, x, y, cn)
    xs, xo, ys, yo = dev(z, xn, y, c), dev(z, xn, y, cn), dev(z, x, yn, c), dev(z, x, yn, cn)
    bar = pltpu.get_barrier_semaphore()
    greet(bar, linear(nxt))
    greet(bar, linear(prv))

    @pl.when(s != 31)
    def _():
        greet(bar, (7, 3))

    ext[64 : 64 + NATURAL, :] = p_ref[...].astype(f32)
    tail[...] = ext[NATURAL : NATURAL + 64, :]
    more = 2 + jnp.where(s == 31, 31, 0)
    meet_neighbours(z, x, y, c, [core, xs, xo, ys, yo], more)

    halves, half = 2, 256

    def hidden_rows(owner, k):
        return hid_ref.at[pl.ds(pl.multiple_of(owner * 512 + k * half, 16), half)]

    def hidden_own(k):
        return h_ref.at[pl.ds(k * half, half)]

    over_y, over_core, over_both = yn * 2 + c, y * 2 + cn, yn * 2 + cn
    halo = remote(tail, ext.at[0:64], ns.at[0], nr.at[0], linear(nxt))
    halo.start()
    sent = []
    for k in range(halves):
        sent.append(remote(hidden_own(k), hidden_rows(f, k), hs.at[0, k], hr.at[0, k], ys))
        sent.append(remote(hidden_own(k), hidden_rows(f, k), hs.at[1, k], hr.at[1, k], core))
    for i, to in enumerate([core, ys, yo]):
        sent.append(remote(pos_ref, posall_ref.at[f], ps.at[i], pr.at[i], to))
    for copy in sent:
        copy.start()
    own = [
        pltpu.make_async_copy(
            h_ref, hid_ref.at[pl.ds(pl.multiple_of(f * 512, 512), 512)], ls.at[0]
        ),
        pltpu.make_async_copy(pos_ref, posall_ref.at[f], ls.at[1]),
    ]
    for copy in own:
        copy.start()
    halo.wait()
    base = 64 - 2 * s

    def lines(first, count, apart, k):
        return ext[pl.ds(base + 8 * first + k, count, stride=8 * apart), :].astype(bf)

    def order(to, first, count, apart):
        for j in range(apart):
            for k in range(8):
                can_ref[to + j * count : to + (j + 1) * count, 128 * k : 128 * k + 128] = lines(
                    first + j, count, apart, k
                )

    @pl.when(z == 0)
    def _():
        for j in range(3):
            for k in range(8):
                at = 128 * (k % 2)
                units[k // 2, j, :, at : at + 128] = lines(j, 128, 3, k)
        can_ref[...] = jnp.zeros_like(can_ref)

    @pl.when((s == 8) | (s == 9) | (s >= 22))
    def _():
        order(0, 0, 384, 1)

    @pl.when(s == 10)
    def _():
        order(0, 0, 256, 1)
        order(256, 256, 32, 4)

    @pl.when((s >= 11) & (s <= 20))
    def _():
        order(0, 0, 96, 4)

    @pl.when(s == 21)
    def _():
        order(0, 0, 32, 4)
        order(128, 128, 256, 1)

    def norm_send(i):
        return remote(nrm_ref, nrm_ref, ns.at[1 + i], nr.at[1], linear(i))

    @pl.when(s == 31)
    def _():
        for k in range(8):
            nrm_ref[:, 128 * k : 128 * k + 128] = ext[pl.ds(base + 8 * 384 + k, 8, stride=8), :]

        def go(i, _):
            norm_send(i).start()
            return 0

        lax.fori_loop(0, 31, go, 0)

    slots = [yn * 2 + c, yn * 2 + cn, y * 2 + cn, y * 2 + c]

    def target(xx, yy, cc):
        at = pl.multiple_of((xx * 4 + yy * 2 + cc) * 128, 128)
        return wq_ref.at[:, pl.ds(at, 128)]

    def up(q):
        unit = units.at[slots[q]]
        return remote(unit, unit, us.at[0, q], ur.at[0, q], dev(z + 1, x, y, c))

    def arrive(ref, sem):
        remote(ref, ref, us.at[0, 0], sem, core).wait_recv()

    mine = target(x, y, c)
    for q in range(4):
        unit = units.at[slots[q]]

        @pl.when(z > 0)
        def _():
            arrive(unit, ur.at[0, q])

        @pl.when(z < 3)
        def _():
            up(q).start()

        if q == 0:
            out = [remote(unit, mine, us.at[1, 0], ur.at[1, 0], ys)]
        elif q == 1:
            out = [remote(unit, mine, us.at[1, 1], ur.at[1, 1], yo)]
        elif q == 2:
            out = [
                remote(unit, mine, us.at[1, 2], ur.at[1, 2], xo),
                remote(unit, mine, us.at[1, 3], ur.at[1, 3], core),
            ]
        else:
            out = [remote(unit, mine, us.at[2, 0], ur.at[2, 0], xs)]
            copy = pltpu.make_async_copy(unit, mine, ls.at[2])
            copy.start()
            own.append(copy)
        for copy in out:
            copy.start()
        sent += out
    for i, cc in enumerate((c, cn)):
        ref = target(x, yn, cc)
        arrive(ref, ur.at[1, i])
        copy = remote(ref, ref, us.at[2, 1 + i], ur.at[2, 1 + i], xs)
        copy.start()
        sent.append(copy)
    for k in range(halves):
        ref = hidden_rows(over_y, k)
        arrive(ref, hr.at[0, k])
        copy = remote(ref, ref, hs.at[2, k], hr.at[2, k], core)
        copy.start()
        sent.append(copy)
    arrive(target(xn, y, cn), ur.at[1, 2])
    arrive(target(x, y, cn), ur.at[1, 3])
    arrive(target(xn, y, c), ur.at[2, 0])
    arrive(target(xn, yn, c), ur.at[2, 1])
    arrive(target(xn, yn, cn), ur.at[2, 2])
    for k in range(halves):
        arrive(hidden_rows(over_core, k), hr.at[1, k])
        arrive(hidden_rows(over_both, k), hr.at[2, k])
    for i, owner in enumerate([over_core, over_y, over_both]):
        arrive(posall_ref.at[owner], pr.at[i])
    for copy in sent:
        copy.wait_send()

    @pl.when(z < 3)
    def _():
        for q in range(4):
            up(q).wait_send()

    for copy in own:
        copy.wait()

    @pl.when(s == 31)
    def _():
        def go(i, _):
            norm_send(i).wait_send()
            return 0

        lax.fori_loop(0, 31, go, 0)

    @pl.when(s != 31)
    def _():
        arrive(nrm_ref, nr.at[1])


def first_gather(share, hidden, places):
    shape = jax.ShapeDtypeStruct
    return pl.pallas_call(
        first_kernel,
        out_shape=(
            shape((2048, D), bf),
            shape((3, D, 256), bf),
            shape((SHARD, D), bf),
            shape((8, D), f32),
            shape((4, 8, 128), f32),
        ),
        in_specs=[VM, VM, VM],
        out_specs=(ANY, ANY, VM, VM, VM),
        scratch_shapes=[
            pltpu.VMEM((64 + NATURAL + 6, 128), f32),
            pltpu.VMEM((64, 128), f32),
            pltpu.VMEM((4, 3, 128, 256), bf),
            DMA((3, 4)), DMA((3, 4)), DMA((3, 2)), DMA((3, 2)),
            DMA((32,)), DMA((2,)), DMA((3,)), DMA((3,)), DMA((3,)),
        ],
        compiler_params=params_for(0, 32),
    )(share, hidden, places)


CHUNKS = 4
CHUNK = SHARD // CHUNKS
UNITS = 3 * CHUNKS
OVER_X = 48


def gather_kernel(c_ref, g_ref, ss, rs, ls):
    z, x, y, c = coords()
    xn, yn, cn = 1 - x, 1 - y, 1 - c
    to_x, to_y, to_core = dev(z, xn, y, c), dev(z, x, yn, c), dev(z, x, y, cn)
    lag, core_lag = 2, 4

    def rows(zz, xx, yy, cc, k, low=0, count=CHUNK):
        s = (zz * 2 + xx) * 4 + yy * 2 + cc - 8
        return g_ref.at[pl.ds(pl.multiple_of(s * SHARD + k * CHUNK + low, 16), count)]

    local = pltpu.make_async_copy(c_ref, rows(jnp.maximum(z, 1), x, y, c, 0, 0, SHARD), ls)

    @pl.when(z >= 1)
    def _():
        local.start()

    meet_neighbours(z, x, y, c, [to_x, to_y, to_core])

    @pl.when(z >= 1)
    def _():
        local.wait()

    ZU, ZD, XO, YO, CO, XD, YD, CX, CY, CXD, CYD = range(11)

    def unit(i):
        r = i // CHUNKS
        k = i - r * CHUNKS
        first = jnp.maximum(z, 1)
        second = jnp.where(z == 2, 1, 2)
        third = jnp.where(z <= 2, 3, 1)
        zz = jnp.where(r == 0, first, jnp.where(r == 1, second, third))
        return zz, k, (zz - 1) * CHUNKS + k

    def send(kind, i):
        zz, k, q = unit(i)
        ref, to = {
            ZU: lambda: (rows(zz, x, y, c, k), dev(z + 1, x, y, c)),
            ZD: lambda: (rows(zz, x, y, c, k), dev(z - 1, x, y, c)),
            XO: lambda: (rows(zz, x, y, c, k), to_x),
            YO: lambda: (rows(zz, x, y, c, k), to_y),
            CO: lambda: (rows(zz, x, y, c, k), to_core),
            YD: lambda: (rows(zz, xn, y, c, k, OVER_X, CHUNK - OVER_X), to_y),
            XD: lambda: (rows(zz, x, yn, c, k, 0, OVER_X), to_x),
            CX: lambda: (rows(zz, xn, y, c, k), to_core),
            CY: lambda: (rows(zz, x, yn, c, k), to_core),
            CXD: lambda: (rows(zz, xn, yn, c, k, 0, OVER_X), to_core),
            CYD: lambda: (rows(zz, xn, yn, c, k, OVER_X, CHUNK - OVER_X), to_core),
        }[kind]()
        return remote(ref, ref, ss.at[kind, q], rs.at[kind, q], to)

    def arrive(kind, i):
        zz, k, q = unit(i)
        ref = {
            ZU: lambda: rows(zz, x, y, c, k),
            ZD: lambda: rows(zz, x, y, c, k),
            XO: lambda: rows(zz, xn, y, c, k),
            YO: lambda: rows(zz, x, yn, c, k),
            XD: lambda: rows(zz, xn, yn, c, k, 0, OVER_X),
            YD: lambda: rows(zz, xn, yn, c, k, OVER_X, CHUNK - OVER_X),
            CO: lambda: rows(zz, x, y, cn, k),
            CX: lambda: rows(zz, xn, y, cn, k),
            CY: lambda: rows(zz, x, yn, cn, k),
            CXD: lambda: rows(zz, xn, yn, cn, k, 0, OVER_X),
            CYD: lambda: rows(zz, xn, yn, cn, k, OVER_X, CHUNK - OVER_X),
        }[kind]()
        remote(ref, ref, ss.at[kind, q], rs.at[kind, q], to_core).wait_recv()

    def step(i, _):
        @pl.when(i < UNITS)
        def _():
            zz, _, _ = unit(i)

            @pl.when(zz < z)
            def _():
                arrive(ZU, i)

            @pl.when(zz > z)
            def _():
                arrive(ZD, i)

            @pl.when((zz <= z) & (z < 3))
            def _():
                send(ZU, i).start()

            @pl.when((zz >= z) & (z > 0))
            def _():
                send(ZD, i).start()

            for kind in (XO, YO, CO):
                send(kind, i).start()

        j = i - lag

        @pl.when((j >= 0) & (j < UNITS))
        def _():
            arrive(XO, j)
            send(YD, j).start()
            send(CX, j).start()
            arrive(YO, j)
            send(XD, j).start()
            send(CY, j).start()

        m = i - core_lag

        @pl.when(m >= 0)
        def _():
            arrive(XD, m)
            send(CXD, m).start()
            arrive(YD, m)
            send(CYD, m).start()

        return 0

    lax.fori_loop(0, UNITS + core_lag, step, 0)

    def finish(i, _):
        zz, _, _ = unit(i)
        for kind in (CO, CX, CY, CXD, CYD):
            arrive(kind, i)
        for kind in (XO, YO, CO, YD, XD, CX, CY, CXD, CYD):
            send(kind, i).wait_send()

        @pl.when((zz <= z) & (z < 3))
        def _():
            send(ZU, i).wait_send()

        @pl.when((zz >= z) & (z > 0))
        def _():
            send(ZD, i).wait_send()

        return 0

    lax.fori_loop(0, UNITS, finish, 0)


def gather_others(canonical):
    return pl.pallas_call(
        gather_kernel,
        out_shape=jax.ShapeDtypeStruct((24 * SHARD, D), bf),
        in_specs=[VM],
        out_specs=ANY,
        scratch_shapes=[DMA((11, UNITS)), DMA((11, UNITS)), DMA],
        compiler_params=params_for(1, 16),
    )(canonical)


def reduce_kernel(
    g_ref, o_ref, lb, cb, xb, yb, dxb, dyb, zub, zdb, ss, rs, cs, cr, ls
):
    z, x, y, c = coords()
    xn, yn, cn = 1 - x, 1 - y, 1 - c
    to_x, to_y, to_core = dev(z, xn, y, c), dev(z, x, yn, c), dev(z, x, y, cn)
    lag1, lag2, lag3, lag4 = 1, 2, 3, 4
    XS, YS, DXS, DYS, ZD, ZU = range(6)

    def unit(i):
        r = i // CHUNKS
        return 3 - r, i - r * CHUNKS

    def rows(zz, xx, yy, cc, k):
        s = (zz * 2 + xx) * 4 + yy * 2 + cc - 8
        return g_ref.at[pl.ds(pl.multiple_of(s * SHARD + k * CHUNK, 16), CHUNK)]

    places = [(xn, yn), (xn, y), (x, yn), (x, y)]

    def load(i, p):
        zz, k = unit(i)
        xx, yy = places[p]
        return pltpu.make_async_copy(rows(zz, xx, yy, c, k), lb.at[i, p], ls.at[i, p])

    def to_sibling(i, p):
        zz, k = unit(i)
        xx, yy = places[p]
        return remote(rows(zz, xx, yy, cn, k), cb.at[i, p], cs.at[i, p], cr.at[i, p], to_core)

    def load_all(i, _):
        for p in range(4):
            load(i, p).start()
        return 0

    lax.fori_loop(0, UNITS, load_all, 0)
    meet_neighbours(z, x, y, c, [to_x, to_y, to_core])

    def send_all(i, _):
        for p in range(4):
            to_sibling(i, p).start()
        return 0

    lax.fori_loop(0, UNITS, send_all, 0)

    def over(kind, src, dst, i, to):
        return remote(src, dst, ss.at[kind, i], rs.at[kind, i], to)

    def diag_x(i):
        return over(DXS, lb.at[i, 0, 0:OVER_X], dxb.at[i], i, to_x)

    def diag_y(i):
        return over(DYS, lb.at[i, 0, OVER_X:CHUNK], dyb.at[i], i, to_y)

    def whole_x(i):
        return over(XS, lb.at[i, 1], xb.at[i], i, to_x)

    def whole_y(i):
        return over(YS, lb.at[i, 2], yb.at[i], i, to_y)

    def down(i):
        return over(ZD, lb.at[i, 3], zub.at[i], i, dev(z - 1, x, y, c))

    def up(i):
        return over(ZU, lb.at[i, 3], zdb.at[i], i, dev(z + 1, x, y, c))

    def have(i, p):
        load(i, p).wait()
        to_sibling(i, p).wait_recv()

    def step(i, _):
        @pl.when(i < UNITS)
        def _():
            have(i, 0)
            add_tiles(lb.at[i, 0], CHUNK, lb.at[i, 0], cb.at[i, 0])
            diag_x(i).start()
            diag_y(i).start()

        j = i - lag1

        @pl.when((j >= 0) & (j < UNITS))
        def _():
            have(j, 1)
            have(j, 2)
            diag_y(j).wait_recv()
            diag_x(j).wait_recv()
            a, b = lb.at[j, 1], cb.at[j, 1]
            low, high = slice(0, OVER_X), slice(OVER_X, CHUNK)
            add_tiles(a.at[low], OVER_X, a.at[low], b.at[low])
            add_tiles(a.at[high], CHUNK - OVER_X, a.at[high], b.at[high], dyb.at[j])
            whole_x(j).start()
            a, b = lb.at[j, 2], cb.at[j, 2]
            add_tiles(a.at[low], OVER_X, a.at[low], b.at[low], dxb.at[j])
            add_tiles(a.at[high], CHUNK - OVER_X, a.at[high], b.at[high])
            whole_y(j).start()

        m = i - lag2

        @pl.when((m >= 0) & (m < UNITS))
        def _():
            zz, k = unit(m)
            have(m, 3)
            whole_x(m).wait_recv()
            whole_y(m).wait_recv()
            parts = [lb.at[m, 3], cb.at[m, 3], xb.at[m], yb.at[m]]

            @pl.when(z != zz)
            def _():
                add_tiles(lb.at[m, 3], CHUNK, *parts)

            @pl.when((z == 3) & (zz < 3))
            def _():
                down(m).start()

            @pl.when(z == 0)
            def _():
                up(m).start()

            @pl.when(z == zz)
            def _():
                add_tiles(o_ref.at[pl.ds(pl.multiple_of(k * CHUNK, 16), CHUNK)], CHUNK, *parts)

        n = i - lag3

        @pl.when((n >= 0) & (n < UNITS))
        def _():
            zz, _ = unit(n)

            @pl.when((z > zz) & (z < 3))
            def _():
                down(n).wait_recv()
                add_tiles(lb.at[n, 3], CHUNK, lb.at[n, 3], zub.at[n])
                down(n).start()

            @pl.when((z < zz) & (z > 0))
            def _():
                up(n).wait_recv()
                add_tiles(lb.at[n, 3], CHUNK, lb.at[n, 3], zdb.at[n])
                up(n).start()

        o = i - lag4

        @pl.when(o >= 0)
        def _():
            zz, k = unit(o)

            @pl.when(z == zz)
            def _():
                dst = o_ref.at[pl.ds(pl.multiple_of(k * CHUNK, 16), CHUNK)]

                @pl.when(z < 3)
                def _():
                    down(o).wait_recv()
                    add_tiles(dst, CHUNK, dst, zub.at[o])

                up(o).wait_recv()
                add_tiles(dst, CHUNK, dst, zdb.at[o])

        return 0

    lax.fori_loop(0, UNITS + lag4, step, 0)

    def finish(i, _):
        zz, _ = unit(i)
        for p in range(4):
            to_sibling(i, p).wait_send()
        for copy in (diag_x(i), diag_y(i), whole_x(i), whole_y(i)):
            copy.wait_send()

        @pl.when(z > zz)
        def _():
            down(i).wait_send()

        @pl.when(z < zz)
        def _():
            up(i).wait_send()

        return 0

    lax.fori_loop(0, UNITS, finish, 0)


def reduce_others(grads):
    def room(*shape):
        return pltpu.VMEM(shape + (D,), bf)

    return pl.pallas_call(
        reduce_kernel,
        out_shape=jax.ShapeDtypeStruct((SHARD, D), f32),
        in_specs=[ANY],
        out_specs=VM,
        scratch_shapes=[
            room(UNITS, 4, CHUNK), room(UNITS, 4, CHUNK),
            room(UNITS, CHUNK), room(UNITS, CHUNK),
            room(UNITS, OVER_X), room(UNITS, CHUNK - OVER_X),
            room(UNITS, CHUNK), room(UNITS, CHUNK),
            DMA((6, UNITS)), DMA((6, UNITS)), DMA((UNITS, 4)), DMA((UNITS, 4)), DMA((UNITS, 4)),
        ],
        compiler_params=params_for(2),
    )(grads)


def last_kernel(
    v_ref, n_ref, can_ref, nrm_ref, st_ref,
    out_ref, ng_ref, sto_ref,
    ext, hal, hsend, av, bv, cv, dv, zv, sums, sv, nc, ny, nsv, nland, sland,
    s1, r1, s2, r2, zs, zr, ms, mr, qs, qr, hsem,
):
    z, x, y, c = coords()
    xn, yn, cn = 1 - x, 1 - y, 1 - c
    s = (z * 2 + x) * 4 + y * 2 + c
    core = dev(z, x, y, cn)
    xs, xo, ys, yo = dev(z, xn, y, c), dev(z, xn, y, cn), dev(z, x, yn, c), dev(z, x, yn, cn)
    prv = lax.rem(s + 31, 32)
    bar = pltpu.get_barrier_semaphore()

    def hello(i, _):
        greet(bar, linear(lax.rem(s + i, 32)))
        return 0

    lax.fori_loop(1, 32, hello, 0)
    pl.semaphore_wait(bar, 31)
    half = 256

    def unit(xx, yy, cc):
        at = pl.multiple_of((xx * 4 + yy * 2 + cc) * 128, 128)
        return v_ref.at[:, pl.ds(at, 128), :]

    def rows(yy, cc, k):
        return n_ref.at[pl.ds(pl.multiple_of((yy * 2 + cc) * 512 + k * half, half), half)]

    far = [remote(rows(yn, cn, k), nc.at[1, k], s2.at[0, k], r2.at[0, k], core) for k in range(2)]
    near = [remote(rows(y, cn, k), nc.at[0, k], s2.at[1, k], r2.at[1, k], core) for k in range(2)]
    opposite = [
        remote(unit(xn, yn, cc), av.at[i], s1.at[i], r1.at[i], xs) for i, cc in enumerate((c, cn))
    ]
    beside = [
        remote(unit(xn, y, c), bv.at[0], s1.at[2], r1.at[2], xs),
        remote(unit(xn, y, cn), bv.at[1], s1.at[3], r1.at[3], xo),
    ]
    sibling = remote(unit(x, y, cn), cv, s1.at[4], r1.at[4], core)
    for copy in far + opposite + beside + [sibling] + near:
        copy.start()

    def tell(i):
        return remote(st_ref, sland.at[s], qs.at[i], qr.at[s], linear(lax.rem(s + i, 32)))

    def tell_all(i, _):
        tell(i).start()
        return 0

    lax.fori_loop(1, 32, tell_all, 0)
    norm_send = remote(nrm_ref, nland.at[s], ms.at[0], mr.at[s], (7, 3))

    @pl.when(s != 31)
    def _():
        norm_send.start()

    later = []
    across = []
    for i, cc in enumerate((c, cn)):
        opposite[i].wait_recv()
        for j in range(3):
            add_rows(sv.at[i, j], unit(x, yn, cc).at[j], av.at[i, j])
        copy = remote(sv.at[i], dv.at[i], s1.at[5 + i], r1.at[5 + i], (ys, yo)[i])
        copy.start()
        across.append(copy)
    for k in range(2):
        far[k].wait_recv()

        def add_far(q, _):
            at = pl.ds(pl.multiple_of(q * 32, 32), 32)
            add_rows(nsv.at[k, at], rows(yn, c, k).at[at], nc.at[1, k, at])
            return 0

        lax.fori_loop(0, half // 32, add_far, 0)
        copy = remote(nsv.at[k], ny.at[k], s2.at[2, k], r2.at[2, k], ys)
        copy.start()
        later.append(copy)

    blocks = [y * 2 + c, y * 2 + cn, yn * 2 + c, yn * 2 + cn]

    def down(q):
        return remote(sums.at[q], zv.at[q], zs.at[q], zr.at[q], dev(z - 1, x, y, c))

    for q in range(4):
        if q == 0:
            beside[0].wait_recv()
            parts = [unit(x, y, c), bv.at[0]]
        elif q == 1:
            sibling.wait_recv()
            beside[1].wait_recv()
            parts = [cv, bv.at[1]]
        else:
            across[q - 2].wait_recv()
            parts = [dv.at[q - 2]]

        @pl.when(z < 3)
        def _():
            remote(sums.at[q], zv.at[q], zs.at[q], zr.at[q], core).wait_recv()

        @pl.when(z == 3)
        def _():
            for j in range(3):
                add_rows(sums.at[q, j], *[part.at[j] for part in parts])
            down(q).start()

        @pl.when((z == 1) | (z == 2))
        def _():
            for j in range(3):
                add_rows(sums.at[q, j], zv.at[q, j], *[part.at[j] for part in parts])
            down(q).start()

        @pl.when(z == 0)
        def _():
            for j in range(3):
                total = zv[q, j].astype(f32)
                for part in parts:
                    total = total + part[j].astype(f32)
                for h in range(2):
                    at = 64 - 2 * s + 8 * j + 2 * blocks[q] + h
                    ext[pl.ds(at, 128, stride=24), :] = total[:, 128 * h : 128 * h + 128]

    base = 64 - 2 * s

    def place(src, first, count, apart):
        for j in range(apart):
            for k in range(8):
                ext[pl.ds(base + 8 * (first + j) + k, count, stride=8 * apart), :] = can_ref[
                    src + j * count : src + (j + 1) * count, 128 * k : 128 * k + 128
                ]

    @pl.when((s == 8) | (s == 9) | (s >= 22))
    def _():
        place(0, 0, 384, 1)

    @pl.when(s == 10)
    def _():
        place(0, 0, 256, 1)
        place(256, 256, 32, 4)

    @pl.when((s >= 11) & (s <= 20))
    def _():
        place(0, 0, 96, 4)

    @pl.when(s == 21)
    def _():
        place(0, 0, 32, 4)
        place(128, 128, 256, 1)

    hsend[...] = ext[0:64, :]
    halo = remote(hsend, hal, hsem.at[0], hsem.at[1], linear(prv))
    halo.start()
    for k in range(2):
        near[k].wait_recv()
        later[k].wait_recv()

        def add_own(q, _):
            at = pl.ds(pl.multiple_of(q * 32, 32), 32)
            to = pl.ds(pl.multiple_of(k * half + q * 32, 32), 32)
            add_rows(ng_ref.at[to], rows(y, c, k).at[at], nc.at[0, k, at], ny.at[k, at])
            return 0

        lax.fori_loop(0, half // 32, add_own, 0)

    def hear(i, _):
        o = lax.rem(s + i, 32)
        remote(st_ref, sland.at[o], qs.at[0], qr.at[o], core).wait_recv()
        return 0

    lax.fori_loop(1, 32, hear, 0)
    sland[pl.ds(s, 1)] = st_ref[...].reshape(1, 8, 128)
    sto_ref[...] = jnp.sum(sland[...], axis=0)
    halo.wait()

    @pl.when(s != 31)
    def _():
        row = lax.broadcasted_iota(jnp.int32, (64, 128), 0)
        end = slice(NATURAL, NATURAL + 64)
        ext[end, :] = jnp.where(row >= 64 - 2 * (s + 1), hal[...], ext[end, :])

    @pl.when(s == 31)
    def _():
        def gather(i, total):
            remote(nrm_ref, nland.at[i], ms.at[0], mr.at[i], core).wait_recv()
            return total + nland[i]

        total = lax.fori_loop(0, 31, gather, nrm_ref[...])
        for k in range(8):
            ext[pl.ds(base + 8 * 384 + k, 8, stride=8), :] = total[:, 128 * k : 128 * k + 128]

    out_ref[...] = ext[64 : 64 + NATURAL, :]
    for copy in far + opposite + beside + [sibling] + near + across + later:
        copy.wait_send()

    @pl.when(z > 0)
    def _():
        for q in range(4):
            down(q).wait_send()

    def told(i, _):
        tell(i).wait_send()
        return 0

    lax.fori_loop(1, 32, told, 0)

    @pl.when(s != 31)
    def _():
        norm_send.wait_send()


def last_reduce(qkv_grads, normed_part, canonical, norm_part, squares):
    shape = jax.ShapeDtypeStruct
    unit = (3, 128, 256)
    room = pltpu.VMEM
    return pl.pallas_call(
        last_kernel,
        out_shape=(shape((NATURAL, 128), f32), shape((512, D), f32), shape((8, 128), f32)),
        in_specs=[VM] * 5,
        out_specs=(VM, VM, VM),
        scratch_shapes=[
            room((64 + NATURAL + 6, 128), f32), room((64, 128), f32), room((64, 128), f32),
            room((2,) + unit, bf), room((2,) + unit, bf), room(unit, bf), room((2,) + unit, bf),
            room((4,) + unit, bf), room((4,) + unit, bf), room((2,) + unit, bf),
            room((2, 2, 256, D), bf), room((2, 256, D), bf), room((2, 256, D), bf),
            room((32, 8, D), f32), room((32, 8, 128), f32),
            DMA((7,)), DMA((7,)), DMA((3, 2)), DMA((3, 2)), DMA((4,)), DMA((4,)),
            DMA((1,)), DMA((32,)), DMA((32,)), DMA((32,)), DMA((2,)),
        ],
        compiler_params=params_for(3),
    )(qkv_grads, normed_part, canonical, norm_part, squares)


def swap_kernel(n, to_tokens, a_ref, o_ref, ss, rs, ls):
    me = lax.axis_index("fsdp")
    bar = pltpu.get_barrier_semaphore()
    for i in range(1, n):
        pl.semaphore_signal(
            bar, inc=1, device_id={"fsdp": lax.rem(me + i, n)}, device_id_type=MESH
        )
    pl.semaphore_wait(bar, n - 1)
    tokens = (a_ref if to_tokens else o_ref).shape[0] // n
    width = (o_ref if to_tokens else a_ref).shape[1] // n

    def token_block(ref, owner):
        return ref.at[pl.ds(pl.multiple_of(owner * tokens, 16), tokens)]

    def head_block(ref, owner):
        return ref.at[:, pl.ds(pl.multiple_of(owner * width, 128), width)]

    take, put = (token_block, head_block) if to_tokens else (head_block, token_block)
    local = pltpu.make_async_copy(take(a_ref, me), put(o_ref, me), ls)
    local.start()
    copies = []
    for i in range(1, n):
        to = lax.rem(me + i, n)
        copy = pltpu.make_async_remote_copy(
            src_ref=take(a_ref, to), dst_ref=put(o_ref, me), send_sem=ss.at[i], recv_sem=rs.at[i],
            device_id={"fsdp": to}, device_id_type=MESH,
        )
        copy.start()
        copies.append(copy)
    for i in range(1, n):
        copies[i - 1].wait_send()
        ref = put(o_ref, lax.rem(me - i + n, n))
        pltpu.make_async_remote_copy(
            src_ref=ref, dst_ref=ref, send_sem=ss.at[i], recv_sem=rs.at[i],
            device_id={"fsdp": lax.rem(me + i, n)}, device_id_type=MESH,
        ).wait_recv()
    local.wait()


def swap(array, n, to_tokens, collective):
    rows, columns = array.shape
    shape = (rows // n, columns * n) if to_tokens else (rows * n, columns // n)
    return pl.pallas_call(
        functools.partial(swap_kernel, n, to_tokens),
        out_shape=jax.ShapeDtypeStruct(shape, bf),
        in_specs=[VM],
        out_specs=VM,
        scratch_shapes=[DMA((n,)), DMA((n,)), DMA],
        compiler_params=params_for(collective, 32),
    )(array)


def partner(values):
    width = values.shape[-1]
    lane = lax.broadcasted_iota(jnp.int32, values.shape, values.ndim - 1)
    after = pltpu.roll(values, width - 32, values.ndim - 1)
    before = pltpu.roll(values, 32, values.ndim - 1)
    return jnp.where(lane % 64 < 32, after, before)


def qkv_kernel(h_ref, n_ref, w_ref, c_ref, s_ref, o_ref, q_ref, k_ref, v_ref):
    rows = h_ref[...].astype(f32)
    center = rows - jnp.mean(rows, axis=-1, keepdims=True)
    inverse = lax.rsqrt(jnp.mean(center * center, axis=-1, keepdims=True) + EPSILON)
    normed = (center * inverse * n_ref[0:1, :] + n_ref[1:2, :]).astype(bf)
    o_ref[...] = normed
    for j, ref in enumerate((q_ref, k_ref, v_ref)):
        mixed = jnp.dot(normed, w_ref[j], preferred_element_type=f32)
        if j == 2:
            ref[...] = mixed.astype(bf)
        else:
            for at in range(0, mixed.shape[1], 128):
                part = mixed[:, at : at + 128]
                turned = part * c_ref[...] + partner(part) * s_ref[...]
                ref[:, at : at + 128] = turned.astype(bf)


def project(hidden, norm_rows, w_qkv, cosine, sine):
    tokens, width = hidden.shape[0], w_qkv.shape[2]
    block = 256
    rows = lambda w: pl.BlockSpec((block, w), lambda i: (i, 0))
    full = lambda a: pl.BlockSpec(a.shape, lambda i: (0,) * a.ndim)
    shape = jax.ShapeDtypeStruct
    return pl.pallas_call(
        qkv_kernel,
        grid=(tokens // block,),
        in_specs=[rows(D), full(norm_rows), full(w_qkv), rows(128), rows(128)],
        out_specs=[rows(D), rows(width), rows(width), rows(width)],
        out_shape=[shape((tokens, D), bf)] + [shape((tokens, width), bf)] * 3,
        compiler_params=params_for(),
    )(hidden, norm_rows, w_qkv, cosine, sine)


NT = (((1,), (1,)), ((), ()))
TN = (((0,), (0,)), ((), ()))
BLOCK = 512


def one_head(pair, h):
    lane = lax.broadcasted_iota(jnp.int32, pair.shape, 1)
    return jnp.where((lane < 64) if h == 0 else (lane >= 64), pair, jnp.zeros_like(pair))


def causal(scores, i, j):
    key = j * scores.shape[0] + lax.broadcasted_iota(jnp.int32, scores.shape, 0)
    query = i * scores.shape[1] + lax.broadcasted_iota(jnp.int32, scores.shape, 1)
    return jnp.where(key <= query, scores, MASKED)


def attend_kernel(q_ref, k_ref, v_ref, o_ref, low_ref, l_ref):
    i = pl.program_id(1)
    heads = [one_head(q_ref[...], h) for h in range(2)]

    def block(j, carry, masked):
        at = pl.ds(pl.multiple_of(j * BLOCK, BLOCK), BLOCK)
        keys, values = k_ref[at, :], v_ref[at, :]
        out = []
        for h in range(2):
            peak, total, summed = carry[3 * h : 3 * h + 3]
            scores = lax.dot_general(keys, heads[h], NT, preferred_element_type=f32)
            scores = scores * (SCALE * LOG2E)
            if masked:
                scores = causal(scores, i, j)
            new_peak = jnp.maximum(peak, jnp.max(scores, axis=0, keepdims=True))
            weights = jnp.exp2(scores - new_peak)
            shrink = jnp.exp2(peak - new_peak)
            total = total * shrink + jnp.sum(weights, axis=0, keepdims=True)
            part = lax.dot_general(
                values[:, 64 * h : 64 * h + 64], weights.astype(bf), TN, preferred_element_type=f32
            )
            out += [new_peak, total, summed * shrink + part]
        return tuple(out)

    start = (
        jnp.full((1, BLOCK), MASKED, f32), jnp.zeros((1, BLOCK), f32), jnp.zeros((64, BLOCK), f32)
    ) * 2
    carry = lax.fori_loop(0, i, lambda j, carry: block(j, carry, False), start)
    peak0, total0, sum0, peak1, total1, sum1 = block(i, carry, True)
    out = jnp.concatenate([sum0 / total0, sum1 / total1], axis=0).T
    o_ref[...] = out
    low_ref[...] = out.astype(bf)
    logs = jnp.concatenate([peak0 + jnp.log2(total0), peak1 + jnp.log2(total1)], axis=0)
    l_ref[...] = logs.reshape(1, 2, BLOCK)


def attend(queries, keys, values):
    tokens, width = queries.shape
    pairs = width // 128
    block = pl.BlockSpec((BLOCK, 128), lambda p, i: (i, p))
    full = pl.BlockSpec((tokens, 128), lambda p, i: (0, p))
    logs = pl.BlockSpec((1, 2, BLOCK), lambda p, i: (p, 0, i))
    shape = jax.ShapeDtypeStruct
    return pl.pallas_call(
        attend_kernel,
        grid=(pairs, tokens // BLOCK),
        in_specs=[block, full, full],
        out_specs=[block, block, logs],
        out_shape=[
            shape((tokens, width), f32), shape((tokens, width), bf), shape((pairs, 2, tokens), f32)
        ],
        compiler_params=params_for(),
    )(queries, keys, values)


def attend_back_kernel(
    q_ref, k_ref, v_ref, g_ref, a_ref, l_ref, cq_ref, sq_ref, c_ref, s_ref,
    dq_ref, dk_ref, dv_ref, dk, dv,
):
    i = pl.program_id(1)

    @pl.when(i == 0)
    def _():
        dk[...] = jnp.zeros_like(dk)
        dv[...] = jnp.zeros_like(dv)

    queries, grads = q_ref[...], g_ref[...]
    heads = [one_head(queries, h) for h in range(2)]
    grad_heads = [one_head(grads, h) for h in range(2)]
    both_heads = jnp.concatenate(heads, axis=0)
    both_grads = jnp.concatenate(grad_heads, axis=0)
    products = (a_ref[...] * grads.astype(f32)).T
    dots = [jnp.sum(products[64 * h : 64 * h + 64], axis=0, keepdims=True) for h in range(2)]
    logs = l_ref[0]

    def block(j, sums, masked):
        at = pl.ds(pl.multiple_of(j * BLOCK, BLOCK), BLOCK)
        keys, values = k_ref[at, :], v_ref[at, :]
        weights, score_grads = [], []
        for h in range(2):
            scores = lax.dot_general(keys, heads[h], NT, preferred_element_type=f32)
            scores = scores * (SCALE * LOG2E)
            if masked:
                scores = causal(scores, i, j)
            prob = jnp.exp2(scores - logs[h : h + 1])
            prob_grad = lax.dot_general(values, grad_heads[h], NT, preferred_element_type=f32)
            score_grads.append((prob * (prob_grad - dots[h])).astype(bf))
            weights.append(prob.astype(bf))
        dv[at, :] += jnp.dot(
            jnp.concatenate(weights, axis=1), both_grads, preferred_element_type=f32
        )
        dk[at, :] += jnp.dot(
            jnp.concatenate(score_grads, axis=1), both_heads, preferred_element_type=f32
        )
        return tuple(
            sums[h] + lax.dot_general(score_grads[h], keys, TN, preferred_element_type=f32)
            for h in range(2)
        )

    zero = jnp.zeros((BLOCK, 128), f32)
    sums = lax.fori_loop(0, i, lambda j, sums: block(j, sums, False), (zero, zero))
    sums = block(i, sums, True)
    lane = lax.broadcasted_iota(jnp.int32, zero.shape, 1)
    query_grad = jnp.where(lane < 64, sums[0], sums[1]) * SCALE
    dq_ref[...] = (query_grad * cq_ref[...] - partner(query_grad) * sq_ref[...]).astype(bf)

    @pl.when(i == pl.num_programs(1) - 1)
    def _():
        def turn(t, _):
            at = pl.ds(pl.multiple_of(t * 256, 256), 256)
            key_grad = dk[at, :] * SCALE
            turned = key_grad * c_ref[at, :] - partner(key_grad) * s_ref[at, :]
            dk_ref[at, :] = turned.astype(bf)
            dv_ref[at, :] = dv[at, :].astype(bf)
            return 0

        lax.fori_loop(0, dk.shape[0] // 256, turn, 0)


def attend_back(queries, keys, values, grads, attended, logs, cosine, sine):
    tokens, width = queries.shape
    block = pl.BlockSpec((BLOCK, 128), lambda p, i: (i, p))
    full = pl.BlockSpec((tokens, 128), lambda p, i: (0, p))
    table_block = pl.BlockSpec((BLOCK, 128), lambda p, i: (i, 0))
    table = pl.BlockSpec((tokens, 128), lambda p, i: (0, 0))
    log_block = pl.BlockSpec((1, 2, BLOCK), lambda p, i: (p, 0, i))
    return pl.pallas_call(
        attend_back_kernel,
        grid=(width // 128, tokens // BLOCK),
        in_specs=[block, full, full, block, block, log_block, table_block, table_block, table, table],
        out_specs=[block, full, full],
        out_shape=[jax.ShapeDtypeStruct((tokens, width), bf)] * 3,
        scratch_shapes=[pltpu.VMEM((tokens, 128), f32), pltpu.VMEM((tokens, 128), f32)],
        compiler_params=params_for(),
    )(queries, keys, values, grads, attended, logs, cosine, sine, cosine, sine)


def norm_forward(values, gain_row, shift_row):
    center = values - jnp.mean(values, axis=-1, keepdims=True)
    spread = jnp.mean(center * center, axis=-1, keepdims=True)
    inverse = lax.rsqrt(spread + EPSILON)
    unit_rows = center * inverse
    return (unit_rows * gain_row + shift_row, unit_rows, inverse)


def norm_backward(grad_rows, unit_rows, inverse, gain_row):
    scaled = grad_rows * gain_row
    first_mean = jnp.mean(scaled, axis=-1, keepdims=True)
    second_mean = jnp.mean(scaled * unit_rows, axis=-1, keepdims=True)
    return inverse * (scaled - first_mean - unit_rows * second_mean)


def norm_sums(grad_rows, unit_rows):
    return jnp.sum(grad_rows * unit_rows, axis=0), jnp.sum(grad_rows, axis=0)


def up_from_shards(rows):
    pieces = [rows[:128].reshape(1, 4, 32, D), rows[128:3968].reshape(10, 4, 96, D)]
    pieces.append(rows[3968:].reshape(1, 4, 32, D))
    return jnp.concatenate(
        [piece.transpose(0, 2, 1, 3).reshape(-1, FF) for piece in pieces], axis=0
    )


def up_to_shards(grad):
    pieces = [(grad[:32], 1, 32), (grad[32:992], 10, 96), (grad[992:], 1, 32)]
    return jnp.concatenate(
        [
            piece.reshape(blocks, rows, 4, D).transpose(0, 2, 1, 3).reshape(-1, D)
            for piece, blocks, rows in pieces
        ],
        axis=0,
    )


def dots(a, b, contract):
    return lax.dot_general(a, b, ((contract[:1], contract[1:]), ((), ())), preferred_element_type=f32)


def per_device(lines, hidden_in, params, cotangent, source_ids, corpus_weight, positions):
    devices = lax.axis_size(("dp", "fsdp"))
    width = lax.axis_size("fsdp")
    hidden = hidden_in[0]
    tokens = hidden.shape[0]
    place = lax.axis_index("fsdp")
    if lines:
        places = jnp.pad(positions.astype(f32).reshape(4, 128), ((0, 4), (0, 0)))
        hidden_all, w_qkv, canonical, norm_rows, places = first_gather(
            params.reshape(NATURAL, 128), hidden, places
        )
        places = places[:, :4].reshape(-1)
    else:
        whole = lax.all_gather(params, ("dp", "fsdp"), axis=0, tiled=True)
        ends = [0, 3 * D * D, 4 * D * D, 4 * D * D + D * FF, 4 * D * D + 2 * D * FF]
        parts = [whole[a:b] for a, b in zip(ends, ends[1:])]
        w_qkv = lax.dynamic_index_in_dim(
            parts[0].reshape(D, 3, width, D // width).transpose(1, 2, 0, 3), place, 1, False
        )
        w_out, w_up, w_down = parts[1].reshape(D, D), parts[2].reshape(D, FF), parts[3].reshape(FF, D)
        norm_rows = whole[ends[-1] :].reshape(8, D).astype(f32)
        hidden_all = lax.all_gather(hidden, "fsdp", axis=0, tiled=True)
        places = lax.all_gather(positions[0].astype(f32), "fsdp", axis=0, tiled=True)

    lane = jnp.arange(128) % 64
    frequency = jnp.exp((lane % 32).astype(f32) * (-2.0 * math.log(10000.0) / HEAD_DIM))
    angles = places[:, None] * frequency
    cosine = jnp.cos(angles)
    sine = jnp.where(lane < 32, -1.0, 1.0) * jnp.sin(angles)
    normed_all, queries, keys, values = project(hidden_all, norm_rows, w_qkv, cosine, sine)
    attended_all, attended_low, logs = attend(queries, keys, values)
    attended = swap(attended_low, width, True, 4)
    if lines:
        others = gather_others(canonical)
        w_out, w_up, w_down = others[:D], up_from_shards(others[D : 5 * D]), others[5 * D :]

    inputs = hidden.astype(f32)
    branch = dots(attended, w_out, (1, 0))
    branch_norm, branch_unit, branch_inverse = norm_forward(branch, norm_rows[2], norm_rows[3])
    residual = inputs + branch_norm
    entered, entered_unit, entered_inverse = norm_forward(residual, norm_rows[4], norm_rows[5])
    entered_low = entered.astype(bf)
    lifted = dots(entered_low, w_up, (1, 0))
    activated = jax.nn.gelu(lifted).astype(bf)
    lowered = dots(activated, w_down, (1, 0))
    lowered_norm, lowered_unit, lowered_inverse = norm_forward(lowered, norm_rows[6], norm_rows[7])
    output = (residual + lowered_norm).astype(bf)
    squares = jnp.stack([jnp.mean(branch * branch), jnp.mean(lowered * lowered)])

    source_table = jnp.arange(corpus_weight.shape[0], dtype=jnp.int32)
    row_scale = jnp.sum(jnp.where(source_ids[0] == source_table, corpus_weight, 0.0))
    upstream = cotangent[0].astype(f32) * row_scale
    lowered_grad = norm_backward(upstream, lowered_unit, lowered_inverse, norm_rows[6]).astype(bf)
    grad_down = dots(activated, lowered_grad, (0, 0))
    activated_grad = dots(lowered_grad, w_down, (1, 1))
    lifted_grad = jax.vjp(jax.nn.gelu, lifted)[1](activated_grad)[0].astype(bf)
    grad_up = dots(entered_low, lifted_grad, (0, 0))
    entered_grad = dots(lifted_grad, w_up, (1, 1))
    residual_grad = upstream + norm_backward(
        entered_grad, entered_unit, entered_inverse, norm_rows[4]
    )
    branch_grad = norm_backward(residual_grad, branch_unit, branch_inverse, norm_rows[2]).astype(bf)
    grad_out = dots(attended, branch_grad, (0, 0))
    attended_grad = dots(branch_grad, w_out, (1, 1)).astype(bf)
    if lines:
        flat = jnp.concatenate(
            [grad_out.astype(bf), up_to_shards(grad_up.astype(bf)), grad_down.astype(bf)], axis=0
        )
        owned = reduce_others(flat)

    grads_all = swap(attended_grad, width, False, 5)
    mixed_grad = attend_back(
        queries, keys, values, grads_all, attended_all, logs, cosine, sine
    )
    grad_qkv = jnp.stack([dots(normed_all, part, (0, 0)) for part in mixed_grad])
    normed_part = sum(dots(part, w_qkv[j], (1, 1)) for j, part in enumerate(mixed_grad))
    _, unit_all, _ = norm_forward(hidden_all.astype(f32), norm_rows[0], norm_rows[1])
    norm_part = jnp.stack(
        [
            *norm_sums(normed_part, unit_all),
            *norm_sums(residual_grad, branch_unit),
            *norm_sums(entered_grad, entered_unit),
            *norm_sums(upstream, lowered_unit),
        ]
    )
    if lines:
        told = jnp.zeros((8, 128), f32).at[0, :2].set(squares)
        param_grads, normed_grad, told = last_reduce(
            grad_qkv.astype(bf), normed_part.astype(bf), owned, norm_part, told
        )
        param_grads = param_grads.reshape(-1)
        squares = told[0, :2]
    else:
        spread = jnp.zeros((3, width, D, D // width), f32)
        spread = lax.dynamic_update_slice_in_dim(spread, grad_qkv[:, None], place, 1)
        flat = jnp.concatenate(
            [
                part.reshape(-1)
                for part in (spread.transpose(2, 0, 1, 3), grad_out, grad_up, grad_down, norm_part)
            ]
        )
        param_grads = lax.psum_scatter(flat, ("dp", "fsdp"), scatter_dimension=0, tiled=True)
        normed_grad = lax.psum_scatter(normed_part, "fsdp", scatter_dimension=0, tiled=True)
        squares = lax.psum(squares, ("dp", "fsdp"))
    statistics = squares / devices
    _, normed_unit, normed_inverse = norm_forward(inputs, norm_rows[0], norm_rows[1])
    into_input = norm_backward(normed_grad, normed_unit, normed_inverse, norm_rows[0])
    input_grad = (residual_grad + into_input).astype(bf)
    return (output[None], input_grad[None], param_grads, statistics)


def solution(mesh):
    lines = (mesh.shape["dp"], mesh.shape["fsdp"]) == (8, 4)
    in_specs = (
        P("dp", "fsdp", None),
        P(("dp", "fsdp")),
        P("dp", "fsdp", None),
        P("dp"),
        P(),
        P("dp", "fsdp"),
    )
    out_specs = (P("dp", "fsdp", None), P("dp", "fsdp", None), P(("dp", "fsdp")), P())
    return jax.shard_map(
        functools.partial(per_device, lines),
        mesh=mesh,
        in_specs=in_specs,
        out_specs=out_specs,
        check_vma=False,
    )
```

```python
import functools
import math

import jax
import jax.numpy as jnp
from jax import lax
from jax.experimental import pallas as pl
from jax.experimental.pallas import tpu as pltpu
from jax.sharding import PartitionSpec as P

D = 1024
HEADS = 16
HEAD_DIM = 64
FF = 4096
EPSILON = 1e-05
MASKED = -1e30
SCALE = 1.0 / math.sqrt(HEAD_DIM)
LOG2E = 1.4426950408889634

MESH = pl.DeviceIdType.MESH
bf = jnp.bfloat16
f32 = jnp.float32
SHARD = 384
NATURAL = 3074
MIB = 2**20

VM = pl.BlockSpec(memory_space=pltpu.VMEM)
ANY = pl.BlockSpec(memory_space=pl.ANY)
DMA = pltpu.SemaphoreType.DMA


def params_for(collective=None, mib=48):
    if collective is None:
        return pltpu.CompilerParams(vmem_limit_bytes=mib * MIB)
    return pltpu.CompilerParams(
        collective_id=collective, has_side_effects=True, vmem_limit_bytes=mib * MIB
    )


def coords():
    dp, fs = lax.axis_index("dp"), lax.axis_index("fsdp")
    return dp // 2, lax.rem(dp, 2), fs // 2, lax.rem(fs, 2)


def dev(z, x, y, c):
    return (z * 2 + x, y * 2 + c)


def linear(i):
    return (i // 4, lax.rem(i, 4))


def remote(src, dst, send, recv, to):
    return pltpu.make_async_remote_copy(
        src_ref=src, dst_ref=dst, send_sem=send, recv_sem=recv, device_id=to, device_id_type=MESH
    )


def greet(bar, device):
    pl.semaphore_signal(bar, inc=1, device_id=device, device_id_type=MESH)


def meet_neighbours(z, x, y, c, plane, more=0):
    bar = pltpu.get_barrier_semaphore()
    for device in plane:
        greet(bar, device)

    @pl.when(z < 3)
    def _():
        greet(bar, dev(z + 1, x, y, c))

    @pl.when(z > 0)
    def _():
        greet(bar, dev(z - 1, x, y, c))

    line = jnp.where(z < 3, 1, 0) + jnp.where(z > 0, 1, 0)
    pl.semaphore_wait(bar, len(plane) + line + more)


def add_rows(dst, *srcs):
    total = srcs[0][...].astype(f32)
    for part in srcs[1:]:
        total = total + part[...].astype(f32)
    dst[...] = total.astype(dst.dtype)


def add_tiles(dst, rows, *srcs):
    for at in range(0, rows, 16):
        add_rows(dst.at[at : at + 16], *[part.at[at : at + 16] for part in srcs])


def first_kernel(
    p_ref, h_ref, pos_ref,
    hid_ref, wq_ref, can_ref, nrm_ref, posall_ref,
    ext, tail, units, us, ur, hs, hr, ns, nr, ps, pr, ls,
):
    z, x, y, c = coords()
    xn, yn, cn = 1 - x, 1 - y, 1 - c
    s = (z * 2 + x) * 4 + y * 2 + c
    f = y * 2 + c
    nxt, prv = lax.rem(s + 1, 32), lax.rem(s + 31, 32)
    core = dev(z, x, y, cn)
    xs, xo, ys, yo = dev(z, xn, y, c), dev(z, xn, y, cn), dev(z, x, yn, c), dev(z, x, yn, cn)
    bar = pltpu.get_barrier_semaphore()
    greet(bar, linear(nxt))
    greet(bar, linear(prv))

    @pl.when(s != 31)
    def _():
        greet(bar, (7, 3))

    ext[64 : 64 + NATURAL, :] = p_ref[...].astype(f32)
    tail[...] = ext[NATURAL : NATURAL + 64, :]
    more = 2 + jnp.where(s == 31, 31, 0)
    meet_neighbours(z, x, y, c, [core, xs, xo, ys, yo], more)

    halves, half = 2, 256

    def hidden_rows(owner, k):
        return hid_ref.at[pl.ds(pl.multiple_of(owner * 512 + k * half, 16), half)]

    def hidden_own(k):
        return h_ref.at[pl.ds(k * half, half)]

    over_y, over_core, over_both = yn * 2 + c, y * 2 + cn, yn * 2 + cn
    halo = remote(tail, ext.at[0:64], ns.at[0], nr.at[0], linear(nxt))
    halo.start()
    sent = []
    for k in range(halves):
        sent.append(remote(hidden_own(k), hidden_rows(f, k), hs.at[0, k], hr.at[0, k], ys))
        sent.append(remote(hidden_own(k), hidden_rows(f, k), hs.at[1, k], hr.at[1, k], core))
    for i, to in enumerate([core, ys, yo]):
        sent.append(remote(pos_ref, posall_ref.at[f], ps.at[i], pr.at[i], to))
    for copy in sent:
        copy.start()
    own = [
        pltpu.make_async_copy(
            h_ref, hid_ref.at[pl.ds(pl.multiple_of(f * 512, 512), 512)], ls.at[0]
        ),
        pltpu.make_async_copy(pos_ref, posall_ref.at[f], ls.at[1]),
    ]
    for copy in own:
        copy.start()
    halo.wait()
    base = 64 - 2 * s

    def lines(first, count, apart, k):
        return ext[pl.ds(base + 8 * first + k, count, stride=8 * apart), :].astype(bf)

    def order(to, first, count, apart):
        for j in range(apart):
            for k in range(8):
                can_ref[to + j * count : to + (j + 1) * count, 128 * k : 128 * k + 128] = lines(
                    first + j, count, apart, k
                )

    @pl.when(z == 0)
    def _():
        for j in range(3):
            for k in range(8):
                at = 128 * (k % 2)
                units[k // 2, j, :, at : at + 128] = lines(j, 128, 3, k)
        can_ref[...] = jnp.zeros_like(can_ref)

    @pl.when((s == 8) | (s == 9) | (s >= 22))
    def _():
        order(0, 0, 384, 1)

    @pl.when(s == 10)
    def _():
        order(0, 0, 256, 1)
        order(256, 256, 32, 4)

    @pl.when((s >= 11) & (s <= 20))
    def _():
        order(0, 0, 96, 4)

    @pl.when(s == 21)
    def _():
        order(0, 0, 32, 4)
        order(128, 128, 256, 1)

    def norm_send(i):
        return remote(nrm_ref, nrm_ref, ns.at[1 + i], nr.at[1], linear(i))

    @pl.when(s == 31)
    def _():
        for k in range(8):
            nrm_ref[:, 128 * k : 128 * k + 128] = ext[pl.ds(base + 8 * 384 + k, 8, stride=8), :]

        def go(i, _):
            norm_send(i).start()
            return 0

        lax.fori_loop(0, 31, go, 0)

    slots = [yn * 2 + c, yn * 2 + cn, y * 2 + cn, y * 2 + c]

    def target(xx, yy, cc):
        at = pl.multiple_of((xx * 4 + yy * 2 + cc) * 128, 128)
        return wq_ref.at[:, pl.ds(at, 128)]

    def up(q):
        unit = units.at[slots[q]]
        return remote(unit, unit, us.at[0, q], ur.at[0, q], dev(z + 1, x, y, c))

    def arrive(ref, sem):
        remote(ref, ref, us.at[0, 0], sem, core).wait_recv()

    mine = target(x, y, c)
    for q in range(4):
        unit = units.at[slots[q]]

        @pl.when(z > 0)
        def _():
            arrive(unit, ur.at[0, q])

        @pl.when(z < 3)
        def _():
            up(q).start()

        if q == 0:
            out = [remote(unit, mine, us.at[1, 0], ur.at[1, 0], ys)]
        elif q == 1:
            out = [remote(unit, mine, us.at[1, 1], ur.at[1, 1], yo)]
        elif q == 2:
            out = [
                remote(unit, mine, us.at[1, 2], ur.at[1, 2], xo),
                remote(unit, mine, us.at[1, 3], ur.at[1, 3], core),
            ]
        else:
            out = [remote(unit, mine, us.at[2, 0], ur.at[2, 0], xs)]
            copy = pltpu.make_async_copy(unit, mine, ls.at[2])
            copy.start()
            own.append(copy)
        for copy in out:
            copy.start()
        sent += out
    for i, cc in enumerate((c, cn)):
        ref = target(x, yn, cc)
        arrive(ref, ur.at[1, i])
        copy = remote(ref, ref, us.at[2, 1 + i], ur.at[2, 1 + i], xs)
        copy.start()
        sent.append(copy)
    for k in range(halves):
        ref = hidden_rows(over_y, k)
        arrive(ref, hr.at[0, k])
        copy = remote(ref, ref, hs.at[2, k], hr.at[2, k], core)
        copy.start()
        sent.append(copy)
    arrive(target(xn, y, cn), ur.at[1, 2])
    arrive(target(x, y, cn), ur.at[1, 3])
    arrive(target(xn, y, c), ur.at[2, 0])
    arrive(target(xn, yn, c), ur.at[2, 1])
    arrive(target(xn, yn, cn), ur.at[2, 2])
    for k in range(halves):
        arrive(hidden_rows(over_core, k), hr.at[1, k])
        arrive(hidden_rows(over_both, k), hr.at[2, k])
    for i, owner in enumerate([over_core, over_y, over_both]):
        arrive(posall_ref.at[owner], pr.at[i])
    for copy in sent:
        copy.wait_send()

    @pl.when(z < 3)
    def _():
        for q in range(4):
            up(q).wait_send()

    for copy in own:
        copy.wait()

    @pl.when(s == 31)
    def _():
        def go(i, _):
            norm_send(i).wait_send()
            return 0

        lax.fori_loop(0, 31, go, 0)

    @pl.when(s != 31)
    def _():
        arrive(nrm_ref, nr.at[1])


def first_gather(share, hidden, places):
    shape = jax.ShapeDtypeStruct
    return pl.pallas_call(
        first_kernel,
        out_shape=(
            shape((2048, D), bf),
            shape((3, D, 256), bf),
            shape((SHARD, D), bf),
            shape((8, D), f32),
            shape((4, 8, 128), f32),
        ),
        in_specs=[VM, VM, VM],
        out_specs=(ANY, ANY, VM, VM, VM),
        scratch_shapes=[
            pltpu.VMEM((64 + NATURAL + 6, 128), f32),
            pltpu.VMEM((64, 128), f32),
            pltpu.VMEM((4, 3, 128, 256), bf),
            DMA((3, 4)), DMA((3, 4)), DMA((3, 2)), DMA((3, 2)),
            DMA((32,)), DMA((2,)), DMA((3,)), DMA((3,)), DMA((3,)),
        ],
        compiler_params=params_for(0, 32),
    )(share, hidden, places)


CHUNKS = 4
CHUNK = SHARD // CHUNKS
UNITS = 3 * CHUNKS
OVER_X = 48


def gather_steps(c_ref, g_ref, ss, rs, ls, more):
    z, x, y, c = coords()
    xn, yn, cn = 1 - x, 1 - y, 1 - c
    to_x, to_y, to_core = dev(z, xn, y, c), dev(z, x, yn, c), dev(z, x, y, cn)
    lag, core_lag = 2, 4

    def rows(zz, xx, yy, cc, k, low=0, count=CHUNK):
        s = (zz * 2 + xx) * 4 + yy * 2 + cc - 8
        return g_ref.at[pl.ds(pl.multiple_of(s * SHARD + k * CHUNK + low, 16), count)]

    local = pltpu.make_async_copy(c_ref, rows(jnp.maximum(z, 1), x, y, c, 0, 0, SHARD), ls)

    @pl.when(z >= 1)
    def _():
        local.start()

    meet_neighbours(z, x, y, c, [to_x, to_y, to_core] + more)

    @pl.when(z >= 1)
    def _():
        local.wait()

    ZU, ZD, XO, YO, CO, XD, YD, CX, CY, CXD, CYD = range(11)

    def unit(i):
        r = i // CHUNKS
        k = i - r * CHUNKS
        first = jnp.maximum(z, 1)
        second = jnp.where(z == 2, 1, 2)
        third = jnp.where(z <= 2, 3, 1)
        zz = jnp.where(r == 0, first, jnp.where(r == 1, second, third))
        return zz, k, (zz - 1) * CHUNKS + k

    def send(kind, i):
        zz, k, q = unit(i)
        ref, to = {
            ZU: lambda: (rows(zz, x, y, c, k), dev(z + 1, x, y, c)),
            ZD: lambda: (rows(zz, x, y, c, k), dev(z - 1, x, y, c)),
            XO: lambda: (rows(zz, x, y, c, k), to_x),
            YO: lambda: (rows(zz, x, y, c, k), to_y),
            CO: lambda: (rows(zz, x, y, c, k), to_core),
            YD: lambda: (rows(zz, xn, y, c, k, OVER_X, CHUNK - OVER_X), to_y),
            XD: lambda: (rows(zz, x, yn, c, k, 0, OVER_X), to_x),
            CX: lambda: (rows(zz, xn, y, c, k), to_core),
            CY: lambda: (rows(zz, x, yn, c, k), to_core),
            CXD: lambda: (rows(zz, xn, yn, c, k, 0, OVER_X), to_core),
            CYD: lambda: (rows(zz, xn, yn, c, k, OVER_X, CHUNK - OVER_X), to_core),
        }[kind]()
        return remote(ref, ref, ss.at[kind, q], rs.at[kind, q], to)

    def arrive(kind, i):
        zz, k, q = unit(i)
        ref = {
            ZU: lambda: rows(zz, x, y, c, k),
            ZD: lambda: rows(zz, x, y, c, k),
            XO: lambda: rows(zz, xn, y, c, k),
            YO: lambda: rows(zz, x, yn, c, k),
            XD: lambda: rows(zz, xn, yn, c, k, 0, OVER_X),
            YD: lambda: rows(zz, xn, yn, c, k, OVER_X, CHUNK - OVER_X),
            CO: lambda: rows(zz, x, y, cn, k),
            CX: lambda: rows(zz, xn, y, cn, k),
            CY: lambda: rows(zz, x, yn, cn, k),
            CXD: lambda: rows(zz, xn, yn, cn, k, 0, OVER_X),
            CYD: lambda: rows(zz, xn, yn, cn, k, OVER_X, CHUNK - OVER_X),
        }[kind]()
        remote(ref, ref, ss.at[kind, q], rs.at[kind, q], to_core).wait_recv()

    def step(i, _):
        @pl.when(i < UNITS)
        def _():
            zz, _, _ = unit(i)

            @pl.when(zz < z)
            def _():
                arrive(ZU, i)

            @pl.when(zz > z)
            def _():
                arrive(ZD, i)

            @pl.when((zz <= z) & (z < 3))
            def _():
                send(ZU, i).start()

            @pl.when((zz >= z) & (z > 0))
            def _():
                send(ZD, i).start()

            for kind in (XO, YO, CO):
                send(kind, i).start()

        j = i - lag

        @pl.when((j >= 0) & (j < UNITS))
        def _():
            arrive(XO, j)
            send(YD, j).start()
            send(CX, j).start()
            arrive(YO, j)
            send(XD, j).start()
            send(CY, j).start()

        m = i - core_lag

        @pl.when(m >= 0)
        def _():
            arrive(XD, m)
            send(CXD, m).start()
            arrive(YD, m)
            send(CYD, m).start()

        return 0

    def finish(i, _):
        zz, _, _ = unit(i)
        for kind in (CO, CX, CY, CXD, CYD):
            arrive(kind, i)
        for kind in (XO, YO, CO, YD, XD, CX, CY, CXD, CYD):
            send(kind, i).wait_send()

        @pl.when((zz <= z) & (z < 3))
        def _():
            send(ZU, i).wait_send()

        @pl.when((zz >= z) & (z > 0))
        def _():
            send(ZD, i).wait_send()

        return 0

    return step, UNITS + core_lag, lambda: lax.fori_loop(0, UNITS, finish, 0)


def reduce_steps(
    g_ref, o_ref, lb, cb, xb, yb, dxb, dyb, zub, zdb, ss, rs, cs, cr, ls, more
):
    z, x, y, c = coords()
    xn, yn, cn = 1 - x, 1 - y, 1 - c
    to_x, to_y, to_core = dev(z, xn, y, c), dev(z, x, yn, c), dev(z, x, y, cn)
    lag1, lag2, lag3, lag4 = 1, 2, 3, 4
    XS, YS, DXS, DYS, ZD, ZU = range(6)

    def unit(i):
        r = i // CHUNKS
        return 3 - r, i - r * CHUNKS

    def rows(zz, xx, yy, cc, k):
        s = (zz * 2 + xx) * 4 + yy * 2 + cc - 8
        return g_ref.at[pl.ds(pl.multiple_of(s * SHARD + k * CHUNK, 16), CHUNK)]

    places = [(xn, yn), (xn, y), (x, yn), (x, y)]

    def load(i, p):
        zz, k = unit(i)
        xx, yy = places[p]
        return pltpu.make_async_copy(rows(zz, xx, yy, c, k), lb.at[i, p], ls.at[i, p])

    def to_sibling(i, p):
        zz, k = unit(i)
        xx, yy = places[p]
        return remote(rows(zz, xx, yy, cn, k), cb.at[i, p], cs.at[i, p], cr.at[i, p], to_core)

    def load_all(i, _):
        for p in range(4):
            load(i, p).start()
        return 0

    lax.fori_loop(0, UNITS, load_all, 0)
    meet_neighbours(z, x, y, c, [to_x, to_y, to_core] + more)

    def send_all(i, _):
        for p in range(4):
            to_sibling(i, p).start()
        return 0

    lax.fori_loop(0, UNITS, send_all, 0)

    def over(kind, src, dst, i, to):
        return remote(src, dst, ss.at[kind, i], rs.at[kind, i], to)

    def diag_x(i):
        return over(DXS, lb.at[i, 0, 0:OVER_X], dxb.at[i], i, to_x)

    def diag_y(i):
        return over(DYS, lb.at[i, 0, OVER_X:CHUNK], dyb.at[i], i, to_y)

    def whole_x(i):
        return over(XS, lb.at[i, 1], xb.at[i], i, to_x)

    def whole_y(i):
        return over(YS, lb.at[i, 2], yb.at[i], i, to_y)

    def down(i):
        return over(ZD, lb.at[i, 3], zub.at[i], i, dev(z - 1, x, y, c))

    def up(i):
        return over(ZU, lb.at[i, 3], zdb.at[i], i, dev(z + 1, x, y, c))

    def have(i, p):
        load(i, p).wait()
        to_sibling(i, p).wait_recv()

    def step(i, _):
        @pl.when(i < UNITS)
        def _():
            have(i, 0)
            add_tiles(lb.at[i, 0], CHUNK, lb.at[i, 0], cb.at[i, 0])
            diag_x(i).start()
            diag_y(i).start()

        j = i - lag1

        @pl.when((j >= 0) & (j < UNITS))
        def _():
            have(j, 1)
            have(j, 2)
            diag_y(j).wait_recv()
            diag_x(j).wait_recv()
            a, b = lb.at[j, 1], cb.at[j, 1]
            low, high = slice(0, OVER_X), slice(OVER_X, CHUNK)
            add_tiles(a.at[low], OVER_X, a.at[low], b.at[low])
            add_tiles(a.at[high], CHUNK - OVER_X, a.at[high], b.at[high], dyb.at[j])
            whole_x(j).start()
            a, b = lb.at[j, 2], cb.at[j, 2]
            add_tiles(a.at[low], OVER_X, a.at[low], b.at[low], dxb.at[j])
            add_tiles(a.at[high], CHUNK - OVER_X, a.at[high], b.at[high])
            whole_y(j).start()

        m = i - lag2

        @pl.when((m >= 0) & (m < UNITS))
        def _():
            zz, k = unit(m)
            have(m, 3)
            whole_x(m).wait_recv()
            whole_y(m).wait_recv()
            parts = [lb.at[m, 3], cb.at[m, 3], xb.at[m], yb.at[m]]

            @pl.when(z != zz)
            def _():
                add_tiles(lb.at[m, 3], CHUNK, *parts)

            @pl.when((z == 3) & (zz < 3))
            def _():
                down(m).start()

            @pl.when(z == 0)
            def _():
                up(m).start()

            @pl.when(z == zz)
            def _():
                add_tiles(o_ref.at[pl.ds(pl.multiple_of(k * CHUNK, 16), CHUNK)], CHUNK, *parts)

        n = i - lag3

        @pl.when((n >= 0) & (n < UNITS))
        def _():
            zz, _ = unit(n)

            @pl.when((z > zz) & (z < 3))
            def _():
                down(n).wait_recv()
                add_tiles(lb.at[n, 3], CHUNK, lb.at[n, 3], zub.at[n])
                down(n).start()

            @pl.when((z < zz) & (z > 0))
            def _():
                up(n).wait_recv()
                add_tiles(lb.at[n, 3], CHUNK, lb.at[n, 3], zdb.at[n])
                up(n).start()

        o = i - lag4

        @pl.when(o >= 0)
        def _():
            zz, k = unit(o)

            @pl.when(z == zz)
            def _():
                dst = o_ref.at[pl.ds(pl.multiple_of(k * CHUNK, 16), CHUNK)]

                @pl.when(z < 3)
                def _():
                    down(o).wait_recv()
                    add_tiles(dst, CHUNK, dst, zub.at[o])

                up(o).wait_recv()
                add_tiles(dst, CHUNK, dst, zdb.at[o])

        return 0

    def finish(i, _):
        zz, _ = unit(i)
        for p in range(4):
            to_sibling(i, p).wait_send()
        for copy in (diag_x(i), diag_y(i), whole_x(i), whole_y(i)):
            copy.wait_send()

        @pl.when(z > zz)
        def _():
            down(i).wait_send()

        @pl.when(z < zz)
        def _():
            up(i).wait_send()

        return 0

    return step, UNITS + lag4, lambda: lax.fori_loop(0, UNITS, finish, 0)


def reduce_rooms():
    def room(*shape):
        return pltpu.VMEM(shape + (D,), bf)

    return [
        room(UNITS, 4, CHUNK), room(UNITS, 4, CHUNK),
        room(UNITS, CHUNK), room(UNITS, CHUNK),
        room(UNITS, OVER_X), room(UNITS, CHUNK - OVER_X),
        room(UNITS, CHUNK), room(UNITS, CHUNK),
        DMA((6, UNITS)), DMA((6, UNITS)), DMA((UNITS, 4)), DMA((UNITS, 4)), DMA((UNITS, 4)),
    ]


def last_kernel(
    v_ref, n_ref, can_ref, nrm_ref, st_ref,
    out_ref, ng_ref, sto_ref,
    ext, hal, hsend, av, bv, cv, dv, zv, sums, sv, nc, ny, nsv, nland, sland,
    s1, r1, s2, r2, zs, zr, ms, mr, qs, qr, hsem,
):
    z, x, y, c = coords()
    xn, yn, cn = 1 - x, 1 - y, 1 - c
    s = (z * 2 + x) * 4 + y * 2 + c
    core = dev(z, x, y, cn)
    xs, xo, ys, yo = dev(z, xn, y, c), dev(z, xn, y, cn), dev(z, x, yn, c), dev(z, x, yn, cn)
    prv = lax.rem(s + 31, 32)
    bar = pltpu.get_barrier_semaphore()

    def hello(i, _):
        greet(bar, linear(lax.rem(s + i, 32)))
        return 0

    lax.fori_loop(1, 32, hello, 0)
    pl.semaphore_wait(bar, 31)
    half = 256

    def unit(xx, yy, cc):
        at = pl.multiple_of((xx * 4 + yy * 2 + cc) * 128, 128)
        return v_ref.at[:, pl.ds(at, 128), :]

    def rows(yy, cc, k):
        return n_ref.at[pl.ds(pl.multiple_of((yy * 2 + cc) * 512 + k * half, half), half)]

    far = [remote(rows(yn, cn, k), nc.at[1, k], s2.at[0, k], r2.at[0, k], core) for k in range(2)]
    near = [remote(rows(y, cn, k), nc.at[0, k], s2.at[1, k], r2.at[1, k], core) for k in range(2)]
    opposite = [
        remote(unit(xn, yn, cc), av.at[i], s1.at[i], r1.at[i], xs) for i, cc in enumerate((c, cn))
    ]
    beside = [
        remote(unit(xn, y, c), bv.at[0], s1.at[2], r1.at[2], xs),
        remote(unit(xn, y, cn), bv.at[1], s1.at[3], r1.at[3], xo),
    ]
    sibling = remote(unit(x, y, cn), cv, s1.at[4], r1.at[4], core)
    for copy in far + opposite + beside + [sibling] + near:
        copy.start()

    def tell(i):
        return remote(st_ref, sland.at[s], qs.at[i], qr.at[s], linear(lax.rem(s + i, 32)))

    def tell_all(i, _):
        tell(i).start()
        return 0

    lax.fori_loop(1, 32, tell_all, 0)
    norm_send = remote(nrm_ref, nland.at[s], ms.at[0], mr.at[s], (7, 3))

    @pl.when(s != 31)
    def _():
        norm_send.start()

    later = []
    across = []
    for i, cc in enumerate((c, cn)):
        opposite[i].wait_recv()
        for j in range(3):
            add_rows(sv.at[i, j], unit(x, yn, cc).at[j], av.at[i, j])
        copy = remote(sv.at[i], dv.at[i], s1.at[5 + i], r1.at[5 + i], (ys, yo)[i])
        copy.start()
        across.append(copy)
    for k in range(2):
        far[k].wait_recv()

        def add_far(q, _):
            at = pl.ds(pl.multiple_of(q * 32, 32), 32)
            add_rows(nsv.at[k, at], rows(yn, c, k).at[at], nc.at[1, k, at])
            return 0

        lax.fori_loop(0, half // 32, add_far, 0)
        copy = remote(nsv.at[k], ny.at[k], s2.at[2, k], r2.at[2, k], ys)
        copy.start()
        later.append(copy)

    blocks = [y * 2 + c, y * 2 + cn, yn * 2 + c, yn * 2 + cn]

    def down(q):
        return remote(sums.at[q], zv.at[q], zs.at[q], zr.at[q], dev(z - 1, x, y, c))

    for q in range(4):
        if q == 0:
            beside[0].wait_recv()
            parts = [unit(x, y, c), bv.at[0]]
        elif q == 1:
            sibling.wait_recv()
            beside[1].wait_recv()
            parts = [cv, bv.at[1]]
        else:
            across[q - 2].wait_recv()
            parts = [dv.at[q - 2]]

        @pl.when(z < 3)
        def _():
            remote(sums.at[q], zv.at[q], zs.at[q], zr.at[q], core).wait_recv()

        @pl.when(z == 3)
        def _():
            for j in range(3):
                add_rows(sums.at[q, j], *[part.at[j] for part in parts])
            down(q).start()

        @pl.when((z == 1) | (z == 2))
        def _():
            for j in range(3):
                add_rows(sums.at[q, j], zv.at[q, j], *[part.at[j] for part in parts])
            down(q).start()

        @pl.when(z == 0)
        def _():
            for j in range(3):
                total = zv[q, j].astype(f32)
                for part in parts:
                    total = total + part[j].astype(f32)
                for h in range(2):
                    at = 64 - 2 * s + 8 * j + 2 * blocks[q] + h
                    ext[pl.ds(at, 128, stride=24), :] = total[:, 128 * h : 128 * h + 128]

    base = 64 - 2 * s

    def place(src, first, count, apart):
        for j in range(apart):
            for k in range(8):
                ext[pl.ds(base + 8 * (first + j) + k, count, stride=8 * apart), :] = can_ref[
                    src + j * count : src + (j + 1) * count, 128 * k : 128 * k + 128
                ]

    @pl.when((s == 8) | (s == 9) | (s >= 22))
    def _():
        place(0, 0, 384, 1)

    @pl.when(s == 10)
    def _():
        place(0, 0, 256, 1)
        place(256, 256, 32, 4)

    @pl.when((s >= 11) & (s <= 20))
    def _():
        place(0, 0, 96, 4)

    @pl.when(s == 21)
    def _():
        place(0, 0, 32, 4)
        place(128, 128, 256, 1)

    hsend[...] = ext[0:64, :]
    halo = remote(hsend, hal, hsem.at[0], hsem.at[1], linear(prv))
    halo.start()
    for k in range(2):
        near[k].wait_recv()
        later[k].wait_recv()

        def add_own(q, _):
            at = pl.ds(pl.multiple_of(q * 32, 32), 32)
            to = pl.ds(pl.multiple_of(k * half + q * 32, 32), 32)
            add_rows(ng_ref.at[to], rows(y, c, k).at[at], nc.at[0, k, at], ny.at[k, at])
            return 0

        lax.fori_loop(0, half // 32, add_own, 0)

    def hear(i, _):
        o = lax.rem(s + i, 32)
        remote(st_ref, sland.at[o], qs.at[0], qr.at[o], core).wait_recv()
        return 0

    lax.fori_loop(1, 32, hear, 0)
    sland[pl.ds(s, 1)] = st_ref[...].reshape(1, 8, 128)
    sto_ref[...] = jnp.sum(sland[...], axis=0)
    halo.wait()

    @pl.when(s != 31)
    def _():
        row = lax.broadcasted_iota(jnp.int32, (64, 128), 0)
        end = slice(NATURAL, NATURAL + 64)
        ext[end, :] = jnp.where(row >= 64 - 2 * (s + 1), hal[...], ext[end, :])

    @pl.when(s == 31)
    def _():
        def gather(i, total):
            remote(nrm_ref, nland.at[i], ms.at[0], mr.at[i], core).wait_recv()
            return total + nland[i]

        total = lax.fori_loop(0, 31, gather, nrm_ref[...])
        for k in range(8):
            ext[pl.ds(base + 8 * 384 + k, 8, stride=8), :] = total[:, 128 * k : 128 * k + 128]

    out_ref[...] = ext[64 : 64 + NATURAL, :]
    for copy in far + opposite + beside + [sibling] + near + across + later:
        copy.wait_send()

    @pl.when(z > 0)
    def _():
        for q in range(4):
            down(q).wait_send()

    def told(i, _):
        tell(i).wait_send()
        return 0

    lax.fori_loop(1, 32, told, 0)

    @pl.when(s != 31)
    def _():
        norm_send.wait_send()


def last_reduce(qkv_grads, normed_part, canonical, norm_part, squares):
    shape = jax.ShapeDtypeStruct
    unit = (3, 128, 256)
    room = pltpu.VMEM
    return pl.pallas_call(
        last_kernel,
        out_shape=(shape((NATURAL, 128), f32), shape((512, D), f32), shape((8, 128), f32)),
        in_specs=[VM] * 5,
        out_specs=(VM, VM, VM),
        scratch_shapes=[
            room((64 + NATURAL + 6, 128), f32), room((64, 128), f32), room((64, 128), f32),
            room((2,) + unit, bf), room((2,) + unit, bf), room(unit, bf), room((2,) + unit, bf),
            room((4,) + unit, bf), room((4,) + unit, bf), room((2,) + unit, bf),
            room((2, 2, 256, D), bf), room((2, 256, D), bf), room((2, 256, D), bf),
            room((32, 8, D), f32), room((32, 8, 128), f32),
            DMA((7,)), DMA((7,)), DMA((3, 2)), DMA((3, 2)), DMA((4,)), DMA((4,)),
            DMA((1,)), DMA((32,)), DMA((32,)), DMA((32,)), DMA((2,)),
        ],
        compiler_params=params_for(3),
    )(qkv_grads, normed_part, canonical, norm_part, squares)


def swap_kernel(n, to_tokens, a_ref, o_ref, ss, rs, ls):
    me = lax.axis_index("fsdp")
    bar = pltpu.get_barrier_semaphore()
    for i in range(1, n):
        pl.semaphore_signal(
            bar, inc=1, device_id={"fsdp": lax.rem(me + i, n)}, device_id_type=MESH
        )
    pl.semaphore_wait(bar, n - 1)
    tokens = (a_ref if to_tokens else o_ref).shape[0] // n
    width = (o_ref if to_tokens else a_ref).shape[1] // n

    def token_block(ref, owner):
        return ref.at[pl.ds(pl.multiple_of(owner * tokens, 16), tokens)]

    def head_block(ref, owner):
        return ref.at[:, pl.ds(pl.multiple_of(owner * width, 128), width)]

    take, put = (token_block, head_block) if to_tokens else (head_block, token_block)
    local = pltpu.make_async_copy(take(a_ref, me), put(o_ref, me), ls)
    local.start()
    copies = []
    for i in range(1, n):
        to = lax.rem(me + i, n)
        copy = pltpu.make_async_remote_copy(
            src_ref=take(a_ref, to), dst_ref=put(o_ref, me), send_sem=ss.at[i], recv_sem=rs.at[i],
            device_id={"fsdp": to}, device_id_type=MESH,
        )
        copy.start()
        copies.append(copy)
    for i in range(1, n):
        copies[i - 1].wait_send()
        ref = put(o_ref, lax.rem(me - i + n, n))
        pltpu.make_async_remote_copy(
            src_ref=ref, dst_ref=ref, send_sem=ss.at[i], recv_sem=rs.at[i],
            device_id={"fsdp": lax.rem(me + i, n)}, device_id_type=MESH,
        ).wait_recv()
    local.wait()


def swap(array, n, to_tokens, collective):
    rows, columns = array.shape
    shape = (rows // n, columns * n) if to_tokens else (rows * n, columns // n)
    return pl.pallas_call(
        functools.partial(swap_kernel, n, to_tokens),
        out_shape=jax.ShapeDtypeStruct(shape, bf),
        in_specs=[VM],
        out_specs=VM,
        scratch_shapes=[DMA((n,)), DMA((n,)), DMA],
        compiler_params=params_for(collective, 32),
    )(array)


def partner(values):
    width = values.shape[-1]
    lane = lax.broadcasted_iota(jnp.int32, values.shape, values.ndim - 1)
    after = pltpu.roll(values, width - 32, values.ndim - 1)
    before = pltpu.roll(values, 32, values.ndim - 1)
    return jnp.where(lane % 64 < 32, after, before)


def project_rows(rows, n_ref, w_ref, cosine, sine):
    rows = rows.astype(f32)
    center = rows - jnp.mean(rows, axis=-1, keepdims=True)
    inverse = lax.rsqrt(jnp.mean(center * center, axis=-1, keepdims=True) + EPSILON)
    normed = (center * inverse * n_ref[0:1, :] + n_ref[1:2, :]).astype(bf)
    mixed = [jnp.dot(normed, w_ref[j], preferred_element_type=f32) for j in range(3)]
    for j in range(2):
        parts = [mixed[j][:, at : at + 128] for at in range(0, mixed[j].shape[1], 128)]
        parts = [part * cosine + partner(part) * sine for part in parts]
        mixed[j] = jnp.concatenate(parts, axis=1)
    return [normed] + [part.astype(bf) for part in mixed]


def qkv_kernel(h_ref, n_ref, w_ref, c_ref, s_ref, *out_refs):
    for ref, part in zip(out_refs, project_rows(h_ref[...], n_ref, w_ref, c_ref[...], s_ref[...])):
        ref[...] = part


def project(hidden, norm_rows, w_qkv, cosine, sine):
    tokens, width = hidden.shape[0], w_qkv.shape[2]
    block = 256
    rows = lambda w: pl.BlockSpec((block, w), lambda i: (i, 0))
    full = lambda a: pl.BlockSpec(a.shape, lambda i: (0,) * a.ndim)
    shape = jax.ShapeDtypeStruct
    return pl.pallas_call(
        qkv_kernel,
        grid=(tokens // block,),
        in_specs=[rows(D), full(norm_rows), full(w_qkv), rows(128), rows(128)],
        out_specs=[rows(D), rows(width), rows(width), rows(width)],
        out_shape=[shape((tokens, D), bf)] + [shape((tokens, width), bf)] * 3,
        compiler_params=params_for(),
    )(hidden, norm_rows, w_qkv, cosine, sine)


NT = (((1,), (1,)), ((), ()))
TN = (((0,), (0,)), ((), ()))
BLOCK = 512


def one_head(pair, h):
    lane = lax.broadcasted_iota(jnp.int32, pair.shape, 1)
    return jnp.where((lane < 64) if h == 0 else (lane >= 64), pair, jnp.zeros_like(pair))


def causal(scores, i, j):
    key = j * scores.shape[0] + lax.broadcasted_iota(jnp.int32, scores.shape, 0)
    query = i * scores.shape[1] + lax.broadcasted_iota(jnp.int32, scores.shape, 1)
    return jnp.where(key <= query, scores, MASKED)


def attend_rows(i, queries, k_ref, v_ref):
    heads = [one_head(queries, h) for h in range(2)]

    def block(j, carry, masked):
        at = pl.ds(pl.multiple_of(j * BLOCK, BLOCK), BLOCK)
        keys, values = k_ref[at, :], v_ref[at, :]
        out = []
        for h in range(2):
            peak, total, summed = carry[3 * h : 3 * h + 3]
            scores = lax.dot_general(keys, heads[h], NT, preferred_element_type=f32)
            scores = scores * (SCALE * LOG2E)
            if masked:
                scores = causal(scores, i, j)
            new_peak = jnp.maximum(peak, jnp.max(scores, axis=0, keepdims=True))
            weights = jnp.exp2(scores - new_peak)
            shrink = jnp.exp2(peak - new_peak)
            total = total * shrink + jnp.sum(weights, axis=0, keepdims=True)
            part = lax.dot_general(
                values[:, 64 * h : 64 * h + 64], weights.astype(bf), TN, preferred_element_type=f32
            )
            out += [new_peak, total, summed * shrink + part]
        return tuple(out)

    start = (
        jnp.full((1, BLOCK), MASKED, f32), jnp.zeros((1, BLOCK), f32), jnp.zeros((64, BLOCK), f32)
    ) * 2
    carry = lax.fori_loop(0, i, lambda j, carry: block(j, carry, False), start)
    peak0, total0, sum0, peak1, total1, sum1 = block(i, carry, True)
    out = jnp.concatenate([sum0 / total0, sum1 / total1], axis=0).T
    logs = jnp.concatenate([peak0 + jnp.log2(total0), peak1 + jnp.log2(total1)], axis=0)
    return out, logs


def attend_kernel(q_ref, k_ref, v_ref, o_ref, low_ref, l_ref):
    out, logs = attend_rows(pl.program_id(1), q_ref[...], k_ref, v_ref)
    o_ref[...] = out
    low_ref[...] = out.astype(bf)
    l_ref[...] = logs.reshape(1, 2, BLOCK)


def attend(queries, keys, values):
    tokens, width = queries.shape
    pairs = width // 128
    block = pl.BlockSpec((BLOCK, 128), lambda p, i: (i, p))
    full = pl.BlockSpec((tokens, 128), lambda p, i: (0, p))
    logs = pl.BlockSpec((1, 2, BLOCK), lambda p, i: (p, 0, i))
    shape = jax.ShapeDtypeStruct
    return pl.pallas_call(
        attend_kernel,
        grid=(pairs, tokens // BLOCK),
        in_specs=[block, full, full],
        out_specs=[block, block, logs],
        out_shape=[
            shape((tokens, width), f32), shape((tokens, width), bf), shape((pairs, 2, tokens), f32)
        ],
        compiler_params=params_for(),
    )(queries, keys, values)


def attend_back_rows(i, queries, grads, attended, logs, k_ref, v_ref, dk, dv):
    heads = [one_head(queries, h) for h in range(2)]
    grad_heads = [one_head(grads, h) for h in range(2)]
    both_heads = jnp.concatenate(heads, axis=0)
    both_grads = jnp.concatenate(grad_heads, axis=0)
    products = (attended * grads.astype(f32)).T
    dots = [jnp.sum(products[64 * h : 64 * h + 64], axis=0, keepdims=True) for h in range(2)]

    def block(j, sums, masked):
        at = pl.ds(pl.multiple_of(j * BLOCK, BLOCK), BLOCK)
        keys, values = k_ref[at, :], v_ref[at, :]
        weights, score_grads = [], []
        for h in range(2):
            scores = lax.dot_general(keys, heads[h], NT, preferred_element_type=f32)
            scores = scores * (SCALE * LOG2E)
            if masked:
                scores = causal(scores, i, j)
            prob = jnp.exp2(scores - logs[h : h + 1])
            prob_grad = lax.dot_general(values, grad_heads[h], NT, preferred_element_type=f32)
            score_grads.append((prob * (prob_grad - dots[h])).astype(bf))
            weights.append(prob.astype(bf))
        dv[at, :] += jnp.dot(
            jnp.concatenate(weights, axis=1), both_grads, preferred_element_type=f32
        )
        dk[at, :] += jnp.dot(
            jnp.concatenate(score_grads, axis=1), both_heads, preferred_element_type=f32
        )
        return tuple(
            sums[h] + lax.dot_general(score_grads[h], keys, TN, preferred_element_type=f32)
            for h in range(2)
        )

    zero = jnp.zeros((BLOCK, 128), f32)
    sums = lax.fori_loop(0, i, lambda j, sums: block(j, sums, False), (zero, zero))
    sums = block(i, sums, True)
    lane = lax.broadcasted_iota(jnp.int32, zero.shape, 1)
    return jnp.where(lane < 64, sums[0], sums[1]) * SCALE


def turn_back(grads, cosine, sine):
    return (grads * cosine - partner(grads) * sine).astype(bf)


def finish_keys(dk, dv, c_ref, s_ref, dk_ref, dv_ref):
    def turn(t, _):
        at = pl.ds(pl.multiple_of(t * 256, 256), 256)
        dk_ref[at, :] = turn_back(dk[at, :] * SCALE, c_ref[at, :], s_ref[at, :])
        dv_ref[at, :] = dv[at, :].astype(bf)
        return 0

    lax.fori_loop(0, dk.shape[0] // 256, turn, 0)


def attend_back_kernel(
    q_ref, k_ref, v_ref, g_ref, a_ref, l_ref, cq_ref, sq_ref, c_ref, s_ref,
    dq_ref, dk_ref, dv_ref, dk, dv,
):
    i = pl.program_id(1)

    @pl.when(i == 0)
    def _():
        dk[...] = jnp.zeros_like(dk)
        dv[...] = jnp.zeros_like(dv)

    query_grad = attend_back_rows(
        i, q_ref[...], g_ref[...], a_ref[...], l_ref[0], k_ref, v_ref, dk, dv
    )
    dq_ref[...] = turn_back(query_grad, cq_ref[...], sq_ref[...])

    @pl.when(i == pl.num_programs(1) - 1)
    def _():
        finish_keys(dk, dv, c_ref, s_ref, dk_ref, dv_ref)


def attend_back(queries, keys, values, grads, attended, logs, cosine, sine):
    tokens, width = queries.shape
    block = pl.BlockSpec((BLOCK, 128), lambda p, i: (i, p))
    full = pl.BlockSpec((tokens, 128), lambda p, i: (0, p))
    table_block = pl.BlockSpec((BLOCK, 128), lambda p, i: (i, 0))
    table = pl.BlockSpec((tokens, 128), lambda p, i: (0, 0))
    log_block = pl.BlockSpec((1, 2, BLOCK), lambda p, i: (p, 0, i))
    return pl.pallas_call(
        attend_back_kernel,
        grid=(width // 128, tokens // BLOCK),
        in_specs=[block, full, full, block, block, log_block, table_block, table_block, table, table],
        out_specs=[block, full, full],
        out_shape=[jax.ShapeDtypeStruct((tokens, width), bf)] * 3,
        scratch_shapes=[pltpu.VMEM((tokens, 128), f32), pltpu.VMEM((tokens, 128), f32)],
        compiler_params=params_for(),
    )(queries, keys, values, grads, attended, logs, cosine, sine, cosine, sine)


def swap_copies(take, put, ss, rs, base):
    z, x, y, c = coords()
    others = [(y, 1 - c), (1 - y, c), (1 - y, 1 - c)]
    me = y * 2 + c
    starts, arrivals = [], []
    for i, (yy, cc) in enumerate(others):
        starts.append(
            remote(take(yy * 2 + cc), put(me), ss.at[base + i], rs.at[base + i], dev(z, x, yy, cc))
        )
        ref = put(yy * 2 + cc)
        arrivals.append(remote(ref, ref, ss.at[base + i], rs.at[base + i], dev(z, x, yy, cc)))
    return me, starts, arrivals


def forward_kernel(
    h_ref, n_ref, w_ref, cos_ref, sin_ref, can_ref,
    g_ref, normed_ref, q_ref, k_ref, v_ref, o_ref, l_ref, t_ref,
    low, ss, rs, ls, ts, tr,
):
    z, x, y, c = coords()
    pump, steps, finish = gather_steps(
        can_ref, g_ref, ss, rs, ls, [dev(z, x, 1 - y, 1 - c)]
    )
    pump(0, 0)
    pump(1, 0)

    def project_step(t, _):
        at = pl.ds(pl.multiple_of(t * 256, 256), 256)
        parts = project_rows(h_ref[at, :], n_ref, w_ref, cos_ref[at, :], sin_ref[at, :])
        for ref, part in zip((normed_ref, q_ref, k_ref, v_ref), parts):
            ref[at, :] = part

        @pl.when(lax.rem(t, 4) == 3)
        def _():
            pump(2 + t // 4, 0)

        return 0

    lax.fori_loop(0, 8, project_step, 0)

    def attend_step(t, _):
        p = t // 4
        i = t - 4 * p
        at = pl.ds(pl.multiple_of(i * BLOCK, BLOCK), BLOCK)
        lanes = pl.ds(pl.multiple_of(p * 128, 128), 128)
        out, logs = attend_rows(i, q_ref[at, lanes], k_ref.at[:, lanes], v_ref.at[:, lanes])
        o_ref[at, lanes] = out
        low[at, lanes] = out.astype(bf)
        l_ref[p, :, at] = logs
        pump(4 + t, 0)
        return 0

    lax.fori_loop(0, 8, attend_step, 0)

    def take(owner):
        return low.at[pl.ds(pl.multiple_of(owner * 512, 512), 512)]

    def put(owner):
        return t_ref.at[:, pl.ds(pl.multiple_of(owner * 256, 256), 256)]

    me, starts, arrivals = swap_copies(take, put, ts, tr, 0)
    for copy in starts:
        copy.start()
    own = pltpu.make_async_copy(take(me), put(me), ts.at[3])
    own.start()
    lax.fori_loop(12, steps, pump, 0)
    for copy in arrivals:
        copy.wait_recv()
    for copy in starts:
        copy.wait_send()
    own.wait()
    finish()


def forward(hidden, norm_rows, w_qkv, cosine, sine, canonical):
    shape = jax.ShapeDtypeStruct
    return pl.pallas_call(
        forward_kernel,
        out_shape=(
            shape((24 * SHARD, D), bf), shape((2048, D), bf),
            shape((2048, 256), bf), shape((2048, 256), bf), shape((2048, 256), bf),
            shape((2048, 256), f32), shape((2, 2, 2048), f32), shape((512, D), bf),
        ),
        in_specs=[VM] * 6,
        out_specs=(ANY,) + (VM,) * 7,
        scratch_shapes=[
            pltpu.VMEM((2048, 256), bf),
            DMA((11, UNITS)), DMA((11, UNITS)), DMA, DMA((4,)), DMA((3,)),
        ],
        compiler_params=params_for(1),
    )(hidden, norm_rows, w_qkv, cosine, sine, canonical)


def backward_kernel(
    gw_ref, ag_ref, q_ref, k_ref, v_ref, a_ref, l_ref, cos_ref, sin_ref,
    own_ref, dq_ref, dk_ref, dv_ref,
    grads, dk, dv, ts, tr, *rooms,
):
    z, x, y, c = coords()
    pump, steps, finish = reduce_steps(gw_ref, own_ref, *rooms, [dev(z, x, 1 - y, 1 - c)])

    def take(owner):
        return ag_ref.at[:, pl.ds(pl.multiple_of(owner * 256, 256), 256)]

    def put(owner):
        return grads.at[pl.ds(pl.multiple_of(owner * 512, 512), 512)]

    me, starts, arrivals = swap_copies(take, put, ts, tr, 0)
    for copy in starts:
        copy.start()
    own = pltpu.make_async_copy(take(me), put(me), ts.at[3])
    own.start()
    pump(0, 0)
    pump(1, 0)
    for copy in arrivals:
        copy.wait_recv()
    own.wait()

    def step(t, _):
        p = t // 4
        i = t - 4 * p
        at = pl.ds(pl.multiple_of(i * BLOCK, BLOCK), BLOCK)
        lanes = pl.ds(pl.multiple_of(p * 128, 128), 128)

        @pl.when(i == 0)
        def _():
            dk[...] = jnp.zeros_like(dk)
            dv[...] = jnp.zeros_like(dv)

        query_grad = attend_back_rows(
            i, q_ref[at, lanes], grads[at, lanes], a_ref[at, lanes], l_ref[p, :, at],
            k_ref.at[:, lanes], v_ref.at[:, lanes], dk, dv,
        )
        dq_ref[at, lanes] = turn_back(query_grad, cos_ref[at, :], sin_ref[at, :])

        @pl.when(i == 3)
        def _():
            finish_keys(
                dk, dv, cos_ref, sin_ref, dk_ref.at[:, lanes], dv_ref.at[:, lanes]
            )

        pump(2 + t, 0)
        return 0

    lax.fori_loop(0, 8, step, 0)
    lax.fori_loop(10, steps, pump, 0)
    for copy in starts:
        copy.wait_send()
    finish()


def backward(weight_grads, attended_grad, queries, keys, values, attended, logs, cosine, sine):
    shape = jax.ShapeDtypeStruct
    room = pltpu.VMEM
    return pl.pallas_call(
        backward_kernel,
        out_shape=(shape((SHARD, D), f32),) + (shape((2048, 256), bf),) * 3,
        in_specs=[ANY] + [VM] * 8,
        out_specs=(VM,) * 4,
        scratch_shapes=[
            room((2048, 256), bf), room((2048, 128), f32), room((2048, 128), f32),
            DMA((4,)), DMA((3,)), *reduce_rooms(),
        ],
        compiler_params=params_for(2, 60),
    )(weight_grads, attended_grad, queries, keys, values, attended, logs, cosine, sine)


ROWS = 128
GELU_A = math.sqrt(2.0 / math.pi)
GELU_B = 0.044715


def mean_of(values):
    return jnp.mean(values, axis=-1, keepdims=True)


def unit_of(values):
    center = values - mean_of(values)
    inverse = lax.rsqrt(mean_of(center * center) + EPSILON)
    return center * inverse, inverse


def into_norm(grads, unit, inverse, gain):
    scaled = grads * gain
    return inverse * (scaled - mean_of(scaled) - unit * mean_of(scaled * unit))


def fold(values):
    total = values[0:8]
    for at in range(8, values.shape[0], 8):
        total = total + values[at : at + 8]
    return total


def up_pieces(j):
    pieces = [(D + 32 * j, 0, 32)]
    pieces += [(D + 128 + 384 * i + 96 * j, 32 + 96 * i, 96) for i in range(10)]
    pieces.append((D + 3968 + 32 * j, 992, 32))
    return pieces


def dense_kernel(
    a_ref, h_ref, c_ref, scale_ref, n_ref, w_ref,
    o_ref, rg_ref, ag_ref, gw_ref, ns_ref, sq_ref,
    wo, wu, wd, residual, branch, lowered, entered, act, slope, lgrad, egrad, stage, sums,
    ws, ups, gs,
):
    tokens = a_ref.shape[0]
    pieces = tokens // ROWS
    load_o = pltpu.make_async_copy(w_ref.at[0:D], wo, ws.at[0])
    loads_d = [
        pltpu.make_async_copy(w_ref.at[5 * D + D * j : 6 * D + D * j], wd.at[j], ws.at[1 + j])
        for j in range(4)
    ]
    loads_u = [
        [
            pltpu.make_async_copy(
                w_ref.at[src : src + count], wu.at[j, to : to + count], ups.at[j, i]
            )
            for i, (src, to, count) in enumerate(up_pieces(j))
        ]
        for j in range(4)
    ]
    load_o.start()
    for j in range(4):
        for copy in loads_u[j]:
            copy.start()
    for copy in loads_d:
        copy.start()
    sums[...] = jnp.zeros_like(sums)
    width = 1024

    def columns(t):
        return pl.ds(pl.multiple_of(t * width, width), width)

    def over_columns(body, count=D // width):
        def go(t, _):
            body(columns(t))
            return 0

        lax.fori_loop(0, count, go, 0)

    def over_rows(body):
        def go(t, _):
            body(pl.ds(pl.multiple_of(t * ROWS, ROWS), ROWS))
            return 0

        lax.fori_loop(0, pieces, go, 0)

    load_o.wait()

    def branch_step(at):
        branch[:, at] = jnp.dot(a_ref[...], wo[:, at], preferred_element_type=f32)

    over_columns(branch_step)

    def enter_step(at):
        values = branch[at, :]
        unit, _ = unit_of(values)
        res = h_ref[at, :].astype(f32) + unit * n_ref[2:3, :] + n_ref[3:4, :]
        residual[at, :] = res
        unit, _ = unit_of(res)
        entered[at, :] = (unit * n_ref[4:5, :] + n_ref[5:6, :]).astype(bf)
        sums[0] += fold(values * values)

    over_rows(enter_step)

    for j in range(4):
        for copy in loads_u[j]:
            copy.wait()

        def lift_step(at):
            lifted = jnp.dot(entered[...], wu[j, :, at], preferred_element_type=f32)
            square = lifted * lifted
            tanh = jnp.tanh(lifted * (GELU_A + (GELU_A * GELU_B) * square))
            half = 0.5 + 0.5 * tanh
            act[j, :, at] = (lifted * half).astype(bf)
            slope[j, :, at] = half + lifted * (0.5 - 0.5 * tanh * tanh) * (
                GELU_A + (3.0 * GELU_A * GELU_B) * square
            )

        over_columns(lift_step)
    for copy in loads_d:
        copy.wait()

    def lower_step(at):
        total = jnp.dot(act[0], wd[0, :, at], preferred_element_type=f32)
        for j in range(1, 4):
            total = total + jnp.dot(act[j], wd[j, :, at], preferred_element_type=f32)
        lowered[:, at] = total

    over_columns(lower_step)
    scale = scale_ref[0, 0]

    def out_step(at):
        values = lowered[at, :]
        unit, inverse = unit_of(values)
        o_ref[at, :] = (residual[at, :] + unit * n_ref[6:7, :] + n_ref[7:8, :]).astype(bf)
        upstream = c_ref[at, :].astype(f32) * scale
        lgrad[at, :] = into_norm(upstream, unit, inverse, n_ref[6:7, :]).astype(bf)
        sums[1] += fold(values * values)
        sums[2] += fold(upstream * unit)
        sums[3] += fold(upstream)

    over_rows(out_step)

    def store(buffer, j, slot):
        return [
            pltpu.make_async_copy(
                stage.at[buffer, to : to + count], gw_ref.at[src : src + count], gs.at[slot, i]
            )
            for i, (src, to, count) in enumerate(up_pieces(j))
        ]

    def store_block(buffer, first, slot):
        return [pltpu.make_async_copy(stage.at[buffer], gw_ref.at[first : first + D], gs.at[slot, 0])]

    pending = {}

    def reuse(buffer):
        for copy in pending.pop(buffer, []):
            copy.wait()

    def issue(buffer, copies):
        for copy in copies:
            copy.start()
        pending[buffer] = copies

    for j in range(4):
        reuse(0)

        def down_step(at):
            stage[0, at, :] = lax.dot_general(
                act[j, :, at], lgrad[...], TN, preferred_element_type=f32
            ).astype(bf)

        over_columns(down_step)
        issue(0, store_block(0, 5 * D + D * j, 0))

        def slope_step(at):
            grads = lax.dot_general(lgrad[...], wd[j, at, :], NT, preferred_element_type=f32)
            act[j, :, at] = (grads * slope[j, :, at]).astype(bf)

        over_columns(slope_step)
        reuse(1)

        def up_step(at):
            stage[1, :, at] = lax.dot_general(
                entered[...], act[j, :, at], TN, preferred_element_type=f32
            ).astype(bf)

        over_columns(up_step)
        issue(1, store(1, j, 1))

    def enter_back_step(at):
        total = lax.dot_general(act[0], wu[0, at, :], NT, preferred_element_type=f32)
        for j in range(1, 4):
            total = total + lax.dot_general(act[j], wu[j, at, :], NT, preferred_element_type=f32)
        egrad[:, at] = total

    over_columns(enter_back_step)

    def branch_back_step(at):
        grads = egrad[at, :]
        upstream = c_ref[at, :].astype(f32) * scale
        unit, inverse = unit_of(residual[at, :])
        res_grad = upstream + into_norm(grads, unit, inverse, n_ref[4:5, :])
        rg_ref[at, :] = res_grad
        sums[4] += fold(grads * unit)
        sums[5] += fold(grads)
        unit, inverse = unit_of(branch[at, :])
        lgrad[at, :] = into_norm(res_grad, unit, inverse, n_ref[2:3, :]).astype(bf)
        sums[6] += fold(res_grad * unit)
        sums[7] += fold(res_grad)

    over_rows(branch_back_step)
    reuse(0)

    def out_grad_step(at):
        stage[0, at, :] = lax.dot_general(
            a_ref[:, at], lgrad[...], TN, preferred_element_type=f32
        ).astype(bf)

    over_columns(out_grad_step)
    issue(0, store_block(0, 0, 0))

    def attended_step(at):
        ag_ref[:, at] = lax.dot_general(
            lgrad[...], wo[at, :], NT, preferred_element_type=f32
        ).astype(bf)

    over_columns(attended_step)
    order = [None, None, 6, 7, 4, 5, 2, 3]
    for row, source in enumerate(order):
        if source is None:
            ns_ref[row : row + 1, :] = jnp.zeros((1, D), f32)
        else:
            ns_ref[row : row + 1, :] = jnp.sum(sums[source], axis=0, keepdims=True)
    lane = lax.broadcasted_iota(jnp.int32, (8, 128), 1)
    row = lax.broadcasted_iota(jnp.int32, (8, 128), 0)
    told = jnp.zeros((8, 128), f32)
    for t in range(2):
        told = jnp.where((lane == t) & (row == 0), jnp.sum(sums[t]), told)
    sq_ref[...] = told
    reuse(0)
    reuse(1)


def dense(attended, hidden, cotangent, scale, norm_rows, weights):
    tokens = attended.shape[0]
    shape = jax.ShapeDtypeStruct
    room = pltpu.VMEM
    return pl.pallas_call(
        dense_kernel,
        out_shape=(
            shape((tokens, D), bf), shape((tokens, D), f32), shape((tokens, D), bf),
            shape((9 * D, D), bf), shape((8, D), f32), shape((8, 128), f32),
        ),
        in_specs=[VM, VM, VM, pl.BlockSpec(memory_space=pltpu.SMEM), VM, ANY],
        out_specs=(VM, VM, VM, ANY, VM, VM),
        scratch_shapes=[
            room((D, D), bf), room((4, D, D), bf), room((4, D, D), bf),
            room((tokens, D), f32), room((tokens, D), f32), room((tokens, D), f32),
            room((tokens, D), bf), room((4, tokens, D), bf), room((4, tokens, D), f32),
            room((tokens, D), bf), room((tokens, D), f32), room((2, D, D), bf),
            room((8, 8, D), f32), DMA((5,)), DMA((4, 12)), DMA((2, 12)),
        ],
        compiler_params=params_for(mib=60),
    )(attended, hidden, cotangent, scale, norm_rows, weights)


def norm_forward(values, gain_row, shift_row):
    center = values - jnp.mean(values, axis=-1, keepdims=True)
    spread = jnp.mean(center * center, axis=-1, keepdims=True)
    inverse = lax.rsqrt(spread + EPSILON)
    unit_rows = center * inverse
    return (unit_rows * gain_row + shift_row, unit_rows, inverse)


def norm_backward(grad_rows, unit_rows, inverse, gain_row):
    scaled = grad_rows * gain_row
    first_mean = jnp.mean(scaled, axis=-1, keepdims=True)
    second_mean = jnp.mean(scaled * unit_rows, axis=-1, keepdims=True)
    return inverse * (scaled - first_mean - unit_rows * second_mean)


def norm_sums(grad_rows, unit_rows):
    return jnp.sum(grad_rows * unit_rows, axis=0), jnp.sum(grad_rows, axis=0)


def up_from_shards(rows):
    pieces = [rows[:128].reshape(1, 4, 32, D), rows[128:3968].reshape(10, 4, 96, D)]
    pieces.append(rows[3968:].reshape(1, 4, 32, D))
    return jnp.concatenate(
        [piece.transpose(0, 2, 1, 3).reshape(-1, FF) for piece in pieces], axis=0
    )


def up_to_shards(grad):
    pieces = [(grad[:32], 1, 32), (grad[32:992], 10, 96), (grad[992:], 1, 32)]
    return jnp.concatenate(
        [
            piece.reshape(blocks, rows, 4, D).transpose(0, 2, 1, 3).reshape(-1, D)
            for piece, blocks, rows in pieces
        ],
        axis=0,
    )


def dots(a, b, contract):
    return lax.dot_general(a, b, ((contract[:1], contract[1:]), ((), ())), preferred_element_type=f32)


def per_device(lines, hidden_in, params, cotangent, source_ids, corpus_weight, positions):
    devices = lax.axis_size(("dp", "fsdp"))
    width = lax.axis_size("fsdp")
    hidden = hidden_in[0]
    tokens = hidden.shape[0]
    place = lax.axis_index("fsdp")
    if lines:
        places = jnp.pad(positions.astype(f32).reshape(4, 128), ((0, 4), (0, 0)))
        hidden_all, w_qkv, canonical, norm_rows, places = first_gather(
            params.reshape(NATURAL, 128), hidden, places
        )
        places = places[:, :4].reshape(-1)
    else:
        whole = lax.all_gather(params, ("dp", "fsdp"), axis=0, tiled=True)
        ends = [0, 3 * D * D, 4 * D * D, 4 * D * D + D * FF, 4 * D * D + 2 * D * FF]
        parts = [whole[a:b] for a, b in zip(ends, ends[1:])]
        w_qkv = lax.dynamic_index_in_dim(
            parts[0].reshape(D, 3, width, D // width).transpose(1, 2, 0, 3), place, 1, False
        )
        others = jnp.concatenate(
            [parts[1].reshape(D, D), up_to_shards(parts[2].reshape(D, FF)), parts[3].reshape(FF, D)]
        )
        norm_rows = whole[ends[-1] :].reshape(8, D).astype(f32)
        hidden_all = lax.all_gather(hidden, "fsdp", axis=0, tiled=True)
        places = lax.all_gather(positions[0].astype(f32), "fsdp", axis=0, tiled=True)

    lane = jnp.arange(128) % 64
    frequency = jnp.exp((lane % 32).astype(f32) * (-2.0 * math.log(10000.0) / HEAD_DIM))
    angles = places[:, None] * frequency
    cosine = jnp.cos(angles)
    sine = jnp.where(lane < 32, -1.0, 1.0) * jnp.sin(angles)
    if lines:
        others, normed_all, queries, keys, values, attended_all, logs, attended = forward(
            hidden_all, norm_rows, w_qkv, cosine, sine, canonical
        )
    else:
        normed_all, queries, keys, values = project(hidden_all, norm_rows, w_qkv, cosine, sine)
        attended_all, attended_low, logs = attend(queries, keys, values)
        attended = swap(attended_low, width, True, 4)
    source_table = jnp.arange(corpus_weight.shape[0], dtype=jnp.int32)
    row_scale = jnp.sum(jnp.where(source_ids[0] == source_table, corpus_weight, 0.0))
    output, residual_grad, attended_grad, weight_grads, norm_part, squares = dense(
        attended, hidden, cotangent[0], row_scale.reshape(1, 1), norm_rows, others
    )
    if lines:
        owned, *mixed_grad = backward(
            weight_grads, attended_grad, queries, keys, values, attended_all, logs, cosine, sine
        )
    else:
        grads_all = swap(attended_grad, width, False, 5)
        mixed_grad = attend_back(
            queries, keys, values, grads_all, attended_all, logs, cosine, sine
        )
    grad_qkv = jnp.stack([dots(normed_all, part, (0, 0)) for part in mixed_grad])
    normed_part = sum(dots(part, w_qkv[j], (1, 1)) for j, part in enumerate(mixed_grad))
    _, unit_all, _ = norm_forward(hidden_all.astype(f32), norm_rows[0], norm_rows[1])
    norm_part = jnp.concatenate([jnp.stack(norm_sums(normed_part, unit_all)), norm_part[2:]], axis=0)
    if lines:
        param_grads, normed_grad, squares = last_reduce(
            grad_qkv.astype(bf), normed_part.astype(bf), owned, norm_part, squares
        )
        param_grads = param_grads.reshape(-1)
    else:
        spread = jnp.zeros((3, width, D, D // width), bf)
        spread = lax.dynamic_update_slice_in_dim(spread, grad_qkv.astype(bf)[:, None], place, 1)
        parts = (
            spread.transpose(2, 0, 1, 3),
            weight_grads[:D],
            up_from_shards(weight_grads[D : 5 * D]),
            weight_grads[5 * D :],
            norm_part.astype(bf),
        )
        flat = jnp.concatenate([part.reshape(-1) for part in parts])
        param_grads = lax.psum_scatter(flat, ("dp", "fsdp"), scatter_dimension=0, tiled=True)
        param_grads = param_grads.astype(f32)
        normed_grad = lax.psum_scatter(normed_part, "fsdp", scatter_dimension=0, tiled=True)
        squares = lax.psum(squares, ("dp", "fsdp"))
    statistics = squares[0, :2] / (devices * tokens * D)
    _, normed_unit, normed_inverse = norm_forward(hidden.astype(f32), norm_rows[0], norm_rows[1])
    into_input = norm_backward(normed_grad, normed_unit, normed_inverse, norm_rows[0])
    input_grad = (residual_grad + into_input).astype(bf)
    return (output[None], input_grad[None], param_grads, statistics)


def solution(mesh):
    lines = (mesh.shape["dp"], mesh.shape["fsdp"]) == (8, 4)
    in_specs = (
        P("dp", "fsdp", None),
        P(("dp", "fsdp")),
        P("dp", "fsdp", None),
        P("dp"),
        P(),
        P("dp", "fsdp"),
    )
    out_specs = (P("dp", "fsdp", None), P("dp", "fsdp", None), P(("dp", "fsdp")), P())
    return jax.shard_map(
        functools.partial(per_device, lines),
        mesh=mesh,
        in_specs=in_specs,
        out_specs=out_specs,
        check_vma=False,
    )
```

```python
import functools
import math

import jax
import jax.numpy as jnp
from jax import lax
from jax.experimental import pallas as pl
from jax.experimental.pallas import tpu as pltpu
from jax.sharding import PartitionSpec as P

D = 1024
HEADS = 16
HEAD_DIM = 64
FF = 4096
EPSILON = 1e-05
MASKED = -1e30
SCALE = 1.0 / math.sqrt(HEAD_DIM)
LOG2E = 1.4426950408889634

MESH = pl.DeviceIdType.MESH
bf = jnp.bfloat16
f32 = jnp.float32
SHARD = 384
NATURAL = 3074
MIB = 2**20

VM = pl.BlockSpec(memory_space=pltpu.VMEM)
ANY = pl.BlockSpec(memory_space=pl.ANY)
DMA = pltpu.SemaphoreType.DMA


def params_for(collective=None, mib=48):
    if collective is None:
        return pltpu.CompilerParams(vmem_limit_bytes=mib * MIB)
    return pltpu.CompilerParams(
        collective_id=collective, has_side_effects=True, vmem_limit_bytes=mib * MIB
    )


def coords():
    dp, fs = lax.axis_index("dp"), lax.axis_index("fsdp")
    return dp // 2, lax.rem(dp, 2), fs // 2, lax.rem(fs, 2)


def dev(z, x, y, c):
    return (z * 2 + x, y * 2 + c)


def linear(i):
    return (i // 4, lax.rem(i, 4))


def remote(src, dst, send, recv, to):
    return pltpu.make_async_remote_copy(
        src_ref=src, dst_ref=dst, send_sem=send, recv_sem=recv, device_id=to, device_id_type=MESH
    )


def greet(bar, device):
    pl.semaphore_signal(bar, inc=1, device_id=device, device_id_type=MESH)


def meet_neighbours(z, x, y, c, plane, more=0):
    bar = pltpu.get_barrier_semaphore()
    for device in plane:
        greet(bar, device)

    @pl.when(z < 3)
    def _():
        greet(bar, dev(z + 1, x, y, c))

    @pl.when(z > 0)
    def _():
        greet(bar, dev(z - 1, x, y, c))

    line = jnp.where(z < 3, 1, 0) + jnp.where(z > 0, 1, 0)
    pl.semaphore_wait(bar, len(plane) + line + more)


def add_rows(dst, *srcs):
    total = srcs[0][...].astype(f32)
    for part in srcs[1:]:
        total = total + part[...].astype(f32)
    dst[...] = total.astype(dst.dtype)


def add_tiles(dst, rows, *srcs):
    for at in range(0, rows, 16):
        add_rows(dst.at[at : at + 16], *[part.at[at : at + 16] for part in srcs])


CHUNKS = 4
EARLY = 2
CHUNK = SHARD // CHUNKS


def shard_rows(ref, base, zz, xx, yy, cc, k, low=0, count=CHUNK):
    s = (zz * 2 + xx) * 4 + yy * 2 + cc
    return ref.at[pl.ds(pl.multiple_of((s - base) * SHARD + k * CHUNK + low, 16), count)]


def gather_sems(planes):
    return [DMA((11, planes * CHUNKS)), DMA((11, planes * CHUNKS)), DMA((CHUNKS + 1,))]


def gather_steps(rows, plane_of, planes, own, source, line, over_x, ss, rs, ls):
    z, x, y, c = coords()
    xn, yn, cn = 1 - x, 1 - y, 1 - c
    to_x, to_y, to_core = dev(z, xn, y, c), dev(z, x, yn, c), dev(z, x, y, cn)
    lag, core_lag = 2, 4
    units = planes * CHUNKS
    ZU, ZD, XO, YO, CO, XD, YD, CX, CY, CXD, CYD = range(11)
    rest = CHUNK - over_x

    def unit(i):
        r = i // CHUNKS
        return plane_of(r), i - r * CHUNKS, i

    def send(kind, i):
        zz, k, q = unit(i)
        ref, to = {
            ZU: lambda: (rows(zz, x, y, c, k), dev(z + 1, x, y, c)),
            ZD: lambda: (rows(zz, x, y, c, k), dev(z - 1, x, y, c)),
            XO: lambda: (rows(zz, x, y, c, k), to_x),
            YO: lambda: (rows(zz, x, y, c, k), to_y),
            CO: lambda: (rows(zz, x, y, c, k), to_core),
            YD: lambda: (rows(zz, xn, y, c, k, over_x, rest), to_y),
            XD: lambda: (rows(zz, x, yn, c, k, 0, over_x), to_x),
            CX: lambda: (rows(zz, xn, y, c, k), to_core),
            CY: lambda: (rows(zz, x, yn, c, k), to_core),
            CXD: lambda: (rows(zz, xn, yn, c, k, 0, over_x), to_core),
            CYD: lambda: (rows(zz, xn, yn, c, k, over_x, rest), to_core),
        }[kind]()
        slot = (zz - 1) * CHUNKS + k if line else k
        src = source(k) if kind in (XO, YO, CO) and not line else ref
        return remote(src, ref, ss.at[kind, slot], rs.at[kind, slot], to)

    def arrive(kind, i):
        zz, k, q = unit(i)
        ref = {
            ZU: lambda: rows(zz, x, y, c, k),
            ZD: lambda: rows(zz, x, y, c, k),
            XO: lambda: rows(zz, xn, y, c, k),
            YO: lambda: rows(zz, x, yn, c, k),
            XD: lambda: rows(zz, xn, yn, c, k, 0, over_x),
            YD: lambda: rows(zz, xn, yn, c, k, over_x, rest),
            CO: lambda: rows(zz, x, y, cn, k),
            CX: lambda: rows(zz, xn, y, cn, k),
            CY: lambda: rows(zz, x, yn, cn, k),
            CXD: lambda: rows(zz, xn, yn, cn, k, 0, over_x),
            CYD: lambda: rows(zz, xn, yn, cn, k, over_x, rest),
        }[kind]()
        slot = (zz - 1) * CHUNKS + k if line else k
        remote(ref, ref, ss.at[kind, slot], rs.at[kind, slot], to_core).wait_recv()

    def local(k_plane):
        zz = k_plane
        return [
            pltpu.make_async_copy(source(k), rows(zz, x, y, c, k), ls.at[k]) for k in range(CHUNKS)
        ]

    def start():
        if line:

            @pl.when(own(z))
            def _():
                for copy in local(z):
                    copy.start()
                for copy in local(z):
                    copy.wait()
                for k in range(CHUNKS):
                    send(ZD, k).start()
                    if k < EARLY:
                        send(ZU, k).start()
        else:
            for copy in local(plane_of(0)):
                copy.start()

    def late_up():
        @pl.when(own(z))
        def _():
            for k in range(EARLY, CHUNKS):
                send(ZU, k).start()

    def early(i):
        zz, _, _ = unit(i)
        if line:

            @pl.when(zz < z)
            def _():
                arrive(ZU, i)

            @pl.when(zz > z)
            def _():
                arrive(ZD, i)

            @pl.when((zz < z) & (z < 3))
            def _():
                send(ZU, i).start()

            @pl.when((zz > z) & (z > 0))
            def _():
                send(ZD, i).start()

        for kind in (XO, CO):
            send(kind, i).start()

    def step(i, _):
        @pl.when((i < units) & (i >= (EARLY if line else 0)))
        def _():
            early(i)

        @pl.when(i < units)
        def _():
            send(YO, i).start()

        j = i - lag

        @pl.when((j >= 0) & (j < units))
        def _():
            arrive(XO, j)
            send(YD, j).start()
            send(CX, j).start()
            arrive(YO, j)
            send(XD, j).start()
            send(CY, j).start()

        m = i - core_lag

        @pl.when(m >= 0)
        def _():
            arrive(XD, m)
            send(CXD, m).start()
            arrive(YD, m)
            send(CYD, m).start()

        return 0

    def finish():
        def one(i, _):
            zz, _, _ = unit(i)
            for kind in (CO, CX, CY, CXD, CYD):
                arrive(kind, i)
            for kind in (XO, YO, CO, YD, XD, CX, CY, CXD, CYD):
                send(kind, i).wait_send()
            if line:

                @pl.when((zz <= z) & (z < 3))
                def _():
                    send(ZU, i).wait_send()

                @pl.when((zz >= z) & (z > 0))
                def _():
                    send(ZD, i).wait_send()

            return 0

        lax.fori_loop(0, units, one, 0)
        if not line:
            for copy in local(plane_of(0)):
                copy.wait()

    return start, early, late_up, step, units + core_lag, finish


def reduce_steps(
    rows, planes, line, over_x, out, lb, cb, xb, yb, dxb, dyb, zub, zdb, ss, rs, cs, cr, ls
):
    z, x, y, c = coords()
    xn, yn, cn = 1 - x, 1 - y, 1 - c
    to_x, to_y, to_core = dev(z, xn, y, c), dev(z, x, yn, c), dev(z, x, y, cn)
    lag1, lag2, lag3, lag4 = 1, 2, 3, 4
    XS, YS, DXS, DYS, ZD, ZU = range(6)
    units = len(planes) * CHUNKS

    def unit(i):
        r = i // CHUNKS
        zz = planes[0] if len(planes) == 1 else planes[0] - r
        return zz, i - r * CHUNKS

    places = [(xn, yn), (xn, y), (x, yn), (x, y)]

    def load(i, p):
        zz, k = unit(i)
        xx, yy = places[p]
        return pltpu.make_async_copy(rows(zz, xx, yy, c, k), lb.at[i, p], ls.at[i, p])

    def to_sibling(i, p):
        zz, k = unit(i)
        xx, yy = places[p]
        return remote(rows(zz, xx, yy, cn, k), cb.at[i, p], cs.at[i, p], cr.at[i, p], to_core)

    def start():
        def load_all(i, _):
            for p in range(4):
                load(i, p).start()
                to_sibling(i, p).start()
            return 0

        lax.fori_loop(0, units, load_all, 0)

    def over(kind, src, dst, i, to):
        return remote(src, dst, ss.at[kind, i], rs.at[kind, i], to)

    def diag_x(i):
        return over(DXS, lb.at[i, 0, 0:over_x], dxb.at[i], i, to_x)

    def diag_y(i):
        return over(DYS, lb.at[i, 0, over_x:CHUNK], dyb.at[i], i, to_y)

    def whole_x(i):
        return over(XS, lb.at[i, 1], xb.at[i], i, to_x)

    def whole_y(i):
        return over(YS, lb.at[i, 2], yb.at[i], i, to_y)

    def down(i):
        return over(ZD, lb.at[i, 3], zub.at[i], i, dev(z - 1, x, y, c))

    def up(i):
        return over(ZU, lb.at[i, 3], zdb.at[i], i, dev(z + 1, x, y, c))

    def have(i, p):
        load(i, p).wait()
        to_sibling(i, p).wait_recv()

    def step(i, _):
        @pl.when(i < units)
        def _():
            have(i, 0)
            add_tiles(lb.at[i, 0], CHUNK, lb.at[i, 0], cb.at[i, 0])
            diag_x(i).start()
            diag_y(i).start()

        j = i - lag1

        @pl.when((j >= 0) & (j < units))
        def _():
            have(j, 1)
            have(j, 2)
            diag_y(j).wait_recv()
            diag_x(j).wait_recv()
            a, b = lb.at[j, 1], cb.at[j, 1]
            low, high = slice(0, over_x), slice(over_x, CHUNK)
            add_tiles(a.at[low], over_x, a.at[low], b.at[low])
            add_tiles(a.at[high], CHUNK - over_x, a.at[high], b.at[high], dyb.at[j])
            whole_x(j).start()
            a, b = lb.at[j, 2], cb.at[j, 2]
            add_tiles(a.at[low], over_x, a.at[low], b.at[low], dxb.at[j])
            add_tiles(a.at[high], CHUNK - over_x, a.at[high], b.at[high])
            whole_y(j).start()

        m = i - lag2

        @pl.when((m >= 0) & (m < units))
        def _():
            zz, k = unit(m)
            have(m, 3)
            whole_x(m).wait_recv()
            whole_y(m).wait_recv()
            parts = [lb.at[m, 3], cb.at[m, 3], xb.at[m], yb.at[m]]
            if not line:
                add_tiles(out(k), CHUNK, *parts)
                return

            @pl.when(z != zz)
            def _():
                add_tiles(lb.at[m, 3], CHUNK, *parts)

            @pl.when(z == 3)
            def _():
                down(m).start()

            @pl.when(z == 0)
            def _():
                up(m).start()

            @pl.when(z == zz)
            def _():
                add_tiles(out(k), CHUNK, *parts)

        if not line:
            return 0
        n = i - lag3

        @pl.when((n >= 0) & (n < units))
        def _():
            zz, _ = unit(n)

            @pl.when((z > zz) & (z < 3))
            def _():
                down(n).wait_recv()
                add_tiles(lb.at[n, 3], CHUNK, lb.at[n, 3], zub.at[n])
                down(n).start()

            @pl.when((z < zz) & (z > 0))
            def _():
                up(n).wait_recv()
                add_tiles(lb.at[n, 3], CHUNK, lb.at[n, 3], zdb.at[n])
                up(n).start()

        o = i - lag4

        @pl.when(o >= 0)
        def _():
            zz, k = unit(o)

            @pl.when(z == zz)
            def _():
                down(o).wait_recv()
                add_tiles(out(k), CHUNK, out(k), zub.at[o])
                up(o).wait_recv()
                add_tiles(out(k), CHUNK, out(k), zdb.at[o])

        return 0

    def finish():
        def one(i, _):
            zz, _ = unit(i)
            for p in range(4):
                to_sibling(i, p).wait_send()
            for copy in (diag_x(i), diag_y(i), whole_x(i), whole_y(i)):
                copy.wait_send()
            if line:

                @pl.when(z > zz)
                def _():
                    down(i).wait_send()

                @pl.when(z < zz)
                def _():
                    up(i).wait_send()

            return 0

        lax.fori_loop(0, units, one, 0)

    return start, step, units + (lag4 if line else lag2), finish


def reduce_rooms(planes, line, over_x):
    units = planes * CHUNKS

    def room(*shape):
        return pltpu.VMEM(shape + (D,), bf)

    lines = units if line else 1
    return [
        room(units, 4, CHUNK), room(units, 4, CHUNK),
        room(units, CHUNK), room(units, CHUNK),
        room(units, over_x), room(units, CHUNK - over_x),
        room(lines, CHUNK), room(lines, CHUNK),
        DMA((6, units)), DMA((6, units)), DMA((units, 4)), DMA((units, 4)), DMA((units, 4)),
    ]


def swap_kernel(n, to_tokens, a_ref, o_ref, ss, rs, ls):
    me = lax.axis_index("fsdp")
    bar = pltpu.get_barrier_semaphore()
    for i in range(1, n):
        pl.semaphore_signal(
            bar, inc=1, device_id={"fsdp": lax.rem(me + i, n)}, device_id_type=MESH
        )
    pl.semaphore_wait(bar, n - 1)
    tokens = (a_ref if to_tokens else o_ref).shape[0] // n
    width = (o_ref if to_tokens else a_ref).shape[1] // n

    def token_block(ref, owner):
        return ref.at[pl.ds(pl.multiple_of(owner * tokens, 16), tokens)]

    def head_block(ref, owner):
        return ref.at[:, pl.ds(pl.multiple_of(owner * width, 128), width)]

    take, put = (token_block, head_block) if to_tokens else (head_block, token_block)
    local = pltpu.make_async_copy(take(a_ref, me), put(o_ref, me), ls)
    local.start()
    copies = []
    for i in range(1, n):
        to = lax.rem(me + i, n)
        copy = pltpu.make_async_remote_copy(
            src_ref=take(a_ref, to), dst_ref=put(o_ref, me), send_sem=ss.at[i], recv_sem=rs.at[i],
            device_id={"fsdp": to}, device_id_type=MESH,
        )
        copy.start()
        copies.append(copy)
    for i in range(1, n):
        copies[i - 1].wait_send()
        ref = put(o_ref, lax.rem(me - i + n, n))
        pltpu.make_async_remote_copy(
            src_ref=ref, dst_ref=ref, send_sem=ss.at[i], recv_sem=rs.at[i],
            device_id={"fsdp": lax.rem(me + i, n)}, device_id_type=MESH,
        ).wait_recv()
    local.wait()


def swap(array, n, to_tokens, collective):
    rows, columns = array.shape
    shape = (rows // n, columns * n) if to_tokens else (rows * n, columns // n)
    return pl.pallas_call(
        functools.partial(swap_kernel, n, to_tokens),
        out_shape=jax.ShapeDtypeStruct(shape, bf),
        in_specs=[VM],
        out_specs=VM,
        scratch_shapes=[DMA((n,)), DMA((n,)), DMA],
        compiler_params=params_for(collective, 32),
    )(array)


def partner(values):
    width = values.shape[-1]
    lane = lax.broadcasted_iota(jnp.int32, values.shape, values.ndim - 1)
    after = pltpu.roll(values, width - 32, values.ndim - 1)
    before = pltpu.roll(values, 32, values.ndim - 1)
    return jnp.where(lane % 64 < 32, after, before)


def project_rows(rows, n_ref, w_ref, cosine, sine):
    rows = rows.astype(f32)
    center = rows - jnp.mean(rows, axis=-1, keepdims=True)
    inverse = lax.rsqrt(jnp.mean(center * center, axis=-1, keepdims=True) + EPSILON)
    normed = (center * inverse * n_ref[0:1, :] + n_ref[1:2, :]).astype(bf)
    mixed = [jnp.dot(normed, w_ref[j], preferred_element_type=f32) for j in range(3)]
    for j in range(2):
        parts = [mixed[j][:, at : at + 128] for at in range(0, mixed[j].shape[1], 128)]
        parts = [part * cosine + partner(part) * sine for part in parts]
        mixed[j] = jnp.concatenate(parts, axis=1)
    return [normed] + [part.astype(bf) for part in mixed]


def qkv_kernel(h_ref, n_ref, w_ref, c_ref, s_ref, *out_refs):
    for ref, part in zip(out_refs, project_rows(h_ref[...], n_ref, w_ref, c_ref[...], s_ref[...])):
        ref[...] = part


def project(hidden, norm_rows, w_qkv, cosine, sine):
    tokens, width = hidden.shape[0], w_qkv.shape[2]
    block = 256
    rows = lambda w: pl.BlockSpec((block, w), lambda i: (i, 0))
    full = lambda a: pl.BlockSpec(a.shape, lambda i: (0,) * a.ndim)
    shape = jax.ShapeDtypeStruct
    return pl.pallas_call(
        qkv_kernel,
        grid=(tokens // block,),
        in_specs=[rows(D), full(norm_rows), full(w_qkv), rows(128), rows(128)],
        out_specs=[rows(D), rows(width), rows(width), rows(width)],
        out_shape=[shape((tokens, D), bf)] + [shape((tokens, width), bf)] * 3,
        compiler_params=params_for(),
    )(hidden, norm_rows, w_qkv, cosine, sine)


NT = (((1,), (1,)), ((), ()))
TN = (((0,), (0,)), ((), ()))
BLOCK = 512


def one_head(pair, h):
    lane = lax.broadcasted_iota(jnp.int32, pair.shape, 1)
    return jnp.where((lane < 64) if h == 0 else (lane >= 64), pair, jnp.zeros_like(pair))


def causal(scores, i, j):
    key = j * scores.shape[0] + lax.broadcasted_iota(jnp.int32, scores.shape, 0)
    query = i * scores.shape[1] + lax.broadcasted_iota(jnp.int32, scores.shape, 1)
    return jnp.where(key <= query, scores, MASKED)


def attend_rows(i, queries, k_ref, v_ref):
    heads = [one_head(queries, h) for h in range(2)]

    def block(j, carry, masked):
        at = pl.ds(pl.multiple_of(j * BLOCK, BLOCK), BLOCK)
        keys, values = k_ref[at, :], v_ref[at, :]
        out = []
        for h in range(2):
            peak, total, summed = carry[3 * h : 3 * h + 3]
            scores = lax.dot_general(keys, heads[h], NT, preferred_element_type=f32)
            scores = scores * (SCALE * LOG2E)
            if masked:
                scores = causal(scores, i, j)
            new_peak = jnp.maximum(peak, jnp.max(scores, axis=0, keepdims=True))
            weights = jnp.exp2(scores - new_peak)
            shrink = jnp.exp2(peak - new_peak)
            total = total * shrink + jnp.sum(weights, axis=0, keepdims=True)
            part = lax.dot_general(
                values[:, 64 * h : 64 * h + 64], weights.astype(bf), TN, preferred_element_type=f32
            )
            out += [new_peak, total, summed * shrink + part]
        return tuple(out)

    start = (
        jnp.full((1, BLOCK), MASKED, f32), jnp.zeros((1, BLOCK), f32), jnp.zeros((64, BLOCK), f32)
    ) * 2
    carry = lax.fori_loop(0, i, lambda j, carry: block(j, carry, False), start)
    peak0, total0, sum0, peak1, total1, sum1 = block(i, carry, True)
    out = jnp.concatenate([sum0 / total0, sum1 / total1], axis=0).T
    logs = jnp.concatenate([peak0 + jnp.log2(total0), peak1 + jnp.log2(total1)], axis=0)
    return out, logs


def attend_kernel(q_ref, k_ref, v_ref, o_ref, low_ref, l_ref):
    out, logs = attend_rows(pl.program_id(1), q_ref[...], k_ref, v_ref)
    o_ref[...] = out
    low_ref[...] = out.astype(bf)
    l_ref[...] = logs.reshape(1, 2, BLOCK)


def attend(queries, keys, values):
    tokens, width = queries.shape
    pairs = width // 128
    block = pl.BlockSpec((BLOCK, 128), lambda p, i: (i, p))
    full = pl.BlockSpec((tokens, 128), lambda p, i: (0, p))
    logs = pl.BlockSpec((1, 2, BLOCK), lambda p, i: (p, 0, i))
    shape = jax.ShapeDtypeStruct
    return pl.pallas_call(
        attend_kernel,
        grid=(pairs, tokens // BLOCK),
        in_specs=[block, full, full],
        out_specs=[block, block, logs],
        out_shape=[
            shape((tokens, width), f32), shape((tokens, width), bf), shape((pairs, 2, tokens), f32)
        ],
        compiler_params=params_for(),
    )(queries, keys, values)


def attend_back_rows(i, queries, grads, attended, logs, k_ref, v_ref, dk, dv):
    heads = [one_head(queries, h) for h in range(2)]
    grad_heads = [one_head(grads, h) for h in range(2)]
    both_heads = jnp.concatenate(heads, axis=0)
    both_grads = jnp.concatenate(grad_heads, axis=0)
    products = (attended * grads.astype(f32)).T
    dots = [jnp.sum(products[64 * h : 64 * h + 64], axis=0, keepdims=True) for h in range(2)]

    def block(j, sums, masked):
        at = pl.ds(pl.multiple_of(j * BLOCK, BLOCK), BLOCK)
        keys, values = k_ref[at, :], v_ref[at, :]
        weights, score_grads = [], []
        for h in range(2):
            scores = lax.dot_general(keys, heads[h], NT, preferred_element_type=f32)
            scores = scores * (SCALE * LOG2E)
            if masked:
                scores = causal(scores, i, j)
            prob = jnp.exp2(scores - logs[h : h + 1])
            prob_grad = lax.dot_general(values, grad_heads[h], NT, preferred_element_type=f32)
            score_grads.append((prob * (prob_grad - dots[h])).astype(bf))
            weights.append(prob.astype(bf))
        dv[at, :] += jnp.dot(
            jnp.concatenate(weights, axis=1), both_grads, preferred_element_type=f32
        )
        dk[at, :] += jnp.dot(
            jnp.concatenate(score_grads, axis=1), both_heads, preferred_element_type=f32
        )
        return tuple(
            sums[h] + lax.dot_general(score_grads[h], keys, TN, preferred_element_type=f32)
            for h in range(2)
        )

    zero = jnp.zeros((BLOCK, 128), f32)
    sums = lax.fori_loop(0, i, lambda j, sums: block(j, sums, False), (zero, zero))
    sums = block(i, sums, True)
    lane = lax.broadcasted_iota(jnp.int32, zero.shape, 1)
    return jnp.where(lane < 64, sums[0], sums[1]) * SCALE


def turn_back(grads, cosine, sine):
    return (grads * cosine - partner(grads) * sine).astype(bf)


def finish_keys(dk, dv, c_ref, s_ref, dk_ref, dv_ref):
    def turn(t, _):
        at = pl.ds(pl.multiple_of(t * 256, 256), 256)
        dk_ref[at, :] = turn_back(dk[at, :] * SCALE, c_ref[at, :], s_ref[at, :])
        dv_ref[at, :] = dv[at, :].astype(bf)
        return 0

    lax.fori_loop(0, dk.shape[0] // 256, turn, 0)


def attend_back_kernel(
    q_ref, k_ref, v_ref, g_ref, a_ref, l_ref, cq_ref, sq_ref, c_ref, s_ref,
    dq_ref, dk_ref, dv_ref, dk, dv,
):
    i = pl.program_id(1)

    @pl.when(i == 0)
    def _():
        dk[...] = jnp.zeros_like(dk)
        dv[...] = jnp.zeros_like(dv)

    query_grad = attend_back_rows(
        i, q_ref[...], g_ref[...], a_ref[...], l_ref[0], k_ref, v_ref, dk, dv
    )
    dq_ref[...] = turn_back(query_grad, cq_ref[...], sq_ref[...])

    @pl.when(i == pl.num_programs(1) - 1)
    def _():
        finish_keys(dk, dv, c_ref, s_ref, dk_ref, dv_ref)


def attend_back(queries, keys, values, grads, attended, logs, cosine, sine):
    tokens, width = queries.shape
    block = pl.BlockSpec((BLOCK, 128), lambda p, i: (i, p))
    full = pl.BlockSpec((tokens, 128), lambda p, i: (0, p))
    table_block = pl.BlockSpec((BLOCK, 128), lambda p, i: (i, 0))
    table = pl.BlockSpec((tokens, 128), lambda p, i: (0, 0))
    log_block = pl.BlockSpec((1, 2, BLOCK), lambda p, i: (p, 0, i))
    return pl.pallas_call(
        attend_back_kernel,
        grid=(width // 128, tokens // BLOCK),
        in_specs=[block, full, full, block, block, log_block, table_block, table_block, table, table],
        out_specs=[block, full, full],
        out_shape=[jax.ShapeDtypeStruct((tokens, width), bf)] * 3,
        scratch_shapes=[pltpu.VMEM((tokens, 128), f32), pltpu.VMEM((tokens, 128), f32)],
        compiler_params=params_for(),
    )(queries, keys, values, grads, attended, logs, cosine, sine, cosine, sine)


def swap_copies(take, put, ss, rs, base):
    z, x, y, c = coords()
    others = [(y, 1 - c), (1 - y, c), (1 - y, 1 - c)]
    me = y * 2 + c
    starts, arrivals = [], []
    for i, (yy, cc) in enumerate(others):
        starts.append(
            remote(take(yy * 2 + cc), put(me), ss.at[base + i], rs.at[base + i], dev(z, x, yy, cc))
        )
        ref = put(yy * 2 + cc)
        arrivals.append(remote(ref, ref, ss.at[base + i], rs.at[base + i], dev(z, x, yy, cc)))
    return me, starts, arrivals


def forward_kernel(
    p_ref, h_ref, pos_ref,
    g_ref, col_ref, hid_out, wq_out, nrm_ref, cos_out, sin_out,
    normed_out, q_out, k_out, v_out, o_out, l_ref, t_ref,
    ext, tail, units, can_ref, posall_ref, low,
    hid_ref, wq_ref, cos_ref, sin_ref, normed_ref, q_ref, k_ref, v_ref, o_ref,
    us, ur, hs, hr, ns, nr, ps, pr, keep_sem, ss, rs, ls, ts, tr, cs, cr, outs,
):
    keeps = [
        pltpu.make_async_copy(src, dst, outs.at[i])
        for i, (src, dst) in enumerate(
            [
                (hid_ref, hid_out), (wq_ref, wq_out), (cos_ref, cos_out), (sin_ref, sin_out),
                (normed_ref, normed_out), (q_ref, q_out), (k_ref, k_out), (v_ref, v_out),
                (o_ref, o_out),
            ]
        )
    ]
    z, x, y, c = coords()
    xn, yn, cn = 1 - x, 1 - y, 1 - c
    s = (z * 2 + x) * 4 + y * 2 + c
    f = y * 2 + c
    nxt, prv = lax.rem(s + 1, 32), lax.rem(s + 31, 32)
    core = dev(z, x, y, cn)
    xs, xo, ys, yo = dev(z, xn, y, c), dev(z, xn, y, cn), dev(z, x, yn, c), dev(z, x, yn, cn)
    bar = pltpu.get_barrier_semaphore()
    greet(bar, linear(nxt))
    greet(bar, linear(prv))

    @pl.when(s != 31)
    def _():
        greet(bar, (7, 3))

    ext[64 : 64 + NATURAL, :] = p_ref[...].astype(f32)
    tail[...] = ext[NATURAL : NATURAL + 64, :]
    more = 2 + jnp.where(s == 31, 31, 0)
    meet_neighbours(z, x, y, c, [core, xs, xo, ys, yo], more)
    halves, half = 4, 128

    def hidden_rows(owner, k):
        return hid_ref.at[pl.ds(pl.multiple_of(owner * 512 + k * half, 16), half)]

    def hidden_own(k):
        return h_ref.at[pl.ds(k * half, half)]

    over_y, over_core, over_both = yn * 2 + c, y * 2 + cn, yn * 2 + cn
    halo = remote(tail, ext.at[0:64], ns.at[0], nr.at[0], linear(nxt))
    halo.start()
    sent = []
    for i, to in enumerate([core, ys, yo]):
        sent.append(remote(pos_ref, posall_ref.at[f], ps.at[i], pr.at[i], to))
    for k in range(halves):
        sent.append(remote(hidden_own(k), hidden_rows(f, k), hs.at[1, k], hr.at[1, k], core))
    for copy in sent:
        copy.start()
    rows_over_y = [
        remote(hidden_own(k), hidden_rows(f, k), hs.at[0, k], hr.at[0, k], ys) for k in range(halves)
    ]
    sent += rows_over_y
    for k in range(halves):

        @pl.when(k <= z)
        def _():
            rows_over_y[k].start()

    hid_ref[pl.ds(pl.multiple_of(f * 512, 512), 512)] = h_ref[...]
    posall_ref[pl.ds(f, 1)] = pos_ref[...].reshape(1, 8, 128)
    halo.wait()
    base = 64 - 2 * s

    def lines(first, count, apart, k):
        return ext[pl.ds(base + 8 * first + k, count, stride=8 * apart), :].astype(bf)

    def order(to, first, count, apart):
        for j in range(apart):
            for k in range(8):
                can_ref[to + j * count : to + (j + 1) * count, 128 * k : 128 * k + 128] = lines(
                    first + j, count, apart, k
                )

    @pl.when(z == 0)
    def _():
        for j in range(3):
            for k in range(8):
                at = 128 * (k % 2)
                units[k // 2, j, :, at : at + 128] = lines(j, 128, 3, k)

    @pl.when((s == 8) | (s == 9) | (s >= 22))
    def _():
        order(0, 0, 384, 1)

    @pl.when(s == 10)
    def _():
        order(0, 0, 256, 1)
        order(256, 256, 32, 4)

    @pl.when((s >= 11) & (s <= 20))
    def _():
        order(0, 0, 96, 4)

    @pl.when(s == 21)
    def _():
        order(0, 0, 32, 4)
        order(128, 128, 256, 1)

    def norm_send(i):
        return remote(nrm_ref, nrm_ref, ns.at[1 + i], nr.at[1], linear(i))

    @pl.when(s == 31)
    def _():
        for k in range(8):
            nrm_ref[:, 128 * k : 128 * k + 128] = ext[pl.ds(base + 8 * 384 + k, 8, stride=8), :]

        def go(i, _):
            norm_send(i).start()
            return 0

        lax.fori_loop(0, 31, go, 0)

    def column(k):
        return col_ref.at[pl.ds(pl.multiple_of(k * CHUNK, CHUNK), CHUNK)]

    def down(k):
        return remote(column(k), column(k), cs.at[k], cr.at[k], dev(z - 1, x, y, c))

    keep = pltpu.make_async_copy(can_ref, col_ref, keep_sem)

    @pl.when(z == 3)
    def _():
        keep.start()
        keep.wait()

    def down_step(k):
        @pl.when(z < 3)
        def _():
            down(k).wait_recv()

        @pl.when(z > 0)
        def _():
            down(k).start()

    def arrive(ref, sem):
        remote(ref, ref, us.at[0, 0, 0], sem, core).wait_recv()

    for i, owner in enumerate([over_core, over_y, over_both]):
        arrive(posall_ref.at[owner], pr.at[i])

    def tables():
        lane = lax.broadcasted_iota(jnp.int32, (1, 128), 1) % 64
        turn = (lane % 32).astype(f32) * (-2.0 * math.log(10000.0) / HEAD_DIM)
        frequency = jnp.exp(turn)

        def one(t, _):
            row = posall_ref[t // 4, pl.ds(lax.rem(t, 4), 1), :]
            angles = jnp.broadcast_to(row, (128, 128)).T * frequency
            at = pl.ds(pl.multiple_of(t * 128, 128), 128)
            cos_ref[at, :] = jnp.cos(angles)
            sine = jnp.sin(angles)
            sin_ref[at, :] = jnp.where(lane < 32, -sine, sine)
            return 0

        lax.fori_loop(0, 16, one, 0)

    @pl.when(z >= 2)
    def _():
        tables()

    first = jnp.where(z >= 2, 2, 1)
    start, early, late_up, pump, steps, finish = gather_steps(
        functools.partial(shard_rows, g_ref, 8),
        lambda r: jnp.where(r == 0, first, 3 - first), 2,
        lambda zz: (zz == 1) | (zz == 2),
        lambda k: can_ref.at[k * CHUNK : k * CHUNK + CHUNK],
        True, FORWARD_X, ss, rs, ls,
    )
    start()

    @pl.when(z >= 1)
    def _():
        for i in range(EARLY):
            early(i)

    slots = [yn * 2 + c, yn * 2 + cn, y * 2 + cn, y * 2 + c]

    def target(xx, yy, cc, h):
        at = pl.multiple_of((xx * 4 + yy * 2 + cc) * 128 + 64 * h, 64)
        return wq_ref.at[:, pl.ds(at, 64)]

    def piece(q, h):
        return units.at[slots[q], :, 64 * h : 64 * h + 64]

    def up(q, h):
        return remote(piece(q, h), piece(q, h), us.at[0, q, h], ur.at[0, q, h], dev(z + 1, x, y, c))

    for q in range(4):
        for h in range(2):
            unit, mine = piece(q, h), target(x, y, c, h)

            @pl.when(z > 0)
            def _():
                arrive(unit, ur.at[0, q, h])

            @pl.when(z < 3)
            def _():
                up(q, h).start()

            if q == 0:
                out = [remote(unit, mine, us.at[1, 0, h], ur.at[1, 0, h], ys)]
            elif q == 1:
                out = [remote(unit, mine, us.at[1, 1, h], ur.at[1, 1, h], yo)]
            elif q == 2:
                out = [
                    remote(unit, mine, us.at[1, 2, h], ur.at[1, 2, h], xo),
                    remote(unit, mine, us.at[1, 3, h], ur.at[1, 3, h], core),
                ]
            else:
                out = [remote(unit, mine, us.at[2, 0, h], ur.at[2, 0, h], xs)]
                mine[...] = unit[...]
            for copy in out:
                copy.start()
            sent += out
    for k in range(halves):

        @pl.when(k > z)
        def _():
            rows_over_y[k].start()

    @pl.when(z == 3)
    def _():
        for k in range(CHUNKS):
            down_step(k)

    late_up()

    @pl.when(z == 0)
    def _():
        for i in range(EARLY):
            early(i)

    for h in range(2):
        for i, cc in enumerate((c, cn)):
            ref = target(x, yn, cc, h)
            arrive(ref, ur.at[1, i, h])
            copy = remote(ref, ref, us.at[2, 1 + i, h], ur.at[2, 1 + i, h], xs)
            copy.start()
            sent.append(copy)
    pump(0, 0)

    @pl.when(z < 2)
    def _():
        tables()

    for k in range(halves):
        ref = hidden_rows(over_y, k)
        arrive(ref, hr.at[0, k])
        copy = remote(ref, ref, hs.at[2, k], hr.at[2, k], core)
        copy.start()
        sent.append(copy)
    for h in range(2):
        arrive(target(xn, y, cn, h), ur.at[1, 2, h])
        arrive(target(x, y, cn, h), ur.at[1, 3, h])
        arrive(target(xn, y, c, h), ur.at[2, 0, h])
        arrive(target(xn, yn, c, h), ur.at[2, 1, h])
        arrive(target(xn, yn, cn, h), ur.at[2, 2, h])

    @pl.when(s != 31)
    def _():
        arrive(nrm_ref, nr.at[1])

    pump(1, 0)

    def project(owner):
        for k in range(2):
            at = pl.ds(pl.multiple_of(owner * 512 + k * 256, 256), 256)
            parts = project_rows(hid_ref[at, :], nrm_ref, wq_ref, cos_ref[at, :], sin_ref[at, :])
            for ref, part in zip((normed_ref, q_ref, k_ref, v_ref), parts):
                ref[at, :] = part

    def project_step(t, _):
        owner = jnp.where(t == 0, f, jnp.where(t == 1, over_core, jnp.where(t == 2, over_y, over_both)))

        @pl.when(t == 1)
        def _():
            for k in range(halves):
                arrive(hidden_rows(over_core, k), hr.at[1, k])

        @pl.when(t == 3)
        def _():
            for k in range(halves):
                arrive(hidden_rows(over_both, k), hr.at[2, k])

        project(owner)

        @pl.when(lax.rem(t, 2) == 1)
        def _():
            pump(2 + t // 2, 0)

        return 0

    lax.fori_loop(0, 4, project_step, 0)
    for copy in keeps[:8]:
        copy.start()

    def attend_step(t, _):
        p = t // 4
        i = t - 4 * p
        at = pl.ds(pl.multiple_of(i * BLOCK, BLOCK), BLOCK)
        lanes = pl.ds(pl.multiple_of(p * 128, 128), 128)
        out, logs = attend_rows(i, q_ref[at, lanes], k_ref.at[:, lanes], v_ref.at[:, lanes])
        o_ref[at, lanes] = out
        low[at, lanes] = out.astype(bf)
        l_ref[p, :, at] = logs

        @pl.when(i >= 2)
        def _():
            pump(2 + i + 2 * p, 0)

        k = t - 2 * (3 - z)

        @pl.when((z > 0) & (z < 3) & (k >= 0) & (k < CHUNKS))
        def _():
            down_step(k)

        return 0

    lax.fori_loop(0, 8, attend_step, 0)

    def take(owner):
        return low.at[pl.ds(pl.multiple_of(owner * 512, 512), 512)]

    def put(owner):
        return t_ref.at[:, pl.ds(pl.multiple_of(owner * 256, 256), 256)]

    me, starts, arrivals = swap_copies(take, put, ts, tr, 0)
    for copy in starts:
        copy.start()
    own_block = pltpu.make_async_copy(take(me), put(me), outs.at[9])
    own_block.start()
    keeps[8].start()
    lax.fori_loop(8, steps, pump, 0)

    @pl.when(z == 0)
    def _():
        for k in range(CHUNKS):
            down_step(k)

    for copy in arrivals:
        copy.wait_recv()
    for copy in starts + sent:
        copy.wait_send()
    for copy in keeps + [own_block]:
        copy.wait()

    @pl.when(z < 3)
    def _():
        for q in range(4):
            for h in range(2):
                up(q, h).wait_send()

    @pl.when(s == 31)
    def _():
        def go(i, _):
            norm_send(i).wait_send()
            return 0

        lax.fori_loop(0, 31, go, 0)

    @pl.when(z > 0)
    def _():
        for k in range(CHUNKS):
            down(k).wait_send()

    finish()


FORWARD_X = 80


def forward(share, hidden, places):
    shape = jax.ShapeDtypeStruct
    return pl.pallas_call(
        forward_kernel,
        out_shape=(
            shape((16 * SHARD, D), bf), shape((SHARD, D), bf),
            shape((2048, D), bf), shape((3, D, 256), bf), shape((8, D), f32),
            shape((2048, 128), f32), shape((2048, 128), f32), shape((2048, D), bf),
            shape((2048, 256), bf), shape((2048, 256), bf), shape((2048, 256), bf),
            shape((2048, 256), f32), shape((2, 2, 2048), f32), shape((512, D), bf),
        ),
        in_specs=[VM] * 3,
        out_specs=(ANY,) * 4 + (VM,) + (ANY,) * 7 + (VM, ANY),
        scratch_shapes=[
            pltpu.VMEM((64 + NATURAL + 6, 128), f32),
            pltpu.VMEM((64, 128), f32),
            pltpu.VMEM((4, 3, 128, 256), bf),
            pltpu.VMEM((SHARD, D), bf),
            pltpu.VMEM((4, 8, 128), f32),
            pltpu.VMEM((2048, 256), bf),
            pltpu.VMEM((2048, D), bf),
            pltpu.VMEM((3, D, 256), bf),
            pltpu.VMEM((2048, 128), f32),
            pltpu.VMEM((2048, 128), f32),
            pltpu.VMEM((2048, D), bf),
            pltpu.VMEM((2048, 256), bf),
            pltpu.VMEM((2048, 256), bf),
            pltpu.VMEM((2048, 256), bf),
            pltpu.VMEM((2048, 256), f32),
            DMA((3, 4, 2)), DMA((3, 4, 2)), DMA((3, 4)), DMA((3, 4)),
            DMA((32,)), DMA((2,)), DMA((3,)), DMA((3,)), DMA,
            *gather_sems(2), DMA((3,)), DMA((3,)), DMA((CHUNKS,)), DMA((CHUNKS,)), DMA((10,)),
        ],
        compiler_params=params_for(0),
    )(share, hidden, places)


def backward_kernel(
    gw_ref, part_ref, ag_ref, q_hbm, k_hbm, v_hbm, a_hbm, l_ref, cos_hbm, sin_hbm,
    normed_hbm, hid_hbm, wq_hbm, rg_hbm, nrm_ref, nsum_ref, st_ref,
    out_ref, ig_ref, sto_ref,
    grads, dk, dv, q_ref, k_ref, v_ref, a_ref, cos_ref, sin_ref, normed, hid, wq,
    own_ref, vg, nsum,
    ext, hal, hsend, av, bv, cv, acv, zv, sums, sv, nc, ny, nland, sland, land,
    lsem, hsems, rgs, ts, tr, cs, cr, s1, r1, s2, r2, zs, zr, ms, mr, qs, qr, hsem, *rooms,
):
    z, x, y, c = coords()
    xn, yn, cn = 1 - x, 1 - y, 1 - c
    s = (z * 2 + x) * 4 + y * 2 + c
    me = y * 2 + c
    core = dev(z, x, y, cn)
    xs, xo, ys, yo = dev(z, xn, y, c), dev(z, xn, y, cn), dev(z, x, yn, c), dev(z, x, yn, cn)
    prv = lax.rem(s + 31, 32)

    def take(owner):
        return ag_ref.at[:, pl.ds(pl.multiple_of(owner * 256, 256), 256)]

    def put(owner):
        return grads.at[pl.ds(pl.multiple_of(owner * 512, 512), 512)]

    loads = [
        pltpu.make_async_copy(src, dst, lsem.at[i])
        for i, (src, dst) in enumerate(
            [
                (take(me), put(me)), (q_hbm, q_ref), (k_hbm, k_ref), (v_hbm, v_ref),
                (a_hbm, a_ref), (cos_hbm, cos_ref), (sin_hbm, sin_ref),
                (normed_hbm, normed), (wq_hbm, wq),
            ]
        )
    ]
    for copy in loads:
        copy.start()

    bar = pltpu.get_barrier_semaphore()

    def hello(i, _):
        greet(bar, linear(lax.rem(s + i, 32)))
        return 0

    lax.fori_loop(1, 32, hello, 0)
    pl.semaphore_wait(bar, 31)

    _, starts, arrivals = swap_copies(take, put, ts, tr, 0)
    for copy in starts:
        copy.start()

    def owned(k):
        return own_ref.at[pl.ds(pl.multiple_of(k * CHUNK, CHUNK), CHUNK)]

    start, pump, steps, finish = reduce_steps(
        functools.partial(shard_rows, gw_ref, 8), (2, 1), True, BACKWARD_X, owned, *rooms
    )
    start()

    def tell(i):
        return remote(st_ref, sland.at[s], qs.at[i], qr.at[s], linear(lax.rem(s + i, 32)))

    def tell_all(i, _):
        tell(i).start()
        return 0

    lax.fori_loop(1, 32, tell_all, 0)

    def up(k):
        return remote(land.at[k], land.at[k], cs.at[k], cr.at[k], dev(z + 1, x, y, c))

    def part(k):
        return part_ref.at[pl.ds(pl.multiple_of(k * CHUNK, CHUNK), CHUNK)]

    def up_step(k):
        @pl.when(z > 0)
        def _():
            up(k).wait_recv()

        @pl.when(z == 0)
        def _():
            add_tiles(land.at[k], CHUNK, part(k))

        @pl.when((z > 0) & (z < 3))
        def _():
            add_tiles(land.at[k], CHUNK, part(k), land.at[k])

        @pl.when(z < 3)
        def _():
            up(k).start()

        @pl.when(z == 3)
        def _():
            add_tiles(owned(k), CHUNK, part(k), land.at[k])

    pump(0, 0)
    pump(1, 0)
    for copy in loads[:7]:
        copy.wait()
    for copy in arrivals:
        copy.wait_recv()

    def step(t, _):
        p = t // 4
        i = t - 4 * p
        at = pl.ds(pl.multiple_of(i * BLOCK, BLOCK), BLOCK)
        lanes = pl.ds(pl.multiple_of(p * 128, 128), 128)

        @pl.when(i == 0)
        def _():
            dk[...] = jnp.zeros_like(dk)
            dv[...] = jnp.zeros_like(dv)

        query_grad = attend_back_rows(
            i, q_ref[at, lanes], grads[at, lanes], a_ref[at, lanes], l_ref[p, :, at],
            k_ref.at[:, lanes], v_ref.at[:, lanes], dk, dv,
        )
        q_ref[at, lanes] = turn_back(query_grad, cos_ref[at, :], sin_ref[at, :])

        @pl.when(i == 3)
        def _():
            finish_keys(
                dk, dv, cos_ref, sin_ref, k_ref.at[:, lanes], v_ref.at[:, lanes]
            )

        pump(2 + t, 0)
        k = t - 2 * z

        @pl.when((z < 3) & (k >= 0) & (k < CHUNKS))
        def _():
            up_step(k)

        return 0

    lax.fori_loop(0, 8, step, 0)
    for copy in loads[7:]:
        copy.wait()
    d_refs = (q_ref, k_ref, v_ref)
    residual = [
        pltpu.make_async_copy(
            rg_hbm.at[:, 128 * i : 128 * i + 128],
            (dk, dv)[i // 4].at[512 * (i % 4) : 512 * (i % 4) + 512],
            rgs.at[i],
        )
        for i in range(8)
    ]
    for copy in residual:
        copy.start()

    def block_grad(xx, yy):
        at = pl.ds(pl.multiple_of((xx * 2 + yy) * 256, 256), 256)
        for j in range(3):
            vg[j, at, :] = lax.dot_general(
                normed[:, at], d_refs[j][...], TN, preferred_element_type=f32
            ).astype(bf)

    def unit(xx, yy, cc):
        at = pl.multiple_of((xx * 4 + yy * 2 + cc) * 128, 128)
        return vg.at[:, pl.ds(at, 128), :]

    half = 256

    def rows(yy, cc, k):
        return normed.at[pl.ds(pl.multiple_of((yy * 2 + cc) * 512 + k * half, half), half)]

    order = [(yn, cn), (yn, c), (y, cn), (y, c)]

    def row_load(n):
        yy, cc = order[n // 2]
        at = pl.ds(pl.multiple_of((yy * 2 + cc) * 512 + n % 2 * half, half), half)
        return pltpu.make_async_copy(hid_hbm.at[at], hid.at[n % 2], hsems.at[n])

    for n in range(2):
        row_load(n).start()

    opposite = [
        remote(unit(xn, yn, cc), av.at[i], s1.at[i], r1.at[i], xs) for i, cc in enumerate((c, cn))
    ]
    beside = [
        remote(unit(xn, y, c), bv.at[0], s1.at[2], r1.at[2], xs),
        remote(unit(xn, y, cn), bv.at[1], s1.at[3], r1.at[3], xo),
    ]
    sibling = remote(unit(x, y, cn), cv, s1.at[4], r1.at[4], core)
    block_grad(xn, yn)
    for copy in opposite:
        copy.start()
    block_grad(xn, y)
    for copy in beside:
        copy.start()
    block_grad(x, yn)
    across = []
    for i, cc in enumerate((c, cn)):
        opposite[i].wait_recv()
        for j in range(3):
            add_rows(sv.at[i, j], unit(x, yn, cc).at[j], av.at[i, j])
        copy = remote(sv.at[i], acv.at[i], s1.at[5 + i], r1.at[5 + i], (ys, yo)[i])
        copy.start()
        across.append(copy)
    block_grad(x, y)
    sibling.start()

    nsum[...] = jnp.zeros_like(nsum)
    gain = nrm_ref[0:1, :]

    def row_grad(m):
        yy, cc = order[m]
        for k in range(2):
            n = 2 * m + k
            row_load(n).wait()
            at = pl.ds(pl.multiple_of((yy * 2 + cc) * 512 + k * half, half), half)
            total = lax.dot_general(q_ref[at, :], wq[0], NT, preferred_element_type=f32)
            for j in range(1, 3):
                total = total + lax.dot_general(
                    d_refs[j][at, :], wq[j], NT, preferred_element_type=f32
                )
            normed[at, :] = total.astype(bf)
            unit_rows, _ = unit_of(hid[k].astype(f32))
            nsum[0] += fold(total * unit_rows)
            nsum[1] += fold(total)
            if n < 6:
                row_load(n + 2).start()

    far = [remote(rows(yn, cn, k), nc.at[1, k], s2.at[0, k], r2.at[0, k], core) for k in range(2)]
    near = [remote(rows(y, cn, k), nc.at[0, k], s2.at[1, k], r2.at[1, k], core) for k in range(2)]
    row_grad(0)
    for copy in far:
        copy.start()
    row_grad(1)
    later = []
    for k in range(2):
        far[k].wait_recv()

        def add_far(q, _):
            at = pl.ds(pl.multiple_of(q * 32, 32), 32)
            here = rows(yn, c, k).at[at]
            add_rows(here, here, nc.at[1, k, at])
            return 0

        lax.fori_loop(0, half // 32, add_far, 0)
        copy = remote(rows(yn, c, k), ny.at[k], s2.at[2, k], r2.at[2, k], ys)
        copy.start()
        later.append(copy)

    blocks = [y * 2 + c, y * 2 + cn, yn * 2 + c, yn * 2 + cn]

    def down(q):
        return remote(sums.at[q], zv.at[q], zs.at[q], zr.at[q], dev(z - 1, x, y, c))

    for q in range(4):
        if q == 0:
            beside[0].wait_recv()
            parts = [unit(x, y, c), bv.at[0]]
        elif q == 1:
            sibling.wait_recv()
            beside[1].wait_recv()
            parts = [cv, bv.at[1]]
        else:
            across[q - 2].wait_recv()
            parts = [acv.at[q - 2]]

        @pl.when(z < 3)
        def _():
            remote(sums.at[q], zv.at[q], zs.at[q], zr.at[q], core).wait_recv()

        @pl.when(z == 3)
        def _():
            for j in range(3):
                add_rows(sums.at[q, j], *[part.at[j] for part in parts])
            down(q).start()

        @pl.when((z == 1) | (z == 2))
        def _():
            for j in range(3):
                add_rows(sums.at[q, j], zv.at[q, j], *[part.at[j] for part in parts])
            down(q).start()

        @pl.when(z == 0)
        def _():
            for j in range(3):
                total = zv[q, j].astype(f32)
                for part in parts:
                    total = total + part[j].astype(f32)
                for h in range(2):
                    at = 64 - 2 * s + 8 * j + 2 * blocks[q] + h
                    ext[pl.ds(at, 128, stride=24), :] = total[:, 128 * h : 128 * h + 128]

    row_grad(2)
    for copy in near:
        copy.start()
    row_grad(3)
    nsum_ref_rows = jnp.sum(nsum[...], axis=1)
    hsum = nland.at[s]
    hsum[0:2, :] = nsum_ref_rows
    hsum[2:8, :] = nsum_ref[2:8, :]
    norm_send = remote(hsum, hsum, ms.at[0], mr.at[s], (7, 3))

    @pl.when(s != 31)
    def _():
        norm_send.start()

    lax.fori_loop(10, steps, pump, 0)

    @pl.when(z == 3)
    def _():
        for k in range(CHUNKS):
            up_step(k)

    base = 64 - 2 * s

    def place(src, first, count, apart):
        for j in range(apart):
            for k in range(8):
                ext[pl.ds(base + 8 * (first + j) + k, count, stride=8 * apart), :] = own_ref[
                    src + j * count : src + (j + 1) * count, 128 * k : 128 * k + 128
                ]

    @pl.when((s == 8) | (s == 9) | (s >= 22))
    def _():
        place(0, 0, 384, 1)

    @pl.when(s == 10)
    def _():
        place(0, 0, 256, 1)
        place(256, 256, 32, 4)

    @pl.when((s >= 11) & (s <= 20))
    def _():
        place(0, 0, 96, 4)

    @pl.when(s == 21)
    def _():
        place(0, 0, 32, 4)
        place(128, 128, 256, 1)

    hsend[...] = ext[0:64, :]
    halo = remote(hsend, hal, hsem.at[0], hsem.at[1], linear(prv))
    halo.start()
    for copy in residual:
        copy.wait()
    for k in range(2):
        near[k].wait_recv()
        later[k].wait_recv()
        at = pl.ds(pl.multiple_of(me * 512 + k * half, half), half)
        to = slice(k * half, k * half + half)
        total = normed[at, :].astype(f32) + nc[0, k].astype(f32) + ny[k].astype(f32)
        unit_rows, inverse = unit_of(hid[k].astype(f32))
        into = into_norm(total, unit_rows, inverse, gain)
        for i in range(8):
            lanes = slice(128 * i, 128 * i + 128)
            first = 512 * (i % 4) + k * half
            ig_ref[to, lanes] = ((dk, dv)[i // 4][first : first + half] + into[:, lanes]).astype(bf)

    def hear(i, _):
        o = lax.rem(s + i, 32)
        remote(st_ref, sland.at[o], qs.at[0], qr.at[o], core).wait_recv()
        return 0

    lax.fori_loop(1, 32, hear, 0)
    sland[pl.ds(s, 1)] = st_ref[...].reshape(1, 8, 128)
    sto_ref[...] = jnp.sum(sland[...], axis=0)
    halo.wait()

    @pl.when(s != 31)
    def _():
        row = lax.broadcasted_iota(jnp.int32, (64, 128), 0)
        end = slice(NATURAL, NATURAL + 64)
        ext[end, :] = jnp.where(row >= 64 - 2 * (s + 1), hal[...], ext[end, :])

    @pl.when(s == 31)
    def _():
        def gather(i, total):
            remote(nland.at[i], nland.at[i], ms.at[0], mr.at[i], core).wait_recv()
            return total + nland[i]

        total = lax.fori_loop(0, 31, gather, nland[31])
        for k in range(8):
            ext[pl.ds(base + 8 * 384 + k, 8, stride=8), :] = total[:, 128 * k : 128 * k + 128]

    out_ref[...] = ext[64 : 64 + NATURAL, :]
    for copy in far + opposite + beside + [sibling] + near + across + later + starts:
        copy.wait_send()

    @pl.when(z > 0)
    def _():
        for q in range(4):
            down(q).wait_send()

    @pl.when(z < 3)
    def _():
        for k in range(CHUNKS):
            up(k).wait_send()

    def told(i, _):
        tell(i).wait_send()
        return 0

    lax.fori_loop(1, 32, told, 0)

    @pl.when(s != 31)
    def _():
        norm_send.wait_send()

    finish()


BACKWARD_X = 64


def backward(*operands):
    shape = jax.ShapeDtypeStruct
    room = pltpu.VMEM
    unit = (3, 128, 256)
    return pl.pallas_call(
        backward_kernel,
        out_shape=(shape((NATURAL, 128), f32), shape((512, D), bf), shape((8, 128), f32)),
        in_specs=[ANY, VM] + [ANY] * 5 + [VM] + [ANY] * 6 + [VM] * 3,
        out_specs=(VM,) * 3,
        scratch_shapes=[
            room((2048, 256), bf), room((2048, 128), f32), room((2048, 128), f32),
            room((2048, 256), bf), room((2048, 256), bf), room((2048, 256), bf),
            room((2048, 256), f32), room((2048, 128), f32), room((2048, 128), f32),
            room((2048, D), bf), room((2, 256, D), bf), room((3, D, 256), bf),
            room((SHARD, D), f32), room((3, D, 256), bf), room((2, 8, D), f32),
            room((64 + NATURAL + 6, 128), f32), room((64, 128), f32), room((64, 128), f32),
            room((2,) + unit, bf), room((2,) + unit, bf), room(unit, bf), room((2,) + unit, bf),
            room((4,) + unit, bf), room((4,) + unit, bf), room((2,) + unit, bf),
            room((2, 2, 256, D), bf), room((2, 256, D), bf),
            room((32, 8, D), f32), room((32, 8, 128), f32),
            room((CHUNKS, CHUNK, D), bf),
            DMA((9,)), DMA((8,)), DMA((8,)), DMA((3,)), DMA((3,)), DMA((CHUNKS,)), DMA((CHUNKS,)),
            DMA((7,)), DMA((7,)), DMA((3, 2)), DMA((3, 2)), DMA((4,)), DMA((4,)),
            DMA((1,)), DMA((32,)), DMA((32,)), DMA((32,)), DMA((2,)),
            *reduce_rooms(2, True, BACKWARD_X),
        ],
        compiler_params=params_for(2, 63),
    )(*operands)


ROWS = 128
GELU_A = math.sqrt(2.0 / math.pi)
GELU_B = 0.044715


def mean_of(values):
    return jnp.mean(values, axis=-1, keepdims=True)


def unit_of(values):
    center = values - mean_of(values)
    inverse = lax.rsqrt(mean_of(center * center) + EPSILON)
    return center * inverse, inverse


def into_norm(grads, unit, inverse, gain):
    scaled = grads * gain
    return inverse * (scaled - mean_of(scaled) - unit * mean_of(scaled * unit))


def fold(values):
    total = values[0:8]
    for at in range(8, values.shape[0], 8):
        total = total + values[at : at + 8]
    return total


def up_pieces(j):
    pieces = [(D + 32 * j, 0, 32)]
    pieces += [(D + 128 + 384 * i + 96 * j, 32 + 96 * i, 96) for i in range(10)]
    pieces.append((D + 3968 + 32 * j, 992, 32))
    return pieces


def dense_kernel(
    lines, a_ref, h_ref, c_ref, scale_ref, n_ref, w_ref, col_ref,
    o_ref, rg_ref, ag_ref, gw_ref, ns_ref, sq_ref, part_ref,
    wo, wu, wd, branch, lowered, entered, act, slope, lgrad, stage, sums,
    ws, ups, gs, *rooms,
):
    tokens = a_ref.shape[0]
    residual, egrad = rg_ref, lowered
    start = finish = reduce_start = reduce_finish = lambda: None
    pump = reduce_pump = lambda i, _: 0
    steps = reduce_count = 0
    if lines:
        z, x, y, c = coords()
        sems, rooms = rooms[:3], rooms[3:]

        def source(k):
            return col_ref.at[pl.ds(pl.multiple_of(k * CHUNK, CHUNK), CHUNK)]

        def down_rows(zz, xx, yy, cc, k, low=0, count=CHUNK):
            s = xx * 4 + yy * 2 + cc
            return wd.at[pl.ds(pl.multiple_of(D + s * SHARD + k * CHUNK + low, 16), count)]

        start, _, _, pump, steps, finish = gather_steps(
            down_rows, lambda r: 3, 1, None, source, False, 48, *sems
        )
        reduce_start, reduce_pump, reduce_count, reduce_finish = reduce_steps(
            functools.partial(shard_rows, gw_ref, 8), (3,), False, 48,
            lambda k: part_ref.at[pl.ds(pl.multiple_of(k * CHUNK, CHUNK), CHUNK)], *rooms
        )
        bar = pltpu.get_barrier_semaphore()
        for device in (dev(z, 1 - x, y, c), dev(z, x, 1 - y, c), dev(z, x, y, 1 - c)):
            greet(bar, device)
        pl.semaphore_wait(bar, 3)
    else:
        part_ref[...] = jnp.zeros_like(part_ref)
    pieces = tokens // ROWS
    load_o = pltpu.make_async_copy(w_ref.at[0:D], wo, ws.at[0])
    loads_d = [
        pltpu.make_async_copy(
            w_ref.at[5 * D + D * j : 6 * D + D * j], wd.at[D * j : D * j + D], ws.at[1 + j]
        )
        for j in range(1 if lines else 4)
    ]
    loads_u = [
        [
            pltpu.make_async_copy(
                w_ref.at[src : src + count], wu.at[j, to : to + count], ups.at[j, i]
            )
            for i, (src, to, count) in enumerate(up_pieces(j))
        ]
        for j in range(4)
    ]
    load_o.start()
    for j in range(4):
        for copy in loads_u[j]:
            copy.start()
    for copy in loads_d:
        copy.start()
    start()
    pump(0, 0)
    pump(1, 0)
    sums[...] = jnp.zeros_like(sums)
    width = 1024

    def columns(t):
        return pl.ds(pl.multiple_of(t * width, width), width)

    def over_columns(body, count=D // width):
        def go(t, _):
            body(columns(t))
            return 0

        lax.fori_loop(0, count, go, 0)

    def over_rows(body):
        def go(t, _):
            body(pl.ds(pl.multiple_of(t * ROWS, ROWS), ROWS))
            return 0

        lax.fori_loop(0, pieces, go, 0)

    load_o.wait()

    def branch_step(at):
        branch[:, at] = jnp.dot(a_ref[...], wo[:, at], preferred_element_type=f32)

    over_columns(branch_step)

    def enter_step(at):
        values = branch[at, :]
        unit, _ = unit_of(values)
        res = h_ref[at, :].astype(f32) + unit * n_ref[2:3, :] + n_ref[3:4, :]
        residual[at, :] = res
        unit, _ = unit_of(res)
        entered[at, :] = (unit * n_ref[4:5, :] + n_ref[5:6, :]).astype(bf)
        sums[0] += fold(values * values)

    over_rows(enter_step)
    pump(2, 0)

    for j in range(4):
        for copy in loads_u[j]:
            copy.wait()

        def lift_step(at):
            lifted = jnp.dot(entered[...], wu[j, :, at], preferred_element_type=f32)
            square = lifted * lifted
            tanh = jnp.tanh(lifted * (GELU_A + (GELU_A * GELU_B) * square))
            half = 0.5 + 0.5 * tanh
            act[j, :, at] = (lifted * half).astype(bf)
            slope[j, :, at] = half + lifted * (0.5 - 0.5 * tanh * tanh) * (
                GELU_A + (3.0 * GELU_A * GELU_B) * square
            )

        over_columns(lift_step)
        pump(3 + j, 0)
    lax.fori_loop(7, steps, pump, 0)
    finish()
    for copy in loads_d:
        copy.wait()

    def lower_step(at):
        total = jnp.dot(act[0], wd[0:D, at], preferred_element_type=f32)
        for j in range(1, 4):
            total = total + jnp.dot(act[j], wd[D * j : D * j + D, at], preferred_element_type=f32)
        lowered[:, at] = total

    over_columns(lower_step)
    scale = scale_ref[0, 0]

    def out_step(at):
        values = lowered[at, :]
        unit, inverse = unit_of(values)
        o_ref[at, :] = (residual[at, :] + unit * n_ref[6:7, :] + n_ref[7:8, :]).astype(bf)
        upstream = c_ref[at, :].astype(f32) * scale
        lgrad[at, :] = into_norm(upstream, unit, inverse, n_ref[6:7, :]).astype(bf)
        sums[1] += fold(values * values)
        sums[2] += fold(upstream * unit)
        sums[3] += fold(upstream)

    over_rows(out_step)

    def store(buffer, j, slot):
        return [
            pltpu.make_async_copy(
                stage.at[buffer, to : to + count], gw_ref.at[src : src + count], gs.at[slot, i]
            )
            for i, (src, to, count) in enumerate(up_pieces(j))
        ]

    def store_block(buffer, first, slot):
        return [pltpu.make_async_copy(stage.at[buffer], gw_ref.at[first : first + D], gs.at[slot, 0])]

    pending = {}

    def reuse(buffer):
        for copy in pending.pop(buffer, []):
            copy.wait()

    def issue(buffer, copies):
        for copy in copies:
            copy.start()
        pending[buffer] = copies

    for n, j in enumerate((1, 2, 3, 0)):
        buffer = n % 2
        reuse(buffer)

        def down_step(at):
            stage[buffer, at, :] = lax.dot_general(
                act[j, :, at], lgrad[...], TN, preferred_element_type=f32
            ).astype(bf)

        over_columns(down_step)
        issue(buffer, store_block(buffer, 5 * D + D * j, buffer))
        if n == 2:
            reuse(1)
            reuse(0)
            reduce_start()
    for j in range(4):

        def slope_step(at):
            grads = lax.dot_general(
                lgrad[...], wd[D * j : D * j + D, :], NT, preferred_element_type=f32
            )
            act[j, :, at] = (grads * slope[j, :, at]).astype(bf)

        over_columns(slope_step)
        buffer = j % 2
        reuse(buffer)

        def up_step(at):
            stage[buffer, :, at] = lax.dot_general(
                entered[...], act[j, :, at], TN, preferred_element_type=f32
            ).astype(bf)

        over_columns(up_step)
        issue(buffer, store(buffer, j, buffer))
        reduce_pump(j, 0)

    def enter_back_step(at):
        total = lax.dot_general(act[0], wu[0, at, :], NT, preferred_element_type=f32)
        for j in range(1, 4):
            total = total + lax.dot_general(act[j], wu[j, at, :], NT, preferred_element_type=f32)
        egrad[:, at] = total

    over_columns(enter_back_step)
    reduce_pump(4, 0)

    def branch_back_step(at):
        grads = egrad[at, :]
        upstream = c_ref[at, :].astype(f32) * scale
        unit, inverse = unit_of(residual[at, :])
        res_grad = upstream + into_norm(grads, unit, inverse, n_ref[4:5, :])
        rg_ref[at, :] = res_grad
        sums[4] += fold(grads * unit)
        sums[5] += fold(grads)
        unit, inverse = unit_of(branch[at, :])
        lgrad[at, :] = into_norm(res_grad, unit, inverse, n_ref[2:3, :]).astype(bf)
        sums[6] += fold(res_grad * unit)
        sums[7] += fold(res_grad)

    over_rows(branch_back_step)
    reduce_pump(5, 0)
    reuse(0)

    def out_grad_step(at):
        stage[0, at, :] = lax.dot_general(
            a_ref[:, at], lgrad[...], TN, preferred_element_type=f32
        ).astype(bf)

    over_columns(out_grad_step)
    issue(0, store_block(0, 0, 0))

    def attended_step(at):
        ag_ref[:, at] = lax.dot_general(
            lgrad[...], wo[at, :], NT, preferred_element_type=f32
        ).astype(bf)

    over_columns(attended_step)
    order = [None, None, 6, 7, 4, 5, 2, 3]
    for row, source in enumerate(order):
        if source is None:
            ns_ref[row : row + 1, :] = jnp.zeros((1, D), f32)
        else:
            ns_ref[row : row + 1, :] = jnp.sum(sums[source], axis=0, keepdims=True)
    lane = lax.broadcasted_iota(jnp.int32, (8, 128), 1)
    row = lax.broadcasted_iota(jnp.int32, (8, 128), 0)
    told = jnp.zeros((8, 128), f32)
    for t in range(2):
        told = jnp.where((lane == t) & (row == 0), jnp.sum(sums[t]), told)
    sq_ref[...] = told
    reuse(0)
    reuse(1)
    reduce_finish()


def dense(lines, attended, hidden, cotangent, scale, norm_rows, weights, column):
    tokens = attended.shape[0]
    shape = jax.ShapeDtypeStruct
    room = pltpu.VMEM
    return pl.pallas_call(
        functools.partial(dense_kernel, lines),
        out_shape=(
            shape((tokens, D), bf), shape((tokens, D), f32), shape((tokens, D), bf),
            shape((9 * D, D), bf), shape((8, D), f32), shape((8, 128), f32), shape((SHARD, D), bf),
        ),
        in_specs=[VM, VM, VM, pl.BlockSpec(memory_space=pltpu.SMEM), VM, ANY, ANY],
        out_specs=(VM, VM, VM, ANY, VM, VM, VM),
        scratch_shapes=[
            room((D, D), bf), room((4, D, D), bf), room((4 * D, D), bf),
            room((tokens, D), f32), room((tokens, D), f32),
            room((tokens, D), bf), room((4, tokens, D), bf), room((4, tokens, D), f32),
            room((tokens, D), bf), room((2, D, D), bf),
            room((8, 8, D), f32), DMA((5,)), DMA((4, 12)), DMA((2, 12)),
            *(gather_sems(1) + reduce_rooms(1, False, 48) if lines else []),
        ],
        compiler_params=params_for(5 if lines else None, 62),
    )(attended, hidden, cotangent, scale, norm_rows, weights, column)


def norm_forward(values, gain_row, shift_row):
    center = values - jnp.mean(values, axis=-1, keepdims=True)
    spread = jnp.mean(center * center, axis=-1, keepdims=True)
    inverse = lax.rsqrt(spread + EPSILON)
    unit_rows = center * inverse
    return (unit_rows * gain_row + shift_row, unit_rows, inverse)


def norm_backward(grad_rows, unit_rows, inverse, gain_row):
    scaled = grad_rows * gain_row
    first_mean = jnp.mean(scaled, axis=-1, keepdims=True)
    second_mean = jnp.mean(scaled * unit_rows, axis=-1, keepdims=True)
    return inverse * (scaled - first_mean - unit_rows * second_mean)


def norm_sums(grad_rows, unit_rows):
    return jnp.sum(grad_rows * unit_rows, axis=0), jnp.sum(grad_rows, axis=0)


def up_from_shards(rows):
    pieces = [rows[:128].reshape(1, 4, 32, D), rows[128:3968].reshape(10, 4, 96, D)]
    pieces.append(rows[3968:].reshape(1, 4, 32, D))
    return jnp.concatenate(
        [piece.transpose(0, 2, 1, 3).reshape(-1, FF) for piece in pieces], axis=0
    )


def up_to_shards(grad):
    pieces = [(grad[:32], 1, 32), (grad[32:992], 10, 96), (grad[992:], 1, 32)]
    return jnp.concatenate(
        [
            piece.reshape(blocks, rows, 4, D).transpose(0, 2, 1, 3).reshape(-1, D)
            for piece, blocks, rows in pieces
        ],
        axis=0,
    )


def dots(a, b, contract):
    return lax.dot_general(a, b, ((contract[:1], contract[1:]), ((), ())), preferred_element_type=f32)


def per_device(lines, hidden_in, params, cotangent, source_ids, corpus_weight, positions):
    devices = lax.axis_size(("dp", "fsdp"))
    width = lax.axis_size("fsdp")
    hidden = hidden_in[0]
    tokens = hidden.shape[0]
    place = lax.axis_index("fsdp")
    if lines:
        (
            others, column, hidden_all, w_qkv, norm_rows, cosine, sine,
            normed_all, queries, keys, values, attended_all, logs, attended,
        ) = forward(
            params.reshape(NATURAL, 128),
            hidden,
            jnp.pad(positions.astype(f32).reshape(4, 128), ((0, 4), (0, 0))),
        )
    else:
        whole = lax.all_gather(params, ("dp", "fsdp"), axis=0, tiled=True)
        ends = [0, 3 * D * D, 4 * D * D, 4 * D * D + D * FF, 4 * D * D + 2 * D * FF]
        parts = [whole[a:b] for a, b in zip(ends, ends[1:])]
        w_qkv = lax.dynamic_index_in_dim(
            parts[0].reshape(D, 3, width, D // width).transpose(1, 2, 0, 3), place, 1, False
        )
        others = jnp.concatenate(
            [parts[1].reshape(D, D), up_to_shards(parts[2].reshape(D, FF)), parts[3].reshape(FF, D)]
        )
        norm_rows = whole[ends[-1] :].reshape(8, D).astype(f32)
        hidden_all = lax.all_gather(hidden, "fsdp", axis=0, tiled=True)
        places = lax.all_gather(positions[0].astype(f32), "fsdp", axis=0, tiled=True)
        lane = jnp.arange(128) % 64
        frequency = jnp.exp((lane % 32).astype(f32) * (-2.0 * math.log(10000.0) / HEAD_DIM))
        angles = places[:, None] * frequency
        cosine = jnp.cos(angles)
        sine = jnp.where(lane < 32, -1.0, 1.0) * jnp.sin(angles)
        normed_all, queries, keys, values = project(hidden_all, norm_rows, w_qkv, cosine, sine)
        attended_all, attended_low, logs = attend(queries, keys, values)
        attended = swap(attended_low, width, True, 4)
        column = jnp.zeros((SHARD, D), bf)
    source_table = jnp.arange(corpus_weight.shape[0], dtype=jnp.int32)
    row_scale = jnp.sum(jnp.where(source_ids[0] == source_table, corpus_weight, 0.0))
    output, residual_grad, attended_grad, weight_grads, norm_part, squares, part = dense(
        lines, attended, hidden, cotangent[0], row_scale.reshape(1, 1), norm_rows, others, column
    )
    if lines:
        param_grads, input_grad, squares = backward(
            weight_grads, part, attended_grad, queries, keys, values, attended_all, logs,
            cosine, sine, normed_all, hidden_all, w_qkv, residual_grad, norm_rows, norm_part, squares,
        )
        param_grads = param_grads.reshape(-1)
    else:
        grads_all = swap(attended_grad, width, False, 6)
        mixed_grad = attend_back(
            queries, keys, values, grads_all, attended_all, logs, cosine, sine
        )
        grad_qkv = jnp.stack([dots(normed_all, part, (0, 0)) for part in mixed_grad])
        normed_part = sum(dots(part, w_qkv[j], (1, 1)) for j, part in enumerate(mixed_grad))
        _, unit_all, _ = norm_forward(hidden_all.astype(f32), norm_rows[0], norm_rows[1])
        norm_part = jnp.concatenate(
            [jnp.stack(norm_sums(normed_part, unit_all)), norm_part[2:]], axis=0
        )
        spread = jnp.zeros((3, width, D, D // width), bf)
        spread = lax.dynamic_update_slice_in_dim(spread, grad_qkv.astype(bf)[:, None], place, 1)
        parts = (
            spread.transpose(2, 0, 1, 3),
            weight_grads[:D],
            up_from_shards(weight_grads[D : 5 * D]),
            weight_grads[5 * D :],
            norm_part.astype(bf),
        )
        flat = jnp.concatenate([part.reshape(-1) for part in parts])
        param_grads = lax.psum_scatter(flat, ("dp", "fsdp"), scatter_dimension=0, tiled=True)
        param_grads = param_grads.astype(f32)
        normed_grad = lax.psum_scatter(normed_part, "fsdp", scatter_dimension=0, tiled=True)
        squares = lax.psum(squares, ("dp", "fsdp"))
        _, normed_unit, normed_inverse = norm_forward(
            hidden.astype(f32), norm_rows[0], norm_rows[1]
        )
        into_input = norm_backward(normed_grad, normed_unit, normed_inverse, norm_rows[0])
        input_grad = (residual_grad + into_input).astype(bf)
    statistics = squares[0, :2] / (devices * tokens * D)
    return (output[None], input_grad[None], param_grads, statistics)


def solution(mesh):
    lines = (mesh.shape["dp"], mesh.shape["fsdp"]) == (8, 4)
    in_specs = (
        P("dp", "fsdp", None),
        P(("dp", "fsdp")),
        P("dp", "fsdp", None),
        P("dp"),
        P(),
        P("dp", "fsdp"),
    )
    out_specs = (P("dp", "fsdp", None), P("dp", "fsdp", None), P(("dp", "fsdp")), P())
    return jax.shard_map(
        functools.partial(per_device, lines),
        mesh=mesh,
        in_specs=in_specs,
        out_specs=out_specs,
        check_vma=False,
    )
```

```python
import functools
import math

import jax
import jax.numpy as jnp
from jax import lax
from jax.experimental import pallas as pl
from jax.experimental.pallas import tpu as pltpu
from jax.sharding import PartitionSpec as P

D = 1024
HEADS = 16
HEAD_DIM = 64
FF = 4096
EPSILON = 1e-05
MASKED = -1e30
SCALE = 1.0 / math.sqrt(HEAD_DIM)
LOG2E = 1.4426950408889634

MESH = pl.DeviceIdType.MESH
bf = jnp.bfloat16
f32 = jnp.float32
SHARD = 384
NATURAL = 3074
MIB = 2**20

VM = pl.BlockSpec(memory_space=pltpu.VMEM)
ANY = pl.BlockSpec(memory_space=pl.ANY)
DMA = pltpu.SemaphoreType.DMA


def params_for(collective=None, mib=48):
    if collective is None:
        return pltpu.CompilerParams(vmem_limit_bytes=mib * MIB)
    return pltpu.CompilerParams(
        collective_id=collective, has_side_effects=True, vmem_limit_bytes=mib * MIB
    )


def coords():
    dp, fs = lax.axis_index("dp"), lax.axis_index("fsdp")
    return dp // 2, lax.rem(dp, 2), fs // 2, lax.rem(fs, 2)


def dev(z, x, y, c):
    return (z * 2 + x, y * 2 + c)


def linear(i):
    return (i // 4, lax.rem(i, 4))


def remote(src, dst, send, recv, to):
    return pltpu.make_async_remote_copy(
        src_ref=src, dst_ref=dst, send_sem=send, recv_sem=recv, device_id=to, device_id_type=MESH
    )


def greet(bar, device):
    pl.semaphore_signal(bar, inc=1, device_id=device, device_id_type=MESH)


def meet_neighbours(z, x, y, c, plane, more=0):
    bar = pltpu.get_barrier_semaphore()
    for device in plane:
        greet(bar, device)

    @pl.when(z < 3)
    def _():
        greet(bar, dev(z + 1, x, y, c))

    @pl.when(z > 0)
    def _():
        greet(bar, dev(z - 1, x, y, c))

    line = jnp.where(z < 3, 1, 0) + jnp.where(z > 0, 1, 0)
    pl.semaphore_wait(bar, len(plane) + line + more)


def add_rows(dst, *srcs):
    if dst.dtype == bf and len(srcs) == 2:
        dst[...] = srcs[0][...] + srcs[1][...]
        return
    total = srcs[0][...].astype(f32)
    for part in srcs[1:]:
        total = total + part[...].astype(f32)
    dst[...] = total.astype(dst.dtype)


def add_tiles(dst, rows, *srcs):
    for at in range(0, rows, 16):
        add_rows(dst.at[at : at + 16], *[part.at[at : at + 16] for part in srcs])


CHUNKS = 4
AHEAD = 2
EARLY = 2
CHUNK = SHARD // CHUNKS


def shard_rows(ref, base, zz, xx, yy, cc, k, low=0, count=CHUNK):
    s = (zz * 2 + xx) * 4 + yy * 2 + cc
    return ref.at[pl.ds(pl.multiple_of((s - base) * SHARD + k * CHUNK + low, 16), count)]


def gather_sems(planes):
    return [DMA((11, planes * CHUNKS)), DMA((11, planes * CHUNKS)), DMA((CHUNKS + 1,))]


def gather_steps(rows, plane_of, planes, own, source, line, over_x, ss, rs, ls):
    z, x, y, c = coords()
    xn, yn, cn = 1 - x, 1 - y, 1 - c
    to_x, to_y, to_core = dev(z, xn, y, c), dev(z, x, yn, c), dev(z, x, y, cn)
    lag, core_lag = 2, 4
    units = planes * CHUNKS
    ZU, ZD, XO, YO, CO, XD, YD, CX, CY, CXD, CYD = range(11)
    rest = CHUNK - over_x

    def unit(i):
        r = i // CHUNKS
        return plane_of(r), i - r * CHUNKS, i

    def send(kind, i):
        zz, k, q = unit(i)
        ref, to = {
            ZU: lambda: (rows(zz, x, y, c, k), dev(z + 1, x, y, c)),
            ZD: lambda: (rows(zz, x, y, c, k), dev(z - 1, x, y, c)),
            XO: lambda: (rows(zz, x, y, c, k), to_x),
            YO: lambda: (rows(zz, x, y, c, k), to_y),
            CO: lambda: (rows(zz, x, y, c, k), to_core),
            YD: lambda: (rows(zz, xn, y, c, k, over_x, rest), to_y),
            XD: lambda: (rows(zz, x, yn, c, k, 0, over_x), to_x),
            CX: lambda: (rows(zz, xn, y, c, k), to_core),
            CY: lambda: (rows(zz, x, yn, c, k), to_core),
            CXD: lambda: (rows(zz, xn, yn, c, k, 0, over_x), to_core),
            CYD: lambda: (rows(zz, xn, yn, c, k, over_x, rest), to_core),
        }[kind]()
        slot = (zz - 1) * CHUNKS + k if line else k
        src = source(k) if kind in (XO, YO, CO) and not line else ref
        return remote(src, ref, ss.at[kind, slot], rs.at[kind, slot], to)

    def arrive(kind, i):
        zz, k, q = unit(i)
        ref = {
            ZU: lambda: rows(zz, x, y, c, k),
            ZD: lambda: rows(zz, x, y, c, k),
            XO: lambda: rows(zz, xn, y, c, k),
            YO: lambda: rows(zz, x, yn, c, k),
            XD: lambda: rows(zz, xn, yn, c, k, 0, over_x),
            YD: lambda: rows(zz, xn, yn, c, k, over_x, rest),
            CO: lambda: rows(zz, x, y, cn, k),
            CX: lambda: rows(zz, xn, y, cn, k),
            CY: lambda: rows(zz, x, yn, cn, k),
            CXD: lambda: rows(zz, xn, yn, cn, k, 0, over_x),
            CYD: lambda: rows(zz, xn, yn, cn, k, over_x, rest),
        }[kind]()
        slot = (zz - 1) * CHUNKS + k if line else k
        remote(ref, ref, ss.at[kind, slot], rs.at[kind, slot], to_core).wait_recv()

    def local(k_plane):
        zz = k_plane
        return [
            pltpu.make_async_copy(source(k), rows(zz, x, y, c, k), ls.at[k]) for k in range(CHUNKS)
        ]

    def start():
        if line:

            @pl.when(own(z))
            def _():
                for copy in local(z):
                    copy.start()
                for copy in local(z):
                    copy.wait()
                for k in range(CHUNKS):
                    send(ZD, k).start()
                    if k < EARLY:
                        send(ZU, k).start()
        else:
            for copy in local(plane_of(0)):
                copy.start()

    def late_up():
        @pl.when(own(z))
        def _():
            for k in range(EARLY, CHUNKS):
                send(ZU, k).start()

    def early(i):
        zz, _, _ = unit(i)
        if line:

            @pl.when(zz < z)
            def _():
                arrive(ZU, i)

            @pl.when(zz > z)
            def _():
                arrive(ZD, i)

            @pl.when((zz < z) & (z < 3))
            def _():
                send(ZU, i).start()

            @pl.when((zz > z) & (z > 0))
            def _():
                send(ZD, i).start()

        for kind in (XO, CO):
            send(kind, i).start()

    def step(i, _):
        @pl.when((i < units) & (i >= (EARLY if line else 0)))
        def _():
            early(i)

        @pl.when(i < units)
        def _():
            send(YO, i).start()

        j = i - lag

        @pl.when((j >= 0) & (j < units))
        def _():
            arrive(XO, j)
            send(YD, j).start()
            send(CX, j).start()
            arrive(YO, j)
            send(XD, j).start()
            send(CY, j).start()

        m = i - core_lag

        @pl.when(m >= 0)
        def _():
            arrive(XD, m)
            send(CXD, m).start()
            arrive(YD, m)
            send(CYD, m).start()

        return 0

    def finish():
        def one(i, _):
            zz, _, _ = unit(i)
            for kind in (CO, CX, CY, CXD, CYD):
                arrive(kind, i)
            for kind in (XO, YO, CO, YD, XD, CX, CY, CXD, CYD):
                send(kind, i).wait_send()
            if line:

                @pl.when((zz <= z) & (z < 3))
                def _():
                    send(ZU, i).wait_send()

                @pl.when((zz >= z) & (z > 0))
                def _():
                    send(ZD, i).wait_send()

            return 0

        lax.fori_loop(0, units, one, 0)
        if not line:
            for copy in local(plane_of(0)):
                copy.wait()

    return start, early, late_up, step, units + core_lag, finish


def reduce_steps(
    rows, planes, line, over_x, out, lb, cb, xb, yb, dxb, dyb, zub, zdb, ss, rs, cs, cr, ls
):
    z, x, y, c = coords()
    xn, yn, cn = 1 - x, 1 - y, 1 - c
    to_x, to_y, to_core = dev(z, xn, y, c), dev(z, x, yn, c), dev(z, x, y, cn)
    lag1, lag2, lag3, lag4 = 1, 2, 3, 4
    XS, YS, DXS, DYS, ZD, ZU = range(6)
    units = len(planes) * CHUNKS

    def unit(i):
        r = i // CHUNKS
        zz = planes[0] if len(planes) == 1 else planes[0] - r
        return zz, i - r * CHUNKS

    places = [(xn, yn), (xn, y), (x, yn), (x, y)]

    def load(i, p):
        zz, k = unit(i)
        xx, yy = places[p]
        return pltpu.make_async_copy(rows(zz, xx, yy, c, k), lb.at[i, p], ls.at[i, p])

    def to_sibling(i, p):
        zz, k = unit(i)
        xx, yy = places[p]
        return remote(rows(zz, xx, yy, cn, k), cb.at[i, p], cs.at[i, p], cr.at[i, p], to_core)

    def fetch(i, _):
        for p in range(4):
            load(i, p).start()
            to_sibling(i, p).start()
        return 0

    def start():
        lax.fori_loop(0, AHEAD, fetch, 0)

    def over(kind, src, dst, i, to):
        return remote(src, dst, ss.at[kind, i], rs.at[kind, i], to)

    def diag_x(i):
        return over(DXS, lb.at[i, 0, 0:over_x], dxb.at[i], i, to_x)

    def diag_y(i):
        return over(DYS, lb.at[i, 0, over_x:CHUNK], dyb.at[i], i, to_y)

    def whole_x(i):
        return over(XS, lb.at[i, 1], xb.at[i], i, to_x)

    def whole_y(i):
        return over(YS, lb.at[i, 2], yb.at[i], i, to_y)

    def down(i):
        return over(ZD, lb.at[i, 3], zub.at[i], i, dev(z - 1, x, y, c))

    def up(i):
        return over(ZU, lb.at[i, 3], zdb.at[i], i, dev(z + 1, x, y, c))

    def have(i, p):
        load(i, p).wait()
        to_sibling(i, p).wait_recv()

    def step(i, _):
        @pl.when(i + AHEAD < units)
        def _():
            fetch(i + AHEAD, 0)

        @pl.when(i < units)
        def _():
            have(i, 0)
            add_tiles(lb.at[i, 0], CHUNK, lb.at[i, 0], cb.at[i, 0])
            diag_x(i).start()
            diag_y(i).start()

        j = i - lag1

        @pl.when((j >= 0) & (j < units))
        def _():
            have(j, 1)
            have(j, 2)
            diag_y(j).wait_recv()
            diag_x(j).wait_recv()
            a, b = lb.at[j, 1], cb.at[j, 1]
            low, high = slice(0, over_x), slice(over_x, CHUNK)
            add_tiles(a.at[low], over_x, a.at[low], b.at[low])
            add_tiles(a.at[high], CHUNK - over_x, a.at[high], b.at[high], dyb.at[j])
            whole_x(j).start()
            a, b = lb.at[j, 2], cb.at[j, 2]
            add_tiles(a.at[low], over_x, a.at[low], b.at[low], dxb.at[j])
            add_tiles(a.at[high], CHUNK - over_x, a.at[high], b.at[high])
            whole_y(j).start()

        m = i - lag2

        @pl.when((m >= 0) & (m < units))
        def _():
            zz, k = unit(m)
            have(m, 3)
            whole_x(m).wait_recv()
            whole_y(m).wait_recv()
            parts = [lb.at[m, 3], cb.at[m, 3], xb.at[m], yb.at[m]]
            if not line:
                add_tiles(out(k), CHUNK, *parts)
                return

            @pl.when(z != zz)
            def _():
                add_tiles(lb.at[m, 3], CHUNK, *parts)

            @pl.when(z == 3)
            def _():
                down(m).start()

            @pl.when(z == 0)
            def _():
                up(m).start()

            @pl.when(z == zz)
            def _():
                add_tiles(out(k), CHUNK, *parts)

        if not line:
            return 0
        n = i - lag3

        @pl.when((n >= 0) & (n < units))
        def _():
            zz, _ = unit(n)

            @pl.when((z > zz) & (z < 3))
            def _():
                down(n).wait_recv()
                add_tiles(lb.at[n, 3], CHUNK, lb.at[n, 3], zub.at[n])
                down(n).start()

            @pl.when((z < zz) & (z > 0))
            def _():
                up(n).wait_recv()
                add_tiles(lb.at[n, 3], CHUNK, lb.at[n, 3], zdb.at[n])
                up(n).start()

        o = i - lag4

        @pl.when(o >= 0)
        def _():
            zz, k = unit(o)

            @pl.when(z == zz)
            def _():
                down(o).wait_recv()
                add_tiles(out(k), CHUNK, out(k), zub.at[o])
                up(o).wait_recv()
                add_tiles(out(k), CHUNK, out(k), zdb.at[o])

        return 0

    def finish():
        def one(i, _):
            zz, _ = unit(i)
            for p in range(4):
                to_sibling(i, p).wait_send()
            for copy in (diag_x(i), diag_y(i), whole_x(i), whole_y(i)):
                copy.wait_send()
            if line:

                @pl.when(z > zz)
                def _():
                    down(i).wait_send()

                @pl.when(z < zz)
                def _():
                    up(i).wait_send()

            return 0

        lax.fori_loop(0, units, one, 0)

    return start, step, units + (lag4 if line else lag2), finish


def reduce_rooms(planes, line, over_x):
    units = planes * CHUNKS

    def room(*shape):
        return pltpu.VMEM(shape + (D,), bf)

    lines = units if line else 1
    return [
        room(units, 4, CHUNK), room(units, 4, CHUNK),
        room(units, CHUNK), room(units, CHUNK),
        room(units, over_x), room(units, CHUNK - over_x),
        room(lines, CHUNK), room(lines, CHUNK),
        DMA((6, units)), DMA((6, units)), DMA((units, 4)), DMA((units, 4)), DMA((units, 4)),
    ]


def swap_kernel(n, to_tokens, a_ref, o_ref, ss, rs, ls):
    me = lax.axis_index("fsdp")
    bar = pltpu.get_barrier_semaphore()
    for i in range(1, n):
        pl.semaphore_signal(
            bar, inc=1, device_id={"fsdp": lax.rem(me + i, n)}, device_id_type=MESH
        )
    pl.semaphore_wait(bar, n - 1)
    tokens = (a_ref if to_tokens else o_ref).shape[0] // n
    width = (o_ref if to_tokens else a_ref).shape[1] // n

    def token_block(ref, owner):
        return ref.at[pl.ds(pl.multiple_of(owner * tokens, 16), tokens)]

    def head_block(ref, owner):
        return ref.at[:, pl.ds(pl.multiple_of(owner * width, 128), width)]

    take, put = (token_block, head_block) if to_tokens else (head_block, token_block)
    local = pltpu.make_async_copy(take(a_ref, me), put(o_ref, me), ls)
    local.start()
    copies = []
    for i in range(1, n):
        to = lax.rem(me + i, n)
        copy = pltpu.make_async_remote_copy(
            src_ref=take(a_ref, to), dst_ref=put(o_ref, me), send_sem=ss.at[i], recv_sem=rs.at[i],
            device_id={"fsdp": to}, device_id_type=MESH,
        )
        copy.start()
        copies.append(copy)
    for i in range(1, n):
        copies[i - 1].wait_send()
        ref = put(o_ref, lax.rem(me - i + n, n))
        pltpu.make_async_remote_copy(
            src_ref=ref, dst_ref=ref, send_sem=ss.at[i], recv_sem=rs.at[i],
            device_id={"fsdp": lax.rem(me + i, n)}, device_id_type=MESH,
        ).wait_recv()
    local.wait()


def swap(array, n, to_tokens, collective):
    rows, columns = array.shape
    shape = (rows // n, columns * n) if to_tokens else (rows * n, columns // n)
    return pl.pallas_call(
        functools.partial(swap_kernel, n, to_tokens),
        out_shape=jax.ShapeDtypeStruct(shape, bf),
        in_specs=[VM],
        out_specs=VM,
        scratch_shapes=[DMA((n,)), DMA((n,)), DMA],
        compiler_params=params_for(collective, 32),
    )(array)


def partner(values):
    width = values.shape[-1]
    lane = lax.broadcasted_iota(jnp.int32, values.shape, values.ndim - 1)
    after = pltpu.roll(values, width - 32, values.ndim - 1)
    before = pltpu.roll(values, 32, values.ndim - 1)
    return jnp.where(lane % 64 < 32, after, before)


def normed_rows(rows, n_ref):
    rows = rows.astype(f32)
    center = rows - jnp.mean(rows, axis=-1, keepdims=True)
    inverse = lax.rsqrt(jnp.mean(center * center, axis=-1, keepdims=True) + EPSILON)
    return (center * inverse * n_ref[0:1, :] + n_ref[1:2, :]).astype(bf)


def project_rows(normed, w_ref, cosine, sine):
    mixed = [jnp.dot(normed, w_ref[j], preferred_element_type=f32) for j in range(3)]
    for j in range(2):
        parts = [mixed[j][:, at : at + 128] for at in range(0, mixed[j].shape[1], 128)]
        parts = [part * cosine + partner(part) * sine for part in parts]
        mixed[j] = jnp.concatenate(parts, axis=1)
    return [part.astype(bf) for part in mixed]


def qkv_kernel(h_ref, n_ref, w_ref, c_ref, s_ref, *out_refs):
    normed = normed_rows(h_ref[...], n_ref)
    out_refs[0][...] = normed
    for ref, part in zip(out_refs[1:], project_rows(normed, w_ref, c_ref[...], s_ref[...])):
        ref[...] = part


def project(hidden, norm_rows, w_qkv, cosine, sine):
    tokens, width = hidden.shape[0], w_qkv.shape[2]
    block = 256
    rows = lambda w: pl.BlockSpec((block, w), lambda i: (i, 0))
    full = lambda a: pl.BlockSpec(a.shape, lambda i: (0,) * a.ndim)
    shape = jax.ShapeDtypeStruct
    return pl.pallas_call(
        qkv_kernel,
        grid=(tokens // block,),
        in_specs=[rows(D), full(norm_rows), full(w_qkv), rows(128), rows(128)],
        out_specs=[rows(D), rows(width), rows(width), rows(width)],
        out_shape=[shape((tokens, D), bf)] + [shape((tokens, width), bf)] * 3,
        compiler_params=params_for(),
    )(hidden, norm_rows, w_qkv, cosine, sine)


NT = (((1,), (1,)), ((), ()))
TN = (((0,), (0,)), ((), ()))
BLOCK = 512


def one_head(pair, h):
    lane = lax.broadcasted_iota(jnp.int32, pair.shape, 1)
    return jnp.where((lane < 64) if h == 0 else (lane >= 64), pair, jnp.zeros_like(pair))


def causal(scores, i, j):
    key = j * scores.shape[0] + lax.broadcasted_iota(jnp.int32, scores.shape, 0)
    query = i * scores.shape[1] + lax.broadcasted_iota(jnp.int32, scores.shape, 1)
    return jnp.where(key <= query, scores, MASKED)


def attend_rows(i, queries, k_ref, v_ref):
    heads = [one_head(queries, h) for h in range(2)]

    def block(j, carry, masked):
        at = pl.ds(pl.multiple_of(j * BLOCK, BLOCK), BLOCK)
        keys, values = k_ref[at, :], v_ref[at, :]
        out = []
        for h in range(2):
            peak, total, summed = carry[3 * h : 3 * h + 3]
            scores = lax.dot_general(keys, heads[h], NT, preferred_element_type=f32)
            scores = scores * (SCALE * LOG2E)
            if masked:
                scores = causal(scores, i, j)
            new_peak = jnp.maximum(peak, jnp.max(scores, axis=0, keepdims=True))
            weights = jnp.exp2(scores - new_peak)
            shrink = jnp.exp2(peak - new_peak)
            total = total * shrink + jnp.sum(weights, axis=0, keepdims=True)
            part = lax.dot_general(
                values[:, 64 * h : 64 * h + 64], weights.astype(bf), TN, preferred_element_type=f32
            )
            out += [new_peak, total, summed * shrink + part]
        return tuple(out)

    start = (
        jnp.full((1, BLOCK), MASKED, f32), jnp.zeros((1, BLOCK), f32), jnp.zeros((64, BLOCK), f32)
    ) * 2
    carry = lax.fori_loop(0, i, lambda j, carry: block(j, carry, False), start)
    peak0, total0, sum0, peak1, total1, sum1 = block(i, carry, True)
    out = jnp.concatenate([sum0 / total0, sum1 / total1], axis=0).T
    logs = jnp.concatenate([peak0 + jnp.log2(total0), peak1 + jnp.log2(total1)], axis=0)
    return out, logs


def attend_kernel(q_ref, k_ref, v_ref, o_ref, low_ref, l_ref):
    out, logs = attend_rows(pl.program_id(1), q_ref[...], k_ref, v_ref)
    o_ref[...] = out
    low_ref[...] = out.astype(bf)
    l_ref[...] = logs.reshape(1, 2, BLOCK)


def attend(queries, keys, values):
    tokens, width = queries.shape
    pairs = width // 128
    block = pl.BlockSpec((BLOCK, 128), lambda p, i: (i, p))
    full = pl.BlockSpec((tokens, 128), lambda p, i: (0, p))
    logs = pl.BlockSpec((1, 2, BLOCK), lambda p, i: (p, 0, i))
    shape = jax.ShapeDtypeStruct
    return pl.pallas_call(
        attend_kernel,
        grid=(pairs, tokens // BLOCK),
        in_specs=[block, full, full],
        out_specs=[block, block, logs],
        out_shape=[
            shape((tokens, width), f32), shape((tokens, width), bf), shape((pairs, 2, tokens), f32)
        ],
        compiler_params=params_for(),
    )(queries, keys, values)


def attend_back_rows(i, queries, grads, attended, logs, k_ref, v_ref, dk, dv):
    heads = [one_head(queries, h) for h in range(2)]
    grad_heads = [one_head(grads, h) for h in range(2)]
    both_heads = jnp.concatenate(heads, axis=0)
    both_grads = jnp.concatenate(grad_heads, axis=0)
    products = (attended * grads.astype(f32)).T
    dots = [jnp.sum(products[64 * h : 64 * h + 64], axis=0, keepdims=True) for h in range(2)]

    def block(j, sums, masked):
        at = pl.ds(pl.multiple_of(j * BLOCK, BLOCK), BLOCK)
        keys, values = k_ref[at, :], v_ref[at, :]
        weights, score_grads = [], []
        for h in range(2):
            scores = lax.dot_general(keys, heads[h], NT, preferred_element_type=f32)
            scores = scores * (SCALE * LOG2E)
            if masked:
                scores = causal(scores, i, j)
            prob = jnp.exp2(scores - logs[h : h + 1])
            prob_grad = lax.dot_general(values, grad_heads[h], NT, preferred_element_type=f32)
            score_grads.append((prob * (prob_grad - dots[h])).astype(bf))
            weights.append(prob.astype(bf))
        dv[at, :] += jnp.dot(
            jnp.concatenate(weights, axis=1), both_grads, preferred_element_type=f32
        )
        dk[at, :] += jnp.dot(
            jnp.concatenate(score_grads, axis=1), both_heads, preferred_element_type=f32
        )
        return tuple(
            sums[h] + lax.dot_general(score_grads[h], keys, TN, preferred_element_type=f32)
            for h in range(2)
        )

    zero = jnp.zeros((BLOCK, 128), f32)
    sums = lax.fori_loop(0, i, lambda j, sums: block(j, sums, False), (zero, zero))
    sums = block(i, sums, True)
    lane = lax.broadcasted_iota(jnp.int32, zero.shape, 1)
    return jnp.where(lane < 64, sums[0], sums[1]) * SCALE


def turn_back(grads, cosine, sine):
    return (grads * cosine - partner(grads) * sine).astype(bf)


def finish_keys(dk, dv, c_ref, s_ref, dk_ref, dv_ref):
    def turn(t, _):
        at = pl.ds(pl.multiple_of(t * 256, 256), 256)
        dk_ref[at, :] = turn_back(dk[at, :] * SCALE, c_ref[at, :], s_ref[at, :])
        dv_ref[at, :] = dv[at, :].astype(bf)
        return 0

    lax.fori_loop(0, dk.shape[0] // 256, turn, 0)


def attend_back_kernel(
    q_ref, k_ref, v_ref, g_ref, a_ref, l_ref, cq_ref, sq_ref, c_ref, s_ref,
    dq_ref, dk_ref, dv_ref, dk, dv,
):
    i = pl.program_id(1)

    @pl.when(i == 0)
    def _():
        dk[...] = jnp.zeros_like(dk)
        dv[...] = jnp.zeros_like(dv)

    query_grad = attend_back_rows(
        i, q_ref[...], g_ref[...], a_ref[...], l_ref[0], k_ref, v_ref, dk, dv
    )
    dq_ref[...] = turn_back(query_grad, cq_ref[...], sq_ref[...])

    @pl.when(i == pl.num_programs(1) - 1)
    def _():
        finish_keys(dk, dv, c_ref, s_ref, dk_ref, dv_ref)


def attend_back(queries, keys, values, grads, attended, logs, cosine, sine):
    tokens, width = queries.shape
    block = pl.BlockSpec((BLOCK, 128), lambda p, i: (i, p))
    full = pl.BlockSpec((tokens, 128), lambda p, i: (0, p))
    table_block = pl.BlockSpec((BLOCK, 128), lambda p, i: (i, 0))
    table = pl.BlockSpec((tokens, 128), lambda p, i: (0, 0))
    log_block = pl.BlockSpec((1, 2, BLOCK), lambda p, i: (p, 0, i))
    return pl.pallas_call(
        attend_back_kernel,
        grid=(width // 128, tokens // BLOCK),
        in_specs=[block, full, full, block, block, log_block, table_block, table_block, table, table],
        out_specs=[block, full, full],
        out_shape=[jax.ShapeDtypeStruct((tokens, width), bf)] * 3,
        scratch_shapes=[pltpu.VMEM((tokens, 128), f32), pltpu.VMEM((tokens, 128), f32)],
        compiler_params=params_for(),
    )(queries, keys, values, grads, attended, logs, cosine, sine, cosine, sine)


def swap_copies(take, put, ss, rs, base):
    z, x, y, c = coords()
    others = [(y, 1 - c), (1 - y, c), (1 - y, 1 - c)]
    me = y * 2 + c
    starts, arrivals = [], []
    for i, (yy, cc) in enumerate(others):
        starts.append(
            remote(take(yy * 2 + cc), put(me), ss.at[base + i], rs.at[base + i], dev(z, x, yy, cc))
        )
        ref = put(yy * 2 + cc)
        arrivals.append(remote(ref, ref, ss.at[base + i], rs.at[base + i], dev(z, x, yy, cc)))
    return me, starts, arrivals


def forward_kernel(
    p_ref, h_ref, pos_ref,
    g_ref, col_ref, hid_out, wq_out, nrm_ref, cos_out, sin_out,
    normed_out, q_out, k_out, v_out, o_out, l_ref, t_ref,
    ext, tail, units, can_ref, posall_ref, low,
    hid_ref, wq_ref, cos_ref, sin_ref, normed_ref, q_ref, k_ref, v_ref, o_ref,
    us, ur, hs, hr, ns, nr, ps, pr, keep_sem, ss, rs, ls, ts, tr, cs, cr, outs,
):
    keeps = [
        pltpu.make_async_copy(src, dst, outs.at[i])
        for i, (src, dst) in enumerate(
            [
                (hid_ref, hid_out), (wq_ref, wq_out), (cos_ref, cos_out), (sin_ref, sin_out),
                (normed_ref, normed_out), (q_ref, q_out), (k_ref, k_out), (v_ref, v_out),
                (o_ref, o_out),
            ]
        )
    ]
    z, x, y, c = coords()
    xn, yn, cn = 1 - x, 1 - y, 1 - c
    s = (z * 2 + x) * 4 + y * 2 + c
    f = y * 2 + c
    nxt, prv = lax.rem(s + 1, 32), lax.rem(s + 31, 32)
    core = dev(z, x, y, cn)
    xs, xo, ys, yo = dev(z, xn, y, c), dev(z, xn, y, cn), dev(z, x, yn, c), dev(z, x, yn, cn)
    bar = pltpu.get_barrier_semaphore()
    greet(bar, linear(nxt))
    greet(bar, linear(prv))

    @pl.when(s != 31)
    def _():
        greet(bar, (7, 3))

    ext[64 : 64 + NATURAL, :] = p_ref[...].astype(f32)
    tail[...] = ext[NATURAL : NATURAL + 64, :]
    more = 2 + jnp.where(s == 31, 31, 0)
    meet_neighbours(z, x, y, c, [core, xs, xo, ys, yo], more)
    halves, half = 4, 128

    def hidden_rows(owner, k):
        return hid_ref.at[pl.ds(pl.multiple_of(owner * 512 + k * half, 16), half)]

    def hidden_own(k):
        return h_ref.at[pl.ds(k * half, half)]

    over_y, over_core, over_both = yn * 2 + c, y * 2 + cn, yn * 2 + cn
    halo = remote(tail, ext.at[0:64], ns.at[0], nr.at[0], linear(nxt))
    halo.start()
    sent = []
    for i, to in enumerate([core, ys, yo]):
        sent.append(remote(pos_ref, posall_ref.at[f], ps.at[i], pr.at[i], to))
    for k in range(halves):
        sent.append(remote(hidden_own(k), hidden_rows(f, k), hs.at[1, k], hr.at[1, k], core))
    for copy in sent:
        copy.start()
    rows_over_y = [
        remote(hidden_own(k), hidden_rows(f, k), hs.at[0, k], hr.at[0, k], ys) for k in range(halves)
    ]
    sent += rows_over_y
    for k in range(halves):

        @pl.when(k <= z)
        def _():
            rows_over_y[k].start()

    hid_ref[pl.ds(pl.multiple_of(f * 512, 512), 512)] = h_ref[...]
    posall_ref[pl.ds(f, 1)] = pos_ref[...].reshape(1, 8, 128)
    halo.wait()
    base = 64 - 2 * s

    def lines(first, count, apart, k):
        return ext[pl.ds(base + 8 * first + k, count, stride=8 * apart), :].astype(bf)

    def order(to, first, count, apart):
        for j in range(apart):
            for k in range(8):
                can_ref[to + j * count : to + (j + 1) * count, 128 * k : 128 * k + 128] = lines(
                    first + j, count, apart, k
                )

    @pl.when(z == 0)
    def _():
        for j in range(3):
            for k in range(8):
                at = 128 * (k % 2)
                units[k // 2, j, :, at : at + 128] = lines(j, 128, 3, k)

    @pl.when((s == 8) | (s == 9) | (s >= 22))
    def _():
        order(0, 0, 384, 1)

    @pl.when(s == 10)
    def _():
        order(0, 0, 256, 1)
        order(256, 256, 32, 4)

    @pl.when((s >= 11) & (s <= 20))
    def _():
        order(0, 0, 96, 4)

    @pl.when(s == 21)
    def _():
        order(0, 0, 32, 4)
        order(128, 128, 256, 1)

    def norm_send(i):
        return remote(nrm_ref, nrm_ref, ns.at[1 + i], nr.at[1], linear(i))

    @pl.when(s == 31)
    def _():
        for k in range(8):
            nrm_ref[:, 128 * k : 128 * k + 128] = ext[pl.ds(base + 8 * 384 + k, 8, stride=8), :]

        def go(i, _):
            norm_send(i).start()
            return 0

        lax.fori_loop(0, 31, go, 0)

    def column(k):
        return col_ref.at[pl.ds(pl.multiple_of(k * CHUNK, CHUNK), CHUNK)]

    def down(k):
        return remote(column(k), column(k), cs.at[k], cr.at[k], dev(z - 1, x, y, c))

    keep = pltpu.make_async_copy(can_ref, col_ref, keep_sem)

    @pl.when(z == 3)
    def _():
        keep.start()
        keep.wait()

    def down_step(k):
        @pl.when(z < 3)
        def _():
            down(k).wait_recv()

        @pl.when(z > 0)
        def _():
            down(k).start()

    def arrive(ref, sem):
        remote(ref, ref, us.at[0, 0, 0], sem, core).wait_recv()

    for i, owner in enumerate([over_core, over_y, over_both]):
        arrive(posall_ref.at[owner], pr.at[i])

    def tables():
        lane = lax.broadcasted_iota(jnp.int32, (1, 128), 1) % 64
        turn = (lane % 32).astype(f32) * (-2.0 * math.log(10000.0) / HEAD_DIM)
        frequency = jnp.exp(turn)

        def one(t, _):
            row = posall_ref[t // 4, pl.ds(lax.rem(t, 4), 1), :]
            angles = jnp.broadcast_to(row, (128, 128)).T * frequency
            at = pl.ds(pl.multiple_of(t * 128, 128), 128)
            cos_ref[at, :] = jnp.cos(angles)
            sine = jnp.sin(angles)
            sin_ref[at, :] = jnp.where(lane < 32, -sine, sine)
            return 0

        lax.fori_loop(0, 16, one, 0)

    @pl.when(z >= 2)
    def _():
        tables()

    first = jnp.where(z >= 2, 2, 1)
    start, early, late_up, pump, steps, finish = gather_steps(
        functools.partial(shard_rows, g_ref, 8),
        lambda r: jnp.where(r == 0, first, 3 - first), 2,
        lambda zz: (zz == 1) | (zz == 2),
        lambda k: can_ref.at[k * CHUNK : k * CHUNK + CHUNK],
        True, FORWARD_X, ss, rs, ls,
    )
    start()

    @pl.when(z >= 1)
    def _():
        for i in range(EARLY):
            early(i)

    slots = [yn * 2 + c, yn * 2 + cn, y * 2 + cn, y * 2 + c]

    def target(xx, yy, cc, h):
        at = pl.multiple_of((xx * 4 + yy * 2 + cc) * 128 + 64 * h, 64)
        return wq_ref.at[:, pl.ds(at, 64)]

    def piece(q, h):
        return units.at[slots[q], :, 64 * h : 64 * h + 64]

    def up(q, h):
        return remote(piece(q, h), piece(q, h), us.at[0, q, h], ur.at[0, q, h], dev(z + 1, x, y, c))

    for q in range(4):
        for h in range(2):
            unit, mine = piece(q, h), target(x, y, c, h)

            @pl.when(z > 0)
            def _():
                arrive(unit, ur.at[0, q, h])

            @pl.when(z < 3)
            def _():
                up(q, h).start()

            if q == 0:
                out = [remote(unit, mine, us.at[1, 0, h], ur.at[1, 0, h], ys)]
            elif q == 1:
                out = [remote(unit, mine, us.at[1, 1, h], ur.at[1, 1, h], yo)]
            elif q == 2:
                out = [
                    remote(unit, mine, us.at[1, 2, h], ur.at[1, 2, h], xo),
                    remote(unit, mine, us.at[1, 3, h], ur.at[1, 3, h], core),
                ]
            else:
                out = [remote(unit, mine, us.at[2, 0, h], ur.at[2, 0, h], xs)]
                mine[...] = unit[...]
            for copy in out:
                copy.start()
            sent += out
    for k in range(halves):

        @pl.when(k > z)
        def _():
            rows_over_y[k].start()

    @pl.when(z == 3)
    def _():
        for k in range(CHUNKS):
            down_step(k)

    late_up()

    @pl.when(z == 0)
    def _():
        for i in range(EARLY):
            early(i)

    for h in range(2):
        for i, cc in enumerate((c, cn)):
            ref = target(x, yn, cc, h)
            arrive(ref, ur.at[1, i, h])
            copy = remote(ref, ref, us.at[2, 1 + i, h], ur.at[2, 1 + i, h], xs)
            copy.start()
            sent.append(copy)
    pump(0, 0)

    @pl.when(z < 2)
    def _():
        tables()

    @pl.when(s != 31)
    def _():
        arrive(nrm_ref, nr.at[1])

    def normalise(owner):
        def one(k, _):
            at = pl.ds(pl.multiple_of(owner * 512 + k * 256, 256), 256)
            normed_ref[at, :] = normed_rows(hid_ref[at, :], nrm_ref)
            return 0

        lax.fori_loop(0, 2, one, 0)

    normalise(f)
    for k in range(halves):
        arrive(hidden_rows(over_core, k), hr.at[1, k])
    normalise(over_core)
    for k in range(halves):
        ref = hidden_rows(over_y, k)
        arrive(ref, hr.at[0, k])
        copy = remote(ref, ref, hs.at[2, k], hr.at[2, k], core)
        copy.start()
        sent.append(copy)
    normalise(over_y)
    for k in range(halves):
        arrive(hidden_rows(over_both, k), hr.at[2, k])
    normalise(over_both)
    for h in range(2):
        arrive(target(xn, y, cn, h), ur.at[1, 2, h])
        arrive(target(x, y, cn, h), ur.at[1, 3, h])
        arrive(target(xn, y, c, h), ur.at[2, 0, h])
        arrive(target(xn, yn, c, h), ur.at[2, 1, h])
        arrive(target(xn, yn, cn, h), ur.at[2, 2, h])
    pump(1, 0)

    def project_step(t, _):
        at = pl.ds(pl.multiple_of(t * 256, 256), 256)
        parts = project_rows(normed_ref[at, :], wq_ref, cos_ref[at, :], sin_ref[at, :])
        for ref, part in zip((q_ref, k_ref, v_ref), parts):
            ref[at, :] = part

        @pl.when(lax.rem(t, 4) == 3)
        def _():
            pump(2 + t // 4, 0)

        return 0

    lax.fori_loop(0, 8, project_step, 0)
    for copy in keeps[:8]:
        copy.start()

    def take(p, owner):
        rows = pl.ds(pl.multiple_of(owner * 512, 512), 512)
        return low.at[rows, 128 * p : 128 * p + 128]

    def put(p, owner):
        return t_ref.at[:, pl.ds(pl.multiple_of(owner * 256 + 128 * p, 128), 128)]

    swaps = [
        swap_copies(functools.partial(take, p), functools.partial(put, p), ts, tr, 3 * p)
        for p in range(2)
    ]
    own_blocks = [
        pltpu.make_async_copy(take(p, f), put(p, f), outs.at[9 + p]) for p in range(2)
    ]

    def swap_start(p):
        for copy in swaps[p][1] + [own_blocks[p]]:
            copy.start()

    def attend_step(t, _):
        p = t // 4
        i = t - 4 * p
        at = pl.ds(pl.multiple_of(i * BLOCK, BLOCK), BLOCK)
        lanes = pl.ds(pl.multiple_of(p * 128, 128), 128)
        out, logs = attend_rows(i, q_ref[at, lanes], k_ref.at[:, lanes], v_ref.at[:, lanes])
        o_ref[at, lanes] = out
        low[at, lanes] = out.astype(bf)
        l_ref[p, :, at] = logs

        @pl.when(t == 3)
        def _():
            swap_start(0)

        @pl.when(i >= 2)
        def _():
            pump(2 + i + 2 * p, 0)

        k = t - 2 * (3 - z)

        @pl.when((z > 0) & (z < 3) & (k >= 0) & (k < CHUNKS))
        def _():
            down_step(k)

        return 0

    lax.fori_loop(0, 8, attend_step, 0)

    swap_start(1)
    keeps[8].start()
    lax.fori_loop(8, steps, pump, 0)

    @pl.when(z == 0)
    def _():
        for k in range(CHUNKS):
            down_step(k)

    for _, starts, arrivals in swaps:
        for copy in arrivals:
            copy.wait_recv()
        for copy in starts:
            copy.wait_send()
    for copy in sent:
        copy.wait_send()
    for copy in keeps + own_blocks:
        copy.wait()

    @pl.when(z < 3)
    def _():
        for q in range(4):
            for h in range(2):
                up(q, h).wait_send()

    @pl.when(s == 31)
    def _():
        def go(i, _):
            norm_send(i).wait_send()
            return 0

        lax.fori_loop(0, 31, go, 0)

    @pl.when(z > 0)
    def _():
        for k in range(CHUNKS):
            down(k).wait_send()

    finish()


FORWARD_X = 80


def forward(share, hidden, places):
    shape = jax.ShapeDtypeStruct
    return pl.pallas_call(
        forward_kernel,
        out_shape=(
            shape((16 * SHARD, D), bf), shape((SHARD, D), bf),
            shape((2048, D), bf), shape((3, D, 256), bf), shape((8, D), f32),
            shape((2048, 128), f32), shape((2048, 128), f32), shape((2048, D), bf),
            shape((2048, 256), bf), shape((2048, 256), bf), shape((2048, 256), bf),
            shape((2048, 256), f32), shape((2, 2, 2048), f32), shape((512, D), bf),
        ),
        in_specs=[VM] * 3,
        out_specs=(ANY,) * 4 + (VM,) + (ANY,) * 7 + (VM, ANY),
        scratch_shapes=[
            pltpu.VMEM((64 + NATURAL + 6, 128), f32),
            pltpu.VMEM((64, 128), f32),
            pltpu.VMEM((4, 3, 128, 256), bf),
            pltpu.VMEM((SHARD, D), bf),
            pltpu.VMEM((4, 8, 128), f32),
            pltpu.VMEM((2048, 256), bf),
            pltpu.VMEM((2048, D), bf),
            pltpu.VMEM((3, D, 256), bf),
            pltpu.VMEM((2048, 128), f32),
            pltpu.VMEM((2048, 128), f32),
            pltpu.VMEM((2048, D), bf),
            pltpu.VMEM((2048, 256), bf),
            pltpu.VMEM((2048, 256), bf),
            pltpu.VMEM((2048, 256), bf),
            pltpu.VMEM((2048, 256), f32),
            DMA((3, 4, 2)), DMA((3, 4, 2)), DMA((3, 4)), DMA((3, 4)),
            DMA((32,)), DMA((2,)), DMA((3,)), DMA((3,)), DMA,
            *gather_sems(2), DMA((6,)), DMA((6,)), DMA((CHUNKS,)), DMA((CHUNKS,)), DMA((11,)),
        ],
        compiler_params=params_for(0, 62),
    )(share, hidden, places)


def backward_kernel(
    gw_ref, part_ref, g_hbm, q_hbm, k_hbm, v_hbm, a_hbm, l_ref, cos_hbm, sin_hbm,
    normed_hbm, hid_hbm, wq_hbm, rg_hbm, nrm_ref, nsum_ref, st_ref,
    out_ref, ig_ref, sto_ref,
    grads, dk, dv, q_ref, k_ref, v_ref, a_ref, cos_ref, sin_ref, normed, hid, wq,
    own_ref, vg, nsum,
    ext, hal, hsend, av, bv, cv, acv, zv, sums, sv, nc, ny, nland, sland, land,
    lsem, hsems, rgs, cs, cr, s1, r1, s2, r2, zs, zr, ms, mr, qs, qr, hsem, *rooms,
):
    z, x, y, c = coords()
    xn, yn, cn = 1 - x, 1 - y, 1 - c
    s = (z * 2 + x) * 4 + y * 2 + c
    me = y * 2 + c
    core = dev(z, x, y, cn)
    xs, xo, ys, yo = dev(z, xn, y, c), dev(z, xn, y, cn), dev(z, x, yn, c), dev(z, x, yn, cn)
    prv = lax.rem(s + 31, 32)

    loads = [
        pltpu.make_async_copy(src, dst, lsem.at[i])
        for i, (src, dst) in enumerate(
            [
                (g_hbm, grads), (q_hbm, q_ref), (k_hbm, k_ref), (v_hbm, v_ref),
                (a_hbm, a_ref), (cos_hbm, cos_ref), (sin_hbm, sin_ref),
                (normed_hbm, normed), (wq_hbm, wq),
            ]
        )
    ]
    for copy in loads:
        copy.start()

    bar = pltpu.get_barrier_semaphore()

    def hello(i, _):
        greet(bar, linear(lax.rem(s + i, 32)))
        return 0

    lax.fori_loop(1, 32, hello, 0)
    pl.semaphore_wait(bar, 31)

    def owned(k):
        return own_ref.at[pl.ds(pl.multiple_of(k * CHUNK, CHUNK), CHUNK)]

    start, pump, steps, finish = reduce_steps(
        functools.partial(shard_rows, gw_ref, 8), (2, 1), True, BACKWARD_X, owned, *rooms
    )
    start()

    def tell(i):
        return remote(st_ref, sland.at[s], qs.at[i], qr.at[s], linear(lax.rem(s + i, 32)))

    def tell_all(i, _):
        tell(i).start()
        return 0

    lax.fori_loop(1, 32, tell_all, 0)

    def up(k):
        return remote(land.at[k], land.at[k], cs.at[k], cr.at[k], dev(z + 1, x, y, c))

    def part(k):
        return part_ref.at[pl.ds(pl.multiple_of(k * CHUNK, CHUNK), CHUNK)]

    def up_step(k):
        @pl.when(z > 0)
        def _():
            up(k).wait_recv()

        @pl.when(z == 0)
        def _():
            add_tiles(land.at[k], CHUNK, part(k))

        @pl.when((z > 0) & (z < 3))
        def _():
            add_tiles(land.at[k], CHUNK, part(k), land.at[k])

        @pl.when(z < 3)
        def _():
            up(k).start()

        @pl.when(z == 3)
        def _():
            add_tiles(owned(k), CHUNK, part(k), land.at[k])

    pump(0, 0)
    pump(1, 0)
    for copy in loads[:7]:
        copy.wait()

    d_refs = (q_ref, k_ref, v_ref)

    def block_grad(p, xx, yy):
        at = pl.ds(pl.multiple_of((xx * 2 + yy) * 256, 256), 256)
        lanes = slice(128 * p, 128 * p + 128)
        for j in range(3):
            vg[j, at, lanes] = lax.dot_general(
                normed[:, at], d_refs[j][:, lanes], TN, preferred_element_type=f32
            ).astype(bf)

    def unit(p, xx, yy, cc):
        at = pl.multiple_of((xx * 4 + yy * 2 + cc) * 128, 128)
        return vg.at[:, pl.ds(at, 128), 128 * p : 128 * p + 128]

    def half_of(ref, p):
        return ref.at[:, :, 128 * p : 128 * p + 128]

    def opposite(p):
        return [
            remote(unit(p, xn, yn, cc), half_of(av.at[i], p), s1.at[p, i], r1.at[p, i], xs)
            for i, cc in enumerate((c, cn))
        ]

    def beside(p):
        return [
            remote(unit(p, xn, y, c), half_of(bv.at[0], p), s1.at[p, 2], r1.at[p, 2], xs),
            remote(unit(p, xn, y, cn), half_of(bv.at[1], p), s1.at[p, 3], r1.at[p, 3], xo),
        ]

    def sibling(p):
        return remote(unit(p, x, y, cn), half_of(cv, p), s1.at[p, 4], r1.at[p, 4], core)

    def across(p):
        return [
            remote(
                half_of(sv.at[i], p), half_of(acv.at[i], p), s1.at[p, 5 + i], r1.at[p, 5 + i], to
            )
            for i, to in enumerate((ys, yo))
        ]

    def weight_start(p):
        block_grad(p, xn, yn)
        for copy in opposite(p):
            copy.start()
        block_grad(p, xn, y)
        for copy in beside(p):
            copy.start()
        block_grad(p, x, yn)
        block_grad(p, x, y)
        sibling(p).start()

    def weight_across(p):
        for i, cc in enumerate((c, cn)):
            opposite(p)[i].wait_recv()
            mine, came, dst = unit(p, x, yn, cc), half_of(av.at[i], p), half_of(sv.at[i], p)
            for j in range(3):
                add_rows(dst.at[j], mine.at[j], came.at[j])
            across(p)[i].start()

    blocks = [y * 2 + c, y * 2 + cn, yn * 2 + c, yn * 2 + cn]

    def down(p, q):
        return remote(
            half_of(sums.at[q], p), half_of(zv.at[q], p), zs.at[p, q], zr.at[p, q],
            dev(z - 1, x, y, c),
        )

    def weight_chain(p):
        for q in range(4):
            if q == 0:
                beside(p)[0].wait_recv()
                parts = [unit(p, x, y, c), half_of(bv.at[0], p)]
            elif q == 1:
                sibling(p).wait_recv()
                beside(p)[1].wait_recv()
                parts = [half_of(cv, p), half_of(bv.at[1], p)]
            else:
                across(p)[q - 2].wait_recv()
                parts = [half_of(acv.at[q - 2], p)]
            total_ref, came = half_of(sums.at[q], p), half_of(zv.at[q], p)

            @pl.when(z < 3)
            def _():
                down(p, q).wait_recv()

            @pl.when(z == 3)
            def _():
                for j in range(3):
                    add_rows(total_ref.at[j], *[part.at[j] for part in parts])
                down(p, q).start()

            @pl.when((z == 1) | (z == 2))
            def _():
                for j in range(3):
                    add_rows(total_ref.at[j], came.at[j], *[part.at[j] for part in parts])
                down(p, q).start()

            @pl.when(z == 0)
            def _():
                for j in range(3):
                    total = came[j].astype(f32)
                    for part in parts:
                        total = total + part[j].astype(f32)
                    at = 64 - 2 * s + 8 * j + 2 * blocks[q] + p
                    ext[pl.ds(at, 128, stride=24), :] = total

    def step(t, _):
        p = t // 4
        i = t - 4 * p
        at = pl.ds(pl.multiple_of(i * BLOCK, BLOCK), BLOCK)
        lanes = pl.ds(pl.multiple_of(p * 128, 128), 128)

        @pl.when(i == 0)
        def _():
            dk[...] = jnp.zeros_like(dk)
            dv[...] = jnp.zeros_like(dv)

        query_grad = attend_back_rows(
            i, q_ref[at, lanes], grads[at, lanes], a_ref[at, lanes], l_ref[p, :, at],
            k_ref.at[:, lanes], v_ref.at[:, lanes], dk, dv,
        )
        q_ref[at, lanes] = turn_back(query_grad, cos_ref[at, :], sin_ref[at, :])

        @pl.when(i == 3)
        def _():
            finish_keys(
                dk, dv, cos_ref, sin_ref, k_ref.at[:, lanes], v_ref.at[:, lanes]
            )

        @pl.when(t == 3)
        def _():
            for copy in loads[7:]:
                copy.wait()
            weight_start(0)

        @pl.when(t == 4)
        def _():
            weight_across(0)

        @pl.when((z > 0) & (t == 8 - z))
        def _():
            weight_chain(0)

        @pl.when(t != 4)
        def _():
            pump(2 + t - t // 5, 0)

        k = t - 2 * z

        @pl.when((z < 3) & (k >= 0) & (k < CHUNKS))
        def _():
            up_step(k)

        return 0

    lax.fori_loop(0, 8, step, 0)
    residual = [
        pltpu.make_async_copy(
            rg_hbm.at[:, 128 * i : 128 * i + 128],
            (dk, dv)[i // 4].at[512 * (i % 4) : 512 * (i % 4) + 512],
            rgs.at[i],
        )
        for i in range(8)
    ]
    for copy in residual:
        copy.start()
    weight_start(1)
    half = 256

    def rows(yy, cc, k):
        return normed.at[pl.ds(pl.multiple_of((yy * 2 + cc) * 512 + k * half, half), half)]

    order = [(yn, cn), (yn, c), (y, cn), (y, c)]

    def row_load(n):
        yy, cc = order[n // 2]
        at = pl.ds(pl.multiple_of((yy * 2 + cc) * 512 + n % 2 * half, half), half)
        return pltpu.make_async_copy(hid_hbm.at[at], hid.at[n % 2], hsems.at[n])

    for n in range(2):
        row_load(n).start()
    nsum[...] = jnp.zeros_like(nsum)
    gain = nrm_ref[0:1, :]

    def row_grad(m):
        yy, cc = order[m]
        for k in range(2):
            n = 2 * m + k
            row_load(n).wait()
            at = pl.ds(pl.multiple_of((yy * 2 + cc) * 512 + k * half, half), half)
            total = lax.dot_general(q_ref[at, :], wq[0], NT, preferred_element_type=f32)
            for j in range(1, 3):
                total = total + lax.dot_general(
                    d_refs[j][at, :], wq[j], NT, preferred_element_type=f32
                )
            normed[at, :] = total.astype(bf)
            unit_rows, _ = unit_of(hid[k].astype(f32))
            nsum[0] += fold(total * unit_rows)
            nsum[1] += fold(total)
            if n < 6:
                row_load(n + 2).start()

    far = [remote(rows(yn, cn, k), nc.at[1, k], s2.at[0, k], r2.at[0, k], core) for k in range(2)]
    near = [remote(rows(y, cn, k), nc.at[0, k], s2.at[1, k], r2.at[1, k], core) for k in range(2)]
    row_grad(0)
    for copy in far:
        copy.start()
    row_grad(1)
    later = []

    def row_across(k):
        far[k].wait_recv()

        def add_far(q, _):
            at = pl.ds(pl.multiple_of(q * 32, 32), 32)
            here = rows(yn, c, k).at[at]
            add_rows(here, here, nc.at[1, k, at])
            return 0

        lax.fori_loop(0, half // 32, add_far, 0)
        copy = remote(rows(yn, c, k), ny.at[k], s2.at[2, k], r2.at[2, k], ys)
        copy.start()
        later.append(copy)

    row_across(0)
    weight_across(1)
    pump(9, 0)
    row_across(1)

    @pl.when(z == 3)
    def _():
        weight_chain(1)

    row_grad(2)
    for copy in near:
        copy.start()
    row_grad(3)
    pump(10, 0)

    @pl.when(z == 0)
    def _():
        weight_chain(0)

    @pl.when(z < 3)
    def _():
        weight_chain(1)

    nsum_ref_rows = jnp.sum(nsum[...], axis=1)
    hsum = nland.at[s]
    hsum[0:2, :] = nsum_ref_rows
    hsum[2:8, :] = nsum_ref[2:8, :]
    norm_send = remote(hsum, hsum, ms.at[0], mr.at[s], (7, 3))

    @pl.when(s != 31)
    def _():
        norm_send.start()

    lax.fori_loop(11, steps, pump, 0)

    @pl.when(z == 3)
    def _():
        for k in range(CHUNKS):
            up_step(k)

    base = 64 - 2 * s

    def place(src, first, count, apart):
        for j in range(apart):
            for k in range(8):
                ext[pl.ds(base + 8 * (first + j) + k, count, stride=8 * apart), :] = own_ref[
                    src + j * count : src + (j + 1) * count, 128 * k : 128 * k + 128
                ]

    @pl.when((s == 8) | (s == 9) | (s >= 22))
    def _():
        place(0, 0, 384, 1)

    @pl.when(s == 10)
    def _():
        place(0, 0, 256, 1)
        place(256, 256, 32, 4)

    @pl.when((s >= 11) & (s <= 20))
    def _():
        place(0, 0, 96, 4)

    @pl.when(s == 21)
    def _():
        place(0, 0, 32, 4)
        place(128, 128, 256, 1)

    hsend[...] = ext[0:64, :]
    halo = remote(hsend, hal, hsem.at[0], hsem.at[1], linear(prv))
    halo.start()
    for copy in residual:
        copy.wait()
    for k in range(2):
        near[k].wait_recv()
        later[k].wait_recv()
        at = pl.ds(pl.multiple_of(me * 512 + k * half, half), half)
        to = slice(k * half, k * half + half)
        total = normed[at, :].astype(f32) + nc[0, k].astype(f32) + ny[k].astype(f32)
        unit_rows, inverse = unit_of(hid[k].astype(f32))
        into = into_norm(total, unit_rows, inverse, gain)
        for i in range(8):
            lanes = slice(128 * i, 128 * i + 128)
            first = 512 * (i % 4) + k * half
            ig_ref[to, lanes] = ((dk, dv)[i // 4][first : first + half] + into[:, lanes]).astype(bf)

    def hear(i, _):
        o = lax.rem(s + i, 32)
        remote(st_ref, sland.at[o], qs.at[0], qr.at[o], core).wait_recv()
        return 0

    lax.fori_loop(1, 32, hear, 0)
    sland[pl.ds(s, 1)] = st_ref[...].reshape(1, 8, 128)
    sto_ref[...] = jnp.sum(sland[...], axis=0)
    halo.wait()

    @pl.when(s != 31)
    def _():
        row = lax.broadcasted_iota(jnp.int32, (64, 128), 0)
        end = slice(NATURAL, NATURAL + 64)
        ext[end, :] = jnp.where(row >= 64 - 2 * (s + 1), hal[...], ext[end, :])

    @pl.when(s == 31)
    def _():
        def gather(i, total):
            remote(nland.at[i], nland.at[i], ms.at[0], mr.at[i], core).wait_recv()
            return total + nland[i]

        total = lax.fori_loop(0, 31, gather, nland[31])
        for k in range(8):
            ext[pl.ds(base + 8 * 384 + k, 8, stride=8), :] = total[:, 128 * k : 128 * k + 128]

    out_ref[...] = ext[64 : 64 + NATURAL, :]
    for copy in far + near + later:
        copy.wait_send()
    for p in range(2):
        for copy in opposite(p) + beside(p) + [sibling(p)] + across(p):
            copy.wait_send()

    @pl.when(z > 0)
    def _():
        for p in range(2):
            for q in range(4):
                down(p, q).wait_send()

    @pl.when(z < 3)
    def _():
        for k in range(CHUNKS):
            up(k).wait_send()

    def told(i, _):
        tell(i).wait_send()
        return 0

    lax.fori_loop(1, 32, told, 0)

    @pl.when(s != 31)
    def _():
        norm_send.wait_send()

    finish()


BACKWARD_X = 48


def backward(*operands):
    shape = jax.ShapeDtypeStruct
    room = pltpu.VMEM
    unit = (3, 128, 256)
    return pl.pallas_call(
        backward_kernel,
        out_shape=(shape((NATURAL, 128), f32), shape((512, D), bf), shape((8, 128), f32)),
        in_specs=[ANY, VM] + [ANY] * 5 + [VM] + [ANY] * 6 + [VM] * 3,
        out_specs=(VM,) * 3,
        scratch_shapes=[
            room((2048, 256), bf), room((2048, 128), f32), room((2048, 128), f32),
            room((2048, 256), bf), room((2048, 256), bf), room((2048, 256), bf),
            room((2048, 256), f32), room((2048, 128), f32), room((2048, 128), f32),
            room((2048, D), bf), room((2, 256, D), bf), room((3, D, 256), bf),
            room((SHARD, D), f32), room((3, D, 256), bf), room((2, 8, D), f32),
            room((64 + NATURAL + 6, 128), f32), room((64, 128), f32), room((64, 128), f32),
            room((2,) + unit, bf), room((2,) + unit, bf), room(unit, bf), room((2,) + unit, bf),
            room((4,) + unit, bf), room((4,) + unit, bf), room((2,) + unit, bf),
            room((2, 2, 256, D), bf), room((2, 256, D), bf),
            room((32, 8, D), f32), room((32, 8, 128), f32),
            room((CHUNKS, CHUNK, D), bf),
            DMA((9,)), DMA((8,)), DMA((8,)), DMA((CHUNKS,)), DMA((CHUNKS,)),
            DMA((2, 7)), DMA((2, 7)), DMA((3, 2)), DMA((3, 2)), DMA((2, 4)), DMA((2, 4)),
            DMA((1,)), DMA((32,)), DMA((32,)), DMA((32,)), DMA((2,)),
            *reduce_rooms(2, True, BACKWARD_X),
        ],
        compiler_params=params_for(2, 63),
    )(*operands)


ROWS = 128
GELU_A = math.sqrt(2.0 / math.pi)
GELU_B = 0.044715


def mean_of(values):
    return jnp.mean(values, axis=-1, keepdims=True)


def unit_of(values):
    center = values - mean_of(values)
    inverse = lax.rsqrt(mean_of(center * center) + EPSILON)
    return center * inverse, inverse


def into_norm(grads, unit, inverse, gain):
    scaled = grads * gain
    return inverse * (scaled - mean_of(scaled) - unit * mean_of(scaled * unit))


def fold(values):
    total = values[0:8]
    for at in range(8, values.shape[0], 8):
        total = total + values[at : at + 8]
    return total


def up_pieces(j):
    pieces = [(D + 32 * j, 0, 32)]
    pieces += [(D + 128 + 384 * i + 96 * j, 32 + 96 * i, 96) for i in range(10)]
    pieces.append((D + 3968 + 32 * j, 992, 32))
    return pieces


def dense_kernel(
    lines, a_ref, h_ref, c_ref, scale_ref, n_ref, w_ref, col_ref,
    o_ref, rg_ref, all_ref, gw_ref, ns_ref, sq_ref, part_ref,
    wo, wu, wd, branch, lowered, entered, act, slope, lgrad, stage, sums,
    ws, ups, gs, *rooms,
):
    tokens = a_ref.shape[0]
    residual, egrad = rg_ref, lowered
    start = finish = reduce_start = reduce_finish = lambda: None
    pump = reduce_pump = lambda i, _: 0
    steps = reduce_count = 0
    if lines:
        z, x, y, c = coords()
        ag_ref, ts, tr, own_sem, *rooms = rooms
        sems, rooms = rooms[:3], rooms[3:]

        def source(k):
            return col_ref.at[pl.ds(pl.multiple_of(k * CHUNK, CHUNK), CHUNK)]

        def down_rows(zz, xx, yy, cc, k, low=0, count=CHUNK):
            s = xx * 4 + yy * 2 + cc
            return wd.at[pl.ds(pl.multiple_of(D + s * SHARD + k * CHUNK + low, 16), count)]

        start, _, _, pump, steps, finish = gather_steps(
            down_rows, lambda r: 3, 1, None, source, False, 48, *sems
        )
        reduce_start, reduce_pump, reduce_count, reduce_finish = reduce_steps(
            functools.partial(shard_rows, gw_ref, 8), (3,), False, DENSE_X,
            lambda k: part_ref.at[pl.ds(pl.multiple_of(k * CHUNK, CHUNK), CHUNK)], *rooms
        )
        bar = pltpu.get_barrier_semaphore()
        for device in (dev(z, 1 - x, y, c), dev(z, x, 1 - y, c), dev(z, x, y, 1 - c)):
            greet(bar, device)
        greet(bar, dev(z, x, 1 - y, 1 - c))
        pl.semaphore_wait(bar, 4)
    else:
        ag_ref = all_ref
        part_ref[...] = jnp.zeros_like(part_ref)
    pieces = tokens // ROWS
    load_o = pltpu.make_async_copy(w_ref.at[0:D], wo, ws.at[0])
    loads_d = [
        pltpu.make_async_copy(
            w_ref.at[5 * D + D * j : 6 * D + D * j], wd.at[D * j : D * j + D], ws.at[1 + j]
        )
        for j in range(1 if lines else 4)
    ]
    loads_u = [
        [
            pltpu.make_async_copy(
                w_ref.at[src : src + count], wu.at[j, to : to + count], ups.at[j, i]
            )
            for i, (src, to, count) in enumerate(up_pieces(j))
        ]
        for j in range(4)
    ]
    load_o.start()
    for j in range(4):
        for copy in loads_u[j]:
            copy.start()
    for copy in loads_d:
        copy.start()
    start()
    pump(0, 0)
    pump(1, 0)
    sums[...] = jnp.zeros_like(sums)
    width = 1024

    def columns(t):
        return pl.ds(pl.multiple_of(t * width, width), width)

    def over_columns(body, count=D // width):
        def go(t, _):
            body(columns(t))
            return 0

        lax.fori_loop(0, count, go, 0)

    def over_rows(body):
        def go(t, _):
            body(pl.ds(pl.multiple_of(t * ROWS, ROWS), ROWS))
            return 0

        lax.fori_loop(0, pieces, go, 0)

    load_o.wait()

    def branch_step(at):
        branch[:, at] = jnp.dot(a_ref[...], wo[:, at], preferred_element_type=f32)

    over_columns(branch_step)

    def enter_step(at):
        values = branch[at, :]
        unit, _ = unit_of(values)
        res = h_ref[at, :].astype(f32) + unit * n_ref[2:3, :] + n_ref[3:4, :]
        residual[at, :] = res
        unit, _ = unit_of(res)
        entered[at, :] = (unit * n_ref[4:5, :] + n_ref[5:6, :]).astype(bf)
        sums[0] += fold(values * values)

    over_rows(enter_step)
    pump(2, 0)

    for j in range(4):
        for copy in loads_u[j]:
            copy.wait()

        def lift_step(at):
            lifted = jnp.dot(entered[...], wu[j, :, at], preferred_element_type=f32)
            square = lifted * lifted
            tanh = jnp.tanh(lifted * (GELU_A + (GELU_A * GELU_B) * square))
            half = 0.5 + 0.5 * tanh
            act[j, :, at] = (lifted * half).astype(bf)
            slope[j, :, at] = half + lifted * (0.5 - 0.5 * tanh * tanh) * (
                GELU_A + (3.0 * GELU_A * GELU_B) * square
            )

        over_columns(lift_step)
        pump(3 + j, 0)
    lax.fori_loop(7, steps, pump, 0)
    finish()
    for copy in loads_d:
        copy.wait()

    def lower_step(at):
        total = jnp.dot(act[0], wd[0:D, at], preferred_element_type=f32)
        for j in range(1, 4):
            total = total + jnp.dot(act[j], wd[D * j : D * j + D, at], preferred_element_type=f32)
        lowered[:, at] = total

    over_columns(lower_step)
    scale = scale_ref[0, 0]

    def out_step(at):
        values = lowered[at, :]
        unit, inverse = unit_of(values)
        o_ref[at, :] = (residual[at, :] + unit * n_ref[6:7, :] + n_ref[7:8, :]).astype(bf)
        upstream = c_ref[at, :].astype(f32) * scale
        lgrad[at, :] = into_norm(upstream, unit, inverse, n_ref[6:7, :]).astype(bf)
        sums[1] += fold(values * values)
        sums[2] += fold(upstream * unit)
        sums[3] += fold(upstream)

    over_rows(out_step)

    def store(buffer, j, slot):
        return [
            pltpu.make_async_copy(
                stage.at[buffer, to : to + count], gw_ref.at[src : src + count], gs.at[slot, i]
            )
            for i, (src, to, count) in enumerate(up_pieces(j))
        ]

    def store_block(buffer, first, slot):
        return [pltpu.make_async_copy(stage.at[buffer], gw_ref.at[first : first + D], gs.at[slot, 0])]

    pending = {}

    def reuse(buffer):
        for copy in pending.pop(buffer, []):
            copy.wait()

    def issue(buffer, copies):
        for copy in copies:
            copy.start()
        pending[buffer] = copies

    for n, j in enumerate((1, 2, 3, 0)):
        buffer = n % 2
        reuse(buffer)

        def down_step(at):
            stage[buffer, at, :] = lax.dot_general(
                act[j, :, at], lgrad[...], TN, preferred_element_type=f32
            ).astype(bf)

        over_columns(down_step)
        issue(buffer, store_block(buffer, 5 * D + D * j, buffer))
        if n == 2:
            reuse(1)
            reuse(0)
            reduce_start()
    for j in range(4):

        def slope_step(at):
            grads = lax.dot_general(
                lgrad[...], wd[D * j : D * j + D, :], NT, preferred_element_type=f32
            )
            act[j, :, at] = (grads * slope[j, :, at]).astype(bf)

        over_columns(slope_step)
        if j % 2:
            reduce_pump(j // 2, 0)

    def enter_back_step(at):
        total = lax.dot_general(act[0], wu[0, at, :], NT, preferred_element_type=f32)
        for j in range(1, 4):
            total = total + lax.dot_general(act[j], wu[j, at, :], NT, preferred_element_type=f32)
        egrad[:, at] = total

    over_columns(enter_back_step)
    reduce_pump(2, 0)

    def branch_back_step(at):
        grads = egrad[at, :]
        upstream = c_ref[at, :].astype(f32) * scale
        unit, inverse = unit_of(residual[at, :])
        res_grad = upstream + into_norm(grads, unit, inverse, n_ref[4:5, :])
        rg_ref[at, :] = res_grad
        sums[4] += fold(grads * unit)
        sums[5] += fold(grads)
        unit, inverse = unit_of(branch[at, :])
        lgrad[at, :] = into_norm(res_grad, unit, inverse, n_ref[2:3, :]).astype(bf)
        sums[6] += fold(res_grad * unit)
        sums[7] += fold(res_grad)

    over_rows(branch_back_step)
    reduce_pump(3, 0)

    def attended_step(at):
        ag_ref[:, at] = lax.dot_general(
            lgrad[...], wo[at, :], NT, preferred_element_type=f32
        ).astype(bf)

    over_columns(attended_step)
    if lines:
        me, starts, arrivals = swap_copies(
            lambda owner: ag_ref.at[:, pl.ds(pl.multiple_of(owner * 256, 256), 256)],
            lambda owner: all_ref.at[pl.ds(pl.multiple_of(owner * 512, 512), 512)],
            ts, tr, 0,
        )
        own = pltpu.make_async_copy(
            ag_ref.at[:, pl.ds(pl.multiple_of(me * 256, 256), 256)],
            all_ref.at[pl.ds(pl.multiple_of(me * 512, 512), 512)],
            own_sem,
        )
        for copy in starts + [own]:
            copy.start()
    for j in range(4):
        buffer = j % 2
        reuse(buffer)

        def up_step(at):
            stage[buffer, :, at] = lax.dot_general(
                entered[...], act[j, :, at], TN, preferred_element_type=f32
            ).astype(bf)

        over_columns(up_step)
        issue(buffer, store(buffer, j, buffer))
        if j % 2:
            reduce_pump(4 + j // 2, 0)
    reuse(0)

    def out_grad_step(at):
        stage[0, at, :] = lax.dot_general(
            a_ref[:, at], lgrad[...], TN, preferred_element_type=f32
        ).astype(bf)

    over_columns(out_grad_step)
    issue(0, store_block(0, 0, 0))
    order = [None, None, 6, 7, 4, 5, 2, 3]
    for row, source in enumerate(order):
        if source is None:
            ns_ref[row : row + 1, :] = jnp.zeros((1, D), f32)
        else:
            ns_ref[row : row + 1, :] = jnp.sum(sums[source], axis=0, keepdims=True)
    lane = lax.broadcasted_iota(jnp.int32, (8, 128), 1)
    row = lax.broadcasted_iota(jnp.int32, (8, 128), 0)
    told = jnp.zeros((8, 128), f32)
    for t in range(2):
        told = jnp.where((lane == t) & (row == 0), jnp.sum(sums[t]), told)
    sq_ref[...] = told
    reuse(0)
    reuse(1)
    if lines:
        own.wait()
        for copy in arrivals:
            copy.wait_recv()
        for copy in starts:
            copy.wait_send()
    reduce_finish()


DENSE_X = 80


def dense(lines, attended, hidden, cotangent, scale, norm_rows, weights, column):
    tokens = attended.shape[0]
    shape = jax.ShapeDtypeStruct
    room = pltpu.VMEM
    return pl.pallas_call(
        functools.partial(dense_kernel, lines),
        out_shape=(
            shape((tokens, D), bf), shape((tokens, D), f32),
            shape((2048, 256) if lines else (tokens, D), bf),
            shape((9 * D, D), bf), shape((8, D), f32), shape((8, 128), f32), shape((SHARD, D), bf),
        ),
        in_specs=[VM, VM, VM, pl.BlockSpec(memory_space=pltpu.SMEM), VM, ANY, ANY],
        out_specs=(VM, VM, ANY if lines else VM, ANY, VM, VM, VM),
        scratch_shapes=[
            room((D, D), bf), room((4, D, D), bf), room((4 * D, D), bf),
            room((tokens, D), f32), room((tokens, D), f32),
            room((tokens, D), bf), room((4, tokens, D), bf), room((4, tokens, D), f32),
            room((tokens, D), bf), room((2, D, D), bf),
            room((8, 8, D), f32), DMA((5,)), DMA((4, 12)), DMA((2, 12)),
            *(
                [room((tokens, D), bf), DMA((3,)), DMA((3,)), DMA]
                + gather_sems(1)
                + reduce_rooms(1, False, DENSE_X)
                if lines
                else []
            ),
        ],
        compiler_params=params_for(5 if lines else None, 62),
    )(attended, hidden, cotangent, scale, norm_rows, weights, column)


def norm_forward(values, gain_row, shift_row):
    center = values - jnp.mean(values, axis=-1, keepdims=True)
    spread = jnp.mean(center * center, axis=-1, keepdims=True)
    inverse = lax.rsqrt(spread + EPSILON)
    unit_rows = center * inverse
    return (unit_rows * gain_row + shift_row, unit_rows, inverse)


def norm_backward(grad_rows, unit_rows, inverse, gain_row):
    scaled = grad_rows * gain_row
    first_mean = jnp.mean(scaled, axis=-1, keepdims=True)
    second_mean = jnp.mean(scaled * unit_rows, axis=-1, keepdims=True)
    return inverse * (scaled - first_mean - unit_rows * second_mean)


def norm_sums(grad_rows, unit_rows):
    return jnp.sum(grad_rows * unit_rows, axis=0), jnp.sum(grad_rows, axis=0)


def up_from_shards(rows):
    pieces = [rows[:128].reshape(1, 4, 32, D), rows[128:3968].reshape(10, 4, 96, D)]
    pieces.append(rows[3968:].reshape(1, 4, 32, D))
    return jnp.concatenate(
        [piece.transpose(0, 2, 1, 3).reshape(-1, FF) for piece in pieces], axis=0
    )


def up_to_shards(grad):
    pieces = [(grad[:32], 1, 32), (grad[32:992], 10, 96), (grad[992:], 1, 32)]
    return jnp.concatenate(
        [
            piece.reshape(blocks, rows, 4, D).transpose(0, 2, 1, 3).reshape(-1, D)
            for piece, blocks, rows in pieces
        ],
        axis=0,
    )


def dots(a, b, contract):
    return lax.dot_general(a, b, ((contract[:1], contract[1:]), ((), ())), preferred_element_type=f32)


def per_device(lines, hidden_in, params, cotangent, source_ids, corpus_weight, positions):
    devices = lax.axis_size(("dp", "fsdp"))
    width = lax.axis_size("fsdp")
    hidden = hidden_in[0]
    tokens = hidden.shape[0]
    place = lax.axis_index("fsdp")
    if lines:
        (
            others, column, hidden_all, w_qkv, norm_rows, cosine, sine,
            normed_all, queries, keys, values, attended_all, logs, attended,
        ) = forward(
            params.reshape(NATURAL, 128),
            hidden,
            jnp.pad(positions.astype(f32).reshape(4, 128), ((0, 4), (0, 0))),
        )
    else:
        whole = lax.all_gather(params, ("dp", "fsdp"), axis=0, tiled=True)
        ends = [0, 3 * D * D, 4 * D * D, 4 * D * D + D * FF, 4 * D * D + 2 * D * FF]
        parts = [whole[a:b] for a, b in zip(ends, ends[1:])]
        w_qkv = lax.dynamic_index_in_dim(
            parts[0].reshape(D, 3, width, D // width).transpose(1, 2, 0, 3), place, 1, False
        )
        others = jnp.concatenate(
            [parts[1].reshape(D, D), up_to_shards(parts[2].reshape(D, FF)), parts[3].reshape(FF, D)]
        )
        norm_rows = whole[ends[-1] :].reshape(8, D).astype(f32)
        hidden_all = lax.all_gather(hidden, "fsdp", axis=0, tiled=True)
        places = lax.all_gather(positions[0].astype(f32), "fsdp", axis=0, tiled=True)
        lane = jnp.arange(128) % 64
        frequency = jnp.exp((lane % 32).astype(f32) * (-2.0 * math.log(10000.0) / HEAD_DIM))
        angles = places[:, None] * frequency
        cosine = jnp.cos(angles)
        sine = jnp.where(lane < 32, -1.0, 1.0) * jnp.sin(angles)
        normed_all, queries, keys, values = project(hidden_all, norm_rows, w_qkv, cosine, sine)
        attended_all, attended_low, logs = attend(queries, keys, values)
        attended = swap(attended_low, width, True, 4)
        column = jnp.zeros((SHARD, D), bf)
    source_table = jnp.arange(corpus_weight.shape[0], dtype=jnp.int32)
    row_scale = jnp.sum(jnp.where(source_ids[0] == source_table, corpus_weight, 0.0))
    output, residual_grad, attended_grad, weight_grads, norm_part, squares, part = dense(
        lines, attended, hidden, cotangent[0], row_scale.reshape(1, 1), norm_rows, others, column
    )
    if lines:
        param_grads, input_grad, squares = backward(
            weight_grads, part, attended_grad, queries, keys, values, attended_all, logs,
            cosine, sine, normed_all, hidden_all, w_qkv, residual_grad, norm_rows, norm_part, squares,
        )
        param_grads = param_grads.reshape(-1)
    else:
        grads_all = swap(attended_grad, width, False, 6)
        mixed_grad = attend_back(
            queries, keys, values, grads_all, attended_all, logs, cosine, sine
        )
        grad_qkv = jnp.stack([dots(normed_all, part, (0, 0)) for part in mixed_grad])
        normed_part = sum(dots(part, w_qkv[j], (1, 1)) for j, part in enumerate(mixed_grad))
        _, unit_all, _ = norm_forward(hidden_all.astype(f32), norm_rows[0], norm_rows[1])
        norm_part = jnp.concatenate(
            [jnp.stack(norm_sums(normed_part, unit_all)), norm_part[2:]], axis=0
        )
        spread = jnp.zeros((3, width, D, D // width), bf)
        spread = lax.dynamic_update_slice_in_dim(spread, grad_qkv.astype(bf)[:, None], place, 1)
        parts = (
            spread.transpose(2, 0, 1, 3),
            weight_grads[:D],
            up_from_shards(weight_grads[D : 5 * D]),
            weight_grads[5 * D :],
            norm_part.astype(bf),
        )
        flat = jnp.concatenate([part.reshape(-1) for part in parts])
        param_grads = lax.psum_scatter(flat, ("dp", "fsdp"), scatter_dimension=0, tiled=True)
        param_grads = param_grads.astype(f32)
        normed_grad = lax.psum_scatter(normed_part, "fsdp", scatter_dimension=0, tiled=True)
        squares = lax.psum(squares, ("dp", "fsdp"))
        _, normed_unit, normed_inverse = norm_forward(
            hidden.astype(f32), norm_rows[0], norm_rows[1]
        )
        into_input = norm_backward(normed_grad, normed_unit, normed_inverse, norm_rows[0])
        input_grad = (residual_grad + into_input).astype(bf)
    statistics = squares[0, :2] / (devices * tokens * D)
    return (output[None], input_grad[None], param_grads, statistics)


def solution(mesh):
    lines = (mesh.shape["dp"], mesh.shape["fsdp"]) == (8, 4)
    in_specs = (
        P("dp", "fsdp", None),
        P(("dp", "fsdp")),
        P("dp", "fsdp", None),
        P("dp"),
        P(),
        P("dp", "fsdp"),
    )
    out_specs = (P("dp", "fsdp", None), P("dp", "fsdp", None), P(("dp", "fsdp")), P())
    return jax.shard_map(
        functools.partial(per_device, lines),
        mesh=mesh,
        in_specs=in_specs,
        out_specs=out_specs,
        check_vma=False,
    )
```

```python
import functools
import math

import jax
import jax.numpy as jnp
from jax import lax
from jax.experimental import pallas as pl
from jax.experimental.pallas import tpu as pltpu
from jax.sharding import PartitionSpec as P

D = 1024
HEADS = 16
HEAD_DIM = 64
FF = 4096
EPSILON = 1e-05
MASKED = -1e30
SCALE = 1.0 / math.sqrt(HEAD_DIM)
LOG2E = 1.4426950408889634

MESH = pl.DeviceIdType.MESH
bf = jnp.bfloat16
f32 = jnp.float32
SHARD = 384
NATURAL = 3074
MIB = 2**20

VM = pl.BlockSpec(memory_space=pltpu.VMEM)
ANY = pl.BlockSpec(memory_space=pl.ANY)
DMA = pltpu.SemaphoreType.DMA


def params_for(collective=None, mib=48):
    if collective is None:
        return pltpu.CompilerParams(vmem_limit_bytes=mib * MIB)
    return pltpu.CompilerParams(
        collective_id=collective, has_side_effects=True, vmem_limit_bytes=mib * MIB
    )


def coords():
    dp, fs = lax.axis_index("dp"), lax.axis_index("fsdp")
    return dp // 2, lax.rem(dp, 2), fs // 2, lax.rem(fs, 2)


def dev(z, x, y, c):
    return (z * 2 + x, y * 2 + c)


def linear(i):
    return (i // 4, lax.rem(i, 4))


def remote(src, dst, send, recv, to):
    return pltpu.make_async_remote_copy(
        src_ref=src, dst_ref=dst, send_sem=send, recv_sem=recv, device_id=to, device_id_type=MESH
    )


def greet(bar, device):
    pl.semaphore_signal(bar, inc=1, device_id=device, device_id_type=MESH)


def meet_neighbours(z, x, y, c, plane, more=0):
    bar = pltpu.get_barrier_semaphore()
    for device in plane:
        greet(bar, device)

    @pl.when(z < 3)
    def _():
        greet(bar, dev(z + 1, x, y, c))

    @pl.when(z > 0)
    def _():
        greet(bar, dev(z - 1, x, y, c))

    line = jnp.where(z < 3, 1, 0) + jnp.where(z > 0, 1, 0)
    pl.semaphore_wait(bar, len(plane) + line + more)


def add_rows(dst, *srcs):
    if dst.dtype == bf and len(srcs) == 2:
        dst[...] = srcs[0][...] + srcs[1][...]
        return
    total = srcs[0][...].astype(f32)
    for part in srcs[1:]:
        total = total + part[...].astype(f32)
    dst[...] = total.astype(dst.dtype)


def add_tiles(dst, rows, *srcs):
    for at in range(0, rows, 16):
        add_rows(dst.at[at : at + 16], *[part.at[at : at + 16] for part in srcs])


CHUNKS = 4
AHEAD = 2
EARLY = 1
CHUNK = SHARD // CHUNKS


def shard_rows(ref, base, zz, xx, yy, cc, k, low=0, count=CHUNK):
    s = (zz * 2 + xx) * 4 + yy * 2 + cc
    return ref.at[pl.ds(pl.multiple_of((s - base) * SHARD + k * CHUNK + low, 16), count)]


def gather_sems(planes):
    return [DMA((11, planes * CHUNKS)), DMA((11, planes * CHUNKS)), DMA((CHUNKS + 1,))]


def gather_steps(rows, plane_of, planes, own, source, line, over_x, ss, rs, ls):
    z, x, y, c = coords()
    xn, yn, cn = 1 - x, 1 - y, 1 - c
    to_x, to_y, to_core = dev(z, xn, y, c), dev(z, x, yn, c), dev(z, x, y, cn)
    lag, core_lag = 2, 4
    units = planes * CHUNKS
    ZU, ZD, XO, YO, CO, XD, YD, CX, CY, CXD, CYD = range(11)
    rest = CHUNK - over_x

    def unit(i):
        r = i // CHUNKS
        return plane_of(r), i - r * CHUNKS, i

    def send(kind, i):
        zz, k, q = unit(i)
        ref, to = {
            ZU: lambda: (rows(zz, x, y, c, k), dev(z + 1, x, y, c)),
            ZD: lambda: (rows(zz, x, y, c, k), dev(z - 1, x, y, c)),
            XO: lambda: (rows(zz, x, y, c, k), to_x),
            YO: lambda: (rows(zz, x, y, c, k), to_y),
            CO: lambda: (rows(zz, x, y, c, k), to_core),
            YD: lambda: (rows(zz, xn, y, c, k, over_x, rest), to_y),
            XD: lambda: (rows(zz, x, yn, c, k, 0, over_x), to_x),
            CX: lambda: (rows(zz, xn, y, c, k), to_core),
            CY: lambda: (rows(zz, x, yn, c, k), to_core),
            CXD: lambda: (rows(zz, xn, yn, c, k, 0, over_x), to_core),
            CYD: lambda: (rows(zz, xn, yn, c, k, over_x, rest), to_core),
        }[kind]()
        slot = (zz - 1) * CHUNKS + k if line else k
        src = source(k) if kind in (XO, YO, CO) and not line else ref
        return remote(src, ref, ss.at[kind, slot], rs.at[kind, slot], to)

    def arrive(kind, i):
        zz, k, q = unit(i)
        ref = {
            ZU: lambda: rows(zz, x, y, c, k),
            ZD: lambda: rows(zz, x, y, c, k),
            XO: lambda: rows(zz, xn, y, c, k),
            YO: lambda: rows(zz, x, yn, c, k),
            XD: lambda: rows(zz, xn, yn, c, k, 0, over_x),
            YD: lambda: rows(zz, xn, yn, c, k, over_x, rest),
            CO: lambda: rows(zz, x, y, cn, k),
            CX: lambda: rows(zz, xn, y, cn, k),
            CY: lambda: rows(zz, x, yn, cn, k),
            CXD: lambda: rows(zz, xn, yn, cn, k, 0, over_x),
            CYD: lambda: rows(zz, xn, yn, cn, k, over_x, rest),
        }[kind]()
        slot = (zz - 1) * CHUNKS + k if line else k
        remote(ref, ref, ss.at[kind, slot], rs.at[kind, slot], to_core).wait_recv()

    def local(k_plane):
        zz = k_plane
        return [
            pltpu.make_async_copy(source(k), rows(zz, x, y, c, k), ls.at[k]) for k in range(CHUNKS)
        ]

    def start():
        if line:

            @pl.when(own(z))
            def _():
                for copy in local(z):
                    copy.start()
                for copy in local(z):
                    copy.wait()
                for k in range(CHUNKS):
                    send(ZD, k).start()
                    if k < EARLY:
                        send(ZU, k).start()
        else:
            for copy in local(plane_of(0)):
                copy.start()
            for i in range(units):
                for kind in (XO, YO, CO):
                    send(kind, i).start()

    def late_up():
        @pl.when(own(z))
        def _():
            for k in range(EARLY, CHUNKS):
                send(ZU, k).start()

    def early(i):
        zz, _, _ = unit(i)
        if line:

            @pl.when(zz < z)
            def _():
                arrive(ZU, i)

            @pl.when(zz > z)
            def _():
                arrive(ZD, i)

            @pl.when((zz < z) & (z < 3))
            def _():
                send(ZU, i).start()

            @pl.when((zz > z) & (z > 0))
            def _():
                send(ZD, i).start()

        for kind in (XO, CO):
            send(kind, i).start()

    def step(i, _):
        if line:

            @pl.when((i < units) & (i >= EARLY))
            def _():
                early(i)

            @pl.when(i < units)
            def _():
                send(YO, i).start()

        j = i - lag

        @pl.when((j >= 0) & (j < units))
        def _():
            arrive(XO, j)
            send(YD, j).start()
            send(CX, j).start()
            arrive(YO, j)
            send(XD, j).start()
            send(CY, j).start()

        m = i - core_lag

        @pl.when(m >= 0)
        def _():
            arrive(XD, m)
            send(CXD, m).start()
            arrive(YD, m)
            send(CYD, m).start()

        return 0

    def finish():
        def one(i, _):
            zz, _, _ = unit(i)
            for kind in (CO, CX, CY, CXD, CYD):
                arrive(kind, i)
            for kind in (XO, YO, CO, YD, XD, CX, CY, CXD, CYD):
                send(kind, i).wait_send()
            if line:

                @pl.when((zz <= z) & (z < 3))
                def _():
                    send(ZU, i).wait_send()

                @pl.when((zz >= z) & (z > 0))
                def _():
                    send(ZD, i).wait_send()

            return 0

        lax.fori_loop(0, units, one, 0)
        if not line:
            for copy in local(plane_of(0)):
                copy.wait()

    return start, early, late_up, step, units + core_lag, finish


def reduce_steps(
    rows, planes, line, over_x, out, lb, cb, xb, yb, dxb, dyb, zub, zdb, ss, rs, cs, cr, ls
):
    z, x, y, c = coords()
    xn, yn, cn = 1 - x, 1 - y, 1 - c
    to_x, to_y, to_core = dev(z, xn, y, c), dev(z, x, yn, c), dev(z, x, y, cn)
    lag1, lag2, lag3, lag4 = 1, 2, 3, 4
    XS, YS, DXS, DYS, ZD, ZU = range(6)
    units = len(planes) * CHUNKS

    def unit(i):
        r = i // CHUNKS
        zz = planes[0] if len(planes) == 1 else planes[0] - r
        return zz, i - r * CHUNKS

    places = [(xn, yn), (xn, y), (x, yn), (x, y)]

    def load(i, p):
        zz, k = unit(i)
        xx, yy = places[p]
        return pltpu.make_async_copy(rows(zz, xx, yy, c, k), lb.at[i, p], ls.at[i, p])

    def to_sibling(i, p):
        zz, k = unit(i)
        xx, yy = places[p]
        return remote(rows(zz, xx, yy, cn, k), cb.at[i, p], cs.at[i, p], cr.at[i, p], to_core)

    def fetch(i, _):
        for p in range(4):
            load(i, p).start()
            to_sibling(i, p).start()
        return 0

    def start():
        lax.fori_loop(0, AHEAD, fetch, 0)

    def over(kind, src, dst, i, to):
        return remote(src, dst, ss.at[kind, i], rs.at[kind, i], to)

    def diag_x(i):
        return over(DXS, lb.at[i, 0, 0:over_x], dxb.at[i], i, to_x)

    def diag_y(i):
        return over(DYS, lb.at[i, 0, over_x:CHUNK], dyb.at[i], i, to_y)

    def whole_x(i):
        return over(XS, lb.at[i, 1], xb.at[i], i, to_x)

    def whole_y(i):
        return over(YS, lb.at[i, 2], yb.at[i], i, to_y)

    def down(i):
        return over(ZD, lb.at[i, 3], zub.at[i], i, dev(z - 1, x, y, c))

    def up(i):
        return over(ZU, lb.at[i, 3], zdb.at[i], i, dev(z + 1, x, y, c))

    def have(i, p):
        load(i, p).wait()
        to_sibling(i, p).wait_recv()

    def step(i, _):
        @pl.when(i + AHEAD < units)
        def _():
            fetch(i + AHEAD, 0)

        @pl.when(i < units)
        def _():
            have(i, 0)
            add_tiles(lb.at[i, 0], CHUNK, lb.at[i, 0], cb.at[i, 0])
            diag_x(i).start()
            diag_y(i).start()

        j = i - lag1

        @pl.when((j >= 0) & (j < units))
        def _():
            have(j, 1)
            have(j, 2)
            diag_y(j).wait_recv()
            diag_x(j).wait_recv()
            a, b = lb.at[j, 1], cb.at[j, 1]
            low, high = slice(0, over_x), slice(over_x, CHUNK)
            add_tiles(a.at[low], over_x, a.at[low], b.at[low])
            add_tiles(a.at[high], CHUNK - over_x, a.at[high], b.at[high], dyb.at[j])
            whole_x(j).start()
            a, b = lb.at[j, 2], cb.at[j, 2]
            add_tiles(a.at[low], over_x, a.at[low], b.at[low], dxb.at[j])
            add_tiles(a.at[high], CHUNK - over_x, a.at[high], b.at[high])
            whole_y(j).start()

        m = i - lag2

        @pl.when((m >= 0) & (m < units))
        def _():
            zz, k = unit(m)
            have(m, 3)
            whole_x(m).wait_recv()
            whole_y(m).wait_recv()
            parts = [lb.at[m, 3], cb.at[m, 3], xb.at[m], yb.at[m]]
            if not line:
                add_tiles(out(k), CHUNK, *parts)
                return

            @pl.when(z != zz)
            def _():
                add_tiles(lb.at[m, 3], CHUNK, *parts)

            @pl.when(z == 3)
            def _():
                down(m).start()

            @pl.when(z == 0)
            def _():
                up(m).start()

            @pl.when(z == zz)
            def _():
                add_tiles(out(k), CHUNK, *parts)

        if not line:
            return 0
        n = i - lag3

        @pl.when((n >= 0) & (n < units))
        def _():
            zz, _ = unit(n)

            @pl.when((z > zz) & (z < 3))
            def _():
                down(n).wait_recv()
                add_tiles(lb.at[n, 3], CHUNK, lb.at[n, 3], zub.at[n])
                down(n).start()

            @pl.when((z < zz) & (z > 0))
            def _():
                up(n).wait_recv()
                add_tiles(lb.at[n, 3], CHUNK, lb.at[n, 3], zdb.at[n])
                up(n).start()

        o = i - lag4

        @pl.when(o >= 0)
        def _():
            zz, k = unit(o)

            @pl.when(z == zz)
            def _():
                down(o).wait_recv()
                add_tiles(out(k), CHUNK, out(k), zub.at[o])
                up(o).wait_recv()
                add_tiles(out(k), CHUNK, out(k), zdb.at[o])

        return 0

    def finish():
        def one(i, _):
            zz, _ = unit(i)
            for p in range(4):
                to_sibling(i, p).wait_send()
            for copy in (diag_x(i), diag_y(i), whole_x(i), whole_y(i)):
                copy.wait_send()
            if line:

                @pl.when(z > zz)
                def _():
                    down(i).wait_send()

                @pl.when(z < zz)
                def _():
                    up(i).wait_send()

            return 0

        lax.fori_loop(0, units, one, 0)

    return start, step, units + (lag4 if line else lag2), finish


def reduce_rooms(planes, line, over_x):
    units = planes * CHUNKS

    def room(*shape):
        return pltpu.VMEM(shape + (D,), bf)

    lines = units if line else 1
    return [
        room(units, 4, CHUNK), room(units, 4, CHUNK),
        room(units, CHUNK), room(units, CHUNK),
        room(units, over_x), room(units, CHUNK - over_x),
        room(lines, CHUNK), room(lines, CHUNK),
        DMA((6, units)), DMA((6, units)), DMA((units, 4)), DMA((units, 4)), DMA((units, 4)),
    ]


def swap_kernel(n, to_tokens, a_ref, o_ref, ss, rs, ls):
    me = lax.axis_index("fsdp")
    bar = pltpu.get_barrier_semaphore()
    for i in range(1, n):
        pl.semaphore_signal(
            bar, inc=1, device_id={"fsdp": lax.rem(me + i, n)}, device_id_type=MESH
        )
    pl.semaphore_wait(bar, n - 1)
    tokens = (a_ref if to_tokens else o_ref).shape[0] // n
    width = (o_ref if to_tokens else a_ref).shape[1] // n

    def token_block(ref, owner):
        return ref.at[pl.ds(pl.multiple_of(owner * tokens, 16), tokens)]

    def head_block(ref, owner):
        return ref.at[:, pl.ds(pl.multiple_of(owner * width, 128), width)]

    take, put = (token_block, head_block) if to_tokens else (head_block, token_block)
    local = pltpu.make_async_copy(take(a_ref, me), put(o_ref, me), ls)
    local.start()
    copies = []
    for i in range(1, n):
        to = lax.rem(me + i, n)
        copy = pltpu.make_async_remote_copy(
            src_ref=take(a_ref, to), dst_ref=put(o_ref, me), send_sem=ss.at[i], recv_sem=rs.at[i],
            device_id={"fsdp": to}, device_id_type=MESH,
        )
        copy.start()
        copies.append(copy)
    for i in range(1, n):
        copies[i - 1].wait_send()
        ref = put(o_ref, lax.rem(me - i + n, n))
        pltpu.make_async_remote_copy(
            src_ref=ref, dst_ref=ref, send_sem=ss.at[i], recv_sem=rs.at[i],
            device_id={"fsdp": lax.rem(me + i, n)}, device_id_type=MESH,
        ).wait_recv()
    local.wait()


def swap(array, n, to_tokens, collective):
    rows, columns = array.shape
    shape = (rows // n, columns * n) if to_tokens else (rows * n, columns // n)
    return pl.pallas_call(
        functools.partial(swap_kernel, n, to_tokens),
        out_shape=jax.ShapeDtypeStruct(shape, bf),
        in_specs=[VM],
        out_specs=VM,
        scratch_shapes=[DMA((n,)), DMA((n,)), DMA],
        compiler_params=params_for(collective, 32),
    )(array)


def partner(values):
    width = values.shape[-1]
    lane = lax.broadcasted_iota(jnp.int32, values.shape, values.ndim - 1)
    after = pltpu.roll(values, width - 32, values.ndim - 1)
    before = pltpu.roll(values, 32, values.ndim - 1)
    return jnp.where(lane % 64 < 32, after, before)


def normed_rows(rows, n_ref):
    rows = rows.astype(f32)
    center = rows - jnp.mean(rows, axis=-1, keepdims=True)
    inverse = lax.rsqrt(jnp.mean(center * center, axis=-1, keepdims=True) + EPSILON)
    return (center * inverse * n_ref[0:1, :] + n_ref[1:2, :]).astype(bf)


def project_rows(normed, w_ref, cosine, sine):
    mixed = [jnp.dot(normed, w_ref[j], preferred_element_type=f32) for j in range(3)]
    for j in range(2):
        parts = [mixed[j][:, at : at + 128] for at in range(0, mixed[j].shape[1], 128)]
        parts = [part * cosine + partner(part) * sine for part in parts]
        mixed[j] = jnp.concatenate(parts, axis=1)
    return [part.astype(bf) for part in mixed]


def qkv_kernel(h_ref, n_ref, w_ref, c_ref, s_ref, *out_refs):
    normed = normed_rows(h_ref[...], n_ref)
    out_refs[0][...] = normed
    for ref, part in zip(out_refs[1:], project_rows(normed, w_ref, c_ref[...], s_ref[...])):
        ref[...] = part


def project(hidden, norm_rows, w_qkv, cosine, sine):
    tokens, width = hidden.shape[0], w_qkv.shape[2]
    block = 256
    rows = lambda w: pl.BlockSpec((block, w), lambda i: (i, 0))
    full = lambda a: pl.BlockSpec(a.shape, lambda i: (0,) * a.ndim)
    shape = jax.ShapeDtypeStruct
    return pl.pallas_call(
        qkv_kernel,
        grid=(tokens // block,),
        in_specs=[rows(D), full(norm_rows), full(w_qkv), rows(128), rows(128)],
        out_specs=[rows(D), rows(width), rows(width), rows(width)],
        out_shape=[shape((tokens, D), bf)] + [shape((tokens, width), bf)] * 3,
        compiler_params=params_for(),
    )(hidden, norm_rows, w_qkv, cosine, sine)


NT = (((1,), (1,)), ((), ()))
TN = (((0,), (0,)), ((), ()))
BLOCK = 512


def one_head(pair, h):
    lane = lax.broadcasted_iota(jnp.int32, pair.shape, 1)
    return jnp.where((lane < 64) if h == 0 else (lane >= 64), pair, jnp.zeros_like(pair))


def causal(scores, i, j):
    key = j * scores.shape[0] + lax.broadcasted_iota(jnp.int32, scores.shape, 0)
    query = i * scores.shape[1] + lax.broadcasted_iota(jnp.int32, scores.shape, 1)
    return jnp.where(key <= query, scores, MASKED)


def attend_rows(i, queries, k_ref, v_ref):
    heads = [one_head(queries, h) for h in range(2)]

    def block(j, carry, masked):
        at = pl.ds(pl.multiple_of(j * BLOCK, BLOCK), BLOCK)
        keys, values = k_ref[at, :], v_ref[at, :]
        out = []
        for h in range(2):
            peak, total, summed = carry[3 * h : 3 * h + 3]
            scores = lax.dot_general(keys, heads[h], NT, preferred_element_type=f32)
            scores = scores * (SCALE * LOG2E)
            if masked:
                scores = causal(scores, i, j)
            new_peak = jnp.maximum(peak, jnp.max(scores, axis=0, keepdims=True))
            weights = jnp.exp2(scores - new_peak)
            shrink = jnp.exp2(peak - new_peak)
            total = total * shrink + jnp.sum(weights, axis=0, keepdims=True)
            part = lax.dot_general(
                values[:, 64 * h : 64 * h + 64], weights.astype(bf), TN, preferred_element_type=f32
            )
            out += [new_peak, total, summed * shrink + part]
        return tuple(out)

    start = (
        jnp.full((1, BLOCK), MASKED, f32), jnp.zeros((1, BLOCK), f32), jnp.zeros((64, BLOCK), f32)
    ) * 2
    carry = lax.fori_loop(0, i, lambda j, carry: block(j, carry, False), start)
    peak0, total0, sum0, peak1, total1, sum1 = block(i, carry, True)
    out = jnp.concatenate([sum0 / total0, sum1 / total1], axis=0).T
    logs = jnp.concatenate([peak0 + jnp.log2(total0), peak1 + jnp.log2(total1)], axis=0)
    return out, logs


def attend_kernel(q_ref, k_ref, v_ref, o_ref, low_ref, l_ref):
    out, logs = attend_rows(pl.program_id(1), q_ref[...], k_ref, v_ref)
    o_ref[...] = out
    low_ref[...] = out.astype(bf)
    l_ref[...] = logs.reshape(1, 2, BLOCK)


def attend(queries, keys, values):
    tokens, width = queries.shape
    pairs = width // 128
    block = pl.BlockSpec((BLOCK, 128), lambda p, i: (i, p))
    full = pl.BlockSpec((tokens, 128), lambda p, i: (0, p))
    logs = pl.BlockSpec((1, 2, BLOCK), lambda p, i: (p, 0, i))
    shape = jax.ShapeDtypeStruct
    return pl.pallas_call(
        attend_kernel,
        grid=(pairs, tokens // BLOCK),
        in_specs=[block, full, full],
        out_specs=[block, block, logs],
        out_shape=[
            shape((tokens, width), f32), shape((tokens, width), bf), shape((pairs, 2, tokens), f32)
        ],
        compiler_params=params_for(),
    )(queries, keys, values)


def attend_back_rows(i, queries, grads, attended, logs, k_ref, v_ref, dk, dv):
    heads = [one_head(queries, h) for h in range(2)]
    grad_heads = [one_head(grads, h) for h in range(2)]
    both_heads = jnp.concatenate(heads, axis=0)
    both_grads = jnp.concatenate(grad_heads, axis=0)
    products = (attended * grads.astype(f32)).T
    dots = [jnp.sum(products[64 * h : 64 * h + 64], axis=0, keepdims=True) for h in range(2)]

    def block(j, sums, masked):
        at = pl.ds(pl.multiple_of(j * BLOCK, BLOCK), BLOCK)
        keys, values = k_ref[at, :], v_ref[at, :]
        weights, score_grads = [], []
        for h in range(2):
            scores = lax.dot_general(keys, heads[h], NT, preferred_element_type=f32)
            scores = scores * (SCALE * LOG2E)
            if masked:
                scores = causal(scores, i, j)
            prob = jnp.exp2(scores - logs[h : h + 1])
            prob_grad = lax.dot_general(values, grad_heads[h], NT, preferred_element_type=f32)
            score_grads.append((prob * (prob_grad - dots[h])).astype(bf))
            weights.append(prob.astype(bf))
        dv[at, :] += jnp.dot(
            jnp.concatenate(weights, axis=1), both_grads, preferred_element_type=f32
        )
        dk[at, :] += jnp.dot(
            jnp.concatenate(score_grads, axis=1), both_heads, preferred_element_type=f32
        )
        return tuple(
            sums[h] + lax.dot_general(score_grads[h], keys, TN, preferred_element_type=f32)
            for h in range(2)
        )

    zero = jnp.zeros((BLOCK, 128), f32)
    sums = lax.fori_loop(0, i, lambda j, sums: block(j, sums, False), (zero, zero))
    sums = block(i, sums, True)
    lane = lax.broadcasted_iota(jnp.int32, zero.shape, 1)
    return jnp.where(lane < 64, sums[0], sums[1]) * SCALE


def turn_back(grads, cosine, sine):
    return (grads * cosine - partner(grads) * sine).astype(bf)


def finish_keys(dk, dv, c_ref, s_ref, dk_ref, dv_ref):
    def turn(t, _):
        at = pl.ds(pl.multiple_of(t * 256, 256), 256)
        dk_ref[at, :] = turn_back(dk[at, :] * SCALE, c_ref[at, :], s_ref[at, :])
        dv_ref[at, :] = dv[at, :].astype(bf)
        return 0

    lax.fori_loop(0, dk.shape[0] // 256, turn, 0)


def attend_back_kernel(
    q_ref, k_ref, v_ref, g_ref, a_ref, l_ref, cq_ref, sq_ref, c_ref, s_ref,
    dq_ref, dk_ref, dv_ref, dk, dv,
):
    i = pl.program_id(1)

    @pl.when(i == 0)
    def _():
        dk[...] = jnp.zeros_like(dk)
        dv[...] = jnp.zeros_like(dv)

    query_grad = attend_back_rows(
        i, q_ref[...], g_ref[...], a_ref[...], l_ref[0], k_ref, v_ref, dk, dv
    )
    dq_ref[...] = turn_back(query_grad, cq_ref[...], sq_ref[...])

    @pl.when(i == pl.num_programs(1) - 1)
    def _():
        finish_keys(dk, dv, c_ref, s_ref, dk_ref, dv_ref)


def attend_back(queries, keys, values, grads, attended, logs, cosine, sine):
    tokens, width = queries.shape
    block = pl.BlockSpec((BLOCK, 128), lambda p, i: (i, p))
    full = pl.BlockSpec((tokens, 128), lambda p, i: (0, p))
    table_block = pl.BlockSpec((BLOCK, 128), lambda p, i: (i, 0))
    table = pl.BlockSpec((tokens, 128), lambda p, i: (0, 0))
    log_block = pl.BlockSpec((1, 2, BLOCK), lambda p, i: (p, 0, i))
    return pl.pallas_call(
        attend_back_kernel,
        grid=(width // 128, tokens // BLOCK),
        in_specs=[block, full, full, block, block, log_block, table_block, table_block, table, table],
        out_specs=[block, full, full],
        out_shape=[jax.ShapeDtypeStruct((tokens, width), bf)] * 3,
        scratch_shapes=[pltpu.VMEM((tokens, 128), f32), pltpu.VMEM((tokens, 128), f32)],
        compiler_params=params_for(),
    )(queries, keys, values, grads, attended, logs, cosine, sine, cosine, sine)


def swap_copies(take, put, ss, rs, base):
    z, x, y, c = coords()
    others = [(y, 1 - c), (1 - y, c), (1 - y, 1 - c)]
    me = y * 2 + c
    starts, arrivals = [], []
    for i, (yy, cc) in enumerate(others):
        starts.append(
            remote(take(yy * 2 + cc), put(me), ss.at[base + i], rs.at[base + i], dev(z, x, yy, cc))
        )
        ref = put(yy * 2 + cc)
        arrivals.append(remote(ref, ref, ss.at[base + i], rs.at[base + i], dev(z, x, yy, cc)))
    return me, starts, arrivals


def forward_kernel(
    p_ref, h_ref, pos_ref,
    g_ref, col_ref, hid_out, wq_out, nrm_ref, cos_out, sin_out,
    normed_out, q_out, k_out, v_out, o_out, l_ref, t_ref,
    ext, tail, units, can_ref, posall_ref, low,
    hid_ref, wq_ref, cos_ref, sin_ref, normed_ref, q_ref, k_ref, v_ref, o_ref,
    us, ur, hs, hr, ns, nr, ps, pr, keep_sem, ss, rs, ls, ts, tr, cs, cr, outs,
):
    keeps = [
        pltpu.make_async_copy(src, dst, outs.at[i])
        for i, (src, dst) in enumerate(
            [
                (hid_ref, hid_out), (wq_ref, wq_out), (cos_ref, cos_out), (sin_ref, sin_out),
                (normed_ref, normed_out), (q_ref, q_out), (k_ref, k_out), (v_ref, v_out),
                (o_ref, o_out),
            ]
        )
    ]
    z, x, y, c = coords()
    xn, yn, cn = 1 - x, 1 - y, 1 - c
    s = (z * 2 + x) * 4 + y * 2 + c
    f = y * 2 + c
    nxt, prv = lax.rem(s + 1, 32), lax.rem(s + 31, 32)
    core = dev(z, x, y, cn)
    xs, xo, ys, yo = dev(z, xn, y, c), dev(z, xn, y, cn), dev(z, x, yn, c), dev(z, x, yn, cn)
    bar = pltpu.get_barrier_semaphore()
    greet(bar, linear(nxt))
    greet(bar, linear(prv))

    @pl.when(s != 31)
    def _():
        greet(bar, (7, 3))

    ext[64 : 64 + NATURAL, :] = p_ref[...].astype(f32)
    tail[...] = ext[NATURAL : NATURAL + 64, :]
    more = 2 + jnp.where(s == 31, 31, 0)
    meet_neighbours(z, x, y, c, [core, xs, xo, ys, yo], more)
    halves, half = 4, 128

    def hidden_rows(owner, k):
        return hid_ref.at[pl.ds(pl.multiple_of(owner * 512 + k * half, 16), half)]

    def hidden_own(k):
        return h_ref.at[pl.ds(k * half, half)]

    over_y, over_core, over_both = yn * 2 + c, y * 2 + cn, yn * 2 + cn
    halo = remote(tail, ext.at[0:64], ns.at[0], nr.at[0], linear(nxt))
    halo.start()
    sent = []
    for i, to in enumerate([core, ys, yo]):
        sent.append(remote(pos_ref, posall_ref.at[f], ps.at[i], pr.at[i], to))
    for k in range(halves):
        sent.append(remote(hidden_own(k), hidden_rows(f, k), hs.at[1, k], hr.at[1, k], core))
    for copy in sent:
        copy.start()
    rows_over_y = [
        remote(hidden_own(k), hidden_rows(f, k), hs.at[0, k], hr.at[0, k], ys) for k in range(halves)
    ]
    sent += rows_over_y
    for k in range(halves):

        @pl.when(k <= z)
        def _():
            rows_over_y[k].start()

    hid_ref[pl.ds(pl.multiple_of(f * 512, 512), 512)] = h_ref[...]
    posall_ref[pl.ds(f, 1)] = pos_ref[...].reshape(1, 8, 128)
    halo.wait()
    base = 64 - 2 * s

    def lines(first, count, apart, k):
        return ext[pl.ds(base + 8 * first + k, count, stride=8 * apart), :].astype(bf)

    def order(to, first, count, apart):
        for j in range(apart):
            for k in range(8):
                can_ref[to + j * count : to + (j + 1) * count, 128 * k : 128 * k + 128] = lines(
                    first + j, count, apart, k
                )

    @pl.when(z == 0)
    def _():
        for j in range(3):
            for k in range(8):
                at = 128 * (k % 2)
                units[k // 2, j, :, at : at + 128] = lines(j, 128, 3, k)

    @pl.when((s == 8) | (s == 9) | (s >= 22))
    def _():
        order(0, 0, 384, 1)

    @pl.when(s == 10)
    def _():
        order(0, 0, 256, 1)
        order(256, 256, 32, 4)

    @pl.when((s >= 11) & (s <= 20))
    def _():
        order(0, 0, 96, 4)

    @pl.when(s == 21)
    def _():
        order(0, 0, 32, 4)
        order(128, 128, 256, 1)

    def norm_send(i):
        return remote(nrm_ref, nrm_ref, ns.at[1 + i], nr.at[1], linear(i))

    @pl.when(s == 31)
    def _():
        for k in range(8):
            nrm_ref[:, 128 * k : 128 * k + 128] = ext[pl.ds(base + 8 * 384 + k, 8, stride=8), :]

        def go(i, _):
            norm_send(i).start()
            return 0

        lax.fori_loop(0, 31, go, 0)

    def column(k):
        return col_ref.at[pl.ds(pl.multiple_of(k * CHUNK, CHUNK), CHUNK)]

    def down(k):
        return remote(column(k), column(k), cs.at[k], cr.at[k], dev(z - 1, x, y, c))

    keep = pltpu.make_async_copy(can_ref, col_ref, keep_sem)

    @pl.when(z == 3)
    def _():
        keep.start()
        keep.wait()

    def down_step(k):
        @pl.when(z < 3)
        def _():
            down(k).wait_recv()

        @pl.when(z > 0)
        def _():
            down(k).start()

    def arrive(ref, sem):
        remote(ref, ref, us.at[0, 0, 0], sem, core).wait_recv()

    for i, owner in enumerate([over_core, over_y, over_both]):
        arrive(posall_ref.at[owner], pr.at[i])

    def tables():
        lane = lax.broadcasted_iota(jnp.int32, (1, 128), 1) % 64
        turn = (lane % 32).astype(f32) * (-2.0 * math.log(10000.0) / HEAD_DIM)
        frequency = jnp.exp(turn)

        def one(t, _):
            row = posall_ref[t // 4, pl.ds(lax.rem(t, 4), 1), :]
            angles = jnp.broadcast_to(row, (128, 128)).T * frequency
            at = pl.ds(pl.multiple_of(t * 128, 128), 128)
            cos_ref[at, :] = jnp.cos(angles)
            sine = jnp.sin(angles)
            sin_ref[at, :] = jnp.where(lane < 32, -sine, sine)
            return 0

        lax.fori_loop(0, 16, one, 0)

    @pl.when(z >= 2)
    def _():
        tables()

    first = jnp.where(z >= 2, 2, 1)
    start, early, late_up, pump, steps, finish = gather_steps(
        functools.partial(shard_rows, g_ref, 8),
        lambda r: jnp.where(r == 0, first, 3 - first), 2,
        lambda zz: (zz == 1) | (zz == 2),
        lambda k: can_ref.at[k * CHUNK : k * CHUNK + CHUNK],
        True, FORWARD_X, ss, rs, ls,
    )
    start()

    @pl.when(z >= 1)
    def _():
        for i in range(EARLY):
            early(i)

    slots = [yn * 2 + c, yn * 2 + cn, y * 2 + cn, y * 2 + c]

    def target(xx, yy, cc, h):
        at = pl.multiple_of((xx * 4 + yy * 2 + cc) * 128 + 64 * h, 64)
        return wq_ref.at[:, pl.ds(at, 64)]

    def piece(q, h):
        return units.at[slots[q], :, 64 * h : 64 * h + 64]

    def up(q, h):
        return remote(piece(q, h), piece(q, h), us.at[0, q, h], ur.at[0, q, h], dev(z + 1, x, y, c))

    for q in range(4):
        for h in range(2):
            unit, mine = piece(q, h), target(x, y, c, h)

            @pl.when(z > 0)
            def _():
                arrive(unit, ur.at[0, q, h])

            @pl.when(z < 3)
            def _():
                up(q, h).start()

            if q == 0:
                out = [remote(unit, mine, us.at[1, 0, h], ur.at[1, 0, h], ys)]
            elif q == 1:
                out = [remote(unit, mine, us.at[1, 1, h], ur.at[1, 1, h], yo)]
            elif q == 2:
                out = [
                    remote(unit, mine, us.at[1, 2, h], ur.at[1, 2, h], xo),
                    remote(unit, mine, us.at[1, 3, h], ur.at[1, 3, h], core),
                ]
            else:
                out = [remote(unit, mine, us.at[2, 0, h], ur.at[2, 0, h], xs)]
                mine[...] = unit[...]
            for copy in out:
                copy.start()
            sent += out
    for k in range(halves):

        @pl.when(k > z)
        def _():
            rows_over_y[k].start()

    @pl.when(z == 3)
    def _():
        for k in range(CHUNKS):
            down_step(k)

    late_up()

    @pl.when(z == 0)
    def _():
        for i in range(EARLY):
            early(i)

    for h in range(2):
        for i, cc in enumerate((c, cn)):
            ref = target(x, yn, cc, h)
            arrive(ref, ur.at[1, i, h])
            copy = remote(ref, ref, us.at[2, 1 + i, h], ur.at[2, 1 + i, h], xs)
            copy.start()
            sent.append(copy)
    pump(0, 0)

    @pl.when(z < 2)
    def _():
        tables()

    @pl.when(s != 31)
    def _():
        arrive(nrm_ref, nr.at[1])

    def normalise(owner):
        def one(k, _):
            at = pl.ds(pl.multiple_of(owner * 512 + k * 256, 256), 256)
            normed_ref[at, :] = normed_rows(hid_ref[at, :], nrm_ref)
            return 0

        lax.fori_loop(0, 2, one, 0)

    normalise(f)
    for k in range(halves):
        arrive(hidden_rows(over_core, k), hr.at[1, k])
    normalise(over_core)
    for k in range(halves):
        ref = hidden_rows(over_y, k)
        arrive(ref, hr.at[0, k])
        copy = remote(ref, ref, hs.at[2, k], hr.at[2, k], core)
        copy.start()
        sent.append(copy)
    normalise(over_y)
    for k in range(halves):
        arrive(hidden_rows(over_both, k), hr.at[2, k])
    normalise(over_both)
    for h in range(2):
        arrive(target(xn, y, cn, h), ur.at[1, 2, h])
        arrive(target(x, y, cn, h), ur.at[1, 3, h])
        arrive(target(xn, y, c, h), ur.at[2, 0, h])
        arrive(target(xn, yn, c, h), ur.at[2, 1, h])
        arrive(target(xn, yn, cn, h), ur.at[2, 2, h])
    pump(1, 0)

    def project_step(t, _):
        at = pl.ds(pl.multiple_of(t * 256, 256), 256)
        parts = project_rows(normed_ref[at, :], wq_ref, cos_ref[at, :], sin_ref[at, :])
        for ref, part in zip((q_ref, k_ref, v_ref), parts):
            ref[at, :] = part

        @pl.when(lax.rem(t, 4) == 3)
        def _():
            pump(2 + t // 4, 0)

        return 0

    lax.fori_loop(0, 8, project_step, 0)
    for copy in keeps[:8]:
        copy.start()

    def take(p, owner):
        rows = pl.ds(pl.multiple_of(owner * 512, 512), 512)
        return low.at[rows, 128 * p : 128 * p + 128]

    def put(p, owner):
        return t_ref.at[:, pl.ds(pl.multiple_of(owner * 256 + 128 * p, 128), 128)]

    swaps = [
        swap_copies(functools.partial(take, p), functools.partial(put, p), ts, tr, 3 * p)
        for p in range(2)
    ]
    own_blocks = [
        pltpu.make_async_copy(take(p, f), put(p, f), outs.at[9 + p]) for p in range(2)
    ]

    def swap_start(p):
        for copy in swaps[p][1] + [own_blocks[p]]:
            copy.start()

    def attend_step(t, _):
        p = t // 4
        i = t - 4 * p
        at = pl.ds(pl.multiple_of(i * BLOCK, BLOCK), BLOCK)
        lanes = pl.ds(pl.multiple_of(p * 128, 128), 128)
        out, logs = attend_rows(i, q_ref[at, lanes], k_ref.at[:, lanes], v_ref.at[:, lanes])
        o_ref[at, lanes] = out
        low[at, lanes] = out.astype(bf)
        l_ref[p, :, at] = logs

        @pl.when(t == 3)
        def _():
            swap_start(0)

        @pl.when(i >= 1)
        def _():
            pump(3 + i + 3 * p, 0)

        k = t - 2 * (3 - z)

        @pl.when((z > 0) & (z < 3) & (k >= 0) & (k < CHUNKS))
        def _():
            down_step(k)

        return 0

    lax.fori_loop(0, 8, attend_step, 0)

    swap_start(1)
    keeps[8].start()
    lax.fori_loop(10, steps, pump, 0)

    @pl.when(z == 0)
    def _():
        for k in range(CHUNKS):
            down_step(k)

    for _, starts, arrivals in swaps:
        for copy in arrivals:
            copy.wait_recv()
        for copy in starts:
            copy.wait_send()
    for copy in sent:
        copy.wait_send()
    for copy in keeps + own_blocks:
        copy.wait()

    @pl.when(z < 3)
    def _():
        for q in range(4):
            for h in range(2):
                up(q, h).wait_send()

    @pl.when(s == 31)
    def _():
        def go(i, _):
            norm_send(i).wait_send()
            return 0

        lax.fori_loop(0, 31, go, 0)

    @pl.when(z > 0)
    def _():
        for k in range(CHUNKS):
            down(k).wait_send()

    finish()


FORWARD_X = 64


def forward(share, hidden, places):
    shape = jax.ShapeDtypeStruct
    return pl.pallas_call(
        forward_kernel,
        out_shape=(
            shape((16 * SHARD, D), bf), shape((SHARD, D), bf),
            shape((2048, D), bf), shape((3, D, 256), bf), shape((8, D), f32),
            shape((2048, 128), f32), shape((2048, 128), f32), shape((2048, D), bf),
            shape((2048, 256), bf), shape((2048, 256), bf), shape((2048, 256), bf),
            shape((2048, 256), f32), shape((2, 2, 2048), f32), shape((512, D), bf),
        ),
        in_specs=[VM] * 3,
        out_specs=(ANY,) * 4 + (VM,) + (ANY,) * 7 + (VM, ANY),
        scratch_shapes=[
            pltpu.VMEM((64 + NATURAL + 6, 128), f32),
            pltpu.VMEM((64, 128), f32),
            pltpu.VMEM((4, 3, 128, 256), bf),
            pltpu.VMEM((SHARD, D), bf),
            pltpu.VMEM((4, 8, 128), f32),
            pltpu.VMEM((2048, 256), bf),
            pltpu.VMEM((2048, D), bf),
            pltpu.VMEM((3, D, 256), bf),
            pltpu.VMEM((2048, 128), f32),
            pltpu.VMEM((2048, 128), f32),
            pltpu.VMEM((2048, D), bf),
            pltpu.VMEM((2048, 256), bf),
            pltpu.VMEM((2048, 256), bf),
            pltpu.VMEM((2048, 256), bf),
            pltpu.VMEM((2048, 256), f32),
            DMA((3, 4, 2)), DMA((3, 4, 2)), DMA((3, 4)), DMA((3, 4)),
            DMA((32,)), DMA((2,)), DMA((3,)), DMA((3,)), DMA,
            *gather_sems(2), DMA((6,)), DMA((6,)), DMA((CHUNKS,)), DMA((CHUNKS,)), DMA((11,)),
        ],
        compiler_params=params_for(0, 62),
    )(share, hidden, places)


def backward_kernel(
    gw_ref, part_ref, g_hbm, q_hbm, k_hbm, v_hbm, a_hbm, l_ref, cos_hbm, sin_hbm,
    normed_hbm, hid_hbm, wq_hbm, rg_hbm, nrm_ref, nsum_ref, st_ref,
    out_ref, ig_ref, sto_ref,
    grads, dk, dv, q_ref, k_ref, v_ref, a_ref, cos_ref, sin_ref, normed, hid, wq,
    own_ref, vg, nsum,
    ext, hal, hsend, av, bv, cv, acv, zv, sums, sv, nc, ny, nland, sland, land,
    lsem, hsems, rgs, cs, cr, s1, r1, s2, r2, zs, zr, ms, mr, qs, qr, hsem, *rooms,
):
    z, x, y, c = coords()
    xn, yn, cn = 1 - x, 1 - y, 1 - c
    s = (z * 2 + x) * 4 + y * 2 + c
    me = y * 2 + c
    core = dev(z, x, y, cn)
    xs, xo, ys, yo = dev(z, xn, y, c), dev(z, xn, y, cn), dev(z, x, yn, c), dev(z, x, yn, cn)
    prv = lax.rem(s + 31, 32)

    loads = [
        pltpu.make_async_copy(src, dst, lsem.at[i])
        for i, (src, dst) in enumerate(
            [
                (g_hbm, grads), (q_hbm, q_ref), (k_hbm, k_ref), (v_hbm, v_ref),
                (a_hbm, a_ref), (cos_hbm, cos_ref), (sin_hbm, sin_ref),
                (normed_hbm, normed), (wq_hbm, wq),
            ]
        )
    ]
    for copy in loads:
        copy.start()

    bar = pltpu.get_barrier_semaphore()

    def hello(i, _):
        greet(bar, linear(lax.rem(s + i, 32)))
        return 0

    lax.fori_loop(1, 32, hello, 0)
    pl.semaphore_wait(bar, 31)

    def owned(k):
        return own_ref.at[pl.ds(pl.multiple_of(k * CHUNK, CHUNK), CHUNK)]

    start, pump, steps, finish = reduce_steps(
        functools.partial(shard_rows, gw_ref, 8), (2, 1), True, BACKWARD_X, owned, *rooms
    )
    start()

    def tell(i):
        return remote(st_ref, sland.at[s], qs.at[i], qr.at[s], linear(lax.rem(s + i, 32)))

    def tell_all(i, _):
        tell(i).start()
        return 0

    lax.fori_loop(1, 32, tell_all, 0)

    def up(k):
        return remote(land.at[k], land.at[k], cs.at[k], cr.at[k], dev(z + 1, x, y, c))

    def part(k):
        return part_ref.at[pl.ds(pl.multiple_of(k * CHUNK, CHUNK), CHUNK)]

    def up_step(k):
        @pl.when(z > 0)
        def _():
            up(k).wait_recv()

        @pl.when(z == 0)
        def _():
            add_tiles(land.at[k], CHUNK, part(k))

        @pl.when((z > 0) & (z < 3))
        def _():
            add_tiles(land.at[k], CHUNK, part(k), land.at[k])

        @pl.when(z < 3)
        def _():
            up(k).start()

        @pl.when(z == 3)
        def _():
            add_tiles(owned(k), CHUNK, part(k), land.at[k])

    pump(0, 0)
    pump(1, 0)
    for copy in loads[:7]:
        copy.wait()

    d_refs = (q_ref, k_ref, v_ref)

    def block_grad(p, xx, yy):
        at = pl.ds(pl.multiple_of((xx * 2 + yy) * 256, 256), 256)
        lanes = slice(128 * p, 128 * p + 128)
        for j in range(3):
            vg[j, at, lanes] = lax.dot_general(
                normed[:, at], d_refs[j][:, lanes], TN, preferred_element_type=f32
            ).astype(bf)

    def unit(p, xx, yy, cc):
        at = pl.multiple_of((xx * 4 + yy * 2 + cc) * 128, 128)
        return vg.at[:, pl.ds(at, 128), 128 * p : 128 * p + 128]

    def half_of(ref, p):
        return ref.at[:, :, 128 * p : 128 * p + 128]

    def opposite(p):
        return [
            remote(unit(p, xn, yn, cc), half_of(av.at[i], p), s1.at[p, i], r1.at[p, i], xs)
            for i, cc in enumerate((c, cn))
        ]

    def beside(p):
        return [
            remote(unit(p, xn, y, c), half_of(bv.at[0], p), s1.at[p, 2], r1.at[p, 2], xs),
            remote(unit(p, xn, y, cn), half_of(bv.at[1], p), s1.at[p, 3], r1.at[p, 3], xo),
        ]

    def sibling(p):
        return remote(unit(p, x, y, cn), half_of(cv, p), s1.at[p, 4], r1.at[p, 4], core)

    def across(p):
        return [
            remote(
                half_of(sv.at[i], p), half_of(acv.at[i], p), s1.at[p, 5 + i], r1.at[p, 5 + i], to
            )
            for i, to in enumerate((ys, yo))
        ]

    def weight_start(p):
        block_grad(p, xn, yn)
        for copy in opposite(p):
            copy.start()
        block_grad(p, xn, y)
        for copy in beside(p):
            copy.start()
        block_grad(p, x, yn)
        block_grad(p, x, y)
        sibling(p).start()

    def weight_across(p):
        for i, cc in enumerate((c, cn)):
            opposite(p)[i].wait_recv()
            mine, came, dst = unit(p, x, yn, cc), half_of(av.at[i], p), half_of(sv.at[i], p)
            for j in range(3):
                add_rows(dst.at[j], mine.at[j], came.at[j])
            across(p)[i].start()

    blocks = [y * 2 + c, y * 2 + cn, yn * 2 + c, yn * 2 + cn]

    def down(p, q):
        return remote(
            half_of(sums.at[q], p), half_of(zv.at[q], p), zs.at[p, q], zr.at[p, q],
            dev(z - 1, x, y, c),
        )

    def weight_chain(p):
        for q in range(4):
            if q == 0:
                beside(p)[0].wait_recv()
                parts = [unit(p, x, y, c), half_of(bv.at[0], p)]
            elif q == 1:
                sibling(p).wait_recv()
                beside(p)[1].wait_recv()
                parts = [half_of(cv, p), half_of(bv.at[1], p)]
            else:
                across(p)[q - 2].wait_recv()
                parts = [half_of(acv.at[q - 2], p)]
            total_ref, came = half_of(sums.at[q], p), half_of(zv.at[q], p)

            @pl.when(z < 3)
            def _():
                down(p, q).wait_recv()

            @pl.when(z == 3)
            def _():
                for j in range(3):
                    add_rows(total_ref.at[j], *[part.at[j] for part in parts])
                down(p, q).start()

            @pl.when((z == 1) | (z == 2))
            def _():
                for j in range(3):
                    add_rows(total_ref.at[j], came.at[j], *[part.at[j] for part in parts])
                down(p, q).start()

            @pl.when(z == 0)
            def _():
                for j in range(3):
                    total = came[j].astype(f32)
                    for part in parts:
                        total = total + part[j].astype(f32)
                    at = 64 - 2 * s + 8 * j + 2 * blocks[q] + p
                    ext[pl.ds(at, 128, stride=24), :] = total

    def step(t, _):
        p = t // 4
        i = t - 4 * p
        at = pl.ds(pl.multiple_of(i * BLOCK, BLOCK), BLOCK)
        lanes = pl.ds(pl.multiple_of(p * 128, 128), 128)

        @pl.when(i == 0)
        def _():
            dk[...] = jnp.zeros_like(dk)
            dv[...] = jnp.zeros_like(dv)

        query_grad = attend_back_rows(
            i, q_ref[at, lanes], grads[at, lanes], a_ref[at, lanes], l_ref[p, :, at],
            k_ref.at[:, lanes], v_ref.at[:, lanes], dk, dv,
        )
        q_ref[at, lanes] = turn_back(query_grad, cos_ref[at, :], sin_ref[at, :])

        @pl.when(i == 3)
        def _():
            finish_keys(
                dk, dv, cos_ref, sin_ref, k_ref.at[:, lanes], v_ref.at[:, lanes]
            )

        @pl.when(t == 3)
        def _():
            for copy in loads[7:]:
                copy.wait()
            weight_start(0)

        @pl.when(t == 4)
        def _():
            weight_across(0)

        @pl.when((z > 0) & (t == 8 - z))
        def _():
            weight_chain(0)

        @pl.when(t != 4)
        def _():
            pump(2 + t - t // 5, 0)

        k = t - 2 * z

        @pl.when((z < 3) & (k >= 0) & (k < CHUNKS))
        def _():
            up_step(k)

        return 0

    lax.fori_loop(0, 8, step, 0)
    residual = [
        pltpu.make_async_copy(
            rg_hbm.at[:, 128 * i : 128 * i + 128],
            (dk, dv)[i // 4].at[512 * (i % 4) : 512 * (i % 4) + 512],
            rgs.at[i],
        )
        for i in range(8)
    ]
    for copy in residual:
        copy.start()
    weight_start(1)
    half = 256

    def rows(yy, cc, k):
        return normed.at[pl.ds(pl.multiple_of((yy * 2 + cc) * 512 + k * half, half), half)]

    order = [(yn, cn), (yn, c), (y, cn), (y, c)]

    def row_load(n):
        yy, cc = order[n // 2]
        at = pl.ds(pl.multiple_of((yy * 2 + cc) * 512 + n % 2 * half, half), half)
        return pltpu.make_async_copy(hid_hbm.at[at], hid.at[n % 2], hsems.at[n])

    for n in range(2):
        row_load(n).start()
    nsum[...] = jnp.zeros_like(nsum)
    gain = nrm_ref[0:1, :]

    def row_grad(m):
        yy, cc = order[m]
        for k in range(2):
            n = 2 * m + k
            row_load(n).wait()
            at = pl.ds(pl.multiple_of((yy * 2 + cc) * 512 + k * half, half), half)
            total = lax.dot_general(q_ref[at, :], wq[0], NT, preferred_element_type=f32)
            for j in range(1, 3):
                total = total + lax.dot_general(
                    d_refs[j][at, :], wq[j], NT, preferred_element_type=f32
                )
            normed[at, :] = total.astype(bf)
            unit_rows, _ = unit_of(hid[k].astype(f32))
            nsum[0] += fold(total * unit_rows)
            nsum[1] += fold(total)
            if n < 6:
                row_load(n + 2).start()

    far = [remote(rows(yn, cn, k), nc.at[1, k], s2.at[0, k], r2.at[0, k], core) for k in range(2)]
    near = [remote(rows(y, cn, k), nc.at[0, k], s2.at[1, k], r2.at[1, k], core) for k in range(2)]
    row_grad(0)
    for copy in far:
        copy.start()
    row_grad(1)
    later = []

    def row_across(k):
        far[k].wait_recv()

        def add_far(q, _):
            at = pl.ds(pl.multiple_of(q * 32, 32), 32)
            here = rows(yn, c, k).at[at]
            add_rows(here, here, nc.at[1, k, at])
            return 0

        lax.fori_loop(0, half // 32, add_far, 0)
        copy = remote(rows(yn, c, k), ny.at[k], s2.at[2, k], r2.at[2, k], ys)
        copy.start()
        later.append(copy)

    row_across(0)
    weight_across(1)
    pump(9, 0)
    row_across(1)

    @pl.when(z == 3)
    def _():
        weight_chain(1)

    row_grad(2)
    for copy in near:
        copy.start()
    row_grad(3)
    pump(10, 0)

    @pl.when(z == 0)
    def _():
        weight_chain(0)

    @pl.when(z < 3)
    def _():
        weight_chain(1)

    nsum_ref_rows = jnp.sum(nsum[...], axis=1)
    hsum = nland.at[s]
    hsum[0:2, :] = nsum_ref_rows
    hsum[2:8, :] = nsum_ref[2:8, :]
    norm_send = remote(hsum, hsum, ms.at[0], mr.at[s], (7, 3))

    @pl.when(s != 31)
    def _():
        norm_send.start()

    lax.fori_loop(11, steps, pump, 0)

    @pl.when(z == 3)
    def _():
        for k in range(CHUNKS):
            up_step(k)

    base = 64 - 2 * s

    def place(src, first, count, apart):
        for j in range(apart):
            for k in range(8):
                ext[pl.ds(base + 8 * (first + j) + k, count, stride=8 * apart), :] = own_ref[
                    src + j * count : src + (j + 1) * count, 128 * k : 128 * k + 128
                ]

    @pl.when((s == 8) | (s == 9) | (s >= 22))
    def _():
        place(0, 0, 384, 1)

    @pl.when(s == 10)
    def _():
        place(0, 0, 256, 1)
        place(256, 256, 32, 4)

    @pl.when((s >= 11) & (s <= 20))
    def _():
        place(0, 0, 96, 4)

    @pl.when(s == 21)
    def _():
        place(0, 0, 32, 4)
        place(128, 128, 256, 1)

    hsend[...] = ext[0:64, :]
    halo = remote(hsend, hal, hsem.at[0], hsem.at[1], linear(prv))
    halo.start()
    for copy in residual:
        copy.wait()
    for k in range(2):
        near[k].wait_recv()
        later[k].wait_recv()
        at = pl.ds(pl.multiple_of(me * 512 + k * half, half), half)
        to = slice(k * half, k * half + half)
        total = normed[at, :].astype(f32) + nc[0, k].astype(f32) + ny[k].astype(f32)
        unit_rows, inverse = unit_of(hid[k].astype(f32))
        into = into_norm(total, unit_rows, inverse, gain)
        for i in range(8):
            lanes = slice(128 * i, 128 * i + 128)
            first = 512 * (i % 4) + k * half
            ig_ref[to, lanes] = ((dk, dv)[i // 4][first : first + half] + into[:, lanes]).astype(bf)

    def hear(i, _):
        o = lax.rem(s + i, 32)
        remote(st_ref, sland.at[o], qs.at[0], qr.at[o], core).wait_recv()
        return 0

    lax.fori_loop(1, 32, hear, 0)
    sland[pl.ds(s, 1)] = st_ref[...].reshape(1, 8, 128)
    sto_ref[...] = jnp.sum(sland[...], axis=0)
    halo.wait()

    @pl.when(s != 31)
    def _():
        row = lax.broadcasted_iota(jnp.int32, (64, 128), 0)
        end = slice(NATURAL, NATURAL + 64)
        ext[end, :] = jnp.where(row >= 64 - 2 * (s + 1), hal[...], ext[end, :])

    @pl.when(s == 31)
    def _():
        def gather(i, total):
            remote(nland.at[i], nland.at[i], ms.at[0], mr.at[i], core).wait_recv()
            return total + nland[i]

        total = lax.fori_loop(0, 31, gather, nland[31])
        for k in range(8):
            ext[pl.ds(base + 8 * 384 + k, 8, stride=8), :] = total[:, 128 * k : 128 * k + 128]

    out_ref[...] = ext[64 : 64 + NATURAL, :]
    for copy in far + near + later:
        copy.wait_send()
    for p in range(2):
        for copy in opposite(p) + beside(p) + [sibling(p)] + across(p):
            copy.wait_send()

    @pl.when(z > 0)
    def _():
        for p in range(2):
            for q in range(4):
                down(p, q).wait_send()

    @pl.when(z < 3)
    def _():
        for k in range(CHUNKS):
            up(k).wait_send()

    def told(i, _):
        tell(i).wait_send()
        return 0

    lax.fori_loop(1, 32, told, 0)

    @pl.when(s != 31)
    def _():
        norm_send.wait_send()

    finish()


BACKWARD_X = 48


def backward(*operands):
    shape = jax.ShapeDtypeStruct
    room = pltpu.VMEM
    unit = (3, 128, 256)
    return pl.pallas_call(
        backward_kernel,
        out_shape=(shape((NATURAL, 128), f32), shape((512, D), bf), shape((8, 128), f32)),
        in_specs=[ANY, VM] + [ANY] * 5 + [VM] + [ANY] * 6 + [VM] * 3,
        out_specs=(VM,) * 3,
        scratch_shapes=[
            room((2048, 256), bf), room((2048, 128), f32), room((2048, 128), f32),
            room((2048, 256), bf), room((2048, 256), bf), room((2048, 256), bf),
            room((2048, 256), f32), room((2048, 128), f32), room((2048, 128), f32),
            room((2048, D), bf), room((2, 256, D), bf), room((3, D, 256), bf),
            room((SHARD, D), f32), room((3, D, 256), bf), room((2, 8, D), f32),
            room((64 + NATURAL + 6, 128), f32), room((64, 128), f32), room((64, 128), f32),
            room((2,) + unit, bf), room((2,) + unit, bf), room(unit, bf), room((2,) + unit, bf),
            room((4,) + unit, bf), room((4,) + unit, bf), room((2,) + unit, bf),
            room((2, 2, 256, D), bf), room((2, 256, D), bf),
            room((32, 8, D), f32), room((32, 8, 128), f32),
            room((CHUNKS, CHUNK, D), bf),
            DMA((9,)), DMA((8,)), DMA((8,)), DMA((CHUNKS,)), DMA((CHUNKS,)),
            DMA((2, 7)), DMA((2, 7)), DMA((3, 2)), DMA((3, 2)), DMA((2, 4)), DMA((2, 4)),
            DMA((1,)), DMA((32,)), DMA((32,)), DMA((32,)), DMA((2,)),
            *reduce_rooms(2, True, BACKWARD_X),
        ],
        compiler_params=params_for(2, 63),
    )(*operands)


ROWS = 128
GELU_A = math.sqrt(2.0 / math.pi)
GELU_B = 0.044715


def mean_of(values):
    return jnp.mean(values, axis=-1, keepdims=True)


def unit_of(values):
    center = values - mean_of(values)
    inverse = lax.rsqrt(mean_of(center * center) + EPSILON)
    return center * inverse, inverse


def into_norm(grads, unit, inverse, gain):
    scaled = grads * gain
    return inverse * (scaled - mean_of(scaled) - unit * mean_of(scaled * unit))


def fold(values):
    total = values[0:8]
    for at in range(8, values.shape[0], 8):
        total = total + values[at : at + 8]
    return total


def up_pieces(j):
    pieces = [(D + 32 * j, 0, 32)]
    pieces += [(D + 128 + 384 * i + 96 * j, 32 + 96 * i, 96) for i in range(10)]
    pieces.append((D + 3968 + 32 * j, 992, 32))
    return pieces


def dense_kernel(
    lines, a_ref, h_ref, c_ref, scale_ref, n_ref, w_ref, col_ref,
    o_ref, rg_ref, all_ref, gw_ref, ns_ref, sq_ref, part_ref,
    wo, wu, wd, branch, lowered, entered, act, slope, lgrad, stage, sums,
    ws, ups, gs, *rooms,
):
    tokens = a_ref.shape[0]
    residual, egrad = rg_ref, lowered
    start = finish = reduce_start = reduce_finish = lambda: None
    pump = reduce_pump = lambda i, _: 0
    steps = reduce_count = 0
    if lines:
        z, x, y, c = coords()
        ag_ref, ts, tr, own_sem, *rooms = rooms
        sems, rooms = rooms[:3], rooms[3:]

        def source(k):
            return col_ref.at[pl.ds(pl.multiple_of(k * CHUNK, CHUNK), CHUNK)]

        def down_rows(zz, xx, yy, cc, k, low=0, count=CHUNK):
            s = xx * 4 + yy * 2 + cc
            return wd.at[pl.ds(pl.multiple_of(D + s * SHARD + k * CHUNK + low, 16), count)]

        start, _, _, pump, steps, finish = gather_steps(
            down_rows, lambda r: 3, 1, None, source, False, 48, *sems
        )
        reduce_start, reduce_pump, reduce_count, reduce_finish = reduce_steps(
            functools.partial(shard_rows, gw_ref, 8), (3,), False, DENSE_X,
            lambda k: part_ref.at[pl.ds(pl.multiple_of(k * CHUNK, CHUNK), CHUNK)], *rooms
        )
        bar = pltpu.get_barrier_semaphore()
        for device in (dev(z, 1 - x, y, c), dev(z, x, 1 - y, c), dev(z, x, y, 1 - c)):
            greet(bar, device)
        greet(bar, dev(z, x, 1 - y, 1 - c))
        pl.semaphore_wait(bar, 4)
    else:
        ag_ref = all_ref
        part_ref[...] = jnp.zeros_like(part_ref)
    pieces = tokens // ROWS
    load_o = pltpu.make_async_copy(w_ref.at[0:D], wo, ws.at[0])
    loads_d = [
        pltpu.make_async_copy(
            w_ref.at[5 * D + D * j : 6 * D + D * j], wd.at[D * j : D * j + D], ws.at[1 + j]
        )
        for j in range(1 if lines else 4)
    ]
    loads_u = [
        [
            pltpu.make_async_copy(
                w_ref.at[src : src + count], wu.at[j, to : to + count], ups.at[j, i]
            )
            for i, (src, to, count) in enumerate(up_pieces(j))
        ]
        for j in range(4)
    ]
    load_o.start()
    for j in range(4):
        for copy in loads_u[j]:
            copy.start()
    for copy in loads_d:
        copy.start()
    start()
    sums[...] = jnp.zeros_like(sums)
    width = 1024

    def columns(t):
        return pl.ds(pl.multiple_of(t * width, width), width)

    def over_columns(body, count=D // width):
        def go(t, _):
            body(columns(t))
            return 0

        lax.fori_loop(0, count, go, 0)

    def over_rows(body):
        def go(t, _):
            body(pl.ds(pl.multiple_of(t * ROWS, ROWS), ROWS))
            return 0

        lax.fori_loop(0, pieces, go, 0)

    load_o.wait()

    def branch_step(at):
        branch[:, at] = jnp.dot(a_ref[...], wo[:, at], preferred_element_type=f32)

    over_columns(branch_step)

    def enter_step(at):
        values = branch[at, :]
        unit, _ = unit_of(values)
        res = h_ref[at, :].astype(f32) + unit * n_ref[2:3, :] + n_ref[3:4, :]
        residual[at, :] = res
        unit, _ = unit_of(res)
        entered[at, :] = (unit * n_ref[4:5, :] + n_ref[5:6, :]).astype(bf)
        sums[0] += fold(values * values)

    over_rows(enter_step)
    pump(2, 0)

    for j in range(4):
        for copy in loads_u[j]:
            copy.wait()

        def lift_step(at):
            lifted = jnp.dot(entered[...], wu[j, :, at], preferred_element_type=f32)
            square = lifted * lifted
            tanh = jnp.tanh(lifted * (GELU_A + (GELU_A * GELU_B) * square))
            half = 0.5 + 0.5 * tanh
            act[j, :, at] = (lifted * half).astype(bf)
            slope[j, :, at] = half + lifted * (0.5 - 0.5 * tanh * tanh) * (
                GELU_A + (3.0 * GELU_A * GELU_B) * square
            )

        over_columns(lift_step)
        pump(3 + j, 0)
    lax.fori_loop(7, steps, pump, 0)
    finish()
    for copy in loads_d:
        copy.wait()

    def lower_step(at):
        total = jnp.dot(act[0], wd[0:D, at], preferred_element_type=f32)
        for j in range(1, 4):
            total = total + jnp.dot(act[j], wd[D * j : D * j + D, at], preferred_element_type=f32)
        lowered[:, at] = total

    over_columns(lower_step)
    scale = scale_ref[0, 0]

    def out_step(at):
        values = lowered[at, :]
        unit, inverse = unit_of(values)
        o_ref[at, :] = (residual[at, :] + unit * n_ref[6:7, :] + n_ref[7:8, :]).astype(bf)
        upstream = c_ref[at, :].astype(f32) * scale
        lgrad[at, :] = into_norm(upstream, unit, inverse, n_ref[6:7, :]).astype(bf)
        sums[1] += fold(values * values)
        sums[2] += fold(upstream * unit)
        sums[3] += fold(upstream)

    over_rows(out_step)

    def store(buffer, j, slot):
        return [
            pltpu.make_async_copy(
                stage.at[buffer, to : to + count], gw_ref.at[src : src + count], gs.at[slot, i]
            )
            for i, (src, to, count) in enumerate(up_pieces(j))
        ]

    def store_block(buffer, first, slot):
        return [pltpu.make_async_copy(stage.at[buffer], gw_ref.at[first : first + D], gs.at[slot, 0])]

    pending = {}

    def reuse(buffer):
        for copy in pending.pop(buffer, []):
            copy.wait()

    def issue(buffer, copies):
        for copy in copies:
            copy.start()
        pending[buffer] = copies

    for n, j in enumerate((1, 2, 3, 0)):
        buffer = n % 2
        reuse(buffer)

        def down_step(at):
            stage[buffer, at, :] = lax.dot_general(
                act[j, :, at], lgrad[...], TN, preferred_element_type=f32
            ).astype(bf)

        over_columns(down_step)
        issue(buffer, store_block(buffer, 5 * D + D * j, buffer))
        if n == 2:
            reuse(1)
            reuse(0)
            reduce_start()
    reduce_pump(0, 0)
    for j in range(4):

        def slope_step(at):
            grads = lax.dot_general(
                lgrad[...], wd[D * j : D * j + D, :], NT, preferred_element_type=f32
            )
            act[j, :, at] = (grads * slope[j, :, at]).astype(bf)

        over_columns(slope_step)
        if j % 2 == 0:
            reduce_pump(1 + j // 2, 0)

    def enter_back_step(at):
        total = lax.dot_general(act[0], wu[0, at, :], NT, preferred_element_type=f32)
        for j in range(1, 4):
            total = total + lax.dot_general(act[j], wu[j, at, :], NT, preferred_element_type=f32)
        egrad[:, at] = total

    over_columns(enter_back_step)
    reduce_pump(3, 0)

    def branch_back_step(at):
        grads = egrad[at, :]
        upstream = c_ref[at, :].astype(f32) * scale
        unit, inverse = unit_of(residual[at, :])
        res_grad = upstream + into_norm(grads, unit, inverse, n_ref[4:5, :])
        rg_ref[at, :] = res_grad
        sums[4] += fold(grads * unit)
        sums[5] += fold(grads)
        unit, inverse = unit_of(branch[at, :])
        lgrad[at, :] = into_norm(res_grad, unit, inverse, n_ref[2:3, :]).astype(bf)
        sums[6] += fold(res_grad * unit)
        sums[7] += fold(res_grad)

    over_rows(branch_back_step)
    reduce_pump(4, 0)

    def attended_step(at):
        ag_ref[:, at] = lax.dot_general(
            lgrad[...], wo[at, :], NT, preferred_element_type=f32
        ).astype(bf)

    over_columns(attended_step)
    if lines:
        me, starts, arrivals = swap_copies(
            lambda owner: ag_ref.at[:, pl.ds(pl.multiple_of(owner * 256, 256), 256)],
            lambda owner: all_ref.at[pl.ds(pl.multiple_of(owner * 512, 512), 512)],
            ts, tr, 0,
        )
        own = pltpu.make_async_copy(
            ag_ref.at[:, pl.ds(pl.multiple_of(me * 256, 256), 256)],
            all_ref.at[pl.ds(pl.multiple_of(me * 512, 512), 512)],
            own_sem,
        )
        for copy in starts + [own]:
            copy.start()
    for j in range(4):
        buffer = j % 2
        reuse(buffer)

        def up_step(at):
            stage[buffer, :, at] = lax.dot_general(
                entered[...], act[j, :, at], TN, preferred_element_type=f32
            ).astype(bf)

        over_columns(up_step)
        issue(buffer, store(buffer, j, buffer))
        if j == 1:
            reduce_pump(5, 0)
    reuse(0)

    def out_grad_step(at):
        stage[0, at, :] = lax.dot_general(
            a_ref[:, at], lgrad[...], TN, preferred_element_type=f32
        ).astype(bf)

    over_columns(out_grad_step)
    issue(0, store_block(0, 0, 0))
    order = [None, None, 6, 7, 4, 5, 2, 3]
    for row, source in enumerate(order):
        if source is None:
            ns_ref[row : row + 1, :] = jnp.zeros((1, D), f32)
        else:
            ns_ref[row : row + 1, :] = jnp.sum(sums[source], axis=0, keepdims=True)
    lane = lax.broadcasted_iota(jnp.int32, (8, 128), 1)
    row = lax.broadcasted_iota(jnp.int32, (8, 128), 0)
    told = jnp.zeros((8, 128), f32)
    for t in range(2):
        told = jnp.where((lane == t) & (row == 0), jnp.sum(sums[t]), told)
    sq_ref[...] = told
    reuse(0)
    reuse(1)
    if lines:
        own.wait()
        for copy in arrivals:
            copy.wait_recv()
        for copy in starts:
            copy.wait_send()
    reduce_finish()


DENSE_X = 64


def dense(lines, attended, hidden, cotangent, scale, norm_rows, weights, column):
    tokens = attended.shape[0]
    shape = jax.ShapeDtypeStruct
    room = pltpu.VMEM
    return pl.pallas_call(
        functools.partial(dense_kernel, lines),
        out_shape=(
            shape((tokens, D), bf), shape((tokens, D), f32),
            shape((2048, 256) if lines else (tokens, D), bf),
            shape((9 * D, D), bf), shape((8, D), f32), shape((8, 128), f32), shape((SHARD, D), bf),
        ),
        in_specs=[VM, VM, VM, pl.BlockSpec(memory_space=pltpu.SMEM), VM, ANY, ANY],
        out_specs=(VM, VM, ANY if lines else VM, ANY, VM, VM, VM),
        scratch_shapes=[
            room((D, D), bf), room((4, D, D), bf), room((4 * D, D), bf),
            room((tokens, D), f32), room((tokens, D), f32),
            room((tokens, D), bf), room((4, tokens, D), bf), room((4, tokens, D), f32),
            room((tokens, D), bf), room((2, D, D), bf),
            room((8, 8, D), f32), DMA((5,)), DMA((4, 12)), DMA((2, 12)),
            *(
                [room((tokens, D), bf), DMA((3,)), DMA((3,)), DMA]
                + gather_sems(1)
                + reduce_rooms(1, False, DENSE_X)
                if lines
                else []
            ),
        ],
        compiler_params=params_for(5 if lines else None, 62),
    )(attended, hidden, cotangent, scale, norm_rows, weights, column)


def norm_forward(values, gain_row, shift_row):
    center = values - jnp.mean(values, axis=-1, keepdims=True)
    spread = jnp.mean(center * center, axis=-1, keepdims=True)
    inverse = lax.rsqrt(spread + EPSILON)
    unit_rows = center * inverse
    return (unit_rows * gain_row + shift_row, unit_rows, inverse)


def norm_backward(grad_rows, unit_rows, inverse, gain_row):
    scaled = grad_rows * gain_row
    first_mean = jnp.mean(scaled, axis=-1, keepdims=True)
    second_mean = jnp.mean(scaled * unit_rows, axis=-1, keepdims=True)
    return inverse * (scaled - first_mean - unit_rows * second_mean)


def norm_sums(grad_rows, unit_rows):
    return jnp.sum(grad_rows * unit_rows, axis=0), jnp.sum(grad_rows, axis=0)


def up_from_shards(rows):
    pieces = [rows[:128].reshape(1, 4, 32, D), rows[128:3968].reshape(10, 4, 96, D)]
    pieces.append(rows[3968:].reshape(1, 4, 32, D))
    return jnp.concatenate(
        [piece.transpose(0, 2, 1, 3).reshape(-1, FF) for piece in pieces], axis=0
    )


def up_to_shards(grad):
    pieces = [(grad[:32], 1, 32), (grad[32:992], 10, 96), (grad[992:], 1, 32)]
    return jnp.concatenate(
        [
            piece.reshape(blocks, rows, 4, D).transpose(0, 2, 1, 3).reshape(-1, D)
            for piece, blocks, rows in pieces
        ],
        axis=0,
    )


def dots(a, b, contract):
    return lax.dot_general(a, b, ((contract[:1], contract[1:]), ((), ())), preferred_element_type=f32)


def per_device(lines, hidden_in, params, cotangent, source_ids, corpus_weight, positions):
    devices = lax.axis_size(("dp", "fsdp"))
    width = lax.axis_size("fsdp")
    hidden = hidden_in[0]
    tokens = hidden.shape[0]
    place = lax.axis_index("fsdp")
    if lines:
        (
            others, column, hidden_all, w_qkv, norm_rows, cosine, sine,
            normed_all, queries, keys, values, attended_all, logs, attended,
        ) = forward(
            params.reshape(NATURAL, 128),
            hidden,
            jnp.pad(positions.astype(f32).reshape(4, 128), ((0, 4), (0, 0))),
        )
    else:
        whole = lax.all_gather(params, ("dp", "fsdp"), axis=0, tiled=True)
        ends = [0, 3 * D * D, 4 * D * D, 4 * D * D + D * FF, 4 * D * D + 2 * D * FF]
        parts = [whole[a:b] for a, b in zip(ends, ends[1:])]
        w_qkv = lax.dynamic_index_in_dim(
            parts[0].reshape(D, 3, width, D // width).transpose(1, 2, 0, 3), place, 1, False
        )
        others = jnp.concatenate(
            [parts[1].reshape(D, D), up_to_shards(parts[2].reshape(D, FF)), parts[3].reshape(FF, D)]
        )
        norm_rows = whole[ends[-1] :].reshape(8, D).astype(f32)
        hidden_all = lax.all_gather(hidden, "fsdp", axis=0, tiled=True)
        places = lax.all_gather(positions[0].astype(f32), "fsdp", axis=0, tiled=True)
        lane = jnp.arange(128) % 64
        frequency = jnp.exp((lane % 32).astype(f32) * (-2.0 * math.log(10000.0) / HEAD_DIM))
        angles = places[:, None] * frequency
        cosine = jnp.cos(angles)
        sine = jnp.where(lane < 32, -1.0, 1.0) * jnp.sin(angles)
        normed_all, queries, keys, values = project(hidden_all, norm_rows, w_qkv, cosine, sine)
        attended_all, attended_low, logs = attend(queries, keys, values)
        attended = swap(attended_low, width, True, 4)
        column = jnp.zeros((SHARD, D), bf)
    source_table = jnp.arange(corpus_weight.shape[0], dtype=jnp.int32)
    row_scale = jnp.sum(jnp.where(source_ids[0] == source_table, corpus_weight, 0.0))
    output, residual_grad, attended_grad, weight_grads, norm_part, squares, part = dense(
        lines, attended, hidden, cotangent[0], row_scale.reshape(1, 1), norm_rows, others, column
    )
    if lines:
        param_grads, input_grad, squares = backward(
            weight_grads, part, attended_grad, queries, keys, values, attended_all, logs,
            cosine, sine, normed_all, hidden_all, w_qkv, residual_grad, norm_rows, norm_part, squares,
        )
        param_grads = param_grads.reshape(-1)
    else:
        grads_all = swap(attended_grad, width, False, 6)
        mixed_grad = attend_back(
            queries, keys, values, grads_all, attended_all, logs, cosine, sine
        )
        grad_qkv = jnp.stack([dots(normed_all, part, (0, 0)) for part in mixed_grad])
        normed_part = sum(dots(part, w_qkv[j], (1, 1)) for j, part in enumerate(mixed_grad))
        _, unit_all, _ = norm_forward(hidden_all.astype(f32), norm_rows[0], norm_rows[1])
        norm_part = jnp.concatenate(
            [jnp.stack(norm_sums(normed_part, unit_all)), norm_part[2:]], axis=0
        )
        spread = jnp.zeros((3, width, D, D // width), bf)
        spread = lax.dynamic_update_slice_in_dim(spread, grad_qkv.astype(bf)[:, None], place, 1)
        parts = (
            spread.transpose(2, 0, 1, 3),
            weight_grads[:D],
            up_from_shards(weight_grads[D : 5 * D]),
            weight_grads[5 * D :],
            norm_part.astype(bf),
        )
        flat = jnp.concatenate([part.reshape(-1) for part in parts])
        param_grads = lax.psum_scatter(flat, ("dp", "fsdp"), scatter_dimension=0, tiled=True)
        param_grads = param_grads.astype(f32)
        normed_grad = lax.psum_scatter(normed_part, "fsdp", scatter_dimension=0, tiled=True)
        squares = lax.psum(squares, ("dp", "fsdp"))
        _, normed_unit, normed_inverse = norm_forward(
            hidden.astype(f32), norm_rows[0], norm_rows[1]
        )
        into_input = norm_backward(normed_grad, normed_unit, normed_inverse, norm_rows[0])
        input_grad = (residual_grad + into_input).astype(bf)
    statistics = squares[0, :2] / (devices * tokens * D)
    return (output[None], input_grad[None], param_grads, statistics)


def solution(mesh):
    lines = (mesh.shape["dp"], mesh.shape["fsdp"]) == (8, 4)
    in_specs = (
        P("dp", "fsdp", None),
        P(("dp", "fsdp")),
        P("dp", "fsdp", None),
        P("dp"),
        P(),
        P("dp", "fsdp"),
    )
    out_specs = (P("dp", "fsdp", None), P("dp", "fsdp", None), P(("dp", "fsdp")), P())
    return jax.shard_map(
        functools.partial(per_device, lines),
        mesh=mesh,
        in_specs=in_specs,
        out_specs=out_specs,
        check_vma=False,
    )
```

```python
import functools
import math

import jax
import jax.numpy as jnp
from jax import lax
from jax.experimental import pallas as pl
from jax.experimental.pallas import tpu as pltpu
from jax.sharding import PartitionSpec as P

D = 1024
HEADS = 16
HEAD_DIM = 64
FF = 4096
EPSILON = 1e-05
MASKED = -1e30
SCALE = 1.0 / math.sqrt(HEAD_DIM)
LOG2E = 1.4426950408889634

MESH = pl.DeviceIdType.MESH
bf = jnp.bfloat16
f32 = jnp.float32
SHARD = 384
NATURAL = 3074
MIB = 2**20

VM = pl.BlockSpec(memory_space=pltpu.VMEM)
ANY = pl.BlockSpec(memory_space=pl.ANY)
DMA = pltpu.SemaphoreType.DMA


def params_for(collective=None, mib=48):
    if collective is None:
        return pltpu.CompilerParams(vmem_limit_bytes=mib * MIB)
    return pltpu.CompilerParams(
        collective_id=collective, has_side_effects=True, vmem_limit_bytes=mib * MIB
    )


def coords():
    dp, fs = lax.axis_index("dp"), lax.axis_index("fsdp")
    return dp // 2, lax.rem(dp, 2), fs // 2, lax.rem(fs, 2)


def dev(z, x, y, c):
    return (z * 2 + x, y * 2 + c)


def linear(i):
    return (i // 4, lax.rem(i, 4))


def remote(src, dst, send, recv, to):
    return pltpu.make_async_remote_copy(
        src_ref=src, dst_ref=dst, send_sem=send, recv_sem=recv, device_id=to, device_id_type=MESH
    )


def greet(bar, device):
    pl.semaphore_signal(bar, inc=1, device_id=device, device_id_type=MESH)


def meet_neighbours(z, x, y, c, plane, more=0):
    bar = pltpu.get_barrier_semaphore()
    for device in plane:
        greet(bar, device)

    @pl.when(z < 3)
    def _():
        greet(bar, dev(z + 1, x, y, c))

    @pl.when(z > 0)
    def _():
        greet(bar, dev(z - 1, x, y, c))

    line = jnp.where(z < 3, 1, 0) + jnp.where(z > 0, 1, 0)
    pl.semaphore_wait(bar, len(plane) + line + more)


def add_rows(dst, *srcs):
    if dst.dtype == bf and len(srcs) == 2:
        dst[...] = srcs[0][...] + srcs[1][...]
        return
    total = srcs[0][...].astype(f32)
    for part in srcs[1:]:
        total = total + part[...].astype(f32)
    dst[...] = total.astype(dst.dtype)


def add_tiles(dst, rows, *srcs):
    for at in range(0, rows, 16):
        add_rows(dst.at[at : at + 16], *[part.at[at : at + 16] for part in srcs])


CHUNKS = 4
AHEAD = 2
EARLY = 1
CHUNK = SHARD // CHUNKS


def shard_rows(ref, base, zz, xx, yy, cc, k, low=0, count=CHUNK):
    s = (zz * 2 + xx) * 4 + yy * 2 + cc
    return ref.at[pl.ds(pl.multiple_of((s - base) * SHARD + k * CHUNK + low, 16), count)]


def gather_sems(planes):
    return [DMA((11, planes * CHUNKS)), DMA((11, planes * CHUNKS)), DMA((CHUNKS + 1,))]


def gather_steps(rows, plane_of, planes, own, source, line, over_x, ss, rs, ls):
    z, x, y, c = coords()
    xn, yn, cn = 1 - x, 1 - y, 1 - c
    to_x, to_y, to_core = dev(z, xn, y, c), dev(z, x, yn, c), dev(z, x, y, cn)
    lag, core_lag = 2, 4
    units = planes * CHUNKS
    ZU, ZD, XO, YO, CO, XD, YD, CX, CY, CXD, CYD = range(11)
    rest = CHUNK - over_x

    def unit(i):
        r = i // CHUNKS
        return plane_of(r), i - r * CHUNKS, i

    def send(kind, i):
        zz, k, q = unit(i)
        ref, to = {
            ZU: lambda: (rows(zz, x, y, c, k), dev(z + 1, x, y, c)),
            ZD: lambda: (rows(zz, x, y, c, k), dev(z - 1, x, y, c)),
            XO: lambda: (rows(zz, x, y, c, k), to_x),
            YO: lambda: (rows(zz, x, y, c, k), to_y),
            CO: lambda: (rows(zz, x, y, c, k), to_core),
            YD: lambda: (rows(zz, xn, y, c, k, over_x, rest), to_y),
            XD: lambda: (rows(zz, x, yn, c, k, 0, over_x), to_x),
            CX: lambda: (rows(zz, xn, y, c, k), to_core),
            CY: lambda: (rows(zz, x, yn, c, k), to_core),
            CXD: lambda: (rows(zz, xn, yn, c, k, 0, over_x), to_core),
            CYD: lambda: (rows(zz, xn, yn, c, k, over_x, rest), to_core),
        }[kind]()
        slot = (zz - 1) * CHUNKS + k if line else k
        src = source(k) if kind in (XO, YO, CO) and not line else ref
        return remote(src, ref, ss.at[kind, slot], rs.at[kind, slot], to)

    def arrive(kind, i):
        zz, k, q = unit(i)
        ref = {
            ZU: lambda: rows(zz, x, y, c, k),
            ZD: lambda: rows(zz, x, y, c, k),
            XO: lambda: rows(zz, xn, y, c, k),
            YO: lambda: rows(zz, x, yn, c, k),
            XD: lambda: rows(zz, xn, yn, c, k, 0, over_x),
            YD: lambda: rows(zz, xn, yn, c, k, over_x, rest),
            CO: lambda: rows(zz, x, y, cn, k),
            CX: lambda: rows(zz, xn, y, cn, k),
            CY: lambda: rows(zz, x, yn, cn, k),
            CXD: lambda: rows(zz, xn, yn, cn, k, 0, over_x),
            CYD: lambda: rows(zz, xn, yn, cn, k, over_x, rest),
        }[kind]()
        slot = (zz - 1) * CHUNKS + k if line else k
        remote(ref, ref, ss.at[kind, slot], rs.at[kind, slot], to_core).wait_recv()

    def local(k_plane):
        zz = k_plane
        return [
            pltpu.make_async_copy(source(k), rows(zz, x, y, c, k), ls.at[k]) for k in range(CHUNKS)
        ]

    def start():
        if line:

            @pl.when(own(z))
            def _():
                for copy in local(z):
                    copy.start()
                for copy in local(z):
                    copy.wait()
                for k in range(CHUNKS):
                    send(ZD, k).start()
                    if k < EARLY:
                        send(ZU, k).start()
        else:
            for copy in local(plane_of(0)):
                copy.start()
            for i in range(units):
                for kind in (XO, YO, CO):
                    send(kind, i).start()

    def late_up():
        @pl.when(own(z))
        def _():
            for k in range(EARLY, CHUNKS):
                send(ZU, k).start()

    def early(i):
        zz, _, _ = unit(i)
        if line:

            @pl.when(zz < z)
            def _():
                arrive(ZU, i)

            @pl.when(zz > z)
            def _():
                arrive(ZD, i)

            @pl.when((zz < z) & (z < 3))
            def _():
                send(ZU, i).start()

            @pl.when((zz > z) & (z > 0))
            def _():
                send(ZD, i).start()

        for kind in (XO, CO):
            send(kind, i).start()

    def step(i, _):
        if line:

            @pl.when((i < units) & (i >= EARLY))
            def _():
                early(i)

            @pl.when(i < units)
            def _():
                send(YO, i).start()

        j = i - lag

        @pl.when((j >= 0) & (j < units))
        def _():
            arrive(XO, j)
            send(YD, j).start()
            send(CX, j).start()
            arrive(YO, j)
            send(XD, j).start()
            send(CY, j).start()

        m = i - core_lag

        @pl.when(m >= 0)
        def _():
            arrive(XD, m)
            send(CXD, m).start()
            arrive(YD, m)
            send(CYD, m).start()

        return 0

    def finish():
        def one(i, _):
            zz, _, _ = unit(i)
            for kind in (CO, CX, CY, CXD, CYD):
                arrive(kind, i)
            for kind in (XO, YO, CO, YD, XD, CX, CY, CXD, CYD):
                send(kind, i).wait_send()
            if line:

                @pl.when((zz <= z) & (z < 3))
                def _():
                    send(ZU, i).wait_send()

                @pl.when((zz >= z) & (z > 0))
                def _():
                    send(ZD, i).wait_send()

            return 0

        lax.fori_loop(0, units, one, 0)
        if not line:
            for copy in local(plane_of(0)):
                copy.wait()

    return start, early, late_up, step, units + core_lag, finish


def reduce_steps(
    rows, planes, line, over_x, out, lb, cb, xb, yb, dxb, dyb, zub, zdb, ss, rs, cs, cr, ls
):
    z, x, y, c = coords()
    xn, yn, cn = 1 - x, 1 - y, 1 - c
    to_x, to_y, to_core = dev(z, xn, y, c), dev(z, x, yn, c), dev(z, x, y, cn)
    lag1, lag2, lag3, lag4 = 1, 2, 3, 4
    XS, YS, DXS, DYS, ZD, ZU = range(6)
    units = len(planes) * CHUNKS

    def unit(i):
        r = i // CHUNKS
        zz = planes[0] if len(planes) == 1 else planes[0] - r
        return zz, i - r * CHUNKS

    places = [(xn, yn), (xn, y), (x, yn), (x, y)]

    def load(i, p):
        zz, k = unit(i)
        xx, yy = places[p]
        return pltpu.make_async_copy(rows(zz, xx, yy, c, k), lb.at[i, p], ls.at[i, p])

    def to_sibling(i, p):
        zz, k = unit(i)
        xx, yy = places[p]
        return remote(rows(zz, xx, yy, cn, k), cb.at[i, p], cs.at[i, p], cr.at[i, p], to_core)

    def fetch(i, _):
        for p in range(4):
            load(i, p).start()
            to_sibling(i, p).start()
        return 0

    def start():
        lax.fori_loop(0, AHEAD, fetch, 0)

    def over(kind, src, dst, i, to):
        return remote(src, dst, ss.at[kind, i], rs.at[kind, i], to)

    def diag_x(i):
        return over(DXS, lb.at[i, 0, 0:over_x], dxb.at[i], i, to_x)

    def diag_y(i):
        return over(DYS, lb.at[i, 0, over_x:CHUNK], dyb.at[i], i, to_y)

    def whole_x(i):
        return over(XS, lb.at[i, 1], xb.at[i], i, to_x)

    def whole_y(i):
        return over(YS, lb.at[i, 2], yb.at[i], i, to_y)

    def down(i):
        return over(ZD, lb.at[i, 3], zub.at[i], i, dev(z - 1, x, y, c))

    def up(i):
        return over(ZU, lb.at[i, 3], zdb.at[i], i, dev(z + 1, x, y, c))

    def have(i, p):
        load(i, p).wait()
        to_sibling(i, p).wait_recv()

    def step(i, _):
        @pl.when(i + AHEAD < units)
        def _():
            fetch(i + AHEAD, 0)

        @pl.when(i < units)
        def _():
            have(i, 0)
            add_tiles(lb.at[i, 0], CHUNK, lb.at[i, 0], cb.at[i, 0])
            diag_x(i).start()
            diag_y(i).start()

        j = i - lag1

        @pl.when((j >= 0) & (j < units))
        def _():
            have(j, 1)
            have(j, 2)
            diag_y(j).wait_recv()
            diag_x(j).wait_recv()
            a, b = lb.at[j, 1], cb.at[j, 1]
            low, high = slice(0, over_x), slice(over_x, CHUNK)
            add_tiles(a.at[low], over_x, a.at[low], b.at[low])
            add_tiles(a.at[high], CHUNK - over_x, a.at[high], b.at[high], dyb.at[j])
            whole_x(j).start()
            a, b = lb.at[j, 2], cb.at[j, 2]
            add_tiles(a.at[low], over_x, a.at[low], b.at[low], dxb.at[j])
            add_tiles(a.at[high], CHUNK - over_x, a.at[high], b.at[high])
            whole_y(j).start()

        m = i - lag2

        @pl.when((m >= 0) & (m < units))
        def _():
            zz, k = unit(m)
            have(m, 3)
            whole_x(m).wait_recv()
            whole_y(m).wait_recv()
            parts = [lb.at[m, 3], cb.at[m, 3], xb.at[m], yb.at[m]]
            if not line:
                add_tiles(out(k), CHUNK, *parts)
                return

            @pl.when(z != zz)
            def _():
                add_tiles(lb.at[m, 3], CHUNK, *parts)

            @pl.when(z == 3)
            def _():
                down(m).start()

            @pl.when(z == 0)
            def _():
                up(m).start()

            @pl.when(z == zz)
            def _():
                add_tiles(out(k), CHUNK, *parts)

        if not line:
            return 0
        n = i - lag3

        @pl.when((n >= 0) & (n < units))
        def _():
            zz, _ = unit(n)

            @pl.when((z > zz) & (z < 3))
            def _():
                down(n).wait_recv()
                add_tiles(lb.at[n, 3], CHUNK, lb.at[n, 3], zub.at[n])
                down(n).start()

            @pl.when((z < zz) & (z > 0))
            def _():
                up(n).wait_recv()
                add_tiles(lb.at[n, 3], CHUNK, lb.at[n, 3], zdb.at[n])
                up(n).start()

        o = i - lag4

        @pl.when(o >= 0)
        def _():
            zz, k = unit(o)

            @pl.when(z == zz)
            def _():
                down(o).wait_recv()
                add_tiles(out(k), CHUNK, out(k), zub.at[o])
                up(o).wait_recv()
                add_tiles(out(k), CHUNK, out(k), zdb.at[o])

        return 0

    def finish():
        def one(i, _):
            zz, _ = unit(i)
            for p in range(4):
                to_sibling(i, p).wait_send()
            for copy in (diag_x(i), diag_y(i), whole_x(i), whole_y(i)):
                copy.wait_send()
            if line:

                @pl.when(z > zz)
                def _():
                    down(i).wait_send()

                @pl.when(z < zz)
                def _():
                    up(i).wait_send()

            return 0

        lax.fori_loop(0, units, one, 0)

    return start, step, units + (lag4 if line else lag2), finish


def reduce_rooms(planes, line, over_x):
    units = planes * CHUNKS

    def room(*shape):
        return pltpu.VMEM(shape + (D,), bf)

    lines = units if line else 1
    return [
        room(units, 4, CHUNK), room(units, 4, CHUNK),
        room(units, CHUNK), room(units, CHUNK),
        room(units, over_x), room(units, CHUNK - over_x),
        room(lines, CHUNK), room(lines, CHUNK),
        DMA((6, units)), DMA((6, units)), DMA((units, 4)), DMA((units, 4)), DMA((units, 4)),
    ]


def swap_kernel(n, to_tokens, a_ref, o_ref, ss, rs, ls):
    me = lax.axis_index("fsdp")
    bar = pltpu.get_barrier_semaphore()
    for i in range(1, n):
        pl.semaphore_signal(
            bar, inc=1, device_id={"fsdp": lax.rem(me + i, n)}, device_id_type=MESH
        )
    pl.semaphore_wait(bar, n - 1)
    tokens = (a_ref if to_tokens else o_ref).shape[0] // n
    width = (o_ref if to_tokens else a_ref).shape[1] // n

    def token_block(ref, owner):
        return ref.at[pl.ds(pl.multiple_of(owner * tokens, 16), tokens)]

    def head_block(ref, owner):
        return ref.at[:, pl.ds(pl.multiple_of(owner * width, 128), width)]

    take, put = (token_block, head_block) if to_tokens else (head_block, token_block)
    local = pltpu.make_async_copy(take(a_ref, me), put(o_ref, me), ls)
    local.start()
    copies = []
    for i in range(1, n):
        to = lax.rem(me + i, n)
        copy = pltpu.make_async_remote_copy(
            src_ref=take(a_ref, to), dst_ref=put(o_ref, me), send_sem=ss.at[i], recv_sem=rs.at[i],
            device_id={"fsdp": to}, device_id_type=MESH,
        )
        copy.start()
        copies.append(copy)
    for i in range(1, n):
        copies[i - 1].wait_send()
        ref = put(o_ref, lax.rem(me - i + n, n))
        pltpu.make_async_remote_copy(
            src_ref=ref, dst_ref=ref, send_sem=ss.at[i], recv_sem=rs.at[i],
            device_id={"fsdp": lax.rem(me + i, n)}, device_id_type=MESH,
        ).wait_recv()
    local.wait()


def swap(array, n, to_tokens, collective):
    rows, columns = array.shape
    shape = (rows // n, columns * n) if to_tokens else (rows * n, columns // n)
    return pl.pallas_call(
        functools.partial(swap_kernel, n, to_tokens),
        out_shape=jax.ShapeDtypeStruct(shape, bf),
        in_specs=[VM],
        out_specs=VM,
        scratch_shapes=[DMA((n,)), DMA((n,)), DMA],
        compiler_params=params_for(collective, 32),
    )(array)


def partner(values):
    width = values.shape[-1]
    lane = lax.broadcasted_iota(jnp.int32, values.shape, values.ndim - 1)
    after = pltpu.roll(values, width - 32, values.ndim - 1)
    before = pltpu.roll(values, 32, values.ndim - 1)
    return jnp.where(lane % 64 < 32, after, before)


def normed_rows(rows, n_ref):
    rows = rows.astype(f32)
    center = rows - jnp.mean(rows, axis=-1, keepdims=True)
    inverse = lax.rsqrt(jnp.mean(center * center, axis=-1, keepdims=True) + EPSILON)
    return (center * inverse * n_ref[0:1, :] + n_ref[1:2, :]).astype(bf)


def project_rows(normed, w_ref, cosine, sine):
    mixed = [jnp.dot(normed, w_ref[j], preferred_element_type=f32) for j in range(3)]
    for j in range(2):
        parts = [mixed[j][:, at : at + 128] for at in range(0, mixed[j].shape[1], 128)]
        parts = [part * cosine + partner(part) * sine for part in parts]
        mixed[j] = jnp.concatenate(parts, axis=1)
    return [part.astype(bf) for part in mixed]


def qkv_kernel(h_ref, n_ref, w_ref, c_ref, s_ref, *out_refs):
    normed = normed_rows(h_ref[...], n_ref)
    out_refs[0][...] = normed
    for ref, part in zip(out_refs[1:], project_rows(normed, w_ref, c_ref[...], s_ref[...])):
        ref[...] = part


def project(hidden, norm_rows, w_qkv, cosine, sine):
    tokens, width = hidden.shape[0], w_qkv.shape[2]
    block = 256
    rows = lambda w: pl.BlockSpec((block, w), lambda i: (i, 0))
    full = lambda a: pl.BlockSpec(a.shape, lambda i: (0,) * a.ndim)
    shape = jax.ShapeDtypeStruct
    return pl.pallas_call(
        qkv_kernel,
        grid=(tokens // block,),
        in_specs=[rows(D), full(norm_rows), full(w_qkv), rows(128), rows(128)],
        out_specs=[rows(D), rows(width), rows(width), rows(width)],
        out_shape=[shape((tokens, D), bf)] + [shape((tokens, width), bf)] * 3,
        compiler_params=params_for(),
    )(hidden, norm_rows, w_qkv, cosine, sine)


NT = (((1,), (1,)), ((), ()))
TN = (((0,), (0,)), ((), ()))
BLOCK = 512


def one_head(pair, h):
    lane = lax.broadcasted_iota(jnp.int32, pair.shape, 1)
    return jnp.where((lane < 64) if h == 0 else (lane >= 64), pair, jnp.zeros_like(pair))


def causal(scores, i, j):
    key = j * scores.shape[0] + lax.broadcasted_iota(jnp.int32, scores.shape, 0)
    query = i * scores.shape[1] + lax.broadcasted_iota(jnp.int32, scores.shape, 1)
    return jnp.where(key <= query, scores, MASKED)


def attend_rows(i, queries, k_ref, v_ref):
    heads = [one_head(queries, h) for h in range(2)]

    def block(j, carry, masked):
        at = pl.ds(pl.multiple_of(j * BLOCK, BLOCK), BLOCK)
        keys, values = k_ref[at, :], v_ref[at, :]
        out = []
        for h in range(2):
            peak, total, summed = carry[3 * h : 3 * h + 3]
            scores = lax.dot_general(keys, heads[h], NT, preferred_element_type=f32)
            scores = scores * (SCALE * LOG2E)
            if masked:
                scores = causal(scores, i, j)
            new_peak = jnp.maximum(peak, jnp.max(scores, axis=0, keepdims=True))
            weights = jnp.exp2(scores - new_peak)
            shrink = jnp.exp2(peak - new_peak)
            total = total * shrink + jnp.sum(weights, axis=0, keepdims=True)
            part = lax.dot_general(
                values[:, 64 * h : 64 * h + 64], weights.astype(bf), TN, preferred_element_type=f32
            )
            out += [new_peak, total, summed * shrink + part]
        return tuple(out)

    start = (
        jnp.full((1, BLOCK), MASKED, f32), jnp.zeros((1, BLOCK), f32), jnp.zeros((64, BLOCK), f32)
    ) * 2
    carry = lax.fori_loop(0, i, lambda j, carry: block(j, carry, False), start)
    peak0, total0, sum0, peak1, total1, sum1 = block(i, carry, True)
    out = jnp.concatenate([sum0 / total0, sum1 / total1], axis=0).T
    logs = jnp.concatenate([peak0 + jnp.log2(total0), peak1 + jnp.log2(total1)], axis=0)
    return out, logs


def attend_kernel(q_ref, k_ref, v_ref, o_ref, low_ref, l_ref):
    out, logs = attend_rows(pl.program_id(1), q_ref[...], k_ref, v_ref)
    o_ref[...] = out
    low_ref[...] = out.astype(bf)
    l_ref[...] = logs.reshape(1, 2, BLOCK)


def attend(queries, keys, values):
    tokens, width = queries.shape
    pairs = width // 128
    block = pl.BlockSpec((BLOCK, 128), lambda p, i: (i, p))
    full = pl.BlockSpec((tokens, 128), lambda p, i: (0, p))
    logs = pl.BlockSpec((1, 2, BLOCK), lambda p, i: (p, 0, i))
    shape = jax.ShapeDtypeStruct
    return pl.pallas_call(
        attend_kernel,
        grid=(pairs, tokens // BLOCK),
        in_specs=[block, full, full],
        out_specs=[block, block, logs],
        out_shape=[
            shape((tokens, width), f32), shape((tokens, width), bf), shape((pairs, 2, tokens), f32)
        ],
        compiler_params=params_for(),
    )(queries, keys, values)


def attend_back_rows(i, queries, grads, attended, logs, k_ref, v_ref, dk, dv):
    heads = [one_head(queries, h) for h in range(2)]
    grad_heads = [one_head(grads, h) for h in range(2)]
    both_heads = jnp.concatenate(heads, axis=0)
    both_grads = jnp.concatenate(grad_heads, axis=0)
    products = (attended * grads.astype(f32)).T
    dots = [jnp.sum(products[64 * h : 64 * h + 64], axis=0, keepdims=True) for h in range(2)]

    def block(j, sums, masked):
        at = pl.ds(pl.multiple_of(j * BLOCK, BLOCK), BLOCK)
        keys, values = k_ref[at, :], v_ref[at, :]
        weights, score_grads = [], []
        for h in range(2):
            scores = lax.dot_general(keys, heads[h], NT, preferred_element_type=f32)
            scores = scores * (SCALE * LOG2E)
            if masked:
                scores = causal(scores, i, j)
            prob = jnp.exp2(scores - logs[h : h + 1])
            prob_grad = lax.dot_general(values, grad_heads[h], NT, preferred_element_type=f32)
            score_grads.append((prob * (prob_grad - dots[h])).astype(bf))
            weights.append(prob.astype(bf))
        dv[at, :] += jnp.dot(
            jnp.concatenate(weights, axis=1), both_grads, preferred_element_type=f32
        )
        dk[at, :] += jnp.dot(
            jnp.concatenate(score_grads, axis=1), both_heads, preferred_element_type=f32
        )
        return tuple(
            sums[h] + lax.dot_general(score_grads[h], keys, TN, preferred_element_type=f32)
            for h in range(2)
        )

    zero = jnp.zeros((BLOCK, 128), f32)
    sums = lax.fori_loop(0, i, lambda j, sums: block(j, sums, False), (zero, zero))
    sums = block(i, sums, True)
    lane = lax.broadcasted_iota(jnp.int32, zero.shape, 1)
    return jnp.where(lane < 64, sums[0], sums[1]) * SCALE


def turn_back(grads, cosine, sine):
    return (grads * cosine - partner(grads) * sine).astype(bf)


def finish_keys(dk, dv, c_ref, s_ref, dk_ref, dv_ref):
    def turn(t, _):
        at = pl.ds(pl.multiple_of(t * 256, 256), 256)
        dk_ref[at, :] = turn_back(dk[at, :] * SCALE, c_ref[at, :], s_ref[at, :])
        dv_ref[at, :] = dv[at, :].astype(bf)
        return 0

    lax.fori_loop(0, dk.shape[0] // 256, turn, 0)


def attend_back_kernel(
    q_ref, k_ref, v_ref, g_ref, a_ref, l_ref, cq_ref, sq_ref, c_ref, s_ref,
    dq_ref, dk_ref, dv_ref, dk, dv,
):
    i = pl.program_id(1)

    @pl.when(i == 0)
    def _():
        dk[...] = jnp.zeros_like(dk)
        dv[...] = jnp.zeros_like(dv)

    query_grad = attend_back_rows(
        i, q_ref[...], g_ref[...], a_ref[...], l_ref[0], k_ref, v_ref, dk, dv
    )
    dq_ref[...] = turn_back(query_grad, cq_ref[...], sq_ref[...])

    @pl.when(i == pl.num_programs(1) - 1)
    def _():
        finish_keys(dk, dv, c_ref, s_ref, dk_ref, dv_ref)


def attend_back(queries, keys, values, grads, attended, logs, cosine, sine):
    tokens, width = queries.shape
    block = pl.BlockSpec((BLOCK, 128), lambda p, i: (i, p))
    full = pl.BlockSpec((tokens, 128), lambda p, i: (0, p))
    table_block = pl.BlockSpec((BLOCK, 128), lambda p, i: (i, 0))
    table = pl.BlockSpec((tokens, 128), lambda p, i: (0, 0))
    log_block = pl.BlockSpec((1, 2, BLOCK), lambda p, i: (p, 0, i))
    return pl.pallas_call(
        attend_back_kernel,
        grid=(width // 128, tokens // BLOCK),
        in_specs=[block, full, full, block, block, log_block, table_block, table_block, table, table],
        out_specs=[block, full, full],
        out_shape=[jax.ShapeDtypeStruct((tokens, width), bf)] * 3,
        scratch_shapes=[pltpu.VMEM((tokens, 128), f32), pltpu.VMEM((tokens, 128), f32)],
        compiler_params=params_for(),
    )(queries, keys, values, grads, attended, logs, cosine, sine, cosine, sine)


def swap_copies(take, put, ss, rs, base):
    z, x, y, c = coords()
    others = [(y, 1 - c), (1 - y, c), (1 - y, 1 - c)]
    me = y * 2 + c
    starts, arrivals = [], []
    for i, (yy, cc) in enumerate(others):
        starts.append(
            remote(take(yy * 2 + cc), put(me), ss.at[base + i], rs.at[base + i], dev(z, x, yy, cc))
        )
        ref = put(yy * 2 + cc)
        arrivals.append(remote(ref, ref, ss.at[base + i], rs.at[base + i], dev(z, x, yy, cc)))
    return me, starts, arrivals


def forward_kernel(
    p_ref, h_ref, pos_ref,
    g_ref, col_ref, hid_out, wq_out, nrm_ref, cos_out, sin_out,
    normed_out, q_out, k_out, v_out, o_out, l_ref, t_ref,
    ext, tail, units, can_ref, posall_ref, low,
    hid_ref, wq_ref, cos_ref, sin_ref, normed_ref, q_ref, k_ref, v_ref, o_ref,
    us, ur, hs, hr, ns, nr, ps, pr, keep_sem, ss, rs, ls, ts, tr, cs, cr, outs,
):
    keeps = [
        pltpu.make_async_copy(src, dst, outs.at[i])
        for i, (src, dst) in enumerate(
            [
                (hid_ref, hid_out), (wq_ref, wq_out), (cos_ref, cos_out), (sin_ref, sin_out),
                (normed_ref, normed_out), (q_ref, q_out), (k_ref, k_out), (v_ref, v_out),
                (o_ref, o_out),
            ]
        )
    ]
    z, x, y, c = coords()
    xn, yn, cn = 1 - x, 1 - y, 1 - c
    s = (z * 2 + x) * 4 + y * 2 + c
    f = y * 2 + c
    nxt, prv = lax.rem(s + 1, 32), lax.rem(s + 31, 32)
    core = dev(z, x, y, cn)
    xs, xo, ys, yo = dev(z, xn, y, c), dev(z, xn, y, cn), dev(z, x, yn, c), dev(z, x, yn, cn)
    bar = pltpu.get_barrier_semaphore()
    greet(bar, linear(nxt))
    greet(bar, linear(prv))

    @pl.when(s != 31)
    def _():
        greet(bar, (7, 3))

    ext[64 : 64 + NATURAL, :] = p_ref[...].astype(f32)
    tail[...] = ext[NATURAL : NATURAL + 64, :]
    more = 2 + jnp.where(s == 31, 31, 0)
    meet_neighbours(z, x, y, c, [core, xs, xo, ys, yo], more)
    halves, half = 4, 128

    def hidden_rows(owner, k):
        return hid_ref.at[pl.ds(pl.multiple_of(owner * 512 + k * half, 16), half)]

    def hidden_own(k):
        return h_ref.at[pl.ds(k * half, half)]

    over_y, over_core, over_both = yn * 2 + c, y * 2 + cn, yn * 2 + cn
    halo = remote(tail, ext.at[0:64], ns.at[0], nr.at[0], linear(nxt))
    halo.start()
    sent = []
    for i, to in enumerate([core, ys, yo]):
        sent.append(remote(pos_ref, posall_ref.at[f], ps.at[i], pr.at[i], to))
    for k in range(halves):
        sent.append(remote(hidden_own(k), hidden_rows(f, k), hs.at[1, k], hr.at[1, k], core))
    for copy in sent:
        copy.start()
    rows_over_y = [
        remote(hidden_own(k), hidden_rows(f, k), hs.at[0, k], hr.at[0, k], ys) for k in range(halves)
    ]
    sent += rows_over_y
    for k in range(halves):

        @pl.when(k <= z)
        def _():
            rows_over_y[k].start()

    hid_ref[pl.ds(pl.multiple_of(f * 512, 512), 512)] = h_ref[...]
    posall_ref[pl.ds(f, 1)] = pos_ref[...].reshape(1, 8, 128)
    halo.wait()
    base = 64 - 2 * s

    def lines(first, count, apart, k):
        return ext[pl.ds(base + 8 * first + k, count, stride=8 * apart), :].astype(bf)

    def order(to, first, count, apart):
        for j in range(apart):
            for k in range(8):
                can_ref[to + j * count : to + (j + 1) * count, 128 * k : 128 * k + 128] = lines(
                    first + j, count, apart, k
                )

    @pl.when(z == 0)
    def _():
        for j in range(3):
            for k in range(8):
                at = 128 * (k % 2)
                units[k // 2, j, :, at : at + 128] = lines(j, 128, 3, k)

    @pl.when((s == 8) | (s == 9) | (s >= 22))
    def _():
        order(0, 0, 384, 1)

    @pl.when(s == 10)
    def _():
        order(0, 0, 256, 1)
        order(256, 256, 32, 4)

    @pl.when((s >= 11) & (s <= 20))
    def _():
        order(0, 0, 96, 4)

    @pl.when(s == 21)
    def _():
        order(0, 0, 32, 4)
        order(128, 128, 256, 1)

    def norm_send(i):
        return remote(nrm_ref, nrm_ref, ns.at[1 + i], nr.at[1], linear(i))

    @pl.when(s == 31)
    def _():
        for k in range(8):
            nrm_ref[:, 128 * k : 128 * k + 128] = ext[pl.ds(base + 8 * 384 + k, 8, stride=8), :]

        def go(i, _):
            norm_send(i).start()
            return 0

        lax.fori_loop(0, 31, go, 0)

    def column(k):
        return col_ref.at[pl.ds(pl.multiple_of(k * CHUNK, CHUNK), CHUNK)]

    def down(k):
        return remote(column(k), column(k), cs.at[k], cr.at[k], dev(z - 1, x, y, c))

    keep = pltpu.make_async_copy(can_ref, col_ref, keep_sem)

    @pl.when(z == 3)
    def _():
        keep.start()
        keep.wait()

    def down_step(k):
        @pl.when(z < 3)
        def _():
            down(k).wait_recv()

        @pl.when(z > 0)
        def _():
            down(k).start()

    def arrive(ref, sem):
        remote(ref, ref, us.at[0, 0, 0], sem, core).wait_recv()

    for i, owner in enumerate([over_core, over_y, over_both]):
        arrive(posall_ref.at[owner], pr.at[i])

    def tables():
        lane = lax.broadcasted_iota(jnp.int32, (1, 128), 1) % 64
        turn = (lane % 32).astype(f32) * (-2.0 * math.log(10000.0) / HEAD_DIM)
        frequency = jnp.exp(turn)

        def one(t, _):
            row = posall_ref[t // 4, pl.ds(lax.rem(t, 4), 1), :]
            angles = jnp.broadcast_to(row, (128, 128)).T * frequency
            at = pl.ds(pl.multiple_of(t * 128, 128), 128)
            cos_ref[at, :] = jnp.cos(angles)
            sine = jnp.sin(angles)
            sin_ref[at, :] = jnp.where(lane < 32, -sine, sine)
            return 0

        lax.fori_loop(0, 16, one, 0)

    @pl.when(z >= 2)
    def _():
        tables()

    first = jnp.where(z >= 2, 2, 1)
    start, early, late_up, pump, steps, finish = gather_steps(
        functools.partial(shard_rows, g_ref, 8),
        lambda r: jnp.where(r == 0, first, 3 - first), 2,
        lambda zz: (zz == 1) | (zz == 2),
        lambda k: can_ref.at[k * CHUNK : k * CHUNK + CHUNK],
        True, FORWARD_X, ss, rs, ls,
    )
    start()

    @pl.when(z >= 1)
    def _():
        for i in range(EARLY):
            early(i)

    slots = [yn * 2 + c, yn * 2 + cn, y * 2 + cn, y * 2 + c]

    def target(xx, yy, cc, h):
        at = pl.multiple_of((xx * 4 + yy * 2 + cc) * 128 + 64 * h, 64)
        return wq_ref.at[:, pl.ds(at, 64)]

    def piece(q, h):
        return units.at[slots[q], :, 64 * h : 64 * h + 64]

    def up(q, h):
        return remote(piece(q, h), piece(q, h), us.at[0, q, h], ur.at[0, q, h], dev(z + 1, x, y, c))

    for q in range(4):
        for h in range(2):
            unit, mine = piece(q, h), target(x, y, c, h)

            @pl.when(z > 0)
            def _():
                arrive(unit, ur.at[0, q, h])

            @pl.when(z < 3)
            def _():
                up(q, h).start()

            if q == 0:
                out = [remote(unit, mine, us.at[1, 0, h], ur.at[1, 0, h], ys)]
            elif q == 1:
                out = [remote(unit, mine, us.at[1, 1, h], ur.at[1, 1, h], yo)]
            elif q == 2:
                out = [
                    remote(unit, mine, us.at[1, 2, h], ur.at[1, 2, h], xo),
                    remote(unit, mine, us.at[1, 3, h], ur.at[1, 3, h], core),
                ]
            else:
                out = [remote(unit, mine, us.at[2, 0, h], ur.at[2, 0, h], xs)]
                mine[...] = unit[...]
            for copy in out:
                copy.start()
            sent += out
    for k in range(halves):

        @pl.when(k > z)
        def _():
            rows_over_y[k].start()

    @pl.when(z == 3)
    def _():
        for k in range(CHUNKS):
            down_step(k)

    late_up()

    @pl.when(z == 0)
    def _():
        for i in range(EARLY):
            early(i)

    for h in range(2):
        for i, cc in enumerate((c, cn)):
            ref = target(x, yn, cc, h)
            arrive(ref, ur.at[1, i, h])
            copy = remote(ref, ref, us.at[2, 1 + i, h], ur.at[2, 1 + i, h], xs)
            copy.start()
            sent.append(copy)
    pump(0, 0)

    @pl.when(z < 2)
    def _():
        tables()

    @pl.when(s != 31)
    def _():
        arrive(nrm_ref, nr.at[1])

    def normalise(owner):
        def one(k, _):
            at = pl.ds(pl.multiple_of(owner * 512 + k * 256, 256), 256)
            normed_ref[at, :] = normed_rows(hid_ref[at, :], nrm_ref)
            return 0

        lax.fori_loop(0, 2, one, 0)

    normalise(f)
    for k in range(halves):
        arrive(hidden_rows(over_core, k), hr.at[1, k])
    normalise(over_core)
    for k in range(halves):
        ref = hidden_rows(over_y, k)
        arrive(ref, hr.at[0, k])
        copy = remote(ref, ref, hs.at[2, k], hr.at[2, k], core)
        copy.start()
        sent.append(copy)
    normalise(over_y)
    for k in range(halves):
        arrive(hidden_rows(over_both, k), hr.at[2, k])
    normalise(over_both)
    for h in range(2):
        arrive(target(xn, y, cn, h), ur.at[1, 2, h])
        arrive(target(x, y, cn, h), ur.at[1, 3, h])
        arrive(target(xn, y, c, h), ur.at[2, 0, h])
        arrive(target(xn, yn, c, h), ur.at[2, 1, h])
        arrive(target(xn, yn, cn, h), ur.at[2, 2, h])
    pump(1, 0)

    def project_step(t, _):
        at = pl.ds(pl.multiple_of(t * 256, 256), 256)
        parts = project_rows(normed_ref[at, :], wq_ref, cos_ref[at, :], sin_ref[at, :])
        for ref, part in zip((q_ref, k_ref, v_ref), parts):
            ref[at, :] = part

        @pl.when(lax.rem(t, 4) == 3)
        def _():
            pump(2 + t // 4, 0)

        return 0

    lax.fori_loop(0, 8, project_step, 0)
    for copy in keeps[:8]:
        copy.start()

    def take(p, owner):
        rows = pl.ds(pl.multiple_of(owner * 512, 512), 512)
        return low.at[rows, 128 * p : 128 * p + 128]

    def put(p, owner):
        return t_ref.at[:, pl.ds(pl.multiple_of(owner * 256 + 128 * p, 128), 128)]

    swaps = [
        swap_copies(functools.partial(take, p), functools.partial(put, p), ts, tr, 3 * p)
        for p in range(2)
    ]
    own_blocks = [
        pltpu.make_async_copy(take(p, f), put(p, f), outs.at[9 + p]) for p in range(2)
    ]

    def swap_start(p):
        for copy in swaps[p][1] + [own_blocks[p]]:
            copy.start()

    def attend_step(t, _):
        p = t // 4
        i = t - 4 * p
        at = pl.ds(pl.multiple_of(i * BLOCK, BLOCK), BLOCK)
        lanes = pl.ds(pl.multiple_of(p * 128, 128), 128)
        out, logs = attend_rows(i, q_ref[at, lanes], k_ref.at[:, lanes], v_ref.at[:, lanes])
        o_ref[at, lanes] = out
        low[at, lanes] = out.astype(bf)
        l_ref[p, :, at] = logs

        @pl.when(t == 3)
        def _():
            swap_start(0)

        @pl.when(i >= 1)
        def _():
            pump(3 + i + 3 * p, 0)

        k = t - 2 * (3 - z)

        @pl.when((z > 0) & (z < 3) & (k >= 0) & (k < CHUNKS))
        def _():
            down_step(k)

        return 0

    lax.fori_loop(0, 8, attend_step, 0)

    swap_start(1)
    keeps[8].start()
    lax.fori_loop(10, steps, pump, 0)

    @pl.when(z == 0)
    def _():
        for k in range(CHUNKS):
            down_step(k)

    for _, starts, arrivals in swaps:
        for copy in arrivals:
            copy.wait_recv()
        for copy in starts:
            copy.wait_send()
    for copy in sent:
        copy.wait_send()
    for copy in keeps + own_blocks:
        copy.wait()

    @pl.when(z < 3)
    def _():
        for q in range(4):
            for h in range(2):
                up(q, h).wait_send()

    @pl.when(s == 31)
    def _():
        def go(i, _):
            norm_send(i).wait_send()
            return 0

        lax.fori_loop(0, 31, go, 0)

    @pl.when(z > 0)
    def _():
        for k in range(CHUNKS):
            down(k).wait_send()

    finish()


FORWARD_X = 64


def forward(share, hidden, places):
    shape = jax.ShapeDtypeStruct
    return pl.pallas_call(
        forward_kernel,
        out_shape=(
            shape((16 * SHARD, D), bf), shape((SHARD, D), bf),
            shape((2048, D), bf), shape((3, D, 256), bf), shape((8, D), f32),
            shape((2048, 128), f32), shape((2048, 128), f32), shape((2048, D), bf),
            shape((2048, 256), bf), shape((2048, 256), bf), shape((2048, 256), bf),
            shape((2048, 256), f32), shape((2, 2, 2048), f32), shape((512, D), bf),
        ),
        in_specs=[VM] * 3,
        out_specs=(ANY,) * 4 + (VM,) + (ANY,) * 7 + (VM, ANY),
        scratch_shapes=[
            pltpu.VMEM((64 + NATURAL + 6, 128), f32),
            pltpu.VMEM((64, 128), f32),
            pltpu.VMEM((4, 3, 128, 256), bf),
            pltpu.VMEM((SHARD, D), bf),
            pltpu.VMEM((4, 8, 128), f32),
            pltpu.VMEM((2048, 256), bf),
            pltpu.VMEM((2048, D), bf),
            pltpu.VMEM((3, D, 256), bf),
            pltpu.VMEM((2048, 128), f32),
            pltpu.VMEM((2048, 128), f32),
            pltpu.VMEM((2048, D), bf),
            pltpu.VMEM((2048, 256), bf),
            pltpu.VMEM((2048, 256), bf),
            pltpu.VMEM((2048, 256), bf),
            pltpu.VMEM((2048, 256), f32),
            DMA((3, 4, 2)), DMA((3, 4, 2)), DMA((3, 4)), DMA((3, 4)),
            DMA((32,)), DMA((2,)), DMA((3,)), DMA((3,)), DMA,
            *gather_sems(2), DMA((6,)), DMA((6,)), DMA((CHUNKS,)), DMA((CHUNKS,)), DMA((11,)),
        ],
        compiler_params=params_for(0, 62),
    )(share, hidden, places)


def backward_kernel(
    gw_ref, part_ref, g_hbm, q_hbm, k_hbm, v_hbm, a_hbm, l_ref, cos_hbm, sin_hbm,
    normed_hbm, hid_hbm, wq_hbm, rg_hbm, nrm_ref, nsum_ref, st_ref,
    out_ref, ig_ref, sto_ref,
    grads, dk, dv, q_ref, k_ref, v_ref, a_ref, cos_ref, sin_ref, normed, hid, wq,
    own_ref, vg, nsum,
    ext, hal, hsend, av, bv, cv, acv, zv, sums, sv, nc, ny, nland, sland, land,
    lsem, hsems, rgs, cs, cr, s1, r1, s2, r2, zs, zr, ms, mr, qs, qr, hsem, *rooms,
):
    z, x, y, c = coords()
    xn, yn, cn = 1 - x, 1 - y, 1 - c
    s = (z * 2 + x) * 4 + y * 2 + c
    me = y * 2 + c
    core = dev(z, x, y, cn)
    xs, xo, ys, yo = dev(z, xn, y, c), dev(z, xn, y, cn), dev(z, x, yn, c), dev(z, x, yn, cn)
    prv = lax.rem(s + 31, 32)

    loads = [
        pltpu.make_async_copy(src, dst, lsem.at[i])
        for i, (src, dst) in enumerate(
            [
                (g_hbm, grads), (q_hbm, q_ref), (k_hbm, k_ref), (v_hbm, v_ref),
                (a_hbm, a_ref), (cos_hbm, cos_ref), (sin_hbm, sin_ref),
                (normed_hbm, normed), (wq_hbm, wq),
            ]
        )
    ]
    for copy in loads:
        copy.start()

    bar = pltpu.get_barrier_semaphore()

    def hello(i, _):
        greet(bar, linear(lax.rem(s + i, 32)))
        return 0

    lax.fori_loop(1, 32, hello, 0)
    pl.semaphore_wait(bar, 31)

    def owned(k):
        return own_ref.at[pl.ds(pl.multiple_of(k * CHUNK, CHUNK), CHUNK)]

    start, pump, steps, finish = reduce_steps(
        functools.partial(shard_rows, gw_ref, 8), (2, 1), True, BACKWARD_X, owned, *rooms
    )
    start()

    def tell(i):
        return remote(st_ref, sland.at[s], qs.at[i], qr.at[s], linear(lax.rem(s + i, 32)))

    def tell_all(i, _):
        tell(i).start()
        return 0

    lax.fori_loop(1, 32, tell_all, 0)

    def up(k):
        return remote(land.at[k], land.at[k], cs.at[k], cr.at[k], dev(z + 1, x, y, c))

    def part(k):
        return part_ref.at[pl.ds(pl.multiple_of(k * CHUNK, CHUNK), CHUNK)]

    def up_step(k):
        @pl.when(z > 0)
        def _():
            up(k).wait_recv()

        @pl.when(z == 0)
        def _():
            add_tiles(land.at[k], CHUNK, part(k))

        @pl.when((z > 0) & (z < 3))
        def _():
            add_tiles(land.at[k], CHUNK, part(k), land.at[k])

        @pl.when(z < 3)
        def _():
            up(k).start()

        @pl.when(z == 3)
        def _():
            add_tiles(owned(k), CHUNK, part(k), land.at[k])

    pump(0, 0)
    pump(1, 0)
    for copy in loads[:7]:
        copy.wait()

    d_refs = (q_ref, k_ref, v_ref)

    def block_grad(p, xx, yy):
        at = pl.ds(pl.multiple_of((xx * 2 + yy) * 256, 256), 256)
        lanes = slice(128 * p, 128 * p + 128)
        for j in range(3):
            vg[j, at, lanes] = lax.dot_general(
                normed[:, at], d_refs[j][:, lanes], TN, preferred_element_type=f32
            ).astype(bf)

    def unit(p, xx, yy, cc):
        at = pl.multiple_of((xx * 4 + yy * 2 + cc) * 128, 128)
        return vg.at[:, pl.ds(at, 128), 128 * p : 128 * p + 128]

    def half_of(ref, p):
        return ref.at[:, :, 128 * p : 128 * p + 128]

    def opposite(p):
        return [
            remote(unit(p, xn, yn, cc), half_of(av.at[i], p), s1.at[p, i], r1.at[p, i], xs)
            for i, cc in enumerate((c, cn))
        ]

    def beside(p):
        return [
            remote(unit(p, xn, y, c), half_of(bv.at[0], p), s1.at[p, 2], r1.at[p, 2], xs),
            remote(unit(p, xn, y, cn), half_of(bv.at[1], p), s1.at[p, 3], r1.at[p, 3], xo),
        ]

    def sibling(p):
        return remote(unit(p, x, y, cn), half_of(cv, p), s1.at[p, 4], r1.at[p, 4], core)

    def across(p):
        return [
            remote(
                half_of(sv.at[i], p), half_of(acv.at[i], p), s1.at[p, 5 + i], r1.at[p, 5 + i], to
            )
            for i, to in enumerate((ys, yo))
        ]

    def weight_start(p):
        block_grad(p, xn, yn)
        for copy in opposite(p):
            copy.start()
        block_grad(p, xn, y)
        for copy in beside(p):
            copy.start()
        block_grad(p, x, yn)
        block_grad(p, x, y)
        sibling(p).start()

    def weight_across(p):
        for i, cc in enumerate((c, cn)):
            opposite(p)[i].wait_recv()
            mine, came, dst = unit(p, x, yn, cc), half_of(av.at[i], p), half_of(sv.at[i], p)
            for j in range(3):
                add_rows(dst.at[j], mine.at[j], came.at[j])
            across(p)[i].start()

    blocks = [y * 2 + c, y * 2 + cn, yn * 2 + c, yn * 2 + cn]

    def down(p, q):
        return remote(
            half_of(sums.at[q], p), half_of(zv.at[q], p), zs.at[p, q], zr.at[p, q],
            dev(z - 1, x, y, c),
        )

    def weight_chain(p):
        for q in range(4):
            if q == 0:
                beside(p)[0].wait_recv()
                parts = [unit(p, x, y, c), half_of(bv.at[0], p)]
            elif q == 1:
                sibling(p).wait_recv()
                beside(p)[1].wait_recv()
                parts = [half_of(cv, p), half_of(bv.at[1], p)]
            else:
                across(p)[q - 2].wait_recv()
                parts = [half_of(acv.at[q - 2], p)]
            total_ref, came = half_of(sums.at[q], p), half_of(zv.at[q], p)

            @pl.when(z < 3)
            def _():
                down(p, q).wait_recv()

            @pl.when(z == 3)
            def _():
                for j in range(3):
                    add_rows(total_ref.at[j], *[part.at[j] for part in parts])
                down(p, q).start()

            @pl.when((z == 1) | (z == 2))
            def _():
                for j in range(3):
                    add_rows(total_ref.at[j], came.at[j], *[part.at[j] for part in parts])
                down(p, q).start()

            @pl.when(z == 0)
            def _():
                for j in range(3):
                    total = came[j].astype(f32)
                    for part in parts:
                        total = total + part[j].astype(f32)
                    at = 64 - 2 * s + 8 * j + 2 * blocks[q] + p
                    ext[pl.ds(at, 128, stride=24), :] = total

    def step(t, _):
        p = t // 4
        i = t - 4 * p
        at = pl.ds(pl.multiple_of(i * BLOCK, BLOCK), BLOCK)
        lanes = pl.ds(pl.multiple_of(p * 128, 128), 128)

        @pl.when(i == 0)
        def _():
            dk[...] = jnp.zeros_like(dk)
            dv[...] = jnp.zeros_like(dv)

        query_grad = attend_back_rows(
            i, q_ref[at, lanes], grads[at, lanes], a_ref[at, lanes], l_ref[p, :, at],
            k_ref.at[:, lanes], v_ref.at[:, lanes], dk, dv,
        )
        q_ref[at, lanes] = turn_back(query_grad, cos_ref[at, :], sin_ref[at, :])

        @pl.when(i == 3)
        def _():
            finish_keys(
                dk, dv, cos_ref, sin_ref, k_ref.at[:, lanes], v_ref.at[:, lanes]
            )

        @pl.when(t == 3)
        def _():
            for copy in loads[7:]:
                copy.wait()
            weight_start(0)

        @pl.when(t == 4)
        def _():
            weight_across(0)

        @pl.when((z > 0) & (t == 8 - z))
        def _():
            weight_chain(0)

        @pl.when(t != 4)
        def _():
            pump(2 + t - t // 5, 0)

        k = t - 2 * z

        @pl.when((z < 3) & (k >= 0) & (k < CHUNKS))
        def _():
            up_step(k)

        return 0

    lax.fori_loop(0, 8, step, 0)
    residual = [
        pltpu.make_async_copy(
            rg_hbm.at[:, 128 * i : 128 * i + 128],
            (dk, dv)[i // 4].at[512 * (i % 4) : 512 * (i % 4) + 512],
            rgs.at[i],
        )
        for i in range(8)
    ]
    for copy in residual:
        copy.start()
    weight_start(1)
    half = 256

    def rows(yy, cc, k):
        return normed.at[pl.ds(pl.multiple_of((yy * 2 + cc) * 512 + k * half, half), half)]

    order = [(yn, cn), (yn, c), (y, cn), (y, c)]

    def row_load(n):
        yy, cc = order[n // 2]
        at = pl.ds(pl.multiple_of((yy * 2 + cc) * 512 + n % 2 * half, half), half)
        return pltpu.make_async_copy(hid_hbm.at[at], hid.at[n % 2], hsems.at[n])

    for n in range(2):
        row_load(n).start()
    nsum[...] = jnp.zeros_like(nsum)
    gain = nrm_ref[0:1, :]

    def row_grad(m):
        yy, cc = order[m]
        for k in range(2):
            n = 2 * m + k
            row_load(n).wait()
            at = pl.ds(pl.multiple_of((yy * 2 + cc) * 512 + k * half, half), half)
            total = lax.dot_general(q_ref[at, :], wq[0], NT, preferred_element_type=f32)
            for j in range(1, 3):
                total = total + lax.dot_general(
                    d_refs[j][at, :], wq[j], NT, preferred_element_type=f32
                )
            normed[at, :] = total.astype(bf)
            unit_rows, _ = unit_of(hid[k].astype(f32))
            nsum[0] += fold(total * unit_rows)
            nsum[1] += fold(total)
            if n < 6:
                row_load(n + 2).start()

    far = [remote(rows(yn, cn, k), nc.at[1, k], s2.at[0, k], r2.at[0, k], core) for k in range(2)]
    near = [remote(rows(y, cn, k), nc.at[0, k], s2.at[1, k], r2.at[1, k], core) for k in range(2)]
    row_grad(0)
    for copy in far:
        copy.start()
    row_grad(1)
    later = []

    def row_across(k):
        far[k].wait_recv()

        def add_far(q, _):
            at = pl.ds(pl.multiple_of(q * 32, 32), 32)
            here = rows(yn, c, k).at[at]
            add_rows(here, here, nc.at[1, k, at])
            return 0

        lax.fori_loop(0, half // 32, add_far, 0)
        copy = remote(rows(yn, c, k), ny.at[k], s2.at[2, k], r2.at[2, k], ys)
        copy.start()
        later.append(copy)

    row_across(0)
    weight_across(1)
    pump(9, 0)
    row_across(1)

    @pl.when(z == 3)
    def _():
        weight_chain(1)

    row_grad(2)
    for copy in near:
        copy.start()
    row_grad(3)
    pump(10, 0)

    @pl.when(z == 0)
    def _():
        weight_chain(0)

    @pl.when(z < 3)
    def _():
        weight_chain(1)

    nsum_ref_rows = jnp.sum(nsum[...], axis=1)
    hsum = nland.at[s]
    hsum[0:2, :] = nsum_ref_rows
    hsum[2:8, :] = nsum_ref[2:8, :]
    norm_send = remote(hsum, hsum, ms.at[0], mr.at[s], (7, 3))

    @pl.when(s != 31)
    def _():
        norm_send.start()

    lax.fori_loop(11, steps, pump, 0)

    @pl.when(z == 3)
    def _():
        for k in range(CHUNKS):
            up_step(k)

    base = 64 - 2 * s

    def place(src, first, count, apart):
        for j in range(apart):
            for k in range(8):
                ext[pl.ds(base + 8 * (first + j) + k, count, stride=8 * apart), :] = own_ref[
                    src + j * count : src + (j + 1) * count, 128 * k : 128 * k + 128
                ]

    @pl.when((s == 8) | (s == 9) | (s >= 22))
    def _():
        place(0, 0, 384, 1)

    @pl.when(s == 10)
    def _():
        place(0, 0, 256, 1)
        place(256, 256, 32, 4)

    @pl.when((s >= 11) & (s <= 20))
    def _():
        place(0, 0, 96, 4)

    @pl.when(s == 21)
    def _():
        place(0, 0, 32, 4)
        place(128, 128, 256, 1)

    hsend[...] = ext[0:64, :]
    halo = remote(hsend, hal, hsem.at[0], hsem.at[1], linear(prv))
    halo.start()
    for copy in residual:
        copy.wait()
    for k in range(2):
        near[k].wait_recv()
        later[k].wait_recv()
        at = pl.ds(pl.multiple_of(me * 512 + k * half, half), half)
        to = slice(k * half, k * half + half)
        total = normed[at, :].astype(f32) + nc[0, k].astype(f32) + ny[k].astype(f32)
        unit_rows, inverse = unit_of(hid[k].astype(f32))
        into = into_norm(total, unit_rows, inverse, gain)
        for i in range(8):
            lanes = slice(128 * i, 128 * i + 128)
            first = 512 * (i % 4) + k * half
            ig_ref[to, lanes] = ((dk, dv)[i // 4][first : first + half] + into[:, lanes]).astype(bf)

    def hear(i, _):
        o = lax.rem(s + i, 32)
        remote(st_ref, sland.at[o], qs.at[0], qr.at[o], core).wait_recv()
        return 0

    lax.fori_loop(1, 32, hear, 0)
    sland[pl.ds(s, 1)] = st_ref[...].reshape(1, 8, 128)
    sto_ref[...] = jnp.sum(sland[...], axis=0)
    halo.wait()

    @pl.when(s != 31)
    def _():
        row = lax.broadcasted_iota(jnp.int32, (64, 128), 0)
        end = slice(NATURAL, NATURAL + 64)
        ext[end, :] = jnp.where(row >= 64 - 2 * (s + 1), hal[...], ext[end, :])

    @pl.when(s == 31)
    def _():
        def gather(i, total):
            remote(nland.at[i], nland.at[i], ms.at[0], mr.at[i], core).wait_recv()
            return total + nland[i]

        total = lax.fori_loop(0, 31, gather, nland[31])
        for k in range(8):
            ext[pl.ds(base + 8 * 384 + k, 8, stride=8), :] = total[:, 128 * k : 128 * k + 128]

    out_ref[...] = ext[64 : 64 + NATURAL, :]
    for copy in far + near + later:
        copy.wait_send()
    for p in range(2):
        for copy in opposite(p) + beside(p) + [sibling(p)] + across(p):
            copy.wait_send()

    @pl.when(z > 0)
    def _():
        for p in range(2):
            for q in range(4):
                down(p, q).wait_send()

    @pl.when(z < 3)
    def _():
        for k in range(CHUNKS):
            up(k).wait_send()

    def told(i, _):
        tell(i).wait_send()
        return 0

    lax.fori_loop(1, 32, told, 0)

    @pl.when(s != 31)
    def _():
        norm_send.wait_send()

    finish()


BACKWARD_X = 48


def backward(*operands):
    shape = jax.ShapeDtypeStruct
    room = pltpu.VMEM
    unit = (3, 128, 256)
    return pl.pallas_call(
        backward_kernel,
        out_shape=(shape((NATURAL, 128), f32), shape((512, D), bf), shape((8, 128), f32)),
        in_specs=[ANY, VM] + [ANY] * 5 + [VM] + [ANY] * 6 + [VM] * 3,
        out_specs=(VM,) * 3,
        scratch_shapes=[
            room((2048, 256), bf), room((2048, 128), f32), room((2048, 128), f32),
            room((2048, 256), bf), room((2048, 256), bf), room((2048, 256), bf),
            room((2048, 256), f32), room((2048, 128), f32), room((2048, 128), f32),
            room((2048, D), bf), room((2, 256, D), bf), room((3, D, 256), bf),
            room((SHARD, D), f32), room((3, D, 256), bf), room((2, 8, D), f32),
            room((64 + NATURAL + 6, 128), f32), room((64, 128), f32), room((64, 128), f32),
            room((2,) + unit, bf), room((2,) + unit, bf), room(unit, bf), room((2,) + unit, bf),
            room((4,) + unit, bf), room((4,) + unit, bf), room((2,) + unit, bf),
            room((2, 2, 256, D), bf), room((2, 256, D), bf),
            room((32, 8, D), f32), room((32, 8, 128), f32),
            room((CHUNKS, CHUNK, D), bf),
            DMA((9,)), DMA((8,)), DMA((8,)), DMA((CHUNKS,)), DMA((CHUNKS,)),
            DMA((2, 7)), DMA((2, 7)), DMA((3, 2)), DMA((3, 2)), DMA((2, 4)), DMA((2, 4)),
            DMA((1,)), DMA((32,)), DMA((32,)), DMA((32,)), DMA((2,)),
            *reduce_rooms(2, True, BACKWARD_X),
        ],
        compiler_params=params_for(2, 63),
    )(*operands)


ROWS = 128
GELU_A = math.sqrt(2.0 / math.pi)
GELU_B = 0.044715


def mean_of(values):
    return jnp.mean(values, axis=-1, keepdims=True)


def unit_of(values):
    center = values - mean_of(values)
    inverse = lax.rsqrt(mean_of(center * center) + EPSILON)
    return center * inverse, inverse


def into_norm(grads, unit, inverse, gain):
    scaled = grads * gain
    return inverse * (scaled - mean_of(scaled) - unit * mean_of(scaled * unit))


def fold(values):
    total = values[0:8]
    for at in range(8, values.shape[0], 8):
        total = total + values[at : at + 8]
    return total


def up_pieces(j):
    pieces = [(D + 32 * j, 0, 32)]
    pieces += [(D + 128 + 384 * i + 96 * j, 32 + 96 * i, 96) for i in range(10)]
    pieces.append((D + 3968 + 32 * j, 992, 32))
    return pieces


def dense_kernel(
    lines, a_ref, h_ref, c_ref, scale_ref, n_ref, w_ref, col_ref,
    o_hbm, rg_hbm, all_ref, gw_ref, ns_ref, sq_ref, part_ref,
    wo, wu, wd, branch, lowered, entered, act, slope, lgrad, stage, sums, o_ref, rg_ref,
    ws, ups, gs, outs, *rooms,
):
    tokens = a_ref.shape[0]
    residual, egrad = rg_ref, lowered
    keep_out = pltpu.make_async_copy(o_ref, o_hbm, outs.at[0])
    keep_grad = pltpu.make_async_copy(rg_ref, rg_hbm, outs.at[1])
    start = finish = reduce_start = reduce_finish = lambda: None
    pump = reduce_pump = lambda i, _: 0
    steps = reduce_count = 0
    if lines:
        z, x, y, c = coords()
        ag_ref, ts, tr, own_sem, *rooms = rooms
        sems, rooms = rooms[:3], rooms[3:]

        def source(k):
            return col_ref.at[pl.ds(pl.multiple_of(k * CHUNK, CHUNK), CHUNK)]

        def down_rows(zz, xx, yy, cc, k, low=0, count=CHUNK):
            s = xx * 4 + yy * 2 + cc
            return wd.at[pl.ds(pl.multiple_of(D + s * SHARD + k * CHUNK + low, 16), count)]

        start, _, _, pump, steps, finish = gather_steps(
            down_rows, lambda r: 3, 1, None, source, False, 48, *sems
        )
        reduce_start, reduce_pump, reduce_count, reduce_finish = reduce_steps(
            functools.partial(shard_rows, gw_ref, 8), (3,), False, DENSE_X,
            lambda k: part_ref.at[pl.ds(pl.multiple_of(k * CHUNK, CHUNK), CHUNK)], *rooms
        )
        bar = pltpu.get_barrier_semaphore()
        for device in (dev(z, 1 - x, y, c), dev(z, x, 1 - y, c), dev(z, x, y, 1 - c)):
            greet(bar, device)
        greet(bar, dev(z, x, 1 - y, 1 - c))
        pl.semaphore_wait(bar, 4)
    else:
        ag_ref = all_ref
        part_ref[...] = jnp.zeros_like(part_ref)
    pieces = tokens // ROWS
    load_o = pltpu.make_async_copy(w_ref.at[0:D], wo, ws.at[0])
    loads_d = [
        pltpu.make_async_copy(
            w_ref.at[5 * D + D * j : 6 * D + D * j], wd.at[D * j : D * j + D], ws.at[1 + j]
        )
        for j in range(1 if lines else 4)
    ]
    loads_u = [
        [
            pltpu.make_async_copy(
                w_ref.at[src : src + count], wu.at[j, to : to + count], ups.at[j, i]
            )
            for i, (src, to, count) in enumerate(up_pieces(j))
        ]
        for j in range(4)
    ]
    load_o.start()
    for j in range(4):
        for copy in loads_u[j]:
            copy.start()
    for copy in loads_d:
        copy.start()
    start()
    sums[...] = jnp.zeros_like(sums)
    width = 1024

    def columns(t):
        return pl.ds(pl.multiple_of(t * width, width), width)

    def over_columns(body, count=D // width):
        def go(t, _):
            body(columns(t))
            return 0

        lax.fori_loop(0, count, go, 0)

    def over_rows(body):
        def go(t, _):
            body(pl.ds(pl.multiple_of(t * ROWS, ROWS), ROWS))
            return 0

        lax.fori_loop(0, pieces, go, 0)

    load_o.wait()

    def branch_step(at):
        branch[:, at] = jnp.dot(a_ref[...], wo[:, at], preferred_element_type=f32)

    over_columns(branch_step)

    def enter_step(at):
        values = branch[at, :]
        unit, _ = unit_of(values)
        res = h_ref[at, :].astype(f32) + unit * n_ref[2:3, :] + n_ref[3:4, :]
        residual[at, :] = res
        unit, _ = unit_of(res)
        entered[at, :] = (unit * n_ref[4:5, :] + n_ref[5:6, :]).astype(bf)
        sums[0] += fold(values * values)

    over_rows(enter_step)
    pump(2, 0)

    for j in range(4):
        for copy in loads_u[j]:
            copy.wait()

        def lift_step(at):
            lifted = jnp.dot(entered[...], wu[j, :, at], preferred_element_type=f32)
            square = lifted * lifted
            tanh = jnp.tanh(lifted * (GELU_A + (GELU_A * GELU_B) * square))
            half = 0.5 + 0.5 * tanh
            act[j, :, at] = (lifted * half).astype(bf)
            slope[j, :, at] = half + lifted * (0.5 - 0.5 * tanh * tanh) * (
                GELU_A + (3.0 * GELU_A * GELU_B) * square
            )

        over_columns(lift_step)
        pump(3 + j, 0)
    lax.fori_loop(7, steps, pump, 0)
    finish()
    for copy in loads_d:
        copy.wait()

    def lower_step(at):
        total = jnp.dot(act[0], wd[0:D, at], preferred_element_type=f32)
        for j in range(1, 4):
            total = total + jnp.dot(act[j], wd[D * j : D * j + D, at], preferred_element_type=f32)
        lowered[:, at] = total

    over_columns(lower_step)
    scale = scale_ref[0, 0]

    def out_step(at):
        values = lowered[at, :]
        unit, inverse = unit_of(values)
        o_ref[at, :] = (residual[at, :] + unit * n_ref[6:7, :] + n_ref[7:8, :]).astype(bf)
        upstream = c_ref[at, :].astype(f32) * scale
        lgrad[at, :] = into_norm(upstream, unit, inverse, n_ref[6:7, :]).astype(bf)
        sums[1] += fold(values * values)
        sums[2] += fold(upstream * unit)
        sums[3] += fold(upstream)

    over_rows(out_step)
    keep_out.start()

    def store(buffer, j, slot):
        return [
            pltpu.make_async_copy(
                stage.at[buffer, to : to + count], gw_ref.at[src : src + count], gs.at[slot, i]
            )
            for i, (src, to, count) in enumerate(up_pieces(j))
        ]

    def store_block(buffer, first, slot):
        return [pltpu.make_async_copy(stage.at[buffer], gw_ref.at[first : first + D], gs.at[slot, 0])]

    pending = {}

    def reuse(buffer):
        for copy in pending.pop(buffer, []):
            copy.wait()

    def issue(buffer, copies):
        for copy in copies:
            copy.start()
        pending[buffer] = copies

    for n, j in enumerate((1, 2, 3, 0)):
        buffer = n % 2
        reuse(buffer)

        def down_step(at):
            stage[buffer, at, :] = lax.dot_general(
                act[j, :, at], lgrad[...], TN, preferred_element_type=f32
            ).astype(bf)

        over_columns(down_step)
        issue(buffer, store_block(buffer, 5 * D + D * j, buffer))
        if n == 2:
            reuse(1)
            reuse(0)
            reduce_start()
    reduce_pump(0, 0)
    for j in range(4):

        def slope_step(at):
            grads = lax.dot_general(
                lgrad[...], wd[D * j : D * j + D, :], NT, preferred_element_type=f32
            )
            act[j, :, at] = (grads * slope[j, :, at]).astype(bf)

        over_columns(slope_step)
        if j % 2 == 0:
            reduce_pump(1 + j // 2, 0)

    def enter_back_step(at):
        total = lax.dot_general(act[0], wu[0, at, :], NT, preferred_element_type=f32)
        for j in range(1, 4):
            total = total + lax.dot_general(act[j], wu[j, at, :], NT, preferred_element_type=f32)
        egrad[:, at] = total

    over_columns(enter_back_step)
    reduce_pump(3, 0)

    def branch_back_step(at):
        grads = egrad[at, :]
        upstream = c_ref[at, :].astype(f32) * scale
        unit, inverse = unit_of(residual[at, :])
        res_grad = upstream + into_norm(grads, unit, inverse, n_ref[4:5, :])
        rg_ref[at, :] = res_grad
        sums[4] += fold(grads * unit)
        sums[5] += fold(grads)
        unit, inverse = unit_of(branch[at, :])
        lgrad[at, :] = into_norm(res_grad, unit, inverse, n_ref[2:3, :]).astype(bf)
        sums[6] += fold(res_grad * unit)
        sums[7] += fold(res_grad)

    over_rows(branch_back_step)
    keep_grad.start()
    reduce_pump(4, 0)

    def attended_step(at):
        ag_ref[:, at] = lax.dot_general(
            lgrad[...], wo[at, :], NT, preferred_element_type=f32
        ).astype(bf)

    over_columns(attended_step)
    if lines:
        me, starts, arrivals = swap_copies(
            lambda owner: ag_ref.at[:, pl.ds(pl.multiple_of(owner * 256, 256), 256)],
            lambda owner: all_ref.at[pl.ds(pl.multiple_of(owner * 512, 512), 512)],
            ts, tr, 0,
        )
        own = pltpu.make_async_copy(
            ag_ref.at[:, pl.ds(pl.multiple_of(me * 256, 256), 256)],
            all_ref.at[pl.ds(pl.multiple_of(me * 512, 512), 512)],
            own_sem,
        )
        for copy in starts + [own]:
            copy.start()
    for j in range(4):
        buffer = j % 2
        reuse(buffer)

        def up_step(at):
            stage[buffer, :, at] = lax.dot_general(
                entered[...], act[j, :, at], TN, preferred_element_type=f32
            ).astype(bf)

        over_columns(up_step)
        issue(buffer, store(buffer, j, buffer))
        if j == 1:
            reduce_pump(5, 0)
    reuse(0)

    def out_grad_step(at):
        stage[0, at, :] = lax.dot_general(
            a_ref[:, at], lgrad[...], TN, preferred_element_type=f32
        ).astype(bf)

    over_columns(out_grad_step)
    issue(0, store_block(0, 0, 0))
    order = [None, None, 6, 7, 4, 5, 2, 3]
    for row, source in enumerate(order):
        if source is None:
            ns_ref[row : row + 1, :] = jnp.zeros((1, D), f32)
        else:
            ns_ref[row : row + 1, :] = jnp.sum(sums[source], axis=0, keepdims=True)
    lane = lax.broadcasted_iota(jnp.int32, (8, 128), 1)
    row = lax.broadcasted_iota(jnp.int32, (8, 128), 0)
    told = jnp.zeros((8, 128), f32)
    for t in range(2):
        told = jnp.where((lane == t) & (row == 0), jnp.sum(sums[t]), told)
    sq_ref[...] = told
    reuse(0)
    reuse(1)
    if lines:
        own.wait()
        for copy in arrivals:
            copy.wait_recv()
        for copy in starts:
            copy.wait_send()
    reduce_finish()
    keep_out.wait()
    keep_grad.wait()


DENSE_X = 64


def dense(lines, attended, hidden, cotangent, scale, norm_rows, weights, column):
    tokens = attended.shape[0]
    shape = jax.ShapeDtypeStruct
    room = pltpu.VMEM
    return pl.pallas_call(
        functools.partial(dense_kernel, lines),
        out_shape=(
            shape((tokens, D), bf), shape((tokens, D), f32),
            shape((2048, 256) if lines else (tokens, D), bf),
            shape((9 * D, D), bf), shape((8, D), f32), shape((8, 128), f32), shape((SHARD, D), bf),
        ),
        in_specs=[VM, VM, VM, pl.BlockSpec(memory_space=pltpu.SMEM), VM, ANY, ANY],
        out_specs=(ANY, ANY, ANY if lines else VM, ANY, VM, VM, VM),
        scratch_shapes=[
            room((D, D), bf), room((4, D, D), bf), room((4 * D, D), bf),
            room((tokens, D), f32), room((tokens, D), f32),
            room((tokens, D), bf), room((4, tokens, D), bf), room((4, tokens, D), f32),
            room((tokens, D), bf), room((2, D, D), bf),
            room((8, 8, D), f32), room((tokens, D), bf), room((tokens, D), f32),
            DMA((5,)), DMA((4, 12)), DMA((2, 12)), DMA((2,)),
            *(
                [room((tokens, D), bf), DMA((3,)), DMA((3,)), DMA]
                + gather_sems(1)
                + reduce_rooms(1, False, DENSE_X)
                if lines
                else []
            ),
        ],
        compiler_params=params_for(5 if lines else None, 62),
    )(attended, hidden, cotangent, scale, norm_rows, weights, column)


def norm_forward(values, gain_row, shift_row):
    center = values - jnp.mean(values, axis=-1, keepdims=True)
    spread = jnp.mean(center * center, axis=-1, keepdims=True)
    inverse = lax.rsqrt(spread + EPSILON)
    unit_rows = center * inverse
    return (unit_rows * gain_row + shift_row, unit_rows, inverse)


def norm_backward(grad_rows, unit_rows, inverse, gain_row):
    scaled = grad_rows * gain_row
    first_mean = jnp.mean(scaled, axis=-1, keepdims=True)
    second_mean = jnp.mean(scaled * unit_rows, axis=-1, keepdims=True)
    return inverse * (scaled - first_mean - unit_rows * second_mean)


def norm_sums(grad_rows, unit_rows):
    return jnp.sum(grad_rows * unit_rows, axis=0), jnp.sum(grad_rows, axis=0)


def up_from_shards(rows):
    pieces = [rows[:128].reshape(1, 4, 32, D), rows[128:3968].reshape(10, 4, 96, D)]
    pieces.append(rows[3968:].reshape(1, 4, 32, D))
    return jnp.concatenate(
        [piece.transpose(0, 2, 1, 3).reshape(-1, FF) for piece in pieces], axis=0
    )


def up_to_shards(grad):
    pieces = [(grad[:32], 1, 32), (grad[32:992], 10, 96), (grad[992:], 1, 32)]
    return jnp.concatenate(
        [
            piece.reshape(blocks, rows, 4, D).transpose(0, 2, 1, 3).reshape(-1, D)
            for piece, blocks, rows in pieces
        ],
        axis=0,
    )


def dots(a, b, contract):
    return lax.dot_general(a, b, ((contract[:1], contract[1:]), ((), ())), preferred_element_type=f32)


def per_device(lines, hidden_in, params, cotangent, source_ids, corpus_weight, positions):
    devices = lax.axis_size(("dp", "fsdp"))
    width = lax.axis_size("fsdp")
    hidden = hidden_in[0]
    tokens = hidden.shape[0]
    place = lax.axis_index("fsdp")
    if lines:
        (
            others, column, hidden_all, w_qkv, norm_rows, cosine, sine,
            normed_all, queries, keys, values, attended_all, logs, attended,
        ) = forward(
            params.reshape(NATURAL, 128),
            hidden,
            jnp.pad(positions.astype(f32).reshape(4, 128), ((0, 4), (0, 0))),
        )
    else:
        whole = lax.all_gather(params, ("dp", "fsdp"), axis=0, tiled=True)
        ends = [0, 3 * D * D, 4 * D * D, 4 * D * D + D * FF, 4 * D * D + 2 * D * FF]
        parts = [whole[a:b] for a, b in zip(ends, ends[1:])]
        w_qkv = lax.dynamic_index_in_dim(
            parts[0].reshape(D, 3, width, D // width).transpose(1, 2, 0, 3), place, 1, False
        )
        others = jnp.concatenate(
            [parts[1].reshape(D, D), up_to_shards(parts[2].reshape(D, FF)), parts[3].reshape(FF, D)]
        )
        norm_rows = whole[ends[-1] :].reshape(8, D).astype(f32)
        hidden_all = lax.all_gather(hidden, "fsdp", axis=0, tiled=True)
        places = lax.all_gather(positions[0].astype(f32), "fsdp", axis=0, tiled=True)
        lane = jnp.arange(128) % 64
        frequency = jnp.exp((lane % 32).astype(f32) * (-2.0 * math.log(10000.0) / HEAD_DIM))
        angles = places[:, None] * frequency
        cosine = jnp.cos(angles)
        sine = jnp.where(lane < 32, -1.0, 1.0) * jnp.sin(angles)
        normed_all, queries, keys, values = project(hidden_all, norm_rows, w_qkv, cosine, sine)
        attended_all, attended_low, logs = attend(queries, keys, values)
        attended = swap(attended_low, width, True, 4)
        column = jnp.zeros((SHARD, D), bf)
    source_table = jnp.arange(corpus_weight.shape[0], dtype=jnp.int32)
    row_scale = jnp.sum(jnp.where(source_ids[0] == source_table, corpus_weight, 0.0))
    output, residual_grad, attended_grad, weight_grads, norm_part, squares, part = dense(
        lines, attended, hidden, cotangent[0], row_scale.reshape(1, 1), norm_rows, others, column
    )
    if lines:
        param_grads, input_grad, squares = backward(
            weight_grads, part, attended_grad, queries, keys, values, attended_all, logs,
            cosine, sine, normed_all, hidden_all, w_qkv, residual_grad, norm_rows, norm_part, squares,
        )
        param_grads = param_grads.reshape(-1)
    else:
        grads_all = swap(attended_grad, width, False, 6)
        mixed_grad = attend_back(
            queries, keys, values, grads_all, attended_all, logs, cosine, sine
        )
        grad_qkv = jnp.stack([dots(normed_all, part, (0, 0)) for part in mixed_grad])
        normed_part = sum(dots(part, w_qkv[j], (1, 1)) for j, part in enumerate(mixed_grad))
        _, unit_all, _ = norm_forward(hidden_all.astype(f32), norm_rows[0], norm_rows[1])
        norm_part = jnp.concatenate(
            [jnp.stack(norm_sums(normed_part, unit_all)), norm_part[2:]], axis=0
        )
        spread = jnp.zeros((3, width, D, D // width), bf)
        spread = lax.dynamic_update_slice_in_dim(spread, grad_qkv.astype(bf)[:, None], place, 1)
        parts = (
            spread.transpose(2, 0, 1, 3),
            weight_grads[:D],
            up_from_shards(weight_grads[D : 5 * D]),
            weight_grads[5 * D :],
            norm_part.astype(bf),
        )
        flat = jnp.concatenate([part.reshape(-1) for part in parts])
        param_grads = lax.psum_scatter(flat, ("dp", "fsdp"), scatter_dimension=0, tiled=True)
        param_grads = param_grads.astype(f32)
        normed_grad = lax.psum_scatter(normed_part, "fsdp", scatter_dimension=0, tiled=True)
        squares = lax.psum(squares, ("dp", "fsdp"))
        _, normed_unit, normed_inverse = norm_forward(
            hidden.astype(f32), norm_rows[0], norm_rows[1]
        )
        into_input = norm_backward(normed_grad, normed_unit, normed_inverse, norm_rows[0])
        input_grad = (residual_grad + into_input).astype(bf)
    statistics = squares[0, :2] / (devices * tokens * D)
    return (output[None], input_grad[None], param_grads, statistics)


def solution(mesh):
    lines = (mesh.shape["dp"], mesh.shape["fsdp"]) == (8, 4)
    in_specs = (
        P("dp", "fsdp", None),
        P(("dp", "fsdp")),
        P("dp", "fsdp", None),
        P("dp"),
        P(),
        P("dp", "fsdp"),
    )
    out_specs = (P("dp", "fsdp", None), P("dp", "fsdp", None), P(("dp", "fsdp")), P())
    return jax.shard_map(
        functools.partial(per_device, lines),
        mesh=mesh,
        in_specs=in_specs,
        out_specs=out_specs,
        check_vma=False,
    )
```
